256 devices in a mesh: blk: 64 (over z, x, core), gz: 4 (over y).
Axes of the slice: x: 4, y: 4, z: 8, core: 2. Of those that a mesh axis runs over, the one named last changes fastest.
Arguments:
- sqrt_density: float32 [384, 64, 512], P('blk', None, 'gz'), may hold values from 0.25 to 4, as said below
- ion_charge: float32 [384, 64, 512], P('blk', None, 'gz'), may hold values from 0.2 to 2
- ion_potential: float32 [384, 64, 512], P('blk', None, 'gz'), may hold values from -6 to 6
- hartree_prev: float32 [384, 64, 512], P('blk', None, 'gz'), may hold values from -6 to 6
- hist_steps: float32 [8, 384, 64, 512], P(None, 'blk', None, 'gz'), may hold values from -16 to 16
- hist_changes: float32 [8, 384, 64, 512], P(None, 'blk', None, 'gz'), may hold values from -32 to 32
Outputs:
- new_density: float32 [384, 64, 512], P('blk', None, 'gz')
- hartree: float32 [384, 64, 512], P('blk', None, 'gz')
The draws below stay inside these ranges and needn't reach their ends.
Inputs may be any that keep to these rules, and one draw needn't show every extreme that they name: `sqrt_density`: positive everywhere.
All inputs are finite; a program needn't handle non-finite values.
Results may differ from the reference program's by a relative error of at most 0.006.
Values sent between devices are 32-bit elements; how exact they have to be, the bound alone decides.
No kernel may reach another device: no remote copies, remote signals or barrier semaphores. Data moves between devices by JAX's collectives and lax.ppermute only.
A program may use at most 128 MiB of HBM per device.

```python
import math
import jax
import jax.numpy as jnp
from jax import lax

NY = 64
ITERS = 4
HIST = 8
NX = 384
NZ = 512


def density_field(key):
    noise_key = jax.random.fold_in(key, 101)
    grid_shape = (NX, NY, NZ)
    x_ramp = lax.broadcasted_iota(jnp.float32, grid_shape, 0) / NX
    rough_part = jax.random.uniform(noise_key, grid_shape, jnp.float32, 0.3, 0.9)
    return rough_part * (1.0 + 2.0 * x_ramp)


def history_pair(key):
    density = density_field(key)
    hist_shape = (HIST, NX, NY, NZ)
    scales = jax.random.uniform(jax.random.fold_in(key, 102), (HIST, 1, 1, 1), jnp.float32, 0.3, 1.0)
    steps = scales * (density * density - 2.0)[None] + jax.random.uniform(jax.random.fold_in(key, 103), hist_shape, jnp.float32, -1.0, 1.0)
    rank_order = jax.random.permutation(jax.random.fold_in(key, 104), HIST).astype(jnp.float32)
    jitter = jax.random.uniform(jax.random.fold_in(key, 105), (HIST,), jnp.float32, 0.0, 1.0)
    slopes = -1.0 + 3.0 * (rank_order + jitter) / HIST
    changes = slopes[:, None, None, None] * steps + 0.5 * jax.random.uniform(jax.random.fold_in(key, 106), hist_shape, jnp.float32, -1.0, 1.0)
    return (steps, changes)


def draw_sqrt_density(key, part):
    return density_field(key)


def draw_hist_steps(key, part):
    return history_pair(key)[0]


def draw_hist_changes(key, part):
    return history_pair(key)[1]


def level_of(rng, extent, split, least, high):
    loudness, own = 1.0, jax.random.fold_in(rng, 6)
    for position, parts in split:
        draws = jnp.exp(jax.random.uniform(jax.random.fold_in(own, position), (parts,), jnp.float32, least / len(split), high / len(split)))
        loudness = loudness * jnp.repeat(draws, extent[position] // parts).reshape([-1 if axis == position else 1 for axis in range(len(extent))])
    return loudness


def scatter_about(own_key, extent, spread, reach, split=(), held_as=jnp.bfloat16):
    values = spread * jax.random.normal(own_key, extent, jnp.float32)
    if split:
        values = values * level_of(own_key, extent, split, -0.22, 0.18)
    return jnp.clip(values, -reach, reach).astype(held_as)


def setup_inputs(seed: int = 0) -> dict:
    arg_keys = jax.random.split(jax.random.key(seed), 7)
    sqrt_density = draw_sqrt_density(jax.random.fold_in(arg_keys[6], 71), 0)
    ion_charge = jnp.clip(jnp.exp(math.log(2.0) - 2.3025851 * jax.random.uniform(arg_keys[1], (NX, NY, NZ), jnp.float32) ** level_of(arg_keys[1], (NX, NY, NZ), ((0, 64), (2, 4)), -0.2, 0.2)), 0.2, 2.0)
    ion_potential = scatter_about(arg_keys[2], (NX, NY, NZ), 1.0, 6.0, ((0, 64), (2, 4)), jnp.float32)
    hartree_prev = scatter_about(arg_keys[3], (NX, NY, NZ), 1.0, 6.0, ((0, 64), (2, 4)), jnp.float32)
    hist_steps = draw_hist_steps(jax.random.fold_in(arg_keys[6], 71), 0)
    hist_changes = draw_hist_changes(jax.random.fold_in(arg_keys[6], 71), 0)
    return {"sqrt_density": sqrt_density, "ion_charge": ion_charge, "ion_potential": ion_potential, "hartree_prev": hartree_prev, "hist_steps": hist_steps, "hist_changes": hist_changes}


center = -5369.0 / 1800.0
coeffs = (12.0 / 7.0, -15.0 / 56.0, 10.0 / 189.0, -1.0 / 112.0, 2.0 / 825.0, -1.0 / 4752.0)
screen = 0.0025
spacing = 0.28
source_scale = 4.0 * math.pi * spacing * spacing
tf_scale = 5.0 / 3.0 * 2.871234
step_length = 0.01
damp_floor = 0.2

def laplace(values):
    summed = 3.0 * center * values
    for offset, weight in enumerate(coeffs, 1):
        for grid_axis in range(3):
            summed = summed + weight * (jnp.roll(values, offset, grid_axis) + jnp.roll(values, -offset, grid_axis))
    return summed

def operate(values):
    return screen * values - laplace(values)

def reference(sqrt_density, ion_charge, ion_potential, hartree_prev, hist_steps, hist_changes):
    source = source_scale * (sqrt_density * sqrt_density - ion_charge)
    hartree = hartree_prev
    residual = source - operate(hartree)
    direction = residual
    norm_now = jnp.sum(residual * residual)
    for sweep in range(ITERS):
        applied = operate(direction)
        step_size = norm_now / jnp.sum(direction * applied)
        hartree = hartree + step_size * direction
        residual = residual - step_size * applied
        norm_next = jnp.sum(residual * residual)
        direction = residual + norm_next / norm_now * direction
        norm_now = norm_next
    tf_power = jnp.exp(jnp.log(sqrt_density) * (4.0 / 3.0))
    energy_grad = 2.0 * sqrt_density * (hartree + ion_potential + tf_scale * tf_power) - laplace(sqrt_density) / (spacing * spacing)
    chem_pot = jnp.sum(sqrt_density * energy_grad) / (2.0 * jnp.sum(sqrt_density * sqrt_density))
    gradient = energy_grad - 2.0 * chem_pot * sqrt_density
    pair_count = hist_steps.shape[0]
    damped = []
    inverse_curv = []
    for pair_idx in range(pair_count):
        step_curv = jnp.sum(hist_steps[pair_idx] * hist_changes[pair_idx])
        step_norm = jnp.sum(hist_steps[pair_idx] * hist_steps[pair_idx])
        damping = jnp.where(step_curv >= damp_floor * step_norm, 1.0, (1.0 - damp_floor) * step_norm / jnp.maximum(step_norm - step_curv, (1.0 - damp_floor) * step_norm))
        damped.append(damping * hist_changes[pair_idx] + (1.0 - damping) * hist_steps[pair_idx])
        inverse_curv.append(1.0 / (damping * step_curv + (1.0 - damping) * step_norm))
    search = gradient
    first_coeffs = [None] * pair_count
    for pair_idx in reversed(range(pair_count)):
        first_coeffs[pair_idx] = inverse_curv[pair_idx] * jnp.sum(hist_steps[pair_idx] * search)
        search = search - first_coeffs[pair_idx] * damped[pair_idx]
    scaling = jnp.sum(hist_steps[-1] * damped[-1]) / jnp.sum(damped[-1] * damped[-1])
    result = scaling * search
    for pair_idx in range(pair_count):
        second = inverse_curv[pair_idx] * jnp.sum(damped[pair_idx] * result)
        result = result + (first_coeffs[pair_idx] - second) * hist_steps[pair_idx]
    new_density = sqrt_density - step_length * result
    return (new_density, hartree)
```

```python
import functools
import math

import jax
import jax.numpy as jnp
from jax import lax
from jax.experimental import pallas as pl
from jax.experimental.pallas import tpu as pltpu
from jax.sharding import PartitionSpec as P

center = -5369.0 / 1800.0
coeffs = (12.0 / 7.0, -15.0 / 56.0, 10.0 / 189.0, -1.0 / 112.0, 2.0 / 825.0, -1.0 / 4752.0)
screen = 0.0025
spacing = 0.28
source_scale = 4.0 * math.pi * spacing * spacing
tf_scale = 5.0 / 3.0 * 2.871234
step_length = 0.01
damp_floor = 0.2

SHIFT = 2.0
HIST = 8
REACH = 6
LANES = 128
VMEM_LIMIT = 24 * 1024 * 1024

ROW_GRAM = 0
ROW_BASE = 136
ROW_W = 170
ROW_MOM = 238
PAIRS = tuple((i, j) for i in range(HIST) for j in range(i, HIST))
PAIR_ROW = {pair: row for row, pair in enumerate(PAIRS)}


def two_sum(a, b):
    s = a + b
    bb = s - a
    return s, (a - (s - bb)) + (b - bb)


def quick_sum(a, b):
    s = a + b
    return s, b - (s - a)


def split(a):
    t = 4097.0 * a
    hi = t - (t - a)
    return hi, a - hi


def two_prod(a, b):
    p = a * b
    ah, al = split(a)
    bh, bl = split(b)
    return p, ((ah * bh - p) + ah * bl + al * bh) + al * bl


def df_add(a, b):
    s, e = two_sum(a[0], b[0])
    return quick_sum(s, e + (a[1] + b[1]))


def df_neg(a):
    return (-a[0], -a[1])


def df_sub(a, b):
    return df_add(a, df_neg(b))


def df_scale(a, factor):
    return (a[0] * factor, a[1] * factor)


def df_mul(a, b):
    p, e = two_prod(a[0], b[0])
    return quick_sum(p, e + (a[0] * b[1] + a[1] * b[0]))


def df_div(a, b):
    q1 = a[0] / b[0]
    r = df_sub(a, df_mul(b, (q1, jnp.zeros_like(q1))))
    q2 = r[0] / b[0]
    return quick_sum(q1, q2)


def lane_ids(shape):
    return lax.broadcasted_iota(jnp.int32, shape, len(shape) - 1)


def stencil_plane(i, own, left, right, ext, z_left, z_right):
    def layer(k):
        if k < 0:
            return left[k + REACH]
        if k >= REACH:
            return right[k - REACH]
        return own[k]

    values = own[i]
    rows = values.shape[0]
    lane = lane_ids((rows, LANES))
    tile_lane = lane_ids((8, LANES))
    from_right = z_right[8 * (i // 2) : 8 * (i // 2) + 8, :]
    from_left = z_left[8 * (i // 2) : 8 * (i // 2) + 8, :]
    wraps = []
    for b in range(rows // 8):
        j = 8 * (i % 2) + b
        upper = pltpu.roll(from_right, (LANES - 8 * j) % LANES, 1)
        lower = pltpu.roll(from_left, (2 * LANES - 8 * j - 8) % LANES, 1)
        wraps.append(jnp.where(tile_lane < 64, upper, lower))
    wrap = jnp.concatenate(wraps, axis=0)
    total = (3.0 * center) * values
    for k, weight in enumerate(coeffs, 1):
        pair = layer(i + k) + layer(i - k)
        pair = pair + (ext[i, 8 + k : 8 + k + rows, :] + ext[i, 8 - k : 8 - k + rows, :])
        up = pltpu.roll(jnp.where(lane < k, wrap, values), LANES - k, 1)
        down = pltpu.roll(jnp.where(lane >= LANES - k, wrap, values), k, 1)
        total = total + weight * (pair + (up + down))
    return total, values


def fill_ext(own, ext):
    rows = own.shape[1]
    ext[:, 8 : 8 + rows, :] = own[...]
    ext[:, 0:8, :] = own[:, rows - 8 : rows, :]
    ext[:, 8 + rows : 16 + rows, :] = own[:, 0:8, :]


def pack_faces(src, first_ref, last_ref, base):
    lane = lane_ids((8, LANES))
    for m in range(3):
        first = jnp.zeros((8, LANES), jnp.float32)
        last = jnp.zeros((8, LANES), jnp.float32)
        for j in range(16):
            n = 16 * m + j
            tile = src[n // 8, 8 * (n % 8) : 8 * (n % 8) + 8, :]
            here = (lane >= 8 * j) & (lane < 8 * j + 8)
            first = jnp.where(here, pltpu.roll(tile, 8 * j, 1) if j else tile, first)
            last = jnp.where(here, pltpu.roll(tile, (8 * j + 8) % LANES, 1) if j < 15 else tile, last)
        first_ref[base + 8 * m : base + 8 * m + 8, :] = first
        last_ref[base + 8 * m : base + 8 * m + 8, :] = last


def exact_total(hi, lo):
    for step in (4, 2, 1):
        hi, err = two_sum(hi, pltpu.roll(hi, step, 0))
        lo = lo + pltpu.roll(lo, step, 0) + err
    hi, lo = hi[0:1], lo[0:1]
    for step in (64, 32, 16, 8, 4, 2, 1):
        hi, err = two_sum(hi, pltpu.roll(hi, step, 1))
        lo = lo + pltpu.roll(lo, step, 1) + err
    return quick_sum(hi, lo)


def add_tile(acc, product):
    hi, err = two_sum(acc[0], product)
    return hi, acc[1] + err


def tile_of(ref, i, b):
    return ref[i, pl.ds(pl.multiple_of(8 * b, 8), 8), :]


def exact_dots(pairs):
    zero = jnp.zeros((8, LANES), jnp.float32)

    def body(i, accs):
        for b in range(8):
            accs = tuple(
                add_tile(acc, tile_of(a, i, b) * tile_of(c, i, b)) for acc, (a, c) in zip(accs, pairs)
            )
        return accs

    accs = lax.fori_loop(0, REACH, body, tuple((zero, zero) for _ in pairs))
    return [exact_total(*acc) for acc in accs]


def collapse(acc):
    return jnp.sum(acc, axis=0, keepdims=True)


def pack_kernel(hartree, density, first, last):
    pack_faces(hartree, first, last, 0)
    pack_faces(density, first, last, 24)


def residual_kernel(hartree, left, right, z_left, z_right, density, charge, out, first, last, ext):
    fill_ext(hartree, ext)
    for i in range(REACH):
        lap, values = stencil_plane(i, hartree, left, right, ext, z_left, z_right)
        rho = density[i]
        out[i] = source_scale * (rho * rho - charge[i]) - (screen * values - lap)
    pack_faces(out, first, last, 0)


def basis_kernel(has_prior, *refs):
    if has_prior:
        own, left, right, z_left, z_right, prior, out, first, last, ext = refs
    else:
        own, left, right, z_left, z_right, out, first, last, ext = refs
    fill_ext(own, ext)
    for i in range(REACH):
        lap, values = stencil_plane(i, own, left, right, ext, z_left, z_right)
        moved = (screen / SHIFT - 1.0) * values - (1.0 / SHIFT) * lap
        out[i] = 2.0 * moved - prior[i] if has_prior else moved
    pack_faces(out, first, last, 0)


def gram_kernel(steps, changes, rows):
    zero = jnp.zeros((8, LANES), jnp.float32)

    def run(base, left, right, pairs):
        def body(n, accs):
            i, b = n // 8, n % 8
            at = pl.ds(pl.multiple_of(8 * b, 8), 8)
            l_need = sorted({p for p, _ in pairs})
            r_need = sorted({q for _, q in pairs})
            l_tiles = {p: left[p, i, at, :] for p in l_need}
            r_tiles = l_tiles if left is right else {}
            r_tiles = {q: r_tiles[q] if q in r_tiles else right[q, i, at, :] for q in r_need}
            return tuple(acc + l_tiles[p] * r_tiles[q] for acc, (p, q) in zip(accs, pairs))

        accs = lax.fori_loop(0, 48, body, tuple(zero for _ in pairs))
        for n, acc in enumerate(accs):
            rows[base + n : base + n + 1, :] = collapse(acc)

    run(0, steps, steps, PAIRS)
    run(36, changes, changes, PAIRS)
    run(72, steps, changes, tuple((i, j) for i in range(4) for j in range(8)))
    run(104, steps, changes, tuple((i, j) for i in range(4, 8) for j in range(8)))


def field_dots(steps, changes, others):
    zero = jnp.zeros((8, LANES), jnp.float32)
    count = 2 * HIST

    def body(i, accs):
        accs = list(accs)
        for b in range(8):
            at = pl.ds(8 * b, 8)
            tiles = [other(i, b) for other in others]
            for f in range(count):
                field = steps[f, i, at, :] if f < HIST else changes[f - HIST, i, at, :]
                for o, tile in enumerate(tiles):
                    accs[o * count + f] = accs[o * count + f] + field * tile
        return tuple(accs)

    accs = lax.fori_loop(0, REACH, body, tuple(zero for _ in range(count * len(others))))
    return [collapse(acc) for acc in accs]


def plain_dots(pairs):
    zero = jnp.zeros((8, LANES), jnp.float32)

    def body(i, accs):
        for b in range(8):
            accs = tuple(acc + a(i, b) * c(i, b) for acc, (a, c) in zip(accs, pairs))
        return accs

    return [collapse(acc) for acc in lax.fori_loop(0, REACH, body, tuple(zero for _ in pairs))]


def base_kernel(density, left, right, z_left, z_right, hartree, potential, steps, changes, grad, rows, ext):
    fill_ext(density, ext)
    for i in range(REACH):
        lap, rho = stencil_plane(i, density, left, right, ext, z_left.at[24:48], z_right.at[24:48])
        power = jnp.exp(jnp.log(rho) * (4.0 / 3.0))
        grad[i] = 2.0 * rho * (hartree[i] + potential[i] + tf_scale * power) - lap * (
            1.0 / (spacing * spacing)
        )
    g_tile = lambda i, b: tile_of(grad, i, b)
    r_tile = lambda i, b: tile_of(density, i, b)
    dots = field_dots(steps, changes, [g_tile, r_tile]) + plain_dots([(r_tile, g_tile), (r_tile, r_tile)])
    for n, row in enumerate(dots):
        rows[n : n + 1, :] = row


def basis_dots(vector, density, steps, changes, rows):
    w_tile = lambda i, b: 2.0 * tile_of(density, i, b) * tile_of(vector, i, b)
    r_tile = lambda i, b: tile_of(density, i, b)
    dots = field_dots(steps, changes, [w_tile]) + plain_dots([(r_tile, w_tile)])
    for n, row in enumerate(dots):
        rows[n : n + 1, :] = row


def store_moments(pairs, moments):
    for n, (hi, lo) in enumerate(exact_dots(pairs)):
        moments[2 * n : 2 * n + 1, :] = hi
        moments[2 * n + 1 : 2 * n + 2, :] = lo


def first_dots_kernel(vector, density, steps, changes, rows, moments):
    basis_dots(vector, density, steps, changes, rows)
    store_moments([(vector, vector)], moments)


def dots_kernel(prior, vector, density, steps, changes, rows, moments):
    basis_dots(vector, density, steps, changes, rows)
    store_moments([(prior, vector), (vector, vector)], moments)


def last_dots_kernel(
    prior, vector, density, steps, changes, gram, base, d0, d1, d2, m0, m1, m2, out, rows, own_rows, moments
):
    basis_dots(vector, density, steps, changes, own_rows)
    store_moments([(prior, vector), (vector, vector)], moments)
    rows[ROW_GRAM : ROW_GRAM + 136, :] = gram[0:136, :]
    rows[ROW_BASE : ROW_BASE + 34, :] = base[0:34, :]
    for n, d in enumerate((d0, d1, d2, own_rows)):
        rows[ROW_W + 17 * n : ROW_W + 17 * n + 17, :] = d[0:17, :]
    rows[ROW_MOM:256, :] = jnp.zeros((256 - ROW_MOM, LANES), jnp.float32)
    lane = lane_ids((1, LANES))
    out[0:1, :] = jnp.sum(jnp.transpose(rows[0:128, :]), axis=0, keepdims=True)
    second = jnp.sum(jnp.transpose(rows[128:256, :]), axis=0, keepdims=True)
    at = ROW_MOM - 128
    order = [(m0, 0), (m1, 0), (m1, 1), (m2, 0), (m2, 1), (moments, 0), (moments, 1)]
    for n, (ref, which) in enumerate(order):
        second = jnp.where(lane == at + n, ref[2 * which : 2 * which + 1, :], second)
        second = jnp.where(lane == at + 8 + n, ref[2 * which + 1 : 2 * which + 2, :], second)
    out[1:2, :] = second


def send_kernel(own, left, right, z_left, z_right, sums, out, ext):
    fill_ext(own, ext)
    zero = jnp.zeros((8, LANES), jnp.float32)
    accs = [(zero, zero) for _ in range(2)]
    for i in range(REACH):
        lap, values = stencil_plane(i, own, left, right, ext, z_left, z_right)
        product = values * ((screen / SHIFT - 1.0) * values - (1.0 / SHIFT) * lap)
        for b in range(8):
            accs[b % 2] = add_tile(accs[b % 2], product[8 * b : 8 * b + 8])
    hi, err = two_sum(accs[0][0], accs[1][0])
    hi, lo = exact_total(hi, accs[0][1] + accs[1][1] + err)
    lane = lane_ids((1, LANES))
    at = ROW_MOM - 128
    second = jnp.where(lane == at + 7, hi, jnp.where(lane == at + 15, lo, sums[1:2, :]))
    both = jnp.concatenate([sums[0:1, :], second], axis=0)
    out[...] = jnp.broadcast_to(both[None], out.shape)


def solve_krylov(moment):
    n00, n01, n11, n12, n22, n23, n33, n34 = moment
    nu = [n00, n01]
    nu.append(df_sub(df_scale(n11, 2.0), n00))
    nu.append(df_sub(df_scale(n12, 2.0), n01))
    nu.append(df_sub(df_scale(n22, 2.0), n00))
    nu.append(df_sub(df_scale(n23, 2.0), n01))
    nu.append(df_sub(df_scale(n33, 2.0), n00))

    def gram(i, j):
        if i == j == 0:
            return n00
        return df_scale(df_add(nu[i + j], nu[abs(i - j)]), 0.5)

    def moved(i, j):
        if i == 3 and j == 3:
            return n34
        if j == 0:
            return gram(i, 1)
        return df_scale(df_add(gram(i, j + 1), gram(i, j - 1)), 0.5)

    mat = {(i, j): df_add(moved(i, j), gram(i, j)) for i in range(4) for j in range(i + 1)}
    rhs = [df_scale(gram(i, 0), 1.0 / SHIFT) for i in range(4)]
    low = {}
    for k in range(4):
        for i in range(k + 1, 4):
            low[i, k] = df_div(mat[i, k], mat[k, k])
        for i in range(k + 1, 4):
            for j in range(k + 1, i + 1):
                mat[i, j] = df_sub(mat[i, j], df_mul(low[i, k], mat[j, k]))
            rhs[i] = df_sub(rhs[i], df_mul(low[i, k], rhs[k]))
    sol = [None] * 4
    for k in reversed(range(4)):
        value = df_div(rhs[k], mat[k, k])
        for i in range(k + 1, 4):
            value = df_sub(value, df_mul(low[i, k], sol[i]))
        sol[k] = value
    return [hi + lo for hi, lo in sol]


def final_kernel(received, density, hartree, grad, v0, v1, v2, v3, steps, changes, new_density, new_hartree, spread):
    chains = 8
    parts = [(received[n], jnp.zeros((2, LANES), jnp.float32)) for n in range(chains)]
    for n in range(chains, received.shape[0]):
        parts[n % chains] = add_tile(parts[n % chains], received[n])
    while len(parts) > 1:
        half = len(parts) // 2
        merged = []
        for a, b in zip(parts[:half], parts[half:]):
            hi, err = two_sum(a[0], b[0])
            merged.append((hi, a[1] + b[1] + err))
        parts = merged
    hi, lo = quick_sum(*parts[0])
    spread[0:128, :] = jnp.transpose(jnp.broadcast_to(hi[0:1], (LANES, LANES)))
    spread[128:256, :] = jnp.transpose(jnp.broadcast_to(hi[1:2], (LANES, LANES)))
    spread[256:384, :] = jnp.transpose(jnp.broadcast_to(lo[1:2], (LANES, LANES)))

    def row(n):
        return spread[n : n + 1, :]

    def moment(n):
        low = 128 + ROW_MOM
        a = df_add((row(ROW_MOM + n), row(low + n)), (row(ROW_MOM + 8 + n), row(low + 8 + n)))
        return a

    mix = solve_krylov([moment(n) for n in range(8)])

    def s_s(i, j):
        return row(ROW_GRAM + PAIR_ROW[min(i, j), max(i, j)])

    def y_y(i, j):
        return row(ROW_GRAM + 36 + PAIR_ROW[min(i, j), max(i, j)])

    def s_y(i, j):
        return row(ROW_GRAM + 72 + 8 * i + j)

    pairs = range(HIST)
    theta, rest, inverse = [], [], []
    for i in pairs:
        curv, norm = s_y(i, i), s_s(i, i)
        kept = (1.0 - damp_floor) * norm
        damp = jnp.where(curv >= damp_floor * norm, 1.0, kept / jnp.maximum(norm - curv, kept))
        theta.append(damp)
        rest.append(1.0 - damp)
        inverse.append(1.0 / (damp * curv + (1.0 - damp) * norm))

    def s_bar(i, j):
        return theta[j] * s_y(i, j) + rest[j] * s_s(i, j)

    def bar_bar(i, j):
        return theta[i] * (theta[j] * y_y(i, j) + rest[j] * s_y(j, i)) + rest[i] * s_bar(i, j)

    last = HIST - 1
    scaling = s_bar(last, last) / bar_bar(last, last)

    def energy(n):
        value = row(ROW_BASE + n) if n < 16 else row(ROW_BASE + 32)
        for j in range(4):
            value = value + mix[j] * row(ROW_W + 17 * j + n)
        return value

    chem = energy(16) / row(ROW_BASE + 33)

    def gradient(n):
        return energy(n) - chem * row(ROW_BASE + 16 + n)

    s_grad = [gradient(i) for i in pairs]
    bar_grad = [theta[i] * gradient(HIST + i) + rest[i] * s_grad[i] for i in pairs]

    first = [None] * HIST
    pending = list(s_grad)
    for j in reversed(pairs):
        first[j] = inverse[j] * pending[j]
        for i in range(j):
            pending[i] = pending[i] - first[j] * s_bar(i, j)
    pending = list(bar_grad)
    for j in pairs:
        for i in pairs:
            pending[i] = pending[i] - first[j] * bar_bar(i, j)
    pending = [scaling * value for value in pending]
    step_mix, change_mix = [], []
    for j in pairs:
        net = first[j] - inverse[j] * pending[j]
        for i in range(j + 1, HIST):
            pending[i] = pending[i] + net * s_bar(j, i)
        change_mix.append((-step_length) * (-scaling * first[j] * theta[j]))
        step_mix.append((-step_length) * (net - scaling * first[j] * rest[j]))

    wide = lambda value: jnp.broadcast_to(value, (8, LANES))
    mix = [wide(value) for value in mix]
    chem, gain = wide(chem), wide((-step_length) * scaling)
    step_mix = [wide(value) for value in step_mix]
    change_mix = [wide(value) for value in change_mix]
    basis = (v0, v1, v2, v3)

    @pl.loop(0, REACH)
    def _(i):
        for b in range(8):
            at = pl.ds(8 * b, 8)
            rho = density[i, at, :]
            lift = mix[0] * v0[i, at, :]
            for j in range(1, 4):
                lift = lift + mix[j] * basis[j][i, at, :]
            new_hartree[i, at, :] = hartree[i, at, :] + lift
            slope = grad[i, at, :] + 2.0 * rho * lift - chem * rho
            parts = [rho, gain * slope, step_mix[0] * steps[0, i, at, :], change_mix[0] * changes[0, i, at, :]]
            for f in range(1, HIST):
                parts[2] = parts[2] + step_mix[f] * steps[f, i, at, :]
                parts[3] = parts[3] + change_mix[f] * changes[f, i, at, :]
            new_density[i, at, :] = parts[0] + (parts[1] + (parts[2] + parts[3]))


def call(kernel, outs, args, scratch=(), flops=0):
    whole = pl.BlockSpec(memory_space=pltpu.VMEM)
    shapes = [jax.ShapeDtypeStruct(shape, jnp.float32) for shape in outs]
    size = sum(4 * math.prod(a.shape) for a in (*args, *shapes))
    return pl.pallas_call(
        kernel,
        out_shape=shapes,
        in_specs=[whole] * len(args),
        out_specs=[whole] * len(outs),
        scratch_shapes=[pltpu.VMEM(shape, jnp.float32) for shape in scratch],
        cost_estimate=pl.CostEstimate(flops=flops, bytes_accessed=size, transcendentals=0),
        compiler_params=pltpu.CompilerParams(vmem_limit_bytes=VMEM_LIMIT),
    )(*args)


def ring(axis, step):
    size = lax.axis_size(axis)
    return [(i, (i + step) % size) for i in range(size)]


def x_halo(block):
    return (lax.ppermute(block, "blk", ring("blk", 1)), lax.ppermute(block, "blk", ring("blk", -1)))


def z_halo(first, last):
    return (lax.ppermute(last, "gz", ring("gz", 1)), lax.ppermute(first, "gz", ring("gz", -1)))


def after(values, *earlier):
    return lax.optimization_barrier((tuple(values), earlier))[0]


def on_device(sqrt_density, ion_charge, ion_potential, hartree_prev, hist_steps, hist_changes):
    block = sqrt_density.shape
    ext = (block[0], block[1] + 16, block[2])
    face = (24, LANES)
    stencil_flops = 60 * math.prod(block)
    h_sides = x_halo(hartree_prev)
    faces = call(pack_kernel, [(48, LANES)] * 2, [hartree_prev, sqrt_density])
    h_ends = z_halo(*faces)
    (gram,) = call(gram_kernel, [(136, LANES)], [hist_steps, hist_changes], flops=272 * math.prod(block))
    h_sides = after(h_sides, gram)
    v0, first, last = call(
        residual_kernel,
        [block, face, face],
        [hartree_prev, *h_sides, *h_ends, sqrt_density, ion_charge],
        [ext],
        stencil_flops,
    )
    basis = [v0]
    dots, moments = [], []
    for n in range(3):
        halo = (*x_halo(basis[n]), *z_halo(first, last))
        prior = [basis[n - 1]] if n else []
        rows, moment = call(
            dots_kernel if n else first_dots_kernel,
            [(24, LANES), (8, LANES)],
            [*prior, basis[n], sqrt_density, hist_steps, hist_changes],
            flops=50 * math.prod(block),
        )
        dots.append(rows)
        moments.append(moment)
        done = [rows]
        if n == 1:
            rho_sides = x_halo(after([sqrt_density], v0)[0])
        if n == 2:
            grad, base = call(
                base_kernel,
                [block, (40, LANES)],
                [sqrt_density, *rho_sides, *h_ends, hartree_prev, ion_potential, hist_steps, hist_changes],
                [ext],
                2 * stencil_flops,
            )
            done.append(base)
        halo = after(halo, *done)
        fresh, first, last = call(
            functools.partial(basis_kernel, n > 0),
            [block, face, face],
            [basis[n], *halo, *prior],
            [ext],
            stencil_flops,
        )
        basis.append(fresh)
    halo = (*x_halo(basis[3]), *z_halo(first, last))
    (sums,) = call(
        last_dots_kernel,
        [(2, LANES)],
        [basis[2], basis[3], sqrt_density, hist_steps, hist_changes, gram, base, *dots, *moments],
        [(256, LANES), (24, LANES), (8, LANES)],
        50 * math.prod(block),
    )
    devices = lax.axis_size("blk") * lax.axis_size("gz")
    (outgoing,) = call(send_kernel, [(devices, 2, LANES)], [basis[3], *halo, sums], [ext], stencil_flops)
    received = lax.all_to_all(outgoing, ("blk", "gz"), 0, 0, tiled=True)
    return tuple(
        call(
            final_kernel,
            [block, block],
            [received, sqrt_density, hartree_prev, grad, *basis, hist_steps, hist_changes],
            [(384, LANES)],
            50 * math.prod(block),
        )
    )


def solution(mesh):
    placed = (
        P("blk", None, "gz"),
        P("blk", None, "gz"),
        P("blk", None, "gz"),
        P("blk", None, "gz"),
        P(None, "blk", None, "gz"),
        P(None, "blk", None, "gz"),
    )
    return jax.shard_map(
        on_device,
        mesh=mesh,
        in_specs=placed,
        out_specs=(P("blk", None, "gz"), P("blk", None, "gz")),
        check_vma=False,
    )
```

```python
import functools
import math

import jax
import jax.numpy as jnp
from jax import lax
from jax.experimental import pallas as pl
from jax.experimental.pallas import tpu as pltpu
from jax.sharding import PartitionSpec as P

center = -5369.0 / 1800.0
coeffs = (12.0 / 7.0, -15.0 / 56.0, 10.0 / 189.0, -1.0 / 112.0, 2.0 / 825.0, -1.0 / 4752.0)
screen = 0.0025
spacing = 0.28
source_scale = 4.0 * math.pi * spacing * spacing
tf_scale = 5.0 / 3.0 * 2.871234
step_length = 0.01
damp_floor = 0.2

SHIFT = 2.0
HIST = 8
REACH = 6
LANES = 128
VMEM_LIMIT = 24 * 1024 * 1024

ROW_GRAM = 0
ROW_BASE = 136
ROW_W = 170
ROW_MOM = 238
PAIRS = tuple((i, j) for i in range(HIST) for j in range(i, HIST))
PAIR_ROW = {pair: row for row, pair in enumerate(PAIRS)}


def two_sum(a, b):
    s = a + b
    bb = s - a
    return s, (a - (s - bb)) + (b - bb)


def quick_sum(a, b):
    s = a + b
    return s, b - (s - a)


def split(a):
    t = 4097.0 * a
    hi = t - (t - a)
    return hi, a - hi


def two_prod(a, b):
    p = a * b
    ah, al = split(a)
    bh, bl = split(b)
    return p, ((ah * bh - p) + ah * bl + al * bh) + al * bl


def df_add(a, b):
    s, e = two_sum(a[0], b[0])
    return quick_sum(s, e + (a[1] + b[1]))


def df_neg(a):
    return (-a[0], -a[1])


def df_sub(a, b):
    return df_add(a, df_neg(b))


def df_scale(a, factor):
    return (a[0] * factor, a[1] * factor)


def df_mul(a, b):
    p, e = two_prod(a[0], b[0])
    return quick_sum(p, e + (a[0] * b[1] + a[1] * b[0]))


def df_div(a, b):
    q1 = a[0] / b[0]
    r = df_sub(a, df_mul(b, (q1, jnp.zeros_like(q1))))
    q2 = r[0] / b[0]
    return quick_sum(q1, q2)


def lane_ids(shape):
    return lax.broadcasted_iota(jnp.int32, shape, len(shape) - 1)


def inner_plane(i, own, ext):
    values = own[i]
    rows = values.shape[0]
    lane = lane_ids((rows, LANES))
    total = (3.0 * center) * values
    for k, weight in enumerate(coeffs, 1):
        pair = ext[i, 8 + k : 8 + k + rows, :] + ext[i, 8 - k : 8 - k + rows, :]
        if i + k < REACH:
            pair = pair + own[i + k]
        if i - k >= 0:
            pair = pair + own[i - k]
        up = pltpu.roll(jnp.where(lane < k, 0.0, values), LANES - k, 1)
        down = pltpu.roll(jnp.where(lane >= LANES - k, 0.0, values), k, 1)
        total = total + weight * (pair + (up + down))
    return total, values


def edge_faces(z_left, z_right):
    lane = lane_ids((24, LANES)) % 8
    lower = jnp.zeros((24, LANES), jnp.float32)
    upper = jnp.zeros((24, LANES), jnp.float32)
    for k, weight in enumerate(coeffs, 1):
        lower = lower + jnp.where(lane < k, weight * pltpu.roll(z_left, LANES - 8 + k, 1), 0.0)
        if z_right is not None:
            upper = upper + jnp.where(lane >= 8 - k, weight * pltpu.roll(z_right, 8 - k, 1), 0.0)
    return lower, upper


def edge_plane(i, left, right, faces):
    total = None
    for k, weight in enumerate(coeffs, 1):
        terms = []
        if i - k < 0:
            terms.append(left[i - k + REACH])
        if right is not None and i + k >= REACH:
            terms.append(right[i + k - REACH])
        for term in terms:
            total = weight * term if total is None else total + weight * term
    lane = lane_ids((8, LANES))
    lower, upper = (face[8 * (i // 2) : 8 * (i // 2) + 8] for face in faces)
    tiles = []
    for b in range(total.shape[0] // 8):
        j = 8 * (i % 2) + b
        tile = jnp.where(lane < 8, pltpu.roll(lower, (LANES - 8 * j) % LANES, 1), 0.0)
        if right is not None:
            tile = jnp.where(lane >= LANES - 8, pltpu.roll(upper, (2 * LANES - 8 - 8 * j) % LANES, 1), tile)
        tiles.append(tile)
    return total + jnp.concatenate(tiles, axis=0)


def fill_ext(own, ext):
    rows = own.shape[1]
    ext[:, 8 : 8 + rows, :] = own[...]
    ext[:, 0:8, :] = own[:, rows - 8 : rows, :]
    ext[:, 8 + rows : 16 + rows, :] = own[:, 0:8, :]


def pack_faces(src, first_ref, last_ref, base):
    lane = lane_ids((8, LANES))
    for m in range(3):
        first = jnp.zeros((8, LANES), jnp.float32)
        last = jnp.zeros((8, LANES), jnp.float32)
        for j in range(16):
            n = 16 * m + j
            tile = src[n // 8, 8 * (n % 8) : 8 * (n % 8) + 8, :]
            here = (lane >= 8 * j) & (lane < 8 * j + 8)
            first = jnp.where(here, pltpu.roll(tile, 8 * j, 1) if j else tile, first)
            last = jnp.where(here, pltpu.roll(tile, (8 * j + 8) % LANES, 1) if j < 15 else tile, last)
        first_ref[base + 8 * m : base + 8 * m + 8, :] = first
        last_ref[base + 8 * m : base + 8 * m + 8, :] = last


def exact_total(hi, lo):
    for step in (4, 2, 1):
        hi, err = two_sum(hi, pltpu.roll(hi, step, 0))
        lo = lo + pltpu.roll(lo, step, 0) + err
    hi, lo = hi[0:1], lo[0:1]
    for step in (64, 32, 16, 8, 4, 2, 1):
        hi, err = two_sum(hi, pltpu.roll(hi, step, 1))
        lo = lo + pltpu.roll(lo, step, 1) + err
    return quick_sum(hi, lo)


def add_tile(acc, product):
    hi, err = two_sum(acc[0], product)
    return hi, acc[1] + err


def tile_of(ref, i, b):
    return ref[i, pl.ds(pl.multiple_of(8 * b, 8), 8), :]


def exact_dots(pairs):
    zero = jnp.zeros((8, LANES), jnp.float32)

    def body(i, accs):
        for b in range(8):
            accs = tuple(
                add_tile(acc, tile_of(a, i, b) * tile_of(c, i, b)) for acc, (a, c) in zip(accs, pairs)
            )
        return accs

    accs = lax.fori_loop(0, REACH, body, tuple((zero, zero) for _ in pairs))
    return [exact_total(*acc) for acc in accs]


def collapse(acc):
    return jnp.sum(acc, axis=0, keepdims=True)


def pack_kernel(block, first, last):
    pack_faces(block, first, last, 0)


def inner_residual_kernel(hartree, density, charge, out, ext):
    fill_ext(hartree, ext)
    for i in range(REACH):
        lap, values = inner_plane(i, hartree, ext)
        rho = density[i]
        out[i] = source_scale * (rho * rho - charge[i]) - (screen * values - lap)


def inner_basis_kernel(has_prior, *refs):
    own, prior, out, ext = refs if has_prior else (refs[0], None, *refs[1:])
    fill_ext(own, ext)
    for i in range(REACH):
        lap, values = inner_plane(i, own, ext)
        moved = (screen / SHIFT - 1.0) * values - (1.0 / SHIFT) * lap
        out[i] = 2.0 * moved - prior[i] if has_prior else moved


def edge_kernel(gain, inner, left, right, z_left, z_right, *rest):
    *extra, out, first, last = rest
    for ref, more in zip((first, last), extra):
        ref[24:48, :] = more[...]
    faces = edge_faces(z_left[0:24, :], z_right[0:24, :])
    for i in range(REACH):
        out[i] = inner[i] + gain * edge_plane(i, left, right, faces)
    pack_faces(out, first, last, 0)


def gram_kernel(work, steps, changes, rows):
    zero = jnp.zeros((8, LANES), jnp.float32)

    def run(base, left, right, pairs):
        def body(i, accs):
            for b in range(8):
                at = pl.ds(8 * b, 8)
                l_tiles = {p: left[p, i, at, :] for p in sorted({p for p, _ in pairs})}
                if left is right:
                    r_tiles = l_tiles
                else:
                    r_tiles = {q: right[q, i, at, :] for q in sorted({q for _, q in pairs})}
                accs = tuple(acc + l_tiles[p] * r_tiles[q] for acc, (p, q) in zip(accs, pairs))
            return accs

        accs = lax.fori_loop(0, REACH, body, tuple(zero for _ in pairs))
        for n, acc in enumerate(accs):
            rows[base + n : base + n + 1, :] = collapse(acc)

    if work == "same":
        run(0, steps, steps, PAIRS)
        run(36, changes, changes, PAIRS)
    else:
        run(0, steps, changes, tuple((i, j) for i in range(4) for j in range(8)))
        run(32, steps, changes, tuple((i, j) for i in range(4, 8) for j in range(8)))


def field_dots(steps, changes, others):
    zero = jnp.zeros((8, LANES), jnp.float32)
    count = 2 * HIST

    def body(i, accs):
        accs = list(accs)
        for b in range(8):
            at = pl.ds(8 * b, 8)
            tiles = [other(i, b) for other in others]
            for f in range(count):
                field = steps[f, i, at, :] if f < HIST else changes[f - HIST, i, at, :]
                for o, tile in enumerate(tiles):
                    accs[o * count + f] = accs[o * count + f] + field * tile
        return tuple(accs)

    accs = lax.fori_loop(0, REACH, body, tuple(zero for _ in range(count * len(others))))
    return [collapse(acc) for acc in accs]


def plain_dots(pairs):
    zero = jnp.zeros((8, LANES), jnp.float32)

    def body(i, accs):
        for b in range(8):
            accs = tuple(acc + a(i, b) * c(i, b) for acc, (a, c) in zip(accs, pairs))
        return accs

    return [collapse(acc) for acc in lax.fori_loop(0, REACH, body, tuple(zero for _ in pairs))]


def base_kernel(density, left, right, z_left, z_right, hartree, potential, steps, changes, grad, rows, ext):
    fill_ext(density, ext)
    faces = edge_faces(z_left[24:48, :], z_right[24:48, :])
    for i in range(REACH):
        lap, rho = inner_plane(i, density, ext)
        lap = lap + edge_plane(i, left, right, faces)
        power = jnp.exp(jnp.log(rho) * (4.0 / 3.0))
        grad[i] = 2.0 * rho * (hartree[i] + potential[i] + tf_scale * power) - lap * (
            1.0 / (spacing * spacing)
        )
    g_tile = lambda i, b: tile_of(grad, i, b)
    r_tile = lambda i, b: tile_of(density, i, b)
    dots = field_dots(steps, changes, [g_tile, r_tile]) + plain_dots([(r_tile, g_tile), (r_tile, r_tile)])
    for n, row in enumerate(dots):
        rows[n : n + 1, :] = row


def basis_dots(vector, density, steps, changes, rows):
    w_tile = lambda i, b: 2.0 * tile_of(density, i, b) * tile_of(vector, i, b)
    r_tile = lambda i, b: tile_of(density, i, b)
    dots = field_dots(steps, changes, [w_tile]) + plain_dots([(r_tile, w_tile)])
    for n, row in enumerate(dots):
        rows[n : n + 1, :] = row


def store_moments(pairs, moments):
    for n, (hi, lo) in enumerate(exact_dots(pairs)):
        moments[2 * n : 2 * n + 1, :] = hi
        moments[2 * n + 1 : 2 * n + 2, :] = lo


def first_dots_kernel(vector, density, steps, changes, rows, moments):
    basis_dots(vector, density, steps, changes, rows)
    store_moments([(vector, vector)], moments)


def dots_kernel(prior, vector, density, steps, changes, rows, moments):
    basis_dots(vector, density, steps, changes, rows)
    store_moments([(prior, vector), (vector, vector)], moments)


def last_dots_kernel(
    prior, vector, density, steps, changes, same, cross, base, d0, d1, d2, m0, m1, m2, out, rows, own_rows, moments
):
    basis_dots(vector, density, steps, changes, own_rows)
    store_moments([(prior, vector), (vector, vector)], moments)
    rows[ROW_GRAM : ROW_GRAM + 72, :] = same[...]
    rows[ROW_GRAM + 72 : ROW_GRAM + 136, :] = cross[...]
    rows[ROW_BASE : ROW_BASE + 34, :] = base[0:34, :]
    for n, d in enumerate((d0, d1, d2, own_rows)):
        rows[ROW_W + 17 * n : ROW_W + 17 * n + 17, :] = d[0:17, :]
    rows[ROW_MOM:256, :] = jnp.zeros((256 - ROW_MOM, LANES), jnp.float32)
    lane = lane_ids((1, LANES))
    out[0:1, :] = jnp.sum(jnp.transpose(rows[0:128, :]), axis=0, keepdims=True)
    second = jnp.sum(jnp.transpose(rows[128:256, :]), axis=0, keepdims=True)
    at = ROW_MOM - 128
    order = [(m0, 0), (m1, 0), (m1, 1), (m2, 0), (m2, 1), (moments, 0), (moments, 1)]
    for n, (ref, which) in enumerate(order):
        second = jnp.where(lane == at + n, ref[2 * which : 2 * which + 1, :], second)
        second = jnp.where(lane == at + 8 + n, ref[2 * which + 1 : 2 * which + 2, :], second)
    out[1:2, :] = second


def inner_moment_kernel(own, out, ext):
    fill_ext(own, ext)
    zero = jnp.zeros((8, LANES), jnp.float32)
    accs = [(zero, zero) for _ in range(2)]
    for i in range(REACH):
        lap, values = inner_plane(i, own, ext)
        product = values * ((screen / SHIFT - 1.0) * values - (1.0 / SHIFT) * lap)
        for b in range(8):
            accs[b % 2] = add_tile(accs[b % 2], product[8 * b : 8 * b + 8])
    hi, err = two_sum(accs[0][0], accs[1][0])
    hi, lo = exact_total(hi, accs[0][1] + accs[1][1] + err)
    out[0:1, :] = hi
    out[1:2, :] = lo


def send_kernel(own, left, z_left, inner, sums, out):
    faces = edge_faces(z_left[...], None)
    zero = jnp.zeros((8, LANES), jnp.float32)
    accs = [(zero, zero) for _ in range(2)]
    for i in range(REACH):
        product = own[i] * edge_plane(i, left, None, faces)
        for b in range(8):
            accs[b % 2] = add_tile(accs[b % 2], product[8 * b : 8 * b + 8])
    hi, err = two_sum(accs[0][0], accs[1][0])
    coupling = exact_total(hi, accs[0][1] + accs[1][1] + err)
    hi, lo = df_add(df_scale(coupling, -2.0 / SHIFT), (inner[0:1, :], inner[1:2, :]))
    lane = lane_ids((1, LANES))
    at = ROW_MOM - 128
    second = jnp.where(lane == at + 7, hi, jnp.where(lane == at + 15, lo, sums[1:2, :]))
    both = jnp.concatenate([sums[0:1, :], second], axis=0)
    out[...] = jnp.broadcast_to(both[None], out.shape)


def solve_krylov(moment):
    n00, n01, n11, n12, n22, n23, n33, n34 = moment
    nu = [n00, n01]
    nu.append(df_sub(df_scale(n11, 2.0), n00))
    nu.append(df_sub(df_scale(n12, 2.0), n01))
    nu.append(df_sub(df_scale(n22, 2.0), n00))
    nu.append(df_sub(df_scale(n23, 2.0), n01))
    nu.append(df_sub(df_scale(n33, 2.0), n00))

    def gram(i, j):
        if i == j == 0:
            return n00
        return df_scale(df_add(nu[i + j], nu[abs(i - j)]), 0.5)

    def moved(i, j):
        if i == 3 and j == 3:
            return n34
        if j == 0:
            return gram(i, 1)
        return df_scale(df_add(gram(i, j + 1), gram(i, j - 1)), 0.5)

    mat = {(i, j): df_add(moved(i, j), gram(i, j)) for i in range(4) for j in range(i + 1)}
    rhs = [df_scale(gram(i, 0), 1.0 / SHIFT) for i in range(4)]
    low = {}
    for k in range(4):
        for i in range(k + 1, 4):
            low[i, k] = df_div(mat[i, k], mat[k, k])
        for i in range(k + 1, 4):
            for j in range(k + 1, i + 1):
                mat[i, j] = df_sub(mat[i, j], df_mul(low[i, k], mat[j, k]))
            rhs[i] = df_sub(rhs[i], df_mul(low[i, k], rhs[k]))
    sol = [None] * 4
    for k in reversed(range(4)):
        value = df_div(rhs[k], mat[k, k])
        for i in range(k + 1, 4):
            value = df_sub(value, df_mul(low[i, k], sol[i]))
        sol[k] = value
    return [hi + lo for hi, lo in sol]


def final_kernel(received, density, hartree, grad, v0, v1, v2, v3, steps, changes, new_density, new_hartree, spread):
    chains = 8
    parts = [(received[n], jnp.zeros((2, LANES), jnp.float32)) for n in range(chains)]
    for n in range(chains, received.shape[0]):
        parts[n % chains] = add_tile(parts[n % chains], received[n])
    while len(parts) > 1:
        half = len(parts) // 2
        merged = []
        for a, b in zip(parts[:half], parts[half:]):
            hi, err = two_sum(a[0], b[0])
            merged.append((hi, a[1] + b[1] + err))
        parts = merged
    hi, lo = quick_sum(*parts[0])
    spread[0:128, :] = jnp.transpose(jnp.broadcast_to(hi[0:1], (LANES, LANES)))
    spread[128:256, :] = jnp.transpose(jnp.broadcast_to(hi[1:2], (LANES, LANES)))
    spread[256:384, :] = jnp.transpose(jnp.broadcast_to(lo[1:2], (LANES, LANES)))

    def row(n):
        return spread[n : n + 1, :]

    def moment(n):
        low = 128 + ROW_MOM
        a = df_add((row(ROW_MOM + n), row(low + n)), (row(ROW_MOM + 8 + n), row(low + 8 + n)))
        return a

    mix = solve_krylov([moment(n) for n in range(8)])

    def s_s(i, j):
        return row(ROW_GRAM + PAIR_ROW[min(i, j), max(i, j)])

    def y_y(i, j):
        return row(ROW_GRAM + 36 + PAIR_ROW[min(i, j), max(i, j)])

    def s_y(i, j):
        return row(ROW_GRAM + 72 + 8 * i + j)

    pairs = range(HIST)
    theta, rest, inverse = [], [], []
    for i in pairs:
        curv, norm = s_y(i, i), s_s(i, i)
        kept = (1.0 - damp_floor) * norm
        damp = jnp.where(curv >= damp_floor * norm, 1.0, kept / jnp.maximum(norm - curv, kept))
        theta.append(damp)
        rest.append(1.0 - damp)
        inverse.append(1.0 / (damp * curv + (1.0 - damp) * norm))

    def s_bar(i, j):
        return theta[j] * s_y(i, j) + rest[j] * s_s(i, j)

    def bar_bar(i, j):
        return theta[i] * (theta[j] * y_y(i, j) + rest[j] * s_y(j, i)) + rest[i] * s_bar(i, j)

    last = HIST - 1
    scaling = s_bar(last, last) / bar_bar(last, last)

    def energy(n):
        value = row(ROW_BASE + n) if n < 16 else row(ROW_BASE + 32)
        for j in range(4):
            value = value + mix[j] * row(ROW_W + 17 * j + n)
        return value

    chem = energy(16) / row(ROW_BASE + 33)

    def gradient(n):
        return energy(n) - chem * row(ROW_BASE + 16 + n)

    s_grad = [gradient(i) for i in pairs]
    bar_grad = [theta[i] * gradient(HIST + i) + rest[i] * s_grad[i] for i in pairs]

    first = [None] * HIST
    pending = list(s_grad)
    for j in reversed(pairs):
        first[j] = inverse[j] * pending[j]
        for i in range(j):
            pending[i] = pending[i] - first[j] * s_bar(i, j)
    pending = list(bar_grad)
    for j in pairs:
        for i in pairs:
            pending[i] = pending[i] - first[j] * bar_bar(i, j)
    pending = [scaling * value for value in pending]
    step_mix, change_mix = [], []
    for j in pairs:
        net = first[j] - inverse[j] * pending[j]
        for i in range(j + 1, HIST):
            pending[i] = pending[i] + net * s_bar(j, i)
        change_mix.append((-step_length) * (-scaling * first[j] * theta[j]))
        step_mix.append((-step_length) * (net - scaling * first[j] * rest[j]))

    wide = lambda value: jnp.broadcast_to(value, (8, LANES))
    mix = [wide(value) for value in mix]
    chem, gain = wide(chem), wide((-step_length) * scaling)
    step_mix = [wide(value) for value in step_mix]
    change_mix = [wide(value) for value in change_mix]
    basis = (v0, v1, v2, v3)

    @pl.loop(0, REACH)
    def _(i):
        for b in range(8):
            at = pl.ds(8 * b, 8)
            rho = density[i, at, :]
            lift = mix[0] * v0[i, at, :]
            for j in range(1, 4):
                lift = lift + mix[j] * basis[j][i, at, :]
            new_hartree[i, at, :] = hartree[i, at, :] + lift
            slope = grad[i, at, :] + 2.0 * rho * lift - chem * rho
            parts = [rho, gain * slope, step_mix[0] * steps[0, i, at, :], change_mix[0] * changes[0, i, at, :]]
            for f in range(1, HIST):
                parts[2] = parts[2] + step_mix[f] * steps[f, i, at, :]
                parts[3] = parts[3] + change_mix[f] * changes[f, i, at, :]
            new_density[i, at, :] = parts[0] + (parts[1] + (parts[2] + parts[3]))


def call(kernel, outs, args, scratch=(), flops=0):
    whole = pl.BlockSpec(memory_space=pltpu.VMEM)
    shapes = [jax.ShapeDtypeStruct(shape, jnp.float32) for shape in outs]
    size = sum(4 * math.prod(a.shape) for a in (*args, *shapes))
    return pl.pallas_call(
        kernel,
        out_shape=shapes,
        in_specs=[whole] * len(args),
        out_specs=[whole] * len(outs),
        scratch_shapes=[pltpu.VMEM(shape, jnp.float32) for shape in scratch],
        cost_estimate=pl.CostEstimate(flops=flops, bytes_accessed=size, transcendentals=0),
        compiler_params=pltpu.CompilerParams(vmem_limit_bytes=VMEM_LIMIT),
    )(*args)


def ring(axis, step):
    size = lax.axis_size(axis)
    return [(i, (i + step) % size) for i in range(size)]


def x_halo(block):
    return (lax.ppermute(block, "blk", ring("blk", 1)), lax.ppermute(block, "blk", ring("blk", -1)))


def z_halo(first, last):
    return (lax.ppermute(last, "gz", ring("gz", 1)), lax.ppermute(first, "gz", ring("gz", -1)))


def after(values, *earlier):
    return lax.optimization_barrier((tuple(values), earlier))[0]


def on_device(sqrt_density, ion_charge, ion_potential, hartree_prev, hist_steps, hist_changes):
    block = sqrt_density.shape
    ext = (block[0], block[1] + 16, block[2])
    face = (24, LANES)
    stencil_flops = 60 * math.prod(block)
    cells = math.prod(block)
    history = [hist_steps, hist_changes]
    h_sides = x_halo(hartree_prev)
    h_ends = z_halo(*call(pack_kernel, [face, face], [hartree_prev]))
    rho_sides = x_halo(sqrt_density)
    rho_faces = call(pack_kernel, [face, face], [sqrt_density])
    (inner,) = call(inner_residual_kernel, [block], [hartree_prev, sqrt_density, ion_charge], [ext], stencil_flops)
    halo = after((*h_sides, *h_ends), *rho_sides, inner)
    v0, *faces = call(
        functools.partial(edge_kernel, 1.0),
        [block, (48, LANES), (48, LANES)],
        [inner, *halo, *rho_faces],
        flops=stencil_flops,
    )
    basis = [v0]
    dots, moments = [], []
    for n in range(3):
        halo = (*x_halo(basis[n]), *z_halo(*faces))
        prior = [basis[n - 1]] if n else []
        (inner,) = call(
            functools.partial(inner_basis_kernel, n > 0), [block], [basis[n], *prior], [ext], stencil_flops
        )
        rows, moment = call(
            dots_kernel if n else first_dots_kernel,
            [(24, LANES), (8, LANES)],
            [*prior, basis[n], sqrt_density, *history],
            flops=50 * cells,
        )
        dots.append(rows)
        moments.append(moment)
        done = [inner, rows]
        if n == 0:
            (same,) = call(functools.partial(gram_kernel, "same"), [(72, LANES)], history, flops=144 * cells)
            done.append(same)
            rho_ends = halo[2:]
        if n == 1:
            (cross,) = call(functools.partial(gram_kernel, "cross"), [(64, LANES)], history, flops=128 * cells)
            done.append(cross)
        if n == 2:
            grad, base = call(
                base_kernel,
                [block, (40, LANES)],
                [sqrt_density, *rho_sides, *rho_ends, hartree_prev, ion_potential, *history],
                [ext],
                2 * stencil_flops,
            )
            done.append(base)
        halo = after(halo, *done)
        fresh, *faces = call(
            functools.partial(edge_kernel, -2.0 / SHIFT if n else -1.0 / SHIFT),
            [block, face, face],
            [inner, *halo],
            flops=stencil_flops,
        )
        basis.append(fresh)
    left = lax.ppermute(basis[3], "blk", ring("blk", 1))
    z_left = lax.ppermute(faces[1], "gz", ring("gz", 1))
    (inner,) = call(inner_moment_kernel, [(8, LANES)], [basis[3]], [ext], stencil_flops)
    (sums,) = call(
        last_dots_kernel,
        [(2, LANES)],
        [basis[2], basis[3], sqrt_density, *history, same, cross, base, *dots, *moments],
        [(256, LANES), (24, LANES), (8, LANES)],
        50 * cells,
    )
    left, z_left = after((left, z_left), inner, sums)
    devices = lax.axis_size("blk") * lax.axis_size("gz")
    (outgoing,) = call(send_kernel, [(devices, 2, LANES)], [basis[3], left, z_left, inner, sums], flops=stencil_flops)
    received = lax.all_to_all(outgoing, ("blk", "gz"), 0, 0, tiled=True)
    return tuple(
        call(
            final_kernel,
            [block, block],
            [received, sqrt_density, hartree_prev, grad, *basis, hist_steps, hist_changes],
            [(384, LANES)],
            50 * math.prod(block),
        )
    )


def solution(mesh):
    placed = (
        P("blk", None, "gz"),
        P("blk", None, "gz"),
        P("blk", None, "gz"),
        P("blk", None, "gz"),
        P(None, "blk", None, "gz"),
        P(None, "blk", None, "gz"),
    )
    return jax.shard_map(
        on_device,
        mesh=mesh,
        in_specs=placed,
        out_specs=(P("blk", None, "gz"), P("blk", None, "gz")),
        check_vma=False,
    )
```

```python
import functools
import math

import jax
import jax.numpy as jnp
from jax import lax
from jax.experimental import pallas as pl
from jax.experimental.pallas import tpu as pltpu
from jax.sharding import PartitionSpec as P

center = -5369.0 / 1800.0
coeffs = (12.0 / 7.0, -15.0 / 56.0, 10.0 / 189.0, -1.0 / 112.0, 2.0 / 825.0, -1.0 / 4752.0)
screen = 0.0025
spacing = 0.28
source_scale = 4.0 * math.pi * spacing * spacing
tf_scale = 5.0 / 3.0 * 2.871234
step_length = 0.01
damp_floor = 0.2

SHIFT = 2.0
HIST = 8
REACH = 6
LANES = 128
VMEM_LIMIT = 24 * 1024 * 1024

ROW_GRAM = 0
ROW_BASE = 136
ROW_W = 170
ROW_MOM = 238
PAIRS = tuple((i, j) for i in range(HIST) for j in range(i, HIST))
PAIR_ROW = {pair: row for row, pair in enumerate(PAIRS)}


def two_sum(a, b):
    s = a + b
    bb = s - a
    return s, (a - (s - bb)) + (b - bb)


def quick_sum(a, b):
    s = a + b
    return s, b - (s - a)


def split(a):
    t = 4097.0 * a
    hi = t - (t - a)
    return hi, a - hi


def two_prod(a, b):
    p = a * b
    ah, al = split(a)
    bh, bl = split(b)
    return p, ((ah * bh - p) + ah * bl + al * bh) + al * bl


def df_add(a, b):
    s, e = two_sum(a[0], b[0])
    return quick_sum(s, e + (a[1] + b[1]))


def df_neg(a):
    return (-a[0], -a[1])


def df_sub(a, b):
    return df_add(a, df_neg(b))


def df_scale(a, factor):
    return (a[0] * factor, a[1] * factor)


def df_mul(a, b):
    p, e = two_prod(a[0], b[0])
    return quick_sum(p, e + (a[0] * b[1] + a[1] * b[0]))


def df_div(a, b):
    q1 = a[0] / b[0]
    r = df_sub(a, df_mul(b, (q1, jnp.zeros_like(q1))))
    q2 = r[0] / b[0]
    return quick_sum(q1, q2)


def lane_ids(shape):
    return lax.broadcasted_iota(jnp.int32, shape, len(shape) - 1)


def inner_plane(i, own, ext):
    values = own[i]
    rows = values.shape[0]
    lane = lane_ids((rows, LANES))
    total = (3.0 * center) * values
    for k, weight in enumerate(coeffs, 1):
        pair = ext[i, 8 + k : 8 + k + rows, :] + ext[i, 8 - k : 8 - k + rows, :]
        if i + k < REACH:
            pair = pair + own[i + k]
        if i - k >= 0:
            pair = pair + own[i - k]
        up = pltpu.roll(jnp.where(lane < k, 0.0, values), LANES - k, 1)
        down = pltpu.roll(jnp.where(lane >= LANES - k, 0.0, values), k, 1)
        total = total + weight * (pair + (up + down))
    return total, values


def edge_faces(z_left, z_right):
    lane = lane_ids((24, LANES)) % 8
    lower = jnp.zeros((24, LANES), jnp.float32)
    upper = jnp.zeros((24, LANES), jnp.float32)
    for k, weight in enumerate(coeffs, 1):
        lower = lower + jnp.where(lane < k, weight * pltpu.roll(z_left, LANES - 8 + k, 1), 0.0)
        if z_right is not None:
            upper = upper + jnp.where(lane >= 8 - k, weight * pltpu.roll(z_right, 8 - k, 1), 0.0)
    return lower, upper


def edge_plane(i, left, right, faces):
    total = None
    for k, weight in enumerate(coeffs, 1):
        terms = []
        if i - k < 0:
            terms.append(left[i - k + REACH])
        if right is not None and i + k >= REACH:
            terms.append(right[i + k - REACH])
        for term in terms:
            total = weight * term if total is None else total + weight * term
    lane = lane_ids((8, LANES))
    lower, upper = (face[8 * (i // 2) : 8 * (i // 2) + 8] for face in faces)
    tiles = []
    for b in range(total.shape[0] // 8):
        j = 8 * (i % 2) + b
        tile = jnp.where(lane < 8, pltpu.roll(lower, (LANES - 8 * j) % LANES, 1), 0.0)
        if right is not None:
            tile = jnp.where(lane >= LANES - 8, pltpu.roll(upper, (2 * LANES - 8 - 8 * j) % LANES, 1), tile)
        tiles.append(tile)
    return total + jnp.concatenate(tiles, axis=0)


def fill_ext(own, ext):
    rows = own.shape[1]
    ext[:, 8 : 8 + rows, :] = own[...]
    ext[:, 0:8, :] = own[:, rows - 8 : rows, :]
    ext[:, 8 + rows : 16 + rows, :] = own[:, 0:8, :]


def pack_faces(src, layers):
    lane = lane_ids((8, LANES))
    firsts, lasts = [], []
    for m in range(3):
        first = jnp.zeros((8, LANES), jnp.float32)
        last = jnp.zeros((8, LANES), jnp.float32)
        for j in range(16):
            n = 16 * m + j
            tile = src[layers + n // 8, 8 * (n % 8) : 8 * (n % 8) + 8, :]
            here = (lane >= 8 * j) & (lane < 8 * j + 8)
            first = jnp.where(here, pltpu.roll(tile, 8 * j, 1) if j else tile, first)
            last = jnp.where(here, pltpu.roll(tile, (8 * j + 8) % LANES, 1) if j < 15 else tile, last)
        firsts.append(first)
        lasts.append(last)
    return jnp.concatenate(firsts, axis=0), jnp.concatenate(lasts, axis=0)


def is_odd(axis):
    return lax.rem(lax.axis_index(axis), 2) == 1


def by_partner(lower, upper):
    odd = is_odd("gz")
    return jnp.where(odd, lower, upper), jnp.where(odd, upper, lower)


def by_side(first, second):
    odd = is_odd("gz")
    return jnp.where(odd, first, second), jnp.where(odd, second, first)


def with_sides(near, far, body):
    odd = is_odd("blk")

    @pl.when(odd)
    def _():
        body(near, far)

    @pl.when(jnp.logical_not(odd))
    def _():
        body(far, near)


def exact_total(hi, lo):
    for step in (4, 2, 1):
        hi, err = two_sum(hi, pltpu.roll(hi, step, 0))
        lo = lo + pltpu.roll(lo, step, 0) + err
    hi, lo = hi[0:1], lo[0:1]
    for step in (64, 32, 16, 8, 4, 2, 1):
        hi, err = two_sum(hi, pltpu.roll(hi, step, 1))
        lo = lo + pltpu.roll(lo, step, 1) + err
    return quick_sum(hi, lo)


def add_tile(acc, product):
    hi, err = two_sum(acc[0], product)
    return hi, acc[1] + err


def tile_of(ref, i, b):
    return ref[i, pl.ds(pl.multiple_of(8 * b, 8), 8), :]


def exact_dots(pairs):
    zero = jnp.zeros((8, LANES), jnp.float32)

    def body(i, accs):
        for b in range(8):
            accs = tuple(
                add_tile(acc, tile_of(a, i, b) * tile_of(c, i, b)) for acc, (a, c) in zip(accs, pairs)
            )
        return accs

    accs = lax.fori_loop(0, REACH, body, tuple((zero, zero) for _ in pairs))
    return [exact_total(*acc) for acc in accs]


def collapse(acc):
    return jnp.sum(acc, axis=0, keepdims=True)


def launch_kernel(hartree, density, both, face_a, face_b, sems):
    copies = [
        pltpu.make_async_copy(src, both.at[pl.ds(REACH * n, REACH)], sems.at[n])
        for n, src in enumerate((hartree, density))
    ]
    for copy in copies:
        copy.start()
    for n, copy in enumerate(copies):
        copy.wait()
        rows = slice(24 * n, 24 * n + 24)
        face_a[rows, :], face_b[rows, :] = by_partner(*pack_faces(both, REACH * n))


def inner_residual_kernel(both, charge, out, ext):
    hartree = both.at[pl.ds(0, REACH)]
    fill_ext(hartree, ext)
    for i in range(REACH):
        lap, values = inner_plane(i, hartree, ext)
        rho = both[REACH + i]
        out[i] = source_scale * (rho * rho - charge[i]) - (screen * values - lap)


def inner_basis_kernel(has_prior, *refs):
    own, prior, out, ext = refs if has_prior else (refs[0], None, *refs[1:])
    fill_ext(own, ext)
    for i in range(REACH):
        lap, values = inner_plane(i, own, ext)
        moved = (screen / SHIFT - 1.0) * values - (1.0 / SHIFT) * lap
        out[i] = 2.0 * moved - prior[i] if has_prior else moved


def edge_kernel(gain, last, inner, near, far, z_first, z_second, out, face_a, face_b):
    faces = edge_faces(*by_side(z_first[0:24, :], z_second[0:24, :]))

    def body(left, right):
        for i in range(REACH):
            out[i] = inner[i] + gain * edge_plane(i, left, right, faces)

    with_sides(near, far, body)
    packed = pack_faces(out, 0)
    face_a[...], face_b[...] = packed if last else by_partner(*packed)


def gram_kernel(work, steps, changes, rows):
    zero = jnp.zeros((8, LANES), jnp.float32)

    def run(base, left, right, pairs):
        def body(i, accs):
            for b in range(8):
                at = pl.ds(8 * b, 8)
                l_tiles = {p: left[p, i, at, :] for p in sorted({p for p, _ in pairs})}
                if left is right:
                    r_tiles = l_tiles
                else:
                    r_tiles = {q: right[q, i, at, :] for q in sorted({q for _, q in pairs})}
                accs = tuple(acc + l_tiles[p] * r_tiles[q] for acc, (p, q) in zip(accs, pairs))
            return accs

        accs = lax.fori_loop(0, REACH, body, tuple(zero for _ in pairs))
        for n, acc in enumerate(accs):
            rows[base + n : base + n + 1, :] = collapse(acc)

    if work == "same":
        run(0, steps, steps, PAIRS)
        run(36, changes, changes, PAIRS)
    else:
        run(0, steps, changes, tuple((i, j) for i in range(4) for j in range(8)))
        run(32, steps, changes, tuple((i, j) for i in range(4, 8) for j in range(8)))


def field_dots(steps, changes, others):
    zero = jnp.zeros((8, LANES), jnp.float32)
    count = 2 * HIST

    def body(i, accs):
        accs = list(accs)
        for b in range(8):
            at = pl.ds(8 * b, 8)
            tiles = [other(i, b) for other in others]
            for f in range(count):
                field = steps[f, i, at, :] if f < HIST else changes[f - HIST, i, at, :]
                for o, tile in enumerate(tiles):
                    accs[o * count + f] = accs[o * count + f] + field * tile
        return tuple(accs)

    accs = lax.fori_loop(0, REACH, body, tuple(zero for _ in range(count * len(others))))
    return [collapse(acc) for acc in accs]


def plain_dots(pairs):
    zero = jnp.zeros((8, LANES), jnp.float32)

    def body(i, accs):
        for b in range(8):
            accs = tuple(acc + a(i, b) * c(i, b) for acc, (a, c) in zip(accs, pairs))
        return accs

    return [collapse(acc) for acc in lax.fori_loop(0, REACH, body, tuple(zero for _ in pairs))]


def base_kernel(both, near, far, z_first, z_second, potential, steps, changes, grad, rows, ext):
    hartree = both.at[pl.ds(0, REACH)]
    density = both.at[pl.ds(REACH, REACH)]
    fill_ext(density, ext)
    faces = edge_faces(*by_side(z_first[24:48, :], z_second[24:48, :]))

    def body(left, right):
        for i in range(REACH):
            grad[i] = edge_plane(i, left, right, faces)

    with_sides(near.at[pl.ds(REACH, REACH)], far.at[pl.ds(REACH, REACH)], body)
    for i in range(REACH):
        lap, rho = inner_plane(i, density, ext)
        power = jnp.exp(jnp.log(rho) * (4.0 / 3.0))
        grad[i] = 2.0 * rho * (hartree[i] + potential[i] + tf_scale * power) - (lap + grad[i]) * (
            1.0 / (spacing * spacing)
        )
    g_tile = lambda i, b: tile_of(grad, i, b)
    r_tile = lambda i, b: tile_of(density, i, b)
    dots = field_dots(steps, changes, [g_tile, r_tile]) + plain_dots([(r_tile, g_tile), (r_tile, r_tile)])
    for n, row in enumerate(dots):
        rows[n : n + 1, :] = row


def basis_dots(vector, density, steps, changes, rows):
    w_tile = lambda i, b: 2.0 * tile_of(density, i, b) * tile_of(vector, i, b)
    r_tile = lambda i, b: tile_of(density, i, b)
    dots = field_dots(steps, changes, [w_tile]) + plain_dots([(r_tile, w_tile)])
    for n, row in enumerate(dots):
        rows[n : n + 1, :] = row


def store_moments(pairs, moments):
    for n, (hi, lo) in enumerate(exact_dots(pairs)):
        moments[2 * n : 2 * n + 1, :] = hi
        moments[2 * n + 1 : 2 * n + 2, :] = lo


def first_dots_kernel(vector, density, steps, changes, rows, moments):
    basis_dots(vector, density, steps, changes, rows)
    store_moments([(vector, vector)], moments)


def dots_kernel(prior, vector, density, steps, changes, rows, moments):
    basis_dots(vector, density, steps, changes, rows)
    store_moments([(prior, vector), (vector, vector)], moments)


def last_dots_kernel(
    prior, vector, density, steps, changes, same, cross, base, d0, d1, d2, m0, m1, m2, out, rows, own_rows, moments
):
    basis_dots(vector, density, steps, changes, own_rows)
    store_moments([(prior, vector), (vector, vector)], moments)
    rows[ROW_GRAM : ROW_GRAM + 72, :] = same[...]
    rows[ROW_GRAM + 72 : ROW_GRAM + 136, :] = cross[...]
    rows[ROW_BASE : ROW_BASE + 34, :] = base[0:34, :]
    for n, d in enumerate((d0, d1, d2, own_rows)):
        rows[ROW_W + 17 * n : ROW_W + 17 * n + 17, :] = d[0:17, :]
    rows[ROW_MOM:256, :] = jnp.zeros((256 - ROW_MOM, LANES), jnp.float32)
    lane = lane_ids((1, LANES))
    out[0:1, :] = jnp.sum(jnp.transpose(rows[0:128, :]), axis=0, keepdims=True)
    second = jnp.sum(jnp.transpose(rows[128:256, :]), axis=0, keepdims=True)
    at = ROW_MOM - 128
    order = [(m0, 0), (m1, 0), (m1, 1), (m2, 0), (m2, 1), (moments, 0), (moments, 1)]
    for n, (ref, which) in enumerate(order):
        second = jnp.where(lane == at + n, ref[2 * which : 2 * which + 1, :], second)
        second = jnp.where(lane == at + 8 + n, ref[2 * which + 1 : 2 * which + 2, :], second)
    out[1:2, :] = second


def inner_moment_kernel(own, out, ext):
    fill_ext(own, ext)
    zero = jnp.zeros((8, LANES), jnp.float32)
    accs = [(zero, zero) for _ in range(2)]
    for i in range(REACH):
        lap, values = inner_plane(i, own, ext)
        product = values * ((screen / SHIFT - 1.0) * values - (1.0 / SHIFT) * lap)
        for b in range(8):
            accs[b % 2] = add_tile(accs[b % 2], product[8 * b : 8 * b + 8])
    hi, err = two_sum(accs[0][0], accs[1][0])
    hi, lo = exact_total(hi, accs[0][1] + accs[1][1] + err)
    out[0:1, :] = hi
    out[1:2, :] = lo


def send_kernel(own, left, z_left, inner, sums, out):
    faces = edge_faces(z_left[...], None)
    zero = jnp.zeros((8, LANES), jnp.float32)
    accs = [(zero, zero) for _ in range(2)]
    for i in range(REACH):
        product = own[i] * edge_plane(i, left, None, faces)
        for b in range(8):
            accs[b % 2] = add_tile(accs[b % 2], product[8 * b : 8 * b + 8])
    hi, err = two_sum(accs[0][0], accs[1][0])
    coupling = exact_total(hi, accs[0][1] + accs[1][1] + err)
    hi, lo = df_add(df_scale(coupling, -2.0 / SHIFT), (inner[0:1, :], inner[1:2, :]))
    lane = lane_ids((1, LANES))
    at = ROW_MOM - 128
    second = jnp.where(lane == at + 7, hi, jnp.where(lane == at + 15, lo, sums[1:2, :]))
    both = jnp.concatenate([sums[0:1, :], second], axis=0)
    out[...] = jnp.broadcast_to(both[None], out.shape)


def solve_krylov(moment):
    n00, n01, n11, n12, n22, n23, n33, n34 = moment
    nu = [n00, n01]
    nu.append(df_sub(df_scale(n11, 2.0), n00))
    nu.append(df_sub(df_scale(n12, 2.0), n01))
    nu.append(df_sub(df_scale(n22, 2.0), n00))
    nu.append(df_sub(df_scale(n23, 2.0), n01))
    nu.append(df_sub(df_scale(n33, 2.0), n00))

    def gram(i, j):
        if i == j == 0:
            return n00
        return df_scale(df_add(nu[i + j], nu[abs(i - j)]), 0.5)

    def moved(i, j):
        if i == 3 and j == 3:
            return n34
        if j == 0:
            return gram(i, 1)
        return df_scale(df_add(gram(i, j + 1), gram(i, j - 1)), 0.5)

    mat = {(i, j): df_add(moved(i, j), gram(i, j)) for i in range(4) for j in range(i + 1)}
    rhs = [df_scale(gram(i, 0), 1.0 / SHIFT) for i in range(4)]
    low = {}
    for k in range(4):
        for i in range(k + 1, 4):
            low[i, k] = df_div(mat[i, k], mat[k, k])
        for i in range(k + 1, 4):
            for j in range(k + 1, i + 1):
                mat[i, j] = df_sub(mat[i, j], df_mul(low[i, k], mat[j, k]))
            rhs[i] = df_sub(rhs[i], df_mul(low[i, k], rhs[k]))
    sol = [None] * 4
    for k in reversed(range(4)):
        value = df_div(rhs[k], mat[k, k])
        for i in range(k + 1, 4):
            value = df_sub(value, df_mul(low[i, k], sol[i]))
        sol[k] = value
    return [hi + lo for hi, lo in sol]


def final_kernel(received, density, hartree, grad, v0, v1, v2, v3, steps, changes, new_density, new_hartree, spread):
    chains = 8
    parts = [(received[n], jnp.zeros((2, LANES), jnp.float32)) for n in range(chains)]
    for n in range(chains, received.shape[0]):
        parts[n % chains] = add_tile(parts[n % chains], received[n])
    while len(parts) > 1:
        half = len(parts) // 2
        merged = []
        for a, b in zip(parts[:half], parts[half:]):
            hi, err = two_sum(a[0], b[0])
            merged.append((hi, a[1] + b[1] + err))
        parts = merged
    hi, lo = quick_sum(*parts[0])
    spread[0:128, :] = jnp.transpose(jnp.broadcast_to(hi[0:1], (LANES, LANES)))
    spread[128:256, :] = jnp.transpose(jnp.broadcast_to(hi[1:2], (LANES, LANES)))
    spread[256:384, :] = jnp.transpose(jnp.broadcast_to(lo[1:2], (LANES, LANES)))

    def row(n):
        return spread[n : n + 1, :]

    def moment(n):
        low = 128 + ROW_MOM
        a = df_add((row(ROW_MOM + n), row(low + n)), (row(ROW_MOM + 8 + n), row(low + 8 + n)))
        return a

    mix = solve_krylov([moment(n) for n in range(8)])

    def s_s(i, j):
        return row(ROW_GRAM + PAIR_ROW[min(i, j), max(i, j)])

    def y_y(i, j):
        return row(ROW_GRAM + 36 + PAIR_ROW[min(i, j), max(i, j)])

    def s_y(i, j):
        return row(ROW_GRAM + 72 + 8 * i + j)

    pairs = range(HIST)
    theta, rest, inverse = [], [], []
    for i in pairs:
        curv, norm = s_y(i, i), s_s(i, i)
        kept = (1.0 - damp_floor) * norm
        damp = jnp.where(curv >= damp_floor * norm, 1.0, kept / jnp.maximum(norm - curv, kept))
        theta.append(damp)
        rest.append(1.0 - damp)
        inverse.append(1.0 / (damp * curv + (1.0 - damp) * norm))

    def s_bar(i, j):
        return theta[j] * s_y(i, j) + rest[j] * s_s(i, j)

    def bar_bar(i, j):
        return theta[i] * (theta[j] * y_y(i, j) + rest[j] * s_y(j, i)) + rest[i] * s_bar(i, j)

    last = HIST - 1
    scaling = s_bar(last, last) / bar_bar(last, last)

    def energy(n):
        value = row(ROW_BASE + n) if n < 16 else row(ROW_BASE + 32)
        for j in range(4):
            value = value + mix[j] * row(ROW_W + 17 * j + n)
        return value

    chem = energy(16) / row(ROW_BASE + 33)

    def gradient(n):
        return energy(n) - chem * row(ROW_BASE + 16 + n)

    s_grad = [gradient(i) for i in pairs]
    bar_grad = [theta[i] * gradient(HIST + i) + rest[i] * s_grad[i] for i in pairs]

    first = [None] * HIST
    pending = list(s_grad)
    for j in reversed(pairs):
        first[j] = inverse[j] * pending[j]
        for i in range(j):
            pending[i] = pending[i] - first[j] * s_bar(i, j)
    pending = list(bar_grad)
    for j in pairs:
        for i in pairs:
            pending[i] = pending[i] - first[j] * bar_bar(i, j)
    pending = [scaling * value for value in pending]
    step_mix, change_mix = [], []
    for j in pairs:
        net = first[j] - inverse[j] * pending[j]
        for i in range(j + 1, HIST):
            pending[i] = pending[i] + net * s_bar(j, i)
        change_mix.append((-step_length) * (-scaling * first[j] * theta[j]))
        step_mix.append((-step_length) * (net - scaling * first[j] * rest[j]))

    wide = lambda value: jnp.broadcast_to(value, (8, LANES))
    mix = [wide(value) for value in mix]
    chem, gain = wide(chem), wide((-step_length) * scaling)
    step_mix = [wide(value) for value in step_mix]
    change_mix = [wide(value) for value in change_mix]
    basis = (v0, v1, v2, v3)

    @pl.loop(0, REACH)
    def _(i):
        for b in range(8):
            at = pl.ds(8 * b, 8)
            rho = density[i, at, :]
            lift = mix[0] * v0[i, at, :]
            for j in range(1, 4):
                lift = lift + mix[j] * basis[j][i, at, :]
            new_hartree[i, at, :] = hartree[i, at, :] + lift
            slope = grad[i, at, :] + 2.0 * rho * lift - chem * rho
            parts = [rho, gain * slope, step_mix[0] * steps[0, i, at, :], change_mix[0] * changes[0, i, at, :]]
            for f in range(1, HIST):
                parts[2] = parts[2] + step_mix[f] * steps[f, i, at, :]
                parts[3] = parts[3] + change_mix[f] * changes[f, i, at, :]
            new_density[i, at, :] = parts[0] + (parts[1] + (parts[2] + parts[3]))


def call(kernel, outs, args, scratch=(), flops=0, place=pltpu.VMEM):
    whole = pl.BlockSpec(memory_space=pltpu.VMEM)
    shapes = [jax.ShapeDtypeStruct(shape, jnp.float32) for shape in outs]
    size = sum(4 * math.prod(a.shape) for a in (*args, *shapes))
    return pl.pallas_call(
        kernel,
        out_shape=shapes,
        in_specs=[pl.BlockSpec(memory_space=place)] * len(args),
        out_specs=[whole] * len(outs),
        scratch_shapes=[pltpu.VMEM(s, jnp.float32) if isinstance(s, tuple) else s for s in scratch],
        cost_estimate=pl.CostEstimate(flops=flops, bytes_accessed=size, transcendentals=0),
        compiler_params=pltpu.CompilerParams(vmem_limit_bytes=VMEM_LIMIT),
    )(*args)


def ring(axis, step):
    size = lax.axis_size(axis)
    return [(i, (i + step) % size) for i in range(size)]


def swap(axis, odd_up):
    size = lax.axis_size(axis)
    return [(i, (i + (1 if i % 2 == odd_up else -1)) % size) for i in range(size)]


def x_halo(block):
    far = lax.ppermute(block, "blk", swap("blk", 1))
    return (lax.ppermute(block, "blk", swap("blk", 0)), far)


def z_halo(face_a, face_b):
    return (lax.ppermute(face_a, "gz", swap("gz", 0)), lax.ppermute(face_b, "gz", swap("gz", 1)))


def after(values, *earlier):
    return lax.optimization_barrier((tuple(values), earlier))[0]


def on_device(sqrt_density, ion_charge, ion_potential, hartree_prev, hist_steps, hist_changes):
    block = sqrt_density.shape
    ext = (block[0], block[1] + 16, block[2])
    face = (24, LANES)
    stencil_flops = 60 * math.prod(block)
    cells = math.prod(block)
    history = [hist_steps, hist_changes]
    both, *faces = call(
        launch_kernel,
        [(2 * REACH, *block[1:]), (48, LANES), (48, LANES)],
        [pltpu.with_memory_space_constraint(x, pltpu.HBM) for x in (hartree_prev, sqrt_density)],
        [pltpu.SemaphoreType.DMA((2,))],
        place=pltpu.HBM,
    )
    start = (*x_halo(both), *z_halo(*faces))
    (inner,) = call(inner_residual_kernel, [block], [both, ion_charge], [ext], stencil_flops)
    halo = after(start, inner)
    v0, *faces = call(
        functools.partial(edge_kernel, 1.0, False), [block, face, face], [inner, *halo], flops=stencil_flops
    )
    basis = [v0]
    dots, moments = [], []
    for n in range(3):
        halo = (*x_halo(basis[n]), *z_halo(*faces))
        prior = [basis[n - 1]] if n else []
        (inner,) = call(
            functools.partial(inner_basis_kernel, n > 0), [block], [basis[n], *prior], [ext], stencil_flops
        )
        rows, moment = call(
            dots_kernel if n else first_dots_kernel,
            [(24, LANES), (8, LANES)],
            [*prior, basis[n], sqrt_density, *history],
            flops=50 * cells,
        )
        dots.append(rows)
        moments.append(moment)
        done = [inner, rows]
        if n == 0:
            (same,) = call(functools.partial(gram_kernel, "same"), [(72, LANES)], history, flops=144 * cells)
            done.append(same)
        if n == 1:
            (cross,) = call(functools.partial(gram_kernel, "cross"), [(64, LANES)], history, flops=128 * cells)
            done.append(cross)
        if n == 2:
            grad, base = call(
                base_kernel,
                [block, (40, LANES)],
                [both, *start, ion_potential, *history],
                [ext],
                2 * stencil_flops,
            )
            done.append(base)
        halo = after(halo, *done)
        fresh, *faces = call(
            functools.partial(edge_kernel, -2.0 / SHIFT if n else -1.0 / SHIFT, n == 2),
            [block, face, face],
            [inner, *halo],
            flops=stencil_flops,
        )
        basis.append(fresh)
    left = lax.ppermute(basis[3], "blk", ring("blk", 1))
    z_left = lax.ppermute(faces[1], "gz", ring("gz", 1))
    (inner,) = call(inner_moment_kernel, [(8, LANES)], [basis[3]], [ext], stencil_flops)
    (sums,) = call(
        last_dots_kernel,
        [(2, LANES)],
        [basis[2], basis[3], sqrt_density, *history, same, cross, base, *dots, *moments],
        [(256, LANES), (24, LANES), (8, LANES)],
        50 * cells,
    )
    left, z_left = after((left, z_left), inner, sums)
    devices = lax.axis_size("blk") * lax.axis_size("gz")
    (outgoing,) = call(send_kernel, [(devices, 2, LANES)], [basis[3], left, z_left, inner, sums], flops=stencil_flops)
    received = lax.all_to_all(outgoing, ("blk", "gz"), 0, 0, tiled=True)
    return tuple(
        call(
            final_kernel,
            [block, block],
            [received, sqrt_density, hartree_prev, grad, *basis, hist_steps, hist_changes],
            [(384, LANES)],
            50 * math.prod(block),
        )
    )


def solution(mesh):
    placed = (
        P("blk", None, "gz"),
        P("blk", None, "gz"),
        P("blk", None, "gz"),
        P("blk", None, "gz"),
        P(None, "blk", None, "gz"),
        P(None, "blk", None, "gz"),
    )
    return jax.shard_map(
        on_device,
        mesh=mesh,
        in_specs=placed,
        out_specs=(P("blk", None, "gz"), P("blk", None, "gz")),
        check_vma=False,
    )
```

```python
import functools
import math

import jax
import jax.numpy as jnp
from jax import lax
from jax.experimental import pallas as pl
from jax.experimental.pallas import tpu as pltpu
from jax.sharding import PartitionSpec as P

center = -5369.0 / 1800.0
coeffs = (12.0 / 7.0, -15.0 / 56.0, 10.0 / 189.0, -1.0 / 112.0, 2.0 / 825.0, -1.0 / 4752.0)
screen = 0.0025
spacing = 0.28
source_scale = 4.0 * math.pi * spacing * spacing
tf_scale = 5.0 / 3.0 * 2.871234
step_length = 0.01
damp_floor = 0.2

SHIFT = 2.0
HIST = 8
REACH = 6
LANES = 128
VMEM_LIMIT = 24 * 1024 * 1024

ROW_GRAM = 0
ROW_BASE = 136
ROW_W = 170
ROW_MOM = 238
HALF = 126


def place(n):
    return n if n < HALF else n + LANES - HALF


MOM_LANE = place(ROW_MOM) - LANES
PAIRS = tuple((i, j) for i in range(HIST) for j in range(i, HIST))
PAIR_ROW = {pair: row for row, pair in enumerate(PAIRS)}


def two_sum(a, b):
    s = a + b
    bb = s - a
    return s, (a - (s - bb)) + (b - bb)


def quick_sum(a, b):
    s = a + b
    return s, b - (s - a)


def split(a):
    t = 4097.0 * a
    hi = t - (t - a)
    return hi, a - hi


def two_prod(a, b):
    p = a * b
    ah, al = split(a)
    bh, bl = split(b)
    return p, ((ah * bh - p) + ah * bl + al * bh) + al * bl


def df_add(a, b):
    s, e = two_sum(a[0], b[0])
    return quick_sum(s, e + (a[1] + b[1]))


def df_neg(a):
    return (-a[0], -a[1])


def df_sub(a, b):
    return df_add(a, df_neg(b))


def df_scale(a, factor):
    return (a[0] * factor, a[1] * factor)


def df_mul(a, b):
    p, e = two_prod(a[0], b[0])
    return quick_sum(p, e + (a[0] * b[1] + a[1] * b[0]))


def df_div(a, b):
    q1 = a[0] / b[0]
    r = df_sub(a, df_mul(b, (q1, jnp.zeros_like(q1))))
    q2 = r[0] / b[0]
    return quick_sum(q1, q2)


def lane_ids(shape):
    return lax.broadcasted_iota(jnp.int32, shape, len(shape) - 1)


def inner_plane(i, own, ext):
    values = own[i]
    rows = values.shape[0]
    lane = lane_ids((rows, LANES))
    total = (3.0 * center) * values
    for k, weight in enumerate(coeffs, 1):
        pair = ext[i, 8 + k : 8 + k + rows, :] + ext[i, 8 - k : 8 - k + rows, :]
        if i + k < REACH:
            pair = pair + own[i + k]
        if i - k >= 0:
            pair = pair + own[i - k]
        up = pltpu.roll(jnp.where(lane < k, 0.0, values), LANES - k, 1)
        down = pltpu.roll(jnp.where(lane >= LANES - k, 0.0, values), k, 1)
        total = total + weight * (pair + (up + down))
    return total, values


def edge_faces(z_left, z_right):
    lane = lane_ids((24, LANES)) % 8
    lower = jnp.zeros((24, LANES), jnp.float32)
    upper = jnp.zeros((24, LANES), jnp.float32)
    for k, weight in enumerate(coeffs, 1):
        lower = lower + jnp.where(lane < k, weight * pltpu.roll(z_left, LANES - 8 + k, 1), 0.0)
        if z_right is not None:
            upper = upper + jnp.where(lane >= 8 - k, weight * pltpu.roll(z_right, 8 - k, 1), 0.0)
    return lower, upper


def edge_plane(i, left, right, faces):
    total = None
    for k, weight in enumerate(coeffs, 1):
        terms = []
        if i - k < 0:
            terms.append(left[i - k + REACH])
        if right is not None and i + k >= REACH:
            terms.append(right[i + k - REACH])
        for term in terms:
            total = weight * term if total is None else total + weight * term
    lane = lane_ids((8, LANES))
    lower, upper = (face[8 * (i // 2) : 8 * (i // 2) + 8] for face in faces)
    tiles = []
    for b in range(total.shape[0] // 8):
        j = 8 * (i % 2) + b
        tile = jnp.where(lane < 8, pltpu.roll(lower, (LANES - 8 * j) % LANES, 1), 0.0)
        if right is not None:
            tile = jnp.where(lane >= LANES - 8, pltpu.roll(upper, (2 * LANES - 8 - 8 * j) % LANES, 1), tile)
        tiles.append(tile)
    return total + jnp.concatenate(tiles, axis=0)


def fill_ext(own, ext):
    rows = own.shape[1]
    ext[:, 8 : 8 + rows, :] = own[...]
    ext[:, 0:8, :] = own[:, rows - 8 : rows, :]
    ext[:, 8 + rows : 16 + rows, :] = own[:, 0:8, :]


def pack_faces(src, layers):
    lane = lane_ids((8, LANES))
    firsts, lasts = [], []
    for m in range(3):
        first = jnp.zeros((8, LANES), jnp.float32)
        last = jnp.zeros((8, LANES), jnp.float32)
        for j in range(16):
            n = 16 * m + j
            tile = src[layers + n // 8, 8 * (n % 8) : 8 * (n % 8) + 8, :]
            here = (lane >= 8 * j) & (lane < 8 * j + 8)
            first = jnp.where(here, pltpu.roll(tile, 8 * j, 1) if j else tile, first)
            last = jnp.where(here, pltpu.roll(tile, (8 * j + 8) % LANES, 1) if j < 15 else tile, last)
        firsts.append(first)
        lasts.append(last)
    return jnp.concatenate(firsts, axis=0), jnp.concatenate(lasts, axis=0)


def is_odd(axis):
    return lax.rem(lax.axis_index(axis), 2) == 1


def by_partner(lower, upper):
    odd = is_odd("gz")
    return jnp.where(odd, lower, upper), jnp.where(odd, upper, lower)


def by_side(first, second):
    odd = is_odd("gz")
    return jnp.where(odd, first, second), jnp.where(odd, second, first)


def with_sides(near, far, body):
    odd = is_odd("blk")

    @pl.when(odd)
    def _():
        body(near, far)

    @pl.when(jnp.logical_not(odd))
    def _():
        body(far, near)


def fold(hi, lo, axis, steps):
    for step in steps:
        hi, err = two_sum(hi, pltpu.roll(hi, step, axis))
        lo = lo + pltpu.roll(lo, step, axis) + err
    return hi, lo


def fold_rows(acc):
    hi, lo = fold(*acc, 0, (4, 2, 1))
    return hi[0:1], lo[0:1]


def fold_lanes(hi, lo):
    return quick_sum(*fold(hi, lo, 1, (64, 32, 16, 8, 4, 2, 1)))


def add_tile(acc, product):
    hi, err = two_sum(acc[0], product)
    return hi, acc[1] + err


def tile_of(ref, i, b):
    return ref[i, 8 * b : 8 * b + 8, :]


def store_moments(pairs, moments):
    zero = jnp.zeros((8, LANES), jnp.float32)

    def body(i, accs):
        for b in range(8):
            accs = tuple(
                add_tile(acc, tile_of(a, i, b) * tile_of(c, i, b)) for acc, (a, c) in zip(accs, pairs)
            )
        return accs

    accs = lax.fori_loop(0, REACH, body, tuple((zero, zero) for _ in pairs))
    for n, acc in enumerate(accs):
        moments[2 * n : 2 * n + 1, :], moments[2 * n + 1 : 2 * n + 2, :] = fold_rows(acc)


def collapse(acc):
    return jnp.sum(acc, axis=0, keepdims=True)


def launch_kernel(hartree, density, charge, both, charge_here, face_a, face_b, sems):
    places = (both.at[pl.ds(0, REACH)], both.at[pl.ds(REACH, REACH)], charge_here)
    copies = [
        pltpu.make_async_copy(src, dst, sems.at[n])
        for n, (src, dst) in enumerate(zip((hartree, density, charge), places))
    ]
    for copy in copies:
        copy.start()
    for n in range(2):
        copies[n].wait()
        rows = slice(24 * n, 24 * n + 24)
        face_a[rows, :], face_b[rows, :] = by_partner(*pack_faces(both, REACH * n))
    copies[2].wait()


def inner_residual(both, charge, out, ext):
    hartree = both.at[pl.ds(0, REACH)]
    fill_ext(hartree, ext)
    for i in range(REACH):
        lap, values = inner_plane(i, hartree, ext)
        rho = both[REACH + i]
        out[i] = source_scale * (rho * rho - charge[i]) - (screen * values - lap)


def inner_basis(own, prior, out, ext):
    fill_ext(own, ext)
    for i in range(REACH):
        lap, values = inner_plane(i, own, ext)
        moved = (screen / SHIFT - 1.0) * values - (1.0 / SHIFT) * lap
        out[i] = moved if prior is None else 2.0 * moved - prior[i]


def edge_kernel(gain, last, inner, near, far, z_first, z_second, out, *sent):
    faces = edge_faces(*by_side(z_first[0:24, :], z_second[0:24, :]))

    def body(left, right):
        for i in range(REACH):
            out[i] = inner[i] + gain * edge_plane(i, left, right, faces)

    with_sides(near, far, body)
    packed = pack_faces(out, 0)
    if last:
        sent[0][...] = packed[1]
    else:
        sent[0][...], sent[1][...] = by_partner(*packed)


def store(rows, base, values):
    for n, value in enumerate(values):
        rows[base + n : base + n + 1, :] = value


def gram_dots(left, right, pairs):
    zero = jnp.zeros((8, LANES), jnp.float32)

    def body(i, accs):
        for b in range(8):
            at = pl.ds(8 * b, 8)
            l_tiles = {p: left[p, i, at, :] for p in sorted({p for p, _ in pairs})}
            if left is right:
                r_tiles = l_tiles
            else:
                r_tiles = {q: right[q, i, at, :] for q in sorted({q for _, q in pairs})}
            accs = tuple(acc + l_tiles[p] * r_tiles[q] for acc, (p, q) in zip(accs, pairs))
        return accs

    accs = lax.fori_loop(0, REACH, body, tuple(zero for _ in pairs))
    return [collapse(acc) for acc in accs]


CROSS_PAIRS = tuple((i, j) for i in range(HIST) for j in range(HIST))


def field_dots(steps, changes, others, plain=()):
    zero = jnp.zeros((8, LANES), jnp.float32)
    count = 2 * HIST

    def body(i, accs):
        accs = list(accs)
        for b in range(8):
            at = pl.ds(8 * b, 8)
            tiles = [other(i, b) for other in others]
            for f in range(count):
                field = steps[f, i, at, :] if f < HIST else changes[f - HIST, i, at, :]
                for o, tile in enumerate(tiles):
                    accs[o * count + f] = accs[o * count + f] + field * tile
            for n, (one, two) in enumerate(plain, len(others) * count):
                accs[n] = accs[n] + one(i, b) * two(i, b)
        return tuple(accs)

    total = count * len(others) + len(plain)
    return [collapse(acc) for acc in lax.fori_loop(0, REACH, body, (zero,) * total)]


def base_gradient(both, near, far, z_first, z_second, potential, grad, ext):
    hartree = both.at[pl.ds(0, REACH)]
    density = both.at[pl.ds(REACH, REACH)]
    fill_ext(density, ext)
    faces = edge_faces(*by_side(z_first[24:48, :], z_second[24:48, :]))

    def body(left, right):
        for i in range(REACH):
            grad[i] = edge_plane(i, left, right, faces)

    with_sides(near.at[pl.ds(REACH, REACH)], far.at[pl.ds(REACH, REACH)], body)
    for i in range(REACH):
        lap, rho = inner_plane(i, density, ext)
        power = jnp.exp(jnp.log(rho) * (4.0 / 3.0))
        grad[i] = 2.0 * rho * (hartree[i] + potential[i] + tf_scale * power) - (lap + grad[i]) * (
            1.0 / (spacing * spacing)
        )


def density_tile(both):
    return lambda i, b: tile_of(both, REACH + i, b)


def lifted_tile(both, vector):
    return lambda i, b: 2.0 * tile_of(both, REACH + i, b) * tile_of(vector, i, b)


def side_one(both, charge, steps, inner, rows, ext):
    inner_residual(both, charge, inner, ext)
    store(rows, 0, gram_dots(steps, steps, PAIRS))


def side_two(vector, both, steps, changes, inner, rows, moments, ext):
    inner_basis(vector, None, inner, ext)
    lifted, rho = lifted_tile(both, vector), density_tile(both)
    store(rows, 0, field_dots(steps, changes, [lifted], [(rho, lifted)]))
    store(rows, 17, gram_dots(changes, changes, PAIRS))
    store(rows, 53, gram_dots(steps, changes, CROSS_PAIRS[:32]))
    store_moments([(vector, vector)], moments)


def side_three(prior, vector, both, near, far, z_first, z_second, potential, steps, changes, *outs):
    inner, grad, rows, moments, ext = outs
    inner_basis(vector, prior, inner, ext)
    lifted, rho = lifted_tile(both, vector), density_tile(both)
    values = field_dots(steps, changes, [lifted, rho], [(rho, lifted)])
    store(rows, 0, values[:16] + values[32:] + values[16:32])
    store(rows, 33, gram_dots(steps, changes, CROSS_PAIRS[32:]))
    store_moments([(prior, vector), (vector, vector)], moments)
    base_gradient(both, near, far, z_first, z_second, potential, grad, ext)


def side_four(prior, vector, both, grad, steps, changes, inner, rows, moments, ext):
    inner_basis(vector, prior, inner, ext)
    lifted, rho = lifted_tile(both, vector), density_tile(both)
    slope = lambda i, b: tile_of(grad, i, b)
    values = field_dots(steps, changes, [lifted, slope], [(rho, lifted), (rho, slope), (rho, rho)])
    store(rows, 0, values[:16] + values[32:33] + values[16:32] + values[33:])
    store_moments([(prior, vector), (vector, vector)], moments)


def side_five(prior, vector, both, steps, changes, r1, r2, r3, r4, m2, m3, m4, kept, given, inner, table, m5, ext):
    lifted, rho = lifted_tile(both, vector), density_tile(both)
    own = field_dots(steps, changes, [lifted], [(rho, lifted)])
    store_moments([(prior, vector), (vector, vector)], m5)
    table[...] = jnp.zeros_like(table)

    def put(base, ref, start, count):
        before = max(0, min(count, HALF - base))
        if before:
            table[base : base + before, :] = ref[start : start + before, :]
        if before < count:
            at = place(base + before)
            table[at : at + count - before, :] = ref[start + before : start + count, :]

    put(ROW_GRAM, r1, 0, 36)
    put(ROW_GRAM + 36, r2, 17, 36)
    put(ROW_GRAM + 72, r2, 53, 32)
    put(ROW_GRAM + 104, r3, 33, 32)
    put(ROW_BASE, r3, 17, 16)
    put(ROW_BASE + 16, r4, 17, 18)
    for n, rows in enumerate((r2, r3, r4)):
        put(ROW_W + 17 * n, rows, 0, 17)
    store(table, place(ROW_W + 51), own)

    order = [(m2, 0), (m3, 0), (m3, 1), (m4, 0), (m4, 1), (m5, 0), (m5, 1)]
    zero = jnp.zeros((1, LANES), jnp.float32)
    parts = [
        jnp.concatenate([ref[2 * which + low : 2 * which + low + 1, :] for ref, which in order] + [zero], axis=0)
        for low in range(2)
    ]
    hi, lo = fold_lanes(*parts)
    lane = lane_ids((1, LANES))
    first = jnp.sum(jnp.transpose(table[0:LANES, :]), axis=0, keepdims=True)
    second = jnp.sum(jnp.transpose(table[LANES : 2 * LANES, :]), axis=0, keepdims=True)
    for n in range(7):
        second = jnp.where(lane == MOM_LANE + n, hi[n : n + 1], second)
        second = jnp.where(lane == MOM_LANE + 7 + n, lo[n : n + 1], second)
    odd = is_odd("blk")
    kept[...] = jnp.where(odd, second, first)
    given[...] = jnp.where(odd, first, second)

    fill_ext(vector, ext)
    zero = jnp.zeros((8, LANES), jnp.float32)
    accs = [(zero, zero) for _ in range(2)]
    for i in range(REACH):
        lap, values = inner_plane(i, vector, ext)
        product = values * ((screen / SHIFT - 1.0) * values - (1.0 / SHIFT) * lap)
        for b in range(8):
            accs[b % 2] = add_tile(accs[b % 2], product[8 * b : 8 * b + 8])
    hi, err = two_sum(accs[0][0], accs[1][0])
    inner[0:1, :], inner[1:2, :] = fold_rows((hi, accs[0][1] + accs[1][1] + err))


def send_kernel(own, left, z_left, inner, kept, taken, out):
    faces = edge_faces(z_left[...], None)
    zero = jnp.zeros((8, LANES), jnp.float32)
    accs = [(zero, zero) for _ in range(2)]
    for i in range(REACH):
        product = own[i] * edge_plane(i, left, None, faces)
        for b in range(8):
            accs[b % 2] = add_tile(accs[b % 2], product[8 * b : 8 * b + 8])
    hi, err = two_sum(accs[0][0], accs[1][0])
    coupling = fold_rows((hi, accs[0][1] + accs[1][1] + err))
    hi, lo = fold_lanes(*df_add(df_scale(coupling, -2.0 / SHIFT), (inner[0:1, :], inner[1:2, :])))
    lane = lane_ids((1, LANES))
    row, err = two_sum(kept[...], taken[...])
    low_lane = (lane >= MOM_LANE + 7) & (lane < MOM_LANE + 14) & is_odd("blk")
    row = jnp.where(low_lane, row + pltpu.roll(err, 7, 1), row)
    row = jnp.where(lane == HALF, hi, jnp.where(lane == HALF + 1, lo, row))
    out[...] = jnp.broadcast_to(row, out.shape)


def solve_krylov(moment):
    n00, n01, n11, n12, n22, n23, n33, n34 = moment
    nu = [n00, n01]
    nu.append(df_sub(df_scale(n11, 2.0), n00))
    nu.append(df_sub(df_scale(n12, 2.0), n01))
    nu.append(df_sub(df_scale(n22, 2.0), n00))
    nu.append(df_sub(df_scale(n23, 2.0), n01))
    nu.append(df_sub(df_scale(n33, 2.0), n00))

    def gram(i, j):
        if i == j == 0:
            return n00
        return df_scale(df_add(nu[i + j], nu[abs(i - j)]), 0.5)

    def moved(i, j):
        if i == 3 and j == 3:
            return n34
        if j == 0:
            return gram(i, 1)
        return df_scale(df_add(gram(i, j + 1), gram(i, j - 1)), 0.5)

    mat = {(i, j): df_add(moved(i, j), gram(i, j)) for i in range(4) for j in range(i + 1)}
    rhs = [df_scale(gram(i, 0), 1.0 / SHIFT) for i in range(4)]
    low = {}
    for k in range(4):
        for i in range(k + 1, 4):
            low[i, k] = df_div(mat[i, k], mat[k, k])
        for i in range(k + 1, 4):
            for j in range(k + 1, i + 1):
                mat[i, j] = df_sub(mat[i, j], df_mul(low[i, k], mat[j, k]))
            rhs[i] = df_sub(rhs[i], df_mul(low[i, k], rhs[k]))
    sol = [None] * 4
    for k in reversed(range(4)):
        value = df_div(rhs[k], mat[k, k])
        for i in range(k + 1, 4):
            value = df_sub(value, df_mul(low[i, k], sol[i]))
        sol[k] = value
    return [hi + lo for hi, lo in sol]


def final_kernel(received, both, grad, v0, v1, v2, v3, steps, changes, new_density, new_hartree, spread):
    parts = [(received[8 * n : 8 * n + 8, :], jnp.zeros((8, LANES), jnp.float32)) for n in range(4)]
    for n in range(4, received.shape[0] // 8):
        parts[n % 4] = add_tile(parts[n % 4], received[8 * n : 8 * n + 8, :])
    while len(parts) > 1:
        half = len(parts) // 2
        merged = []
        for a, b in zip(parts[:half], parts[half:]):
            hi, err = two_sum(a[0], b[0])
            merged.append((hi, a[1] + b[1] + err))
        parts = merged
    hi, lo = fold(*parts[0], 0, (1, 2))
    lane = lane_ids((1, LANES))
    last, err = two_sum(hi[3:4], hi[7:8])
    err = err + (lo[3:4] + lo[7:8])
    first = hi[3:4]
    second = jnp.where(lane >= HALF, last, hi[7:8])
    low = jnp.where(lane >= HALF, err, lo[7:8])
    low = low + jnp.where(lane == HALF, pltpu.roll(second, LANES - 1, 1), pltpu.roll(second, LANES - 7, 1))
    for n, value in enumerate((first, second, low)):
        spread[LANES * n : LANES * n + LANES, :] = jnp.transpose(jnp.broadcast_to(value, (LANES, LANES)))

    def row(n):
        return spread[place(n) : place(n) + 1, :]

    def moment(n):
        at = LANES + (MOM_LANE + n if n < 7 else HALF)
        return quick_sum(spread[at : at + 1, :], spread[LANES + at : LANES + at + 1, :])

    mix = solve_krylov([moment(n) for n in range(8)])

    def s_s(i, j):
        return row(ROW_GRAM + PAIR_ROW[min(i, j), max(i, j)])

    def y_y(i, j):
        return row(ROW_GRAM + 36 + PAIR_ROW[min(i, j), max(i, j)])

    def s_y(i, j):
        return row(ROW_GRAM + 72 + 8 * i + j)

    pairs = range(HIST)
    theta, rest, inverse = [], [], []
    for i in pairs:
        curv, norm = s_y(i, i), s_s(i, i)
        kept = (1.0 - damp_floor) * norm
        damp = jnp.where(curv >= damp_floor * norm, 1.0, kept / jnp.maximum(norm - curv, kept))
        theta.append(damp)
        rest.append(1.0 - damp)
        inverse.append(1.0 / (damp * curv + (1.0 - damp) * norm))

    def s_bar(i, j):
        return theta[j] * s_y(i, j) + rest[j] * s_s(i, j)

    def bar_bar(i, j):
        return theta[i] * (theta[j] * y_y(i, j) + rest[j] * s_y(j, i)) + rest[i] * s_bar(i, j)

    last = HIST - 1
    scaling = s_bar(last, last) / bar_bar(last, last)

    def energy(n):
        value = row(ROW_BASE + 16 + n)
        for j in range(4):
            value = value + mix[j] * row(ROW_W + 17 * j + n)
        return value

    chem = energy(16) / row(ROW_BASE + 33)

    def gradient(n):
        return energy(n) - chem * row(ROW_BASE + n)

    s_grad = [gradient(i) for i in pairs]
    bar_grad = [theta[i] * gradient(HIST + i) + rest[i] * s_grad[i] for i in pairs]

    first = [None] * HIST
    pending = list(s_grad)
    for j in reversed(pairs):
        first[j] = inverse[j] * pending[j]
        for i in range(j):
            pending[i] = pending[i] - first[j] * s_bar(i, j)
    pending = list(bar_grad)
    for j in pairs:
        for i in pairs:
            pending[i] = pending[i] - first[j] * bar_bar(i, j)
    pending = [scaling * value for value in pending]
    step_mix, change_mix = [], []
    for j in pairs:
        net = first[j] - inverse[j] * pending[j]
        for i in range(j + 1, HIST):
            pending[i] = pending[i] + net * s_bar(j, i)
        change_mix.append((-step_length) * (-scaling * first[j] * theta[j]))
        step_mix.append((-step_length) * (net - scaling * first[j] * rest[j]))

    wide = lambda value: jnp.broadcast_to(value, (8, LANES))
    mix = [wide(value) for value in mix]
    chem, gain = wide(chem), wide((-step_length) * scaling)
    step_mix = [wide(value) for value in step_mix]
    change_mix = [wide(value) for value in change_mix]
    basis = (v0, v1, v2, v3)

    @pl.loop(0, REACH)
    def _(i):
        for b in range(8):
            at = pl.ds(8 * b, 8)
            rho = both[REACH + i, at, :]
            lift = mix[0] * v0[i, at, :]
            for j in range(1, 4):
                lift = lift + mix[j] * basis[j][i, at, :]
            new_hartree[i, at, :] = both[i, at, :] + lift
            slope = grad[i, at, :] + 2.0 * rho * lift - chem * rho
            parts = [rho, gain * slope, step_mix[0] * steps[0, i, at, :], change_mix[0] * changes[0, i, at, :]]
            for f in range(1, HIST):
                parts[2] = parts[2] + step_mix[f] * steps[f, i, at, :]
                parts[3] = parts[3] + change_mix[f] * changes[f, i, at, :]
            new_density[i, at, :] = parts[0] + (parts[1] + (parts[2] + parts[3]))


def call(kernel, outs, args, scratch=(), flops=0, place=pltpu.VMEM):
    whole = pl.BlockSpec(memory_space=pltpu.VMEM)
    shapes = [jax.ShapeDtypeStruct(shape, jnp.float32) for shape in outs]
    size = sum(4 * math.prod(a.shape) for a in (*args, *shapes))
    return pl.pallas_call(
        kernel,
        out_shape=shapes,
        in_specs=[pl.BlockSpec(memory_space=place)] * len(args),
        out_specs=[whole] * len(outs),
        scratch_shapes=[pltpu.VMEM(s, jnp.float32) if isinstance(s, tuple) else s for s in scratch],
        cost_estimate=pl.CostEstimate(flops=flops, bytes_accessed=size, transcendentals=0),
        compiler_params=pltpu.CompilerParams(vmem_limit_bytes=VMEM_LIMIT),
    )(*args)


def ring(axis, step):
    size = lax.axis_size(axis)
    return [(i, (i + step) % size) for i in range(size)]


def swap(axis, odd_up):
    size = lax.axis_size(axis)
    return [(i, (i + (1 if i % 2 == odd_up else -1)) % size) for i in range(size)]


def x_halo(block):
    far = lax.ppermute(block, "blk", swap("blk", 1))
    return (lax.ppermute(block, "blk", swap("blk", 0)), far)


def z_halo(face_a, face_b):
    return (lax.ppermute(face_a, "gz", swap("gz", 0)), lax.ppermute(face_b, "gz", swap("gz", 1)))


def after(values, *earlier):
    return lax.optimization_barrier((tuple(values), earlier))[0]


def on_device(sqrt_density, ion_charge, ion_potential, hartree_prev, hist_steps, hist_changes):
    block = sqrt_density.shape
    ext = (block[0], block[1] + 16, block[2])
    face = (24, LANES)
    cells = math.prod(block)
    history = [hist_steps, hist_changes]
    cells = math.prod(block)
    history = [hist_steps, hist_changes]
    work = 300 * cells
    inputs = (hartree_prev, sqrt_density, ion_charge)
    both, charge, *faces = call(
        launch_kernel,
        [(2 * REACH, *block[1:]), block, (48, LANES), (48, LANES)],
        [pltpu.with_memory_space_constraint(x, pltpu.HBM) for x in inputs],
        [pltpu.SemaphoreType.DMA((3,))],
        place=pltpu.HBM,
    )
    start = (*x_halo(both), *z_halo(*faces))
    inner, r1 = call(side_one, [block, (40, LANES)], [both, charge, hist_steps], [ext], work)
    v0, *faces = call(
        functools.partial(edge_kernel, 1.0, False), [block, face, face], [inner, *after(start, inner)], flops=work
    )
    halo = (*x_halo(v0), *z_halo(*faces))
    inner, r2, m2 = call(
        side_two, [block, (88, LANES), (8, LANES)], [v0, both, *history], [ext], work
    )
    v1, *faces = call(
        functools.partial(edge_kernel, -1.0 / SHIFT, False),
        [block, face, face],
        [inner, *after(halo, inner)],
        flops=work,
    )
    halo = (*x_halo(v1), *z_halo(*faces))
    inner, grad, r3, m3 = call(
        side_three,
        [block, block, (72, LANES), (8, LANES)],
        [v0, v1, both, *start, ion_potential, *history],
        [ext],
        work,
    )
    v2, *faces = call(
        functools.partial(edge_kernel, -2.0 / SHIFT, False),
        [block, face, face],
        [inner, *after(halo, inner)],
        flops=work,
    )
    halo = (*x_halo(v2), *z_halo(*faces))
    inner, r4, m4 = call(
        side_four, [block, (40, LANES), (8, LANES)], [v1, v2, both, grad, *history], [ext], work
    )
    v3, upper = call(
        functools.partial(edge_kernel, -2.0 / SHIFT, True), [block, face], [inner, *after(halo, inner)], flops=work
    )
    left = lax.ppermute(v3, "blk", ring("blk", 1))
    z_left = lax.ppermute(upper, "gz", ring("gz", 1))
    kept, given, inner = call(
        side_five,
        [(1, LANES), (1, LANES), (8, LANES)],
        [v2, v3, both, *history, r1, r2, r3, r4, m2, m3, m4],
        [(2 * LANES, LANES), (8, LANES), ext],
        work,
    )
    taken = lax.ppermute(given, "blk", swap("blk", 0))
    left, z_left = after((left, z_left), inner, taken)
    devices = lax.axis_size("blk") * lax.axis_size("gz")
    (outgoing,) = call(send_kernel, [(devices, LANES)], [v3, left, z_left, inner, kept, taken], flops=work)
    received = lax.all_to_all(outgoing.reshape(devices, 1, LANES), ("blk", "gz"), 0, 0, tiled=True)
    return tuple(
        call(
            final_kernel,
            [block, block],
            [received.reshape(devices, LANES), both, grad, v0, v1, v2, v3, *history],
            [(3 * LANES, LANES)],
            work,
        )
    )


def solution(mesh):
    placed = (
        P("blk", None, "gz"),
        P("blk", None, "gz"),
        P("blk", None, "gz"),
        P("blk", None, "gz"),
        P(None, "blk", None, "gz"),
        P(None, "blk", None, "gz"),
    )
    return jax.shard_map(
        on_device,
        mesh=mesh,
        in_specs=placed,
        out_specs=(P("blk", None, "gz"), P("blk", None, "gz")),
        check_vma=False,
    )
```

```python
import functools
import math

import jax
import jax.numpy as jnp
from jax import lax
from jax.experimental import pallas as pl
from jax.experimental.pallas import tpu as pltpu
from jax.sharding import PartitionSpec as P

center = -5369.0 / 1800.0
coeffs = (12.0 / 7.0, -15.0 / 56.0, 10.0 / 189.0, -1.0 / 112.0, 2.0 / 825.0, -1.0 / 4752.0)
screen = 0.0025
spacing = 0.28
source_scale = 4.0 * math.pi * spacing * spacing
tf_scale = 5.0 / 3.0 * 2.871234
step_length = 0.01
damp_floor = 0.2

SHIFT = 2.0
HIST = 8
REACH = 6
LANES = 128
VMEM_LIMIT = 24 * 1024 * 1024

ROW_GRAM = 0
ROW_BASE = 136
ROW_W = 170
ROW_MOM = 238
HALF = 126


def place(n):
    return n if n < HALF else n + LANES - HALF


MOM_LANE = place(ROW_MOM) - LANES
PAIRS = tuple((i, j) for i in range(HIST) for j in range(i, HIST))
PAIR_ROW = {pair: row for row, pair in enumerate(PAIRS)}


def two_sum(a, b):
    s = a + b
    bb = s - a
    return s, (a - (s - bb)) + (b - bb)


def quick_sum(a, b):
    s = a + b
    return s, b - (s - a)


def split(a):
    t = 4097.0 * a
    hi = t - (t - a)
    return hi, a - hi


def two_prod(a, b):
    p = a * b
    ah, al = split(a)
    bh, bl = split(b)
    return p, ((ah * bh - p) + ah * bl + al * bh) + al * bl


def df_add(a, b):
    s, e = two_sum(a[0], b[0])
    return quick_sum(s, e + (a[1] + b[1]))


def df_neg(a):
    return (-a[0], -a[1])


def df_sub(a, b):
    return df_add(a, df_neg(b))


def df_scale(a, factor):
    return (a[0] * factor, a[1] * factor)


def df_mul(a, b):
    p, e = two_prod(a[0], b[0])
    return quick_sum(p, e + (a[0] * b[1] + a[1] * b[0]))


def df_div(a, b):
    q1 = a[0] / b[0]
    r = df_sub(a, df_mul(b, (q1, jnp.zeros_like(q1))))
    q2 = r[0] / b[0]
    return quick_sum(q1, q2)


def lane_ids(shape):
    return lax.broadcasted_iota(jnp.int32, shape, len(shape) - 1)


def inner_plane(i, own, ext):
    values = own[i]
    rows = values.shape[0]
    lane = lane_ids((rows, LANES))
    total = (3.0 * center) * values
    for k, weight in enumerate(coeffs, 1):
        pair = ext[i, 8 + k : 8 + k + rows, :] + ext[i, 8 - k : 8 - k + rows, :]
        if i + k < REACH:
            pair = pair + own[i + k]
        if i - k >= 0:
            pair = pair + own[i - k]
        up = pltpu.roll(jnp.where(lane < k, 0.0, values), LANES - k, 1)
        down = pltpu.roll(jnp.where(lane >= LANES - k, 0.0, values), k, 1)
        total = total + weight * (pair + (up + down))
    return total, values


def edge_faces(z_left, z_right):
    lane = lane_ids((24, LANES)) % 8
    lower = jnp.zeros((24, LANES), jnp.float32)
    upper = jnp.zeros((24, LANES), jnp.float32)
    for k, weight in enumerate(coeffs, 1):
        lower = lower + jnp.where(lane < k, weight * pltpu.roll(z_left, LANES - 8 + k, 1), 0.0)
        if z_right is not None:
            upper = upper + jnp.where(lane >= 8 - k, weight * pltpu.roll(z_right, 8 - k, 1), 0.0)
    return lower, upper


def side_plane(i, block, below, rows=slice(None)):
    total = None
    for k, weight in enumerate(coeffs, 1):
        layer = i - k + REACH if below else i + k - REACH
        if 0 <= layer < REACH:
            term = weight * block[layer, rows, :]
            total = term if total is None else total + term
    return total


def z_plane(i, faces, tiles=8):
    lane = lane_ids((8, LANES))
    lower, upper = (face[8 * (i // 2) : 8 * (i // 2) + 8] for face in faces)
    out = []
    for b in range(tiles):
        j = 8 * (i % 2) + b
        tile = jnp.where(lane < 8, pltpu.roll(lower, (LANES - 8 * j) % LANES, 1), 0.0)
        tile = jnp.where(lane >= LANES - 8, pltpu.roll(upper, (2 * LANES - 8 - 8 * j) % LANES, 1), tile)
        out.append(tile)
    return jnp.concatenate(out, axis=0)


def fill_ext(own, ext):
    rows = own.shape[1]
    ext[:, 8 : 8 + rows, :] = own[...]
    ext[:, 0:8, :] = own[:, rows - 8 : rows, :]
    ext[:, 8 + rows : 16 + rows, :] = own[:, 0:8, :]


def pack_faces(src, layers):
    lane = lane_ids((8, LANES))
    firsts, lasts = [], []
    for m in range(3):
        first = jnp.zeros((8, LANES), jnp.float32)
        last = jnp.zeros((8, LANES), jnp.float32)
        for j in range(16):
            n = 16 * m + j
            tile = src[layers + n // 8, 8 * (n % 8) : 8 * (n % 8) + 8, :]
            here = (lane >= 8 * j) & (lane < 8 * j + 8)
            first = jnp.where(here, pltpu.roll(tile, 8 * j, 1) if j else tile, first)
            last = jnp.where(here, pltpu.roll(tile, (8 * j + 8) % LANES, 1) if j < 15 else tile, last)
        firsts.append(first)
        lasts.append(last)
    return jnp.concatenate(firsts, axis=0), jnp.concatenate(lasts, axis=0)


def is_odd(axis):
    return lax.rem(lax.axis_index(axis), 2) == 1


def by_partner(lower, upper):
    odd = is_odd("gz")
    return jnp.where(odd, lower, upper), jnp.where(odd, upper, lower)


def by_side(first, second):
    odd = is_odd("gz")
    return jnp.where(odd, first, second), jnp.where(odd, second, first)


def with_sides(body):
    odd = is_odd("blk")

    @pl.when(odd)
    def _():
        body(True, False)

    @pl.when(jnp.logical_not(odd))
    def _():
        body(False, True)


def fold(hi, lo, axis, steps):
    for step in steps:
        hi, err = two_sum(hi, pltpu.roll(hi, step, axis))
        lo = lo + pltpu.roll(lo, step, axis) + err
    return hi, lo


def fold_rows(acc):
    hi, lo = fold(*acc, 0, (4, 2, 1))
    return hi[0:1], lo[0:1]


def fold_lanes(hi, lo):
    return quick_sum(*fold(hi, lo, 1, (64, 32, 16, 8, 4, 2, 1)))


def add_tile(acc, product):
    hi, err = two_sum(acc[0], product)
    return hi, acc[1] + err


def tile_of(ref, i, b):
    return ref[i, 8 * b : 8 * b + 8, :]


def store_moments(pairs, moments):
    zero = jnp.zeros((8, LANES), jnp.float32)

    def body(i, accs):
        for b in range(8):
            accs = tuple(
                add_tile(acc, tile_of(a, i, b) * tile_of(c, i, b)) for acc, (a, c) in zip(accs, pairs)
            )
        return accs

    accs = lax.fori_loop(0, REACH, body, tuple((zero, zero) for _ in pairs))
    for n, acc in enumerate(accs):
        moments[2 * n : 2 * n + 1, :], moments[2 * n + 1 : 2 * n + 2, :] = fold_rows(acc)


def collapse(acc):
    return jnp.sum(acc, axis=0, keepdims=True)


def launch_kernel(hartree, density, charge, both, charge_here, face_a, face_b, sems):
    places = (both.at[pl.ds(0, REACH)], both.at[pl.ds(REACH, REACH)], charge_here)
    copies = [
        pltpu.make_async_copy(src, dst, sems.at[n])
        for n, (src, dst) in enumerate(zip((hartree, density, charge), places))
    ]
    for copy in copies:
        copy.start()
    for n in range(2):
        copies[n].wait()
        rows = slice(24 * n, 24 * n + 24)
        face_a[rows, :], face_b[rows, :] = by_partner(*pack_faces(both, REACH * n))
    copies[2].wait()


def inner_residual(both, charge, out, ext):
    hartree = both.at[pl.ds(0, REACH)]
    fill_ext(hartree, ext)
    for i in range(REACH):
        lap, values = inner_plane(i, hartree, ext)
        rho = both[REACH + i]
        out[i] = source_scale * (rho * rho - charge[i]) - (screen * values - lap)


def inner_basis(own, prior, out, ext):
    fill_ext(own, ext)
    for i in range(REACH):
        lap, values = inner_plane(i, own, ext)
        moved = (screen / SHIFT - 1.0) * values - (1.0 / SHIFT) * lap
        out[i] = moved if prior is None else 2.0 * moved - prior[i]


def near_kernel(gain, inner, near, z_first, z_second, out):
    faces = edge_faces(*by_side(z_first[0:24, :], z_second[0:24, :]))

    def body(near_below, far_below):
        for i in range(REACH):
            out[i] = inner[i] + gain * (side_plane(i, near, near_below) + z_plane(i, faces))

    with_sides(body)


def far_kernel(gain, inner, far, out):
    def body(near_below, far_below):
        for i in range(REACH):
            out[i] = inner[i] + gain * side_plane(i, far, far_below)

    with_sides(body)


def last_far_kernel(gain, inner, far, out, to_near, to_far):
    half = out.shape[1] // 2

    def body(near_below, far_below):
        for i in range(REACH):
            plane = inner[i] + gain * side_plane(i, far, far_below)
            out[i] = plane
            for ref, below in ((to_near, near_below), (to_far, far_below)):
                ref[i] = plane[:half] if below else plane[half:]

    with_sides(body)


def pack_kernel(block, face_a, face_b):
    face_a[...], face_b[...] = by_partner(*pack_faces(block, 0))


def pack_upper_kernel(block, face):
    face[...] = pack_faces(block, 0)[1]


def store(rows, base, values):
    for n, value in enumerate(values):
        rows[base + n : base + n + 1, :] = value


def gram_dots(left, right, pairs):
    zero = jnp.zeros((8, LANES), jnp.float32)

    def body(i, accs):
        for b in range(8):
            at = pl.ds(8 * b, 8)
            l_tiles = {p: left[p, i, at, :] for p in sorted({p for p, _ in pairs})}
            if left is right:
                r_tiles = l_tiles
            else:
                r_tiles = {q: right[q, i, at, :] for q in sorted({q for _, q in pairs})}
            accs = tuple(acc + l_tiles[p] * r_tiles[q] for acc, (p, q) in zip(accs, pairs))
        return accs

    accs = lax.fori_loop(0, REACH, body, tuple(zero for _ in pairs))
    return [collapse(acc) for acc in accs]


CROSS_PAIRS = tuple((i, j) for i in range(HIST) for j in range(HIST))


def field_dots(steps, changes, others, plain=()):
    zero = jnp.zeros((8, LANES), jnp.float32)
    count = 2 * HIST

    def body(i, accs):
        accs = list(accs)
        for b in range(8):
            at = pl.ds(8 * b, 8)
            tiles = [other(i, b) for other in others]
            for f in range(count):
                field = steps[f, i, at, :] if f < HIST else changes[f - HIST, i, at, :]
                for o, tile in enumerate(tiles):
                    accs[o * count + f] = accs[o * count + f] + field * tile
            for n, (one, two) in enumerate(plain, len(others) * count):
                accs[n] = accs[n] + one(i, b) * two(i, b)
        return tuple(accs)

    total = count * len(others) + len(plain)
    return [collapse(acc) for acc in lax.fori_loop(0, REACH, body, (zero,) * total)]


def base_gradient(both, near, far, z_first, z_second, potential, grad, ext):
    hartree = both.at[pl.ds(0, REACH)]
    density = both.at[pl.ds(REACH, REACH)]
    fill_ext(density, ext)
    faces = edge_faces(*by_side(z_first[24:48, :], z_second[24:48, :]))

    def body(near_below, far_below):
        for i in range(REACH):
            grad[i] = side_plane(i, near, near_below) + side_plane(i, far, far_below) + z_plane(i, faces)

    with_sides(body)
    for i in range(REACH):
        lap, rho = inner_plane(i, density, ext)
        power = jnp.exp(jnp.log(rho) * (4.0 / 3.0))
        grad[i] = 2.0 * rho * (hartree[i] + potential[i] + tf_scale * power) - (lap + grad[i]) * (
            1.0 / (spacing * spacing)
        )


def density_tile(both):
    return lambda i, b: tile_of(both, REACH + i, b)


def lifted_tile(both, vector):
    return lambda i, b: 2.0 * tile_of(both, REACH + i, b) * tile_of(vector, i, b)


def side_one(both, charge, steps, inner, rows, ext):
    inner_residual(both, charge, inner, ext)
    store(rows, 0, gram_dots(steps, steps, PAIRS))


def side_two(vector, both, steps, changes, inner, rows, moments, ext):
    inner_basis(vector, None, inner, ext)
    lifted, rho = lifted_tile(both, vector), density_tile(both)
    store(rows, 0, field_dots(steps, changes, [lifted], [(rho, lifted)]))
    store(rows, 17, gram_dots(changes, changes, PAIRS))
    store(rows, 53, gram_dots(steps, changes, CROSS_PAIRS[:32]))
    store_moments([(vector, vector)], moments)


def side_three(prior, vector, both, near, far, z_first, z_second, potential, steps, changes, *outs):
    inner, grad, rows, moments, ext = outs
    inner_basis(vector, prior, inner, ext)
    lifted, rho = lifted_tile(both, vector), density_tile(both)
    values = field_dots(steps, changes, [lifted, rho], [(rho, lifted)])
    store(rows, 0, values[:16] + values[32:] + values[16:32])
    store(rows, 33, gram_dots(steps, changes, CROSS_PAIRS[32:]))
    store_moments([(prior, vector), (vector, vector)], moments)
    base_gradient(both, near, far, z_first, z_second, potential, grad, ext)


def side_four(prior, vector, both, grad, steps, changes, inner, rows, moments, ext):
    inner_basis(vector, prior, inner, ext)
    lifted, rho = lifted_tile(both, vector), density_tile(both)
    slope = lambda i, b: tile_of(grad, i, b)
    values = field_dots(steps, changes, [lifted, slope], [(rho, lifted), (rho, slope), (rho, rho)])
    store(rows, 0, values[:16] + values[32:33] + values[16:32] + values[33:])
    store_moments([(prior, vector), (vector, vector)], moments)


def side_five(prior, vector, both, steps, changes, r1, r2, r3, r4, m2, m3, m4, kept, given, inner, table, m5, ext):
    lifted, rho = lifted_tile(both, vector), density_tile(both)
    own = field_dots(steps, changes, [lifted], [(rho, lifted)])
    store_moments([(prior, vector), (vector, vector)], m5)
    table[...] = jnp.zeros_like(table)

    def put(base, ref, start, count):
        before = max(0, min(count, HALF - base))
        if before:
            table[base : base + before, :] = ref[start : start + before, :]
        if before < count:
            at = place(base + before)
            table[at : at + count - before, :] = ref[start + before : start + count, :]

    put(ROW_GRAM, r1, 0, 36)
    put(ROW_GRAM + 36, r2, 17, 36)
    put(ROW_GRAM + 72, r2, 53, 32)
    put(ROW_GRAM + 104, r3, 33, 32)
    put(ROW_BASE, r3, 17, 16)
    put(ROW_BASE + 16, r4, 17, 18)
    for n, rows in enumerate((r2, r3, r4)):
        put(ROW_W + 17 * n, rows, 0, 17)
    store(table, place(ROW_W + 51), own)

    order = [(m2, 0), (m3, 0), (m3, 1), (m4, 0), (m4, 1), (m5, 0), (m5, 1)]
    zero = jnp.zeros((1, LANES), jnp.float32)
    parts = [
        jnp.concatenate([ref[2 * which + low : 2 * which + low + 1, :] for ref, which in order] + [zero], axis=0)
        for low in range(2)
    ]
    hi, lo = fold_lanes(*parts)
    lane = lane_ids((1, LANES))
    first = jnp.sum(jnp.transpose(table[0:LANES, :]), axis=0, keepdims=True)
    second = jnp.sum(jnp.transpose(table[LANES : 2 * LANES, :]), axis=0, keepdims=True)
    for n in range(7):
        second = jnp.where(lane == MOM_LANE + n, hi[n : n + 1], second)
        second = jnp.where(lane == MOM_LANE + 7 + n, lo[n : n + 1], second)
    odd = is_odd("blk")
    kept[...] = jnp.where(odd, second, first)
    given[...] = jnp.where(odd, first, second)

    fill_ext(vector, ext)
    zero = jnp.zeros((8, LANES), jnp.float32)
    accs = [(zero, zero) for _ in range(2)]
    for i in range(REACH):
        lap, values = inner_plane(i, vector, ext)
        product = values * ((screen / SHIFT - 1.0) * values - (1.0 / SHIFT) * lap)
        for b in range(8):
            accs[b % 2] = add_tile(accs[b % 2], product[8 * b : 8 * b + 8])
    hi, err = two_sum(accs[0][0], accs[1][0])
    inner[0:1, :], inner[1:2, :] = fold_rows((hi, accs[0][1] + accs[1][1] + err))


def couple(own, block, below, acc):
    half = own.shape[1] // 2
    for i in range(REACH):
        product = own[i, half:, :] * side_plane(i, block, True) if below else own[i, :half, :] * side_plane(i, block, False)
        for b in range(half // 8):
            acc = add_tile(acc, product[8 * b : 8 * b + 8])
    return acc


def couple_kernel(own, near, z_left, inner, kept, taken, row, part):
    zero = jnp.zeros((8, LANES), jnp.float32)
    faces = edge_faces(z_left[...], None)
    acc = (zero, zero)
    for i in range(REACH):
        product = own[i] * z_plane(i, faces)
        for b in range(8):
            acc = add_tile(acc, product[8 * b : 8 * b + 8])
    z_rows = fold_rows(acc)

    def body(near_below, far_below):
        sides = df_add(fold_rows(couple(own, near, near_below, (zero, zero))), z_rows)
        part[0:1, :], part[1:2, :] = df_add(df_scale(sides, -2.0 / SHIFT), (inner[0:1, :], inner[1:2, :]))

    with_sides(body)
    lane = lane_ids((1, LANES))
    total, err = two_sum(kept[...], taken[...])
    low_lane = (lane >= MOM_LANE + 7) & (lane < MOM_LANE + 14) & is_odd("blk")
    row[...] = jnp.where(low_lane, total + pltpu.roll(err, 7, 1), total)


def send_kernel(own, far, part, row, out):
    zero = jnp.zeros((8, LANES), jnp.float32)

    def body(near_below, far_below):
        side = fold_rows(couple(own, far, far_below, (zero, zero)))
        hi, lo = fold_lanes(*df_add(df_scale(side, -2.0 / SHIFT), (part[0:1, :], part[1:2, :])))
        lane = lane_ids((1, LANES))
        value = jnp.where(lane == HALF, hi, jnp.where(lane == HALF + 1, lo, row[...]))
        out[...] = jnp.broadcast_to(value, out.shape)

    with_sides(body)


def solve_krylov(moment):
    n00, n01, n11, n12, n22, n23, n33, n34 = moment
    nu = [n00, n01]
    nu.append(df_sub(df_scale(n11, 2.0), n00))
    nu.append(df_sub(df_scale(n12, 2.0), n01))
    nu.append(df_sub(df_scale(n22, 2.0), n00))
    nu.append(df_sub(df_scale(n23, 2.0), n01))
    nu.append(df_sub(df_scale(n33, 2.0), n00))

    def gram(i, j):
        if i == j == 0:
            return n00
        return df_scale(df_add(nu[i + j], nu[abs(i - j)]), 0.5)

    def moved(i, j):
        if i == 3 and j == 3:
            return n34
        if j == 0:
            return gram(i, 1)
        return df_scale(df_add(gram(i, j + 1), gram(i, j - 1)), 0.5)

    mat = {(i, j): df_add(moved(i, j), gram(i, j)) for i in range(4) for j in range(i + 1)}
    rhs = [df_scale(gram(i, 0), 1.0 / SHIFT) for i in range(4)]
    low = {}
    for k in range(4):
        for i in range(k + 1, 4):
            low[i, k] = df_div(mat[i, k], mat[k, k])
        for i in range(k + 1, 4):
            for j in range(k + 1, i + 1):
                mat[i, j] = df_sub(mat[i, j], df_mul(low[i, k], mat[j, k]))
            rhs[i] = df_sub(rhs[i], df_mul(low[i, k], rhs[k]))
    sol = [None] * 4
    for k in reversed(range(4)):
        value = df_div(rhs[k], mat[k, k])
        for i in range(k + 1, 4):
            value = df_sub(value, df_mul(low[i, k], sol[i]))
        sol[k] = value
    return [hi + lo for hi, lo in sol]


def final_kernel(received, both, grad, v0, v1, v2, v3, steps, changes, new_density, new_hartree, spread):
    parts = [(received[8 * n : 8 * n + 8, :], jnp.zeros((8, LANES), jnp.float32)) for n in range(4)]
    for n in range(4, received.shape[0] // 8):
        parts[n % 4] = add_tile(parts[n % 4], received[8 * n : 8 * n + 8, :])
    while len(parts) > 1:
        half = len(parts) // 2
        merged = []
        for a, b in zip(parts[:half], parts[half:]):
            hi, err = two_sum(a[0], b[0])
            merged.append((hi, a[1] + b[1] + err))
        parts = merged
    hi, lo = fold(*parts[0], 0, (1, 2))
    lane = lane_ids((1, LANES))
    last, err = two_sum(hi[3:4], hi[7:8])
    err = err + (lo[3:4] + lo[7:8])
    first = hi[3:4]
    second = jnp.where(lane >= HALF, last, hi[7:8])
    low = jnp.where(lane >= HALF, err, lo[7:8])
    low = low + jnp.where(lane == HALF, pltpu.roll(second, LANES - 1, 1), pltpu.roll(second, LANES - 7, 1))
    for n, value in enumerate((first, second, low)):
        spread[LANES * n : LANES * n + LANES, :] = jnp.transpose(jnp.broadcast_to(value, (LANES, LANES)))

    def row(n):
        return spread[place(n) : place(n) + 1, :]

    def moment(n):
        at = LANES + (MOM_LANE + n if n < 7 else HALF)
        return quick_sum(spread[at : at + 1, :], spread[LANES + at : LANES + at + 1, :])

    mix = solve_krylov([moment(n) for n in range(8)])

    def s_s(i, j):
        return row(ROW_GRAM + PAIR_ROW[min(i, j), max(i, j)])

    def y_y(i, j):
        return row(ROW_GRAM + 36 + PAIR_ROW[min(i, j), max(i, j)])

    def s_y(i, j):
        return row(ROW_GRAM + 72 + 8 * i + j)

    pairs = range(HIST)
    theta, rest, inverse = [], [], []
    for i in pairs:
        curv, norm = s_y(i, i), s_s(i, i)
        kept = (1.0 - damp_floor) * norm
        damp = jnp.where(curv >= damp_floor * norm, 1.0, kept / jnp.maximum(norm - curv, kept))
        theta.append(damp)
        rest.append(1.0 - damp)
        inverse.append(1.0 / (damp * curv + (1.0 - damp) * norm))

    def s_bar(i, j):
        return theta[j] * s_y(i, j) + rest[j] * s_s(i, j)

    def bar_bar(i, j):
        return theta[i] * (theta[j] * y_y(i, j) + rest[j] * s_y(j, i)) + rest[i] * s_bar(i, j)

    last = HIST - 1
    scaling = s_bar(last, last) / bar_bar(last, last)

    def energy(n):
        value = row(ROW_BASE + 16 + n)
        for j in range(4):
            value = value + mix[j] * row(ROW_W + 17 * j + n)
        return value

    chem = energy(16) / row(ROW_BASE + 33)

    def gradient(n):
        return energy(n) - chem * row(ROW_BASE + n)

    s_grad = [gradient(i) for i in pairs]
    bar_grad = [theta[i] * gradient(HIST + i) + rest[i] * s_grad[i] for i in pairs]

    first = [None] * HIST
    pending = list(s_grad)
    for j in reversed(pairs):
        first[j] = inverse[j] * pending[j]
        for i in range(j):
            pending[i] = pending[i] - first[j] * s_bar(i, j)
    pending = list(bar_grad)
    for j in pairs:
        for i in pairs:
            pending[i] = pending[i] - first[j] * bar_bar(i, j)
    pending = [scaling * value for value in pending]
    step_mix, change_mix = [], []
    for j in pairs:
        net = first[j] - inverse[j] * pending[j]
        for i in range(j + 1, HIST):
            pending[i] = pending[i] + net * s_bar(j, i)
        change_mix.append((-step_length) * (-scaling * first[j] * theta[j]))
        step_mix.append((-step_length) * (net - scaling * first[j] * rest[j]))

    wide = lambda value: jnp.broadcast_to(value, (8, LANES))
    mix = [wide(value) for value in mix]
    chem, gain = wide(chem), wide((-step_length) * scaling)
    step_mix = [wide(value) for value in step_mix]
    change_mix = [wide(value) for value in change_mix]
    basis = (v0, v1, v2, v3)

    @pl.loop(0, REACH)
    def _(i):
        for b in range(8):
            at = pl.ds(8 * b, 8)
            rho = both[REACH + i, at, :]
            lift = mix[0] * v0[i, at, :]
            for j in range(1, 4):
                lift = lift + mix[j] * basis[j][i, at, :]
            new_hartree[i, at, :] = both[i, at, :] + lift
            slope = grad[i, at, :] + 2.0 * rho * lift - chem * rho
            parts = [rho, gain * slope, step_mix[0] * steps[0, i, at, :], change_mix[0] * changes[0, i, at, :]]
            for f in range(1, HIST):
                parts[2] = parts[2] + step_mix[f] * steps[f, i, at, :]
                parts[3] = parts[3] + change_mix[f] * changes[f, i, at, :]
            new_density[i, at, :] = parts[0] + (parts[1] + (parts[2] + parts[3]))


def call(kernel, outs, args, scratch=(), flops=0, place=pltpu.VMEM):
    whole = pl.BlockSpec(memory_space=pltpu.VMEM)
    shapes = [jax.ShapeDtypeStruct(shape, jnp.float32) for shape in outs]
    size = sum(4 * math.prod(a.shape) for a in (*args, *shapes))
    return pl.pallas_call(
        kernel,
        out_shape=shapes,
        in_specs=[pl.BlockSpec(memory_space=place)] * len(args),
        out_specs=[whole] * len(outs),
        scratch_shapes=[pltpu.VMEM(s, jnp.float32) if isinstance(s, tuple) else s for s in scratch],
        cost_estimate=pl.CostEstimate(flops=flops, bytes_accessed=size, transcendentals=0),
        compiler_params=pltpu.CompilerParams(vmem_limit_bytes=VMEM_LIMIT),
    )(*args)


def ring(axis, step):
    size = lax.axis_size(axis)
    return [(i, (i + step) % size) for i in range(size)]


def swap(axis, odd_up):
    size = lax.axis_size(axis)
    return [(i, (i + (1 if i % 2 == odd_up else -1)) % size) for i in range(size)]


def after(values, *earlier):
    return lax.optimization_barrier((tuple(values), earlier))[0]


def from_far(block):
    return lax.ppermute(block, "blk", swap("blk", 1))


def from_near(block, *earlier):
    return lax.ppermute(after((block,), *earlier)[0] if earlier else block, "blk", swap("blk", 0))


def z_halo(face_a, face_b):
    return (lax.ppermute(face_a, "gz", swap("gz", 0)), lax.ppermute(face_b, "gz", swap("gz", 1)))


def on_device(sqrt_density, ion_charge, ion_potential, hartree_prev, hist_steps, hist_changes):
    block = sqrt_density.shape
    ext = (block[0], block[1] + 16, block[2])
    face = (24, LANES)
    cells = math.prod(block)
    history = [hist_steps, hist_changes]
    cells = math.prod(block)
    history = [hist_steps, hist_changes]
    work = 300 * cells
    inputs = (hartree_prev, sqrt_density, ion_charge)
    far = from_far(hartree_prev)
    both, charge, *faces = call(
        launch_kernel,
        [(2 * REACH, *block[1:]), block, (48, LANES), (48, LANES)],
        [pltpu.with_memory_space_constraint(x, pltpu.HBM) for x in inputs],
        [pltpu.SemaphoreType.DMA((3,))],
        place=pltpu.HBM,
    )
    halo = (from_near(hartree_prev, *faces), far)
    ends = z_halo(*faces)
    density_ends = ends

    def advance(gain, inner, halo, ends, last=False):
        near, far = halo
        (mid,) = call(
            functools.partial(near_kernel, gain), [block], [*after((inner,), *ends), near, *ends], flops=work
        )
        half = (REACH, block[1] // 2, LANES)
        return mid, call(
            functools.partial(last_far_kernel if last else far_kernel, gain),
            [block, half, half] if last else [block],
            [mid, far],
            flops=work,
        )

    def exchange(block_now):
        far = from_far(block_now)
        faces = call(pack_kernel, [face, face], [block_now], flops=work)
        return (from_near(block_now, *faces), far), z_halo(*faces)

    inner, r1 = call(side_one, [block, (40, LANES)], [both, charge, hist_steps], [ext], work)
    _, (v0,) = advance(1.0, inner, halo, ends)
    halo, ends = exchange(v0)
    inner, r2, m2 = call(side_two, [block, (88, LANES), (8, LANES)], [v0, both, *history], [ext], work)
    mid, (v1,) = advance(-1.0 / SHIFT, inner, halo, ends)
    late_density = after((sqrt_density,), mid)[0]
    density_halo = (from_near(late_density), from_far(late_density))
    halo, ends = exchange(v1)
    inner, grad, r3, m3 = call(
        side_three,
        [block, block, (72, LANES), (8, LANES)],
        [v0, v1, both, *density_halo, *density_ends, ion_potential, *history],
        [ext],
        work,
    )
    _, (v2,) = advance(-2.0 / SHIFT, inner, halo, ends)
    halo, ends = exchange(v2)
    inner, r4, m4 = call(
        side_four, [block, (40, LANES), (8, LANES)], [v1, v2, both, grad, *history], [ext], work
    )
    _, (v3, to_near, to_far) = advance(-2.0 / SHIFT, inner, halo, ends, last=True)
    far = from_far(to_far)
    (upper,) = call(pack_upper_kernel, [face], [v3], flops=work)
    near = from_near(to_near, upper)
    z_left = lax.ppermute(upper, "gz", ring("gz", 1))
    kept, given, inner = call(
        side_five,
        [(1, LANES), (1, LANES), (8, LANES)],
        [v2, v3, both, *history, r1, r2, r3, r4, m2, m3, m4],
        [(2 * LANES, LANES), (8, LANES), ext],
        work,
    )
    taken = from_near(given)
    row, part = call(
        couple_kernel, [(1, LANES), (8, LANES)], [v3, near, z_left, inner, kept, taken], flops=work
    )
    devices = lax.axis_size("blk") * lax.axis_size("gz")
    (outgoing,) = call(send_kernel, [(devices, LANES)], [v3, far, part, row], flops=work)
    received = lax.all_to_all(outgoing.reshape(devices, 1, LANES), ("blk", "gz"), 0, 0, tiled=True)
    return tuple(
        call(
            final_kernel,
            [block, block],
            [received.reshape(devices, LANES), both, grad, v0, v1, v2, v3, *history],
            [(3 * LANES, LANES)],
            work,
        )
    )


def solution(mesh):
    placed = (
        P("blk", None, "gz"),
        P("blk", None, "gz"),
        P("blk", None, "gz"),
        P("blk", None, "gz"),
        P(None, "blk", None, "gz"),
        P(None, "blk", None, "gz"),
    )
    return jax.shard_map(
        on_device,
        mesh=mesh,
        in_specs=placed,
        out_specs=(P("blk", None, "gz"), P("blk", None, "gz")),
        check_vma=False,
    )
```

```python
import functools
import math

import jax
import jax.numpy as jnp
from jax import lax
from jax.experimental import pallas as pl
from jax.experimental.pallas import tpu as pltpu
from jax.sharding import PartitionSpec as P

center = -5369.0 / 1800.0
coeffs = (12.0 / 7.0, -15.0 / 56.0, 10.0 / 189.0, -1.0 / 112.0, 2.0 / 825.0, -1.0 / 4752.0)
screen = 0.0025
spacing = 0.28
source_scale = 4.0 * math.pi * spacing * spacing
tf_scale = 5.0 / 3.0 * 2.871234
step_length = 0.01
damp_floor = 0.2

SHIFT = 2.0
HIST = 8
REACH = 6
LANES = 128
VMEM_LIMIT = 24 * 1024 * 1024

ROW_GRAM = 0
ROW_BASE = 136
ROW_W = 170
ROW_MOM = 238
HALF = 126


def place(n):
    return n if n < HALF else n + LANES - HALF


MOM_LANE = place(ROW_MOM) - LANES
PAIRS = tuple((i, j) for i in range(HIST) for j in range(i, HIST))
PAIR_ROW = {pair: row for row, pair in enumerate(PAIRS)}


def two_sum(a, b):
    s = a + b
    bb = s - a
    return s, (a - (s - bb)) + (b - bb)


def quick_sum(a, b):
    s = a + b
    return s, b - (s - a)


def split(a):
    t = 4097.0 * a
    hi = t - (t - a)
    return hi, a - hi


def two_prod(a, b):
    p = a * b
    ah, al = split(a)
    bh, bl = split(b)
    return p, ((ah * bh - p) + ah * bl + al * bh) + al * bl


def df_add(a, b):
    s, e = two_sum(a[0], b[0])
    return quick_sum(s, e + (a[1] + b[1]))


def df_neg(a):
    return (-a[0], -a[1])


def df_sub(a, b):
    return df_add(a, df_neg(b))


def df_scale(a, factor):
    return (a[0] * factor, a[1] * factor)


def df_mul(a, b):
    p, e = two_prod(a[0], b[0])
    return quick_sum(p, e + (a[0] * b[1] + a[1] * b[0]))


def df_div(a, b):
    q1 = a[0] / b[0]
    r = df_sub(a, df_mul(b, (q1, jnp.zeros_like(q1))))
    q2 = r[0] / b[0]
    return quick_sum(q1, q2)


def lane_ids(shape):
    return lax.broadcasted_iota(jnp.int32, shape, len(shape) - 1)


def inner_plane(i, own, ext):
    values = own[i]
    rows = values.shape[0]
    lane = lane_ids((rows, LANES))
    total = (3.0 * center) * values
    for k, weight in enumerate(coeffs, 1):
        pair = ext[i, 8 + k : 8 + k + rows, :] + ext[i, 8 - k : 8 - k + rows, :]
        if i + k < REACH:
            pair = pair + own[i + k]
        if i - k >= 0:
            pair = pair + own[i - k]
        up = pltpu.roll(jnp.where(lane < k, 0.0, values), LANES - k, 1)
        down = pltpu.roll(jnp.where(lane >= LANES - k, 0.0, values), k, 1)
        total = total + weight * (pair + (up + down))
    return total, values


def edge_faces(z_left, z_right):
    lane = lane_ids((24, LANES)) % 8
    lower = jnp.zeros((24, LANES), jnp.float32)
    upper = jnp.zeros((24, LANES), jnp.float32)
    for k, weight in enumerate(coeffs, 1):
        lower = lower + jnp.where(lane < k, weight * pltpu.roll(z_left, LANES - 8 + k, 1), 0.0)
        if z_right is not None:
            upper = upper + jnp.where(lane >= 8 - k, weight * pltpu.roll(z_right, 8 - k, 1), 0.0)
    return lower, upper


def side_plane(i, block, below, rows=slice(None)):
    total = None
    for k, weight in enumerate(coeffs, 1):
        layer = i - k + REACH if below else i + k - REACH
        if 0 <= layer < REACH:
            term = weight * block[layer, rows, :]
            total = term if total is None else total + term
    return total


def z_plane(i, faces, tiles=8):
    lane = lane_ids((8, LANES))
    lower, upper = (face[8 * (i // 2) : 8 * (i // 2) + 8] for face in faces)
    out = []
    for b in range(tiles):
        j = 8 * (i % 2) + b
        tile = jnp.where(lane < 8, pltpu.roll(lower, (LANES - 8 * j) % LANES, 1), 0.0)
        tile = jnp.where(lane >= LANES - 8, pltpu.roll(upper, (2 * LANES - 8 - 8 * j) % LANES, 1), tile)
        out.append(tile)
    return jnp.concatenate(out, axis=0)


def fill_ext(own, ext):
    rows = own.shape[1]
    ext[:, 8 : 8 + rows, :] = own[...]
    ext[:, 0:8, :] = own[:, rows - 8 : rows, :]
    ext[:, 8 + rows : 16 + rows, :] = own[:, 0:8, :]


def pack_faces(src, layers):
    lane = lane_ids((8, LANES))
    firsts, lasts = [], []
    for m in range(3):
        first = jnp.zeros((8, LANES), jnp.float32)
        last = jnp.zeros((8, LANES), jnp.float32)
        for j in range(16):
            n = 16 * m + j
            tile = src[layers + n // 8, 8 * (n % 8) : 8 * (n % 8) + 8, :]
            here = (lane >= 8 * j) & (lane < 8 * j + 8)
            first = jnp.where(here, pltpu.roll(tile, 8 * j, 1) if j else tile, first)
            last = jnp.where(here, pltpu.roll(tile, (8 * j + 8) % LANES, 1) if j < 15 else tile, last)
        firsts.append(first)
        lasts.append(last)
    return jnp.concatenate(firsts, axis=0), jnp.concatenate(lasts, axis=0)


def is_odd(axis):
    return lax.rem(lax.axis_index(axis), 2) == 1


def by_partner(lower, upper):
    odd = is_odd("gz")
    return jnp.where(odd, lower, upper), jnp.where(odd, upper, lower)


def by_side(first, second):
    odd = is_odd("gz")
    return jnp.where(odd, first, second), jnp.where(odd, second, first)


def with_sides(body):
    odd = is_odd("blk")

    @pl.when(odd)
    def _():
        body(True, False)

    @pl.when(jnp.logical_not(odd))
    def _():
        body(False, True)


def fold(hi, lo, axis, steps):
    for step in steps:
        hi, err = two_sum(hi, pltpu.roll(hi, step, axis))
        lo = lo + pltpu.roll(lo, step, axis) + err
    return hi, lo


def fold_rows(acc):
    hi, lo = fold(*acc, 0, (4, 2, 1))
    return hi[0:1], lo[0:1]


def fold_lanes(hi, lo):
    return quick_sum(*fold(hi, lo, 1, (64, 32, 16, 8, 4, 2, 1)))


def add_tile(acc, product):
    hi, err = two_sum(acc[0], product)
    return hi, acc[1] + err


def tile_of(ref, i, b):
    return ref[i, 8 * b : 8 * b + 8, :]


def store_moments(pairs, moments):
    zero = jnp.zeros((8, LANES), jnp.float32)

    def body(i, accs):
        for b in range(8):
            accs = tuple(
                add_tile(acc, tile_of(a, i, b) * tile_of(c, i, b)) for acc, (a, c) in zip(accs, pairs)
            )
        return accs

    accs = lax.fori_loop(0, REACH, body, tuple((zero, zero) for _ in pairs))
    for n, acc in enumerate(accs):
        moments[2 * n : 2 * n + 1, :], moments[2 * n + 1 : 2 * n + 2, :] = fold_rows(acc)


def collapse(acc):
    return jnp.sum(acc, axis=0, keepdims=True)


def launch_kernel(hartree, density, charge, both, charge_here, face_a, face_b, sems):
    places = (both.at[pl.ds(0, REACH)], both.at[pl.ds(REACH, REACH)], charge_here)
    copies = [
        pltpu.make_async_copy(src, dst, sems.at[n])
        for n, (src, dst) in enumerate(zip((hartree, density, charge), places))
    ]
    for copy in copies:
        copy.start()
    for n in range(2):
        copies[n].wait()
        rows = slice(24 * n, 24 * n + 24)
        face_a[rows, :], face_b[rows, :] = by_partner(*pack_faces(both, REACH * n))
    copies[2].wait()


def inner_residual(both, charge, out, ext):
    hartree = both.at[pl.ds(0, REACH)]
    fill_ext(hartree, ext)
    for i in range(REACH):
        lap, values = inner_plane(i, hartree, ext)
        rho = both[REACH + i]
        out[i] = source_scale * (rho * rho - charge[i]) - (screen * values - lap)


def inner_basis(own, prior, out, ext):
    fill_ext(own, ext)
    for i in range(REACH):
        lap, values = inner_plane(i, own, ext)
        moved = (screen / SHIFT - 1.0) * values - (1.0 / SHIFT) * lap
        out[i] = moved if prior is None else 2.0 * moved - prior[i]


def z_kernel(gain, inner, z_first, z_second, out):
    faces = edge_faces(*by_side(z_first[0:24, :], z_second[0:24, :]))
    for i in range(REACH):
        out[i] = inner[i] + gain * z_plane(i, faces)


def x_kernel(gain, inner, near, far, out):
    def body(near_below, far_below):
        for i in range(REACH):
            out[i] = inner[i] + gain * (side_plane(i, near, near_below) + side_plane(i, far, far_below))

    with_sides(body)


def last_x_kernel(gain, inner, near, far, out, to_near, to_far):
    half = out.shape[1] // 2

    def body(near_below, far_below):
        for i in range(REACH):
            plane = inner[i] + gain * (side_plane(i, near, near_below) + side_plane(i, far, far_below))
            out[i] = plane
            for ref, below in ((to_near, near_below), (to_far, far_below)):
                ref[i] = plane[:half] if below else plane[half:]

    with_sides(body)


def pack_kernel(block, face_a, face_b):
    face_a[...], face_b[...] = by_partner(*pack_faces(block, 0))


def pack_upper_kernel(block, face):
    face[...] = pack_faces(block, 0)[1]


def store(rows, base, values):
    for n, value in enumerate(values):
        rows[base + n : base + n + 1, :] = value


def gram_dots(left, right, pairs):
    zero = jnp.zeros((8, LANES), jnp.float32)

    def body(i, accs):
        for b in range(8):
            at = pl.ds(8 * b, 8)
            l_tiles = {p: left[p, i, at, :] for p in sorted({p for p, _ in pairs})}
            if left is right:
                r_tiles = l_tiles
            else:
                r_tiles = {q: right[q, i, at, :] for q in sorted({q for _, q in pairs})}
            accs = tuple(acc + l_tiles[p] * r_tiles[q] for acc, (p, q) in zip(accs, pairs))
        return accs

    accs = lax.fori_loop(0, REACH, body, tuple(zero for _ in pairs))
    return [collapse(acc) for acc in accs]


CROSS_PAIRS = tuple((i, j) for i in range(HIST) for j in range(HIST))


def field_dots(steps, changes, others, plain=()):
    zero = jnp.zeros((8, LANES), jnp.float32)
    count = 2 * HIST

    def body(i, accs):
        accs = list(accs)
        for b in range(8):
            at = pl.ds(8 * b, 8)
            tiles = [other(i, b) for other in others]
            for f in range(count):
                field = steps[f, i, at, :] if f < HIST else changes[f - HIST, i, at, :]
                for o, tile in enumerate(tiles):
                    accs[o * count + f] = accs[o * count + f] + field * tile
            for n, (one, two) in enumerate(plain, len(others) * count):
                accs[n] = accs[n] + one(i, b) * two(i, b)
        return tuple(accs)

    total = count * len(others) + len(plain)
    return [collapse(acc) for acc in lax.fori_loop(0, REACH, body, (zero,) * total)]


def base_gradient(both, near, far, z_first, z_second, potential, grad, ext):
    hartree = both.at[pl.ds(0, REACH)]
    density = both.at[pl.ds(REACH, REACH)]
    fill_ext(density, ext)
    faces = edge_faces(*by_side(z_first[24:48, :], z_second[24:48, :]))

    def body(near_below, far_below):
        for i in range(REACH):
            grad[i] = side_plane(i, near, near_below) + side_plane(i, far, far_below) + z_plane(i, faces)

    with_sides(body)
    for i in range(REACH):
        lap, rho = inner_plane(i, density, ext)
        power = jnp.exp(jnp.log(rho) * (4.0 / 3.0))
        grad[i] = 2.0 * rho * (hartree[i] + potential[i] + tf_scale * power) - (lap + grad[i]) * (
            1.0 / (spacing * spacing)
        )


def density_tile(both):
    return lambda i, b: tile_of(both, REACH + i, b)


def lifted_tile(both, vector):
    return lambda i, b: 2.0 * tile_of(both, REACH + i, b) * tile_of(vector, i, b)


def side_one(both, charge, inner, ext):
    inner_residual(both, charge, inner, ext)


def side_two(vector, both, steps, changes, inner, rows, moments, ext):
    inner_basis(vector, None, inner, ext)
    lifted, rho = lifted_tile(both, vector), density_tile(both)
    store(rows, 0, field_dots(steps, changes, [lifted], [(rho, lifted)]))
    store_moments([(vector, vector)], moments)


def side_three(prior, vector, both, near, far, z_first, z_second, potential, steps, changes, *outs):
    inner, grad, rows, moments, ext = outs
    inner_basis(vector, prior, inner, ext)
    lifted, rho = lifted_tile(both, vector), density_tile(both)
    values = field_dots(steps, changes, [lifted, rho], [(rho, lifted)])
    store(rows, 0, values[:16] + values[32:] + values[16:32])
    store(rows, 33, gram_dots(steps, changes, CROSS_PAIRS[32:]))
    store_moments([(prior, vector), (vector, vector)], moments)
    base_gradient(both, near, far, z_first, z_second, potential, grad, ext)


def side_four(prior, vector, both, grad, steps, changes, inner, rows, moments, ext):
    inner_basis(vector, prior, inner, ext)
    lifted, rho = lifted_tile(both, vector), density_tile(both)
    slope = lambda i, b: tile_of(grad, i, b)
    values = field_dots(steps, changes, [lifted, slope], [(rho, lifted), (rho, slope), (rho, rho)])
    store(rows, 0, values[:16] + values[32:33] + values[16:32] + values[33:])
    store(rows, 35, gram_dots(steps, steps, PAIRS))
    store(rows, 71, gram_dots(changes, changes, PAIRS))
    store(rows, 107, gram_dots(steps, changes, CROSS_PAIRS[:32]))
    store_moments([(prior, vector), (vector, vector)], moments)


def side_five(prior, vector, both, steps, changes, r2, r3, r4, m2, m3, m4, kept, given, inner, table, m5, ext):
    lifted, rho = lifted_tile(both, vector), density_tile(both)
    own = field_dots(steps, changes, [lifted], [(rho, lifted)])
    store_moments([(prior, vector), (vector, vector)], m5)
    table[...] = jnp.zeros_like(table)

    def put(base, ref, start, count):
        before = max(0, min(count, HALF - base))
        if before:
            table[base : base + before, :] = ref[start : start + before, :]
        if before < count:
            at = place(base + before)
            table[at : at + count - before, :] = ref[start + before : start + count, :]

    put(ROW_GRAM, r4, 35, 104)
    put(ROW_GRAM + 104, r3, 33, 32)
    put(ROW_BASE, r3, 17, 16)
    put(ROW_BASE + 16, r4, 17, 18)
    for n, rows in enumerate((r2, r3, r4)):
        put(ROW_W + 17 * n, rows, 0, 17)
    store(table, place(ROW_W + 51), own)

    order = [(m2, 0), (m3, 0), (m3, 1), (m4, 0), (m4, 1), (m5, 0), (m5, 1)]
    zero = jnp.zeros((1, LANES), jnp.float32)
    parts = [
        jnp.concatenate([ref[2 * which + low : 2 * which + low + 1, :] for ref, which in order] + [zero], axis=0)
        for low in range(2)
    ]
    hi, lo = fold_lanes(*parts)
    lane = lane_ids((1, LANES))
    first = jnp.sum(jnp.transpose(table[0:LANES, :]), axis=0, keepdims=True)
    second = jnp.sum(jnp.transpose(table[LANES : 2 * LANES, :]), axis=0, keepdims=True)
    for n in range(7):
        second = jnp.where(lane == MOM_LANE + n, hi[n : n + 1], second)
        second = jnp.where(lane == MOM_LANE + 7 + n, lo[n : n + 1], second)
    odd = is_odd("blk")
    kept[...] = jnp.where(odd, second, first)
    given[...] = jnp.where(odd, first, second)

    fill_ext(vector, ext)
    zero = jnp.zeros((8, LANES), jnp.float32)
    accs = [(zero, zero) for _ in range(2)]
    for i in range(REACH):
        lap, values = inner_plane(i, vector, ext)
        product = values * ((screen / SHIFT - 1.0) * values - (1.0 / SHIFT) * lap)
        for b in range(8):
            accs[b % 2] = add_tile(accs[b % 2], product[8 * b : 8 * b + 8])
    hi, err = two_sum(accs[0][0], accs[1][0])
    inner[0:1, :], inner[1:2, :] = fold_rows((hi, accs[0][1] + accs[1][1] + err))


def couple(own, block, below, acc):
    half = own.shape[1] // 2
    for i in range(REACH):
        product = own[i, half:, :] * side_plane(i, block, True) if below else own[i, :half, :] * side_plane(i, block, False)
        for b in range(half // 8):
            acc = add_tile(acc, product[8 * b : 8 * b + 8])
    return acc


def couple_kernel(own, z_left, inner, kept, taken, row, part):
    zero = jnp.zeros((8, LANES), jnp.float32)
    faces = edge_faces(z_left[...], None)
    acc = (zero, zero)
    for i in range(REACH):
        product = own[i] * z_plane(i, faces)
        for b in range(8):
            acc = add_tile(acc, product[8 * b : 8 * b + 8])
    sides = df_scale(fold_rows(acc), -2.0 / SHIFT)
    part[0:1, :], part[1:2, :] = df_add(sides, (inner[0:1, :], inner[1:2, :]))
    lane = lane_ids((1, LANES))
    total, err = two_sum(kept[...], taken[...])
    low_lane = (lane >= MOM_LANE + 7) & (lane < MOM_LANE + 14) & is_odd("blk")
    row[...] = jnp.where(low_lane, total + pltpu.roll(err, 7, 1), total)


def send_kernel(own, far, near, part, row, out):
    zero = jnp.zeros((8, LANES), jnp.float32)

    def body(near_below, far_below):
        acc = couple(own, far, far_below, couple(own, near, near_below, (zero, zero)))
        hi, lo = fold_lanes(*df_add(df_scale(fold_rows(acc), -2.0 / SHIFT), (part[0:1, :], part[1:2, :])))
        lane = lane_ids((1, LANES))
        value = jnp.where(lane == HALF, hi, jnp.where(lane == HALF + 1, lo, row[...]))
        out[...] = jnp.broadcast_to(value, out.shape)

    with_sides(body)


def solve_krylov(moment):
    n00, n01, n11, n12, n22, n23, n33, n34 = moment
    nu = [n00, n01]
    nu.append(df_sub(df_scale(n11, 2.0), n00))
    nu.append(df_sub(df_scale(n12, 2.0), n01))
    nu.append(df_sub(df_scale(n22, 2.0), n00))
    nu.append(df_sub(df_scale(n23, 2.0), n01))
    nu.append(df_sub(df_scale(n33, 2.0), n00))

    def gram(i, j):
        if i == j == 0:
            return n00
        return df_scale(df_add(nu[i + j], nu[abs(i - j)]), 0.5)

    def moved(i, j):
        if i == 3 and j == 3:
            return n34
        if j == 0:
            return gram(i, 1)
        return df_scale(df_add(gram(i, j + 1), gram(i, j - 1)), 0.5)

    mat = {(i, j): df_add(moved(i, j), gram(i, j)) for i in range(4) for j in range(i + 1)}
    rhs = [df_scale(gram(i, 0), 1.0 / SHIFT) for i in range(4)]
    low = {}
    for k in range(4):
        for i in range(k + 1, 4):
            low[i, k] = df_div(mat[i, k], mat[k, k])
        for i in range(k + 1, 4):
            for j in range(k + 1, i + 1):
                mat[i, j] = df_sub(mat[i, j], df_mul(low[i, k], mat[j, k]))
            rhs[i] = df_sub(rhs[i], df_mul(low[i, k], rhs[k]))
    sol = [None] * 4
    for k in reversed(range(4)):
        value = df_div(rhs[k], mat[k, k])
        for i in range(k + 1, 4):
            value = df_sub(value, df_mul(low[i, k], sol[i]))
        sol[k] = value
    return [hi + lo for hi, lo in sol]


def final_kernel(received, both, grad, v0, v1, v2, v3, steps, changes, new_density, new_hartree, spread):
    parts = [(received[8 * n : 8 * n + 8, :], jnp.zeros((8, LANES), jnp.float32)) for n in range(4)]
    for n in range(4, received.shape[0] // 8):
        parts[n % 4] = add_tile(parts[n % 4], received[8 * n : 8 * n + 8, :])
    while len(parts) > 1:
        half = len(parts) // 2
        merged = []
        for a, b in zip(parts[:half], parts[half:]):
            hi, err = two_sum(a[0], b[0])
            merged.append((hi, a[1] + b[1] + err))
        parts = merged
    hi, lo = fold(*parts[0], 0, (1, 2))
    lane = lane_ids((1, LANES))
    last, err = two_sum(hi[3:4], hi[7:8])
    err = err + (lo[3:4] + lo[7:8])
    first = hi[3:4]
    second = jnp.where(lane >= HALF, last, hi[7:8])
    low = jnp.where(lane >= HALF, err, lo[7:8])
    low = low + jnp.where(lane == HALF, pltpu.roll(second, LANES - 1, 1), pltpu.roll(second, LANES - 7, 1))
    for n, value in enumerate((first, second, low)):
        spread[LANES * n : LANES * n + LANES, :] = jnp.transpose(jnp.broadcast_to(value, (LANES, LANES)))

    def row(n):
        return spread[place(n) : place(n) + 1, :]

    def moment(n):
        at = LANES + (MOM_LANE + n if n < 7 else HALF)
        return quick_sum(spread[at : at + 1, :], spread[LANES + at : LANES + at + 1, :])

    mix = solve_krylov([moment(n) for n in range(8)])

    def s_s(i, j):
        return row(ROW_GRAM + PAIR_ROW[min(i, j), max(i, j)])

    def y_y(i, j):
        return row(ROW_GRAM + 36 + PAIR_ROW[min(i, j), max(i, j)])

    def s_y(i, j):
        return row(ROW_GRAM + 72 + 8 * i + j)

    pairs = range(HIST)
    theta, rest, inverse = [], [], []
    for i in pairs:
        curv, norm = s_y(i, i), s_s(i, i)
        kept = (1.0 - damp_floor) * norm
        damp = jnp.where(curv >= damp_floor * norm, 1.0, kept / jnp.maximum(norm - curv, kept))
        theta.append(damp)
        rest.append(1.0 - damp)
        inverse.append(1.0 / (damp * curv + (1.0 - damp) * norm))

    def s_bar(i, j):
        return theta[j] * s_y(i, j) + rest[j] * s_s(i, j)

    def bar_bar(i, j):
        return theta[i] * (theta[j] * y_y(i, j) + rest[j] * s_y(j, i)) + rest[i] * s_bar(i, j)

    last = HIST - 1
    scaling = s_bar(last, last) / bar_bar(last, last)

    def energy(n):
        value = row(ROW_BASE + 16 + n)
        for j in range(4):
            value = value + mix[j] * row(ROW_W + 17 * j + n)
        return value

    chem = energy(16) / row(ROW_BASE + 33)

    def gradient(n):
        return energy(n) - chem * row(ROW_BASE + n)

    s_grad = [gradient(i) for i in pairs]
    bar_grad = [theta[i] * gradient(HIST + i) + rest[i] * s_grad[i] for i in pairs]

    first = [None] * HIST
    pending = list(s_grad)
    for j in reversed(pairs):
        first[j] = inverse[j] * pending[j]
        for i in range(j):
            pending[i] = pending[i] - first[j] * s_bar(i, j)
    pending = list(bar_grad)
    for j in pairs:
        for i in pairs:
            pending[i] = pending[i] - first[j] * bar_bar(i, j)
    pending = [scaling * value for value in pending]
    step_mix, change_mix = [], []
    for j in pairs:
        net = first[j] - inverse[j] * pending[j]
        for i in range(j + 1, HIST):
            pending[i] = pending[i] + net * s_bar(j, i)
        change_mix.append((-step_length) * (-scaling * first[j] * theta[j]))
        step_mix.append((-step_length) * (net - scaling * first[j] * rest[j]))

    wide = lambda value: jnp.broadcast_to(value, (8, LANES))
    mix = [wide(value) for value in mix]
    chem, gain = wide(chem), wide((-step_length) * scaling)
    step_mix = [wide(value) for value in step_mix]
    change_mix = [wide(value) for value in change_mix]
    basis = (v0, v1, v2, v3)

    @pl.loop(0, REACH)
    def _(i):
        for b in range(8):
            at = pl.ds(8 * b, 8)
            rho = both[REACH + i, at, :]
            lift = mix[0] * v0[i, at, :]
            for j in range(1, 4):
                lift = lift + mix[j] * basis[j][i, at, :]
            new_hartree[i, at, :] = both[i, at, :] + lift
            slope = grad[i, at, :] + 2.0 * rho * lift - chem * rho
            parts = [rho, gain * slope, step_mix[0] * steps[0, i, at, :], change_mix[0] * changes[0, i, at, :]]
            for f in range(1, HIST):
                parts[2] = parts[2] + step_mix[f] * steps[f, i, at, :]
                parts[3] = parts[3] + change_mix[f] * changes[f, i, at, :]
            new_density[i, at, :] = parts[0] + (parts[1] + (parts[2] + parts[3]))


def call(kernel, outs, args, scratch=(), flops=0, place=pltpu.VMEM):
    whole = pl.BlockSpec(memory_space=pltpu.VMEM)
    shapes = [jax.ShapeDtypeStruct(shape, jnp.float32) for shape in outs]
    size = sum(4 * math.prod(a.shape) for a in (*args, *shapes))
    return pl.pallas_call(
        kernel,
        out_shape=shapes,
        in_specs=[pl.BlockSpec(memory_space=place)] * len(args),
        out_specs=[whole] * len(outs),
        scratch_shapes=[pltpu.VMEM(s, jnp.float32) if isinstance(s, tuple) else s for s in scratch],
        cost_estimate=pl.CostEstimate(flops=flops, bytes_accessed=size, transcendentals=0),
        compiler_params=pltpu.CompilerParams(vmem_limit_bytes=VMEM_LIMIT),
    )(*args)


def ring(axis, step):
    size = lax.axis_size(axis)
    return [(i, (i + step) % size) for i in range(size)]


def swap(axis, odd_up):
    size = lax.axis_size(axis)
    return [(i, (i + (1 if i % 2 == odd_up else -1)) % size) for i in range(size)]


def after(values, *earlier):
    return lax.optimization_barrier((tuple(values), earlier))[0]


def x_halo(block):
    far = lax.ppermute(block, "blk", swap("blk", 1))
    return (lax.ppermute(block, "blk", swap("blk", 0)), far)


def z_halo(face_a, face_b):
    return (lax.ppermute(face_a, "gz", swap("gz", 0)), lax.ppermute(face_b, "gz", swap("gz", 1)))


def on_device(sqrt_density, ion_charge, ion_potential, hartree_prev, hist_steps, hist_changes):
    block = sqrt_density.shape
    ext = (block[0], block[1] + 16, block[2])
    face = (24, LANES)
    cells = math.prod(block)
    history = [hist_steps, hist_changes]
    cells = math.prod(block)
    history = [hist_steps, hist_changes]
    work = 300 * cells
    inputs = (hartree_prev, sqrt_density, ion_charge)
    halo = x_halo(hartree_prev)
    both, charge, *faces = call(
        launch_kernel,
        [(2 * REACH, *block[1:]), block, (48, LANES), (48, LANES)],
        [pltpu.with_memory_space_constraint(x, pltpu.HBM) for x in inputs],
        [pltpu.SemaphoreType.DMA((3,))],
        place=pltpu.HBM,
    )
    ends = z_halo(*faces)
    density_ends = ends
    half = (REACH, block[1] // 2, LANES)

    def advance(gain, inner, halo, ends, last=False):
        (mid,) = call(functools.partial(z_kernel, gain), [block], [inner, *ends], flops=work)
        return call(
            functools.partial(last_x_kernel if last else x_kernel, gain),
            [block, half, half] if last else [block],
            [mid, *halo],
            flops=work,
        )

    def exchange(block_now):
        halo = x_halo(block_now)
        return halo, z_halo(*call(pack_kernel, [face, face], [block_now], flops=work))

    (inner,) = call(side_one, [block], [both, charge], [ext], work)
    (v0,) = advance(1.0, inner, halo, ends)
    halo, ends = exchange(v0)
    density_halo = x_halo(after((sqrt_density,), v0)[0])
    inner, r2, m2 = call(side_two, [block, (24, LANES), (8, LANES)], [v0, both, *history], [ext], work)
    (v1,) = advance(-1.0 / SHIFT, inner, halo, ends)
    halo, ends = exchange(v1)
    inner, grad, r3, m3 = call(
        side_three,
        [block, block, (72, LANES), (8, LANES)],
        [v0, v1, both, *density_halo, *density_ends, ion_potential, *history],
        [ext],
        work,
    )
    (v2,) = advance(-2.0 / SHIFT, inner, halo, ends)
    halo, ends = exchange(v2)
    inner, r4, m4 = call(
        side_four, [block, (144, LANES), (8, LANES)], [v1, v2, both, grad, *history], [ext], work
    )
    v3, to_near, to_far = advance(-2.0 / SHIFT, inner, halo, ends, last=True)
    far = lax.ppermute(to_far, "blk", swap("blk", 1))
    near = lax.ppermute(to_near, "blk", swap("blk", 0))
    (upper,) = call(pack_upper_kernel, [face], [v3], flops=work)
    z_left = lax.ppermute(upper, "gz", ring("gz", 1))
    kept, given, inner = call(
        side_five,
        [(1, LANES), (1, LANES), (8, LANES)],
        [v2, v3, both, *history, r2, r3, r4, m2, m3, m4],
        [(2 * LANES, LANES), (8, LANES), ext],
        work,
    )
    taken = lax.ppermute(given, "blk", swap("blk", 0))
    row, part = call(
        couple_kernel, [(1, LANES), (8, LANES)], [v3, z_left, inner, kept, taken], flops=work
    )
    devices = lax.axis_size("blk") * lax.axis_size("gz")
    (outgoing,) = call(send_kernel, [(devices, LANES)], [v3, far, near, part, row], flops=work)
    received = lax.all_to_all(outgoing.reshape(devices, 1, LANES), ("blk", "gz"), 0, 0, tiled=True)
    return tuple(
        call(
            final_kernel,
            [block, block],
            [received.reshape(devices, LANES), both, grad, v0, v1, v2, v3, *history],
            [(3 * LANES, LANES)],
            work,
        )
    )


def solution(mesh):
    placed = (
        P("blk", None, "gz"),
        P("blk", None, "gz"),
        P("blk", None, "gz"),
        P("blk", None, "gz"),
        P(None, "blk", None, "gz"),
        P(None, "blk", None, "gz"),
    )
    return jax.shard_map(
        on_device,
        mesh=mesh,
        in_specs=placed,
        out_specs=(P("blk", None, "gz"), P("blk", None, "gz")),
        check_vma=False,
    )
```

```python
import functools
import math

import jax
import jax.numpy as jnp
from jax import lax
from jax.experimental import pallas as pl
from jax.experimental.pallas import tpu as pltpu
from jax.sharding import PartitionSpec as P

center = -5369.0 / 1800.0
coeffs = (12.0 / 7.0, -15.0 / 56.0, 10.0 / 189.0, -1.0 / 112.0, 2.0 / 825.0, -1.0 / 4752.0)
screen = 0.0025
spacing = 0.28
source_scale = 4.0 * math.pi * spacing * spacing
tf_scale = 5.0 / 3.0 * 2.871234
step_length = 0.01
damp_floor = 0.2

SHIFT = 2.0
HIST = 8
REACH = 6
LANES = 128
VMEM_LIMIT = 24 * 1024 * 1024

ROW_GRAM = 0
ROW_BASE = 136
ROW_W = 170
ROW_MOM = 238
HALF = 126


def place(n):
    return n if n < HALF else n + LANES - HALF


MOM_LANE = place(ROW_MOM) - LANES
PAIRS = tuple((i, j) for i in range(HIST) for j in range(i, HIST))
PAIR_ROW = {pair: row for row, pair in enumerate(PAIRS)}


def two_sum(a, b):
    s = a + b
    bb = s - a
    return s, (a - (s - bb)) + (b - bb)


def quick_sum(a, b):
    s = a + b
    return s, b - (s - a)


def split(a):
    t = 4097.0 * a
    hi = t - (t - a)
    return hi, a - hi


def two_prod(a, b):
    p = a * b
    ah, al = split(a)
    bh, bl = split(b)
    return p, ((ah * bh - p) + ah * bl + al * bh) + al * bl


def df_add(a, b):
    s, e = two_sum(a[0], b[0])
    return quick_sum(s, e + (a[1] + b[1]))


def df_neg(a):
    return (-a[0], -a[1])


def df_sub(a, b):
    return df_add(a, df_neg(b))


def df_scale(a, factor):
    return (a[0] * factor, a[1] * factor)


def df_mul(a, b):
    p, e = two_prod(a[0], b[0])
    return quick_sum(p, e + (a[0] * b[1] + a[1] * b[0]))


def df_over(a, b, inverse):
    q = a[0] * inverse
    p, e = two_prod(q, b[0])
    rest = ((a[0] - p) - e) + (a[1] - q * b[1])
    return quick_sum(q, rest * inverse)


def lane_ids(shape):
    return lax.broadcasted_iota(jnp.int32, shape, len(shape) - 1)


def inner_plane(i, own, ext):
    values = own[i]
    rows = values.shape[0]
    lane = lane_ids((rows, LANES))
    total = (3.0 * center) * values
    for k, weight in enumerate(coeffs, 1):
        pair = ext[i, 8 + k : 8 + k + rows, :] + ext[i, 8 - k : 8 - k + rows, :]
        if i + k < REACH:
            pair = pair + own[i + k]
        if i - k >= 0:
            pair = pair + own[i - k]
        up = pltpu.roll(jnp.where(lane < k, 0.0, values), LANES - k, 1)
        down = pltpu.roll(jnp.where(lane >= LANES - k, 0.0, values), k, 1)
        total = total + weight * (pair + (up + down))
    return total, values


def edge_faces(z_left, z_right):
    lane = lane_ids((24, LANES)) % 8
    lower = jnp.zeros((24, LANES), jnp.float32)
    upper = jnp.zeros((24, LANES), jnp.float32)
    for k, weight in enumerate(coeffs, 1):
        lower = lower + jnp.where(lane < k, weight * pltpu.roll(z_left, LANES - 8 + k, 1), 0.0)
        if z_right is not None:
            upper = upper + jnp.where(lane >= 8 - k, weight * pltpu.roll(z_right, 8 - k, 1), 0.0)
    return lower, upper


def side_plane(i, block, below, rows=slice(None)):
    total = None
    for k, weight in enumerate(coeffs, 1):
        layer = i - k + REACH if below else i + k - REACH
        if 0 <= layer < REACH:
            term = weight * block[layer, rows, :]
            total = term if total is None else total + term
    return total


def z_plane(i, faces, tiles=8):
    lane = lane_ids((8, LANES))
    lower, upper = (face[8 * (i // 2) : 8 * (i // 2) + 8] for face in faces)
    out = []
    for b in range(tiles):
        j = 8 * (i % 2) + b
        tile = jnp.where(lane < 8, pltpu.roll(lower, (LANES - 8 * j) % LANES, 1), 0.0)
        tile = jnp.where(lane >= LANES - 8, pltpu.roll(upper, (2 * LANES - 8 - 8 * j) % LANES, 1), tile)
        out.append(tile)
    return jnp.concatenate(out, axis=0)


def fill_ext(own, ext):
    rows = own.shape[1]
    ext[:, 8 : 8 + rows, :] = own[...]
    ext[:, 0:8, :] = own[:, rows - 8 : rows, :]
    ext[:, 8 + rows : 16 + rows, :] = own[:, 0:8, :]


def pack_faces(src, layers):
    lane = lane_ids((8, LANES))
    firsts, lasts = [], []
    for m in range(3):
        first = jnp.zeros((8, LANES), jnp.float32)
        last = jnp.zeros((8, LANES), jnp.float32)
        for j in range(16):
            n = 16 * m + j
            tile = src[layers + n // 8, 8 * (n % 8) : 8 * (n % 8) + 8, :]
            here = (lane >= 8 * j) & (lane < 8 * j + 8)
            first = jnp.where(here, pltpu.roll(tile, 8 * j, 1) if j else tile, first)
            last = jnp.where(here, pltpu.roll(tile, (8 * j + 8) % LANES, 1) if j < 15 else tile, last)
        firsts.append(first)
        lasts.append(last)
    return jnp.concatenate(firsts, axis=0), jnp.concatenate(lasts, axis=0)


def is_odd(axis):
    return lax.rem(lax.axis_index(axis), 2) == 1


def by_partner(lower, upper):
    odd = is_odd("gz")
    return jnp.where(odd, lower, upper), jnp.where(odd, upper, lower)


def by_side(first, second):
    odd = is_odd("gz")
    return jnp.where(odd, first, second), jnp.where(odd, second, first)


def with_sides(body):
    odd = is_odd("blk")

    @pl.when(odd)
    def _():
        body(True, False)

    @pl.when(jnp.logical_not(odd))
    def _():
        body(False, True)


def fold(hi, lo, axis, steps):
    for step in steps:
        hi, err = two_sum(hi, pltpu.roll(hi, step, axis))
        lo = lo + pltpu.roll(lo, step, axis) + err
    return hi, lo


def fold_rows(acc):
    hi, lo = fold(*acc, 0, (4, 2, 1))
    return hi[0:1], lo[0:1]


def fold_lanes(hi, lo):
    return quick_sum(*fold(hi, lo, 1, (64, 32, 16, 8, 4, 2, 1)))


def add_tile(acc, product):
    hi, err = two_sum(acc[0], product)
    return hi, acc[1] + err


def tile_of(ref, i, b):
    return ref[i, 8 * b : 8 * b + 8, :]


def store_moments(pairs, moments):
    zero = jnp.zeros((8, LANES), jnp.float32)

    def body(i, accs):
        for b in range(8):
            accs = tuple(
                add_tile(acc, tile_of(a, i, b) * tile_of(c, i, b)) for acc, (a, c) in zip(accs, pairs)
            )
        return accs

    accs = lax.fori_loop(0, REACH, body, tuple((zero, zero) for _ in pairs))
    for n, acc in enumerate(accs):
        moments[2 * n : 2 * n + 1, :], moments[2 * n + 1 : 2 * n + 2, :] = fold_rows(acc)


def collapse(acc):
    return jnp.sum(acc, axis=0, keepdims=True)


def launch_kernel(hartree, density, charge, both, charge_here, face_a, face_b, sems):
    places = (both.at[pl.ds(0, REACH)], both.at[pl.ds(REACH, REACH)], charge_here)
    copies = [
        pltpu.make_async_copy(src, dst, sems.at[n])
        for n, (src, dst) in enumerate(zip((hartree, density, charge), places))
    ]
    for copy in copies:
        copy.start()
    for n in range(2):
        copies[n].wait()
        rows = slice(24 * n, 24 * n + 24)
        face_a[rows, :], face_b[rows, :] = by_partner(*pack_faces(both, REACH * n))
    copies[2].wait()


def inner_residual(both, charge, out, ext):
    hartree = both.at[pl.ds(0, REACH)]
    fill_ext(hartree, ext)
    for i in range(REACH):
        lap, values = inner_plane(i, hartree, ext)
        rho = both[REACH + i]
        out[i] = source_scale * (rho * rho - charge[i]) - (screen * values - lap)


def inner_basis(own, prior, out, ext):
    fill_ext(own, ext)
    for i in range(REACH):
        lap, values = inner_plane(i, own, ext)
        moved = (screen / SHIFT - 1.0) * values - (1.0 / SHIFT) * lap
        out[i] = moved if prior is None else 2.0 * moved - prior[i]


def z_kernel(gain, inner, z_first, z_second, out):
    faces = edge_faces(*by_side(z_first[0:24, :], z_second[0:24, :]))
    for i in range(REACH):
        out[i] = inner[i] + gain * z_plane(i, faces)


def x_kernel(gain, inner, near, far, out):
    def body(near_below, far_below):
        for i in range(REACH):
            out[i] = inner[i] + gain * (side_plane(i, near, near_below) + side_plane(i, far, far_below))

    with_sides(body)


def last_x_kernel(gain, inner, near, far, out, to_near, to_far):
    half = out.shape[1] // 2

    def body(near_below, far_below):
        for i in range(REACH):
            plane = inner[i] + gain * (side_plane(i, near, near_below) + side_plane(i, far, far_below))
            out[i] = plane
            for ref, below in ((to_near, near_below), (to_far, far_below)):
                ref[i] = plane[:half] if below else plane[half:]

    with_sides(body)


def pack_kernel(block, face_a, face_b):
    face_a[...], face_b[...] = by_partner(*pack_faces(block, 0))


def pack_upper_kernel(block, face):
    face[...] = pack_faces(block, 0)[1]


def store(rows, base, values):
    for n, value in enumerate(values):
        rows[base + n : base + n + 1, :] = value


def gram_dots(left, right, pairs):
    zero = jnp.zeros((8, LANES), jnp.float32)

    def body(i, accs):
        for b in range(8):
            at = pl.ds(8 * b, 8)
            l_tiles = {p: left[p, i, at, :] for p in sorted({p for p, _ in pairs})}
            if left is right:
                r_tiles = l_tiles
            else:
                r_tiles = {q: right[q, i, at, :] for q in sorted({q for _, q in pairs})}
            accs = tuple(acc + l_tiles[p] * r_tiles[q] for acc, (p, q) in zip(accs, pairs))
        return accs

    accs = lax.fori_loop(0, REACH, body, tuple(zero for _ in pairs))
    return [collapse(acc) for acc in accs]


CROSS_PAIRS = tuple((i, j) for i in range(HIST) for j in range(HIST))


def field_dots(steps, changes, others, plain=()):
    zero = jnp.zeros((8, LANES), jnp.float32)
    count = 2 * HIST

    def body(i, accs):
        accs = list(accs)
        for b in range(8):
            at = pl.ds(8 * b, 8)
            tiles = [other(i, b) for other in others]
            for f in range(count):
                field = steps[f, i, at, :] if f < HIST else changes[f - HIST, i, at, :]
                for o, tile in enumerate(tiles):
                    accs[o * count + f] = accs[o * count + f] + field * tile
            for n, (one, two) in enumerate(plain, len(others) * count):
                accs[n] = accs[n] + one(i, b) * two(i, b)
        return tuple(accs)

    total = count * len(others) + len(plain)
    return [collapse(acc) for acc in lax.fori_loop(0, REACH, body, (zero,) * total)]


def base_gradient(both, near, far, z_first, z_second, potential, grad, ext):
    hartree = both.at[pl.ds(0, REACH)]
    density = both.at[pl.ds(REACH, REACH)]
    fill_ext(density, ext)
    faces = edge_faces(*by_side(z_first[24:48, :], z_second[24:48, :]))

    def body(near_below, far_below):
        for i in range(REACH):
            grad[i] = side_plane(i, near, near_below) + side_plane(i, far, far_below) + z_plane(i, faces)

    with_sides(body)
    for i in range(REACH):
        lap, rho = inner_plane(i, density, ext)
        power = jnp.exp(jnp.log(rho) * (4.0 / 3.0))
        grad[i] = 2.0 * rho * (hartree[i] + potential[i] + tf_scale * power) - (lap + grad[i]) * (
            1.0 / (spacing * spacing)
        )


def density_tile(both):
    return lambda i, b: tile_of(both, REACH + i, b)


def lifted_tile(both, vector):
    return lambda i, b: 2.0 * tile_of(both, REACH + i, b) * tile_of(vector, i, b)


FETCHES = 4


def side_one(both, charge, steps, changes, inner, steps_here, changes_here, ext, sems):
    each = HIST // FETCHES
    copies = [
        pltpu.make_async_copy(src.at[pl.ds(each * n, each)], dst.at[pl.ds(each * n, each)], sems.at[FETCHES * m + n])
        for m, (src, dst) in enumerate(((steps, steps_here), (changes, changes_here)))
        for n in range(FETCHES)
    ]
    for copy in copies:
        copy.start()
    inner_residual(both, charge, inner, ext)
    for copy in copies:
        copy.wait()


def side_two(vector, both, steps, changes, inner, rows, moments, ext):
    inner_basis(vector, None, inner, ext)
    lifted, rho = lifted_tile(both, vector), density_tile(both)
    values = field_dots(steps, changes, [lifted, rho], [(rho, lifted)])
    store(rows, 0, values[:16] + values[32:] + values[16:32])
    store_moments([(vector, vector)], moments)


def side_three(prior, vector, both, near, far, z_first, z_second, potential, steps, changes, *outs):
    inner, grad, rows, moments, ext = outs
    inner_basis(vector, prior, inner, ext)
    lifted, rho = lifted_tile(both, vector), density_tile(both)
    store(rows, 0, field_dots(steps, changes, [lifted], [(rho, lifted)]))
    store(rows, 17, gram_dots(steps, changes, CROSS_PAIRS[32:]))
    store_moments([(prior, vector), (vector, vector)], moments)
    base_gradient(both, near, far, z_first, z_second, potential, grad, ext)


def side_four(prior, vector, both, grad, steps, changes, inner, rows, moments, ext):
    inner_basis(vector, prior, inner, ext)
    lifted, rho = lifted_tile(both, vector), density_tile(both)
    slope = lambda i, b: tile_of(grad, i, b)
    values = field_dots(steps, changes, [lifted, slope], [(rho, lifted), (rho, slope), (rho, rho)])
    store(rows, 0, values[:16] + values[32:33] + values[16:32] + values[33:])
    store(rows, 35, gram_dots(steps, steps, PAIRS))
    store(rows, 71, gram_dots(changes, changes, PAIRS))
    store_moments([(prior, vector), (vector, vector)], moments)


def side_five(prior, vector, both, steps, changes, r2, r3, r4, m2, m3, m4, kept, given, inner, table, m5, ext):
    lifted, rho = lifted_tile(both, vector), density_tile(both)
    own = field_dots(steps, changes, [lifted], [(rho, lifted)])
    store_moments([(prior, vector), (vector, vector)], m5)
    table[...] = jnp.zeros_like(table)

    def put(base, ref, start, count):
        before = max(0, min(count, HALF - base))
        if before:
            table[base : base + before, :] = ref[start : start + before, :]
        if before < count:
            at = place(base + before)
            table[at : at + count - before, :] = ref[start + before : start + count, :]

    put(ROW_GRAM, r4, 35, 72)
    store(table, ROW_GRAM + 72, gram_dots(steps, changes, CROSS_PAIRS[:32]))
    put(ROW_GRAM + 104, r3, 17, 32)
    put(ROW_BASE, r2, 17, 16)
    put(ROW_BASE + 16, r4, 17, 18)
    for n, rows in enumerate((r2, r3, r4)):
        put(ROW_W + 17 * n, rows, 0, 17)
    store(table, place(ROW_W + 51), own)

    order = [(m2, 0), (m3, 0), (m3, 1), (m4, 0), (m4, 1), (m5, 0), (m5, 1)]
    zero = jnp.zeros((1, LANES), jnp.float32)
    parts = [
        jnp.concatenate([ref[2 * which + low : 2 * which + low + 1, :] for ref, which in order] + [zero], axis=0)
        for low in range(2)
    ]
    hi, lo = fold_lanes(*parts)
    lane = lane_ids((1, LANES))
    first = jnp.sum(jnp.transpose(table[0:LANES, :]), axis=0, keepdims=True)
    second = jnp.sum(jnp.transpose(table[LANES : 2 * LANES, :]), axis=0, keepdims=True)
    for n in range(7):
        second = jnp.where(lane == MOM_LANE + n, hi[n : n + 1], second)
        second = jnp.where(lane == MOM_LANE + 7 + n, lo[n : n + 1], second)
    odd = is_odd("blk")
    kept[...] = jnp.where(odd, second, first)
    given[...] = jnp.where(odd, first, second)

    fill_ext(vector, ext)
    zero = jnp.zeros((8, LANES), jnp.float32)
    accs = [(zero, zero) for _ in range(2)]
    for i in range(REACH):
        lap, values = inner_plane(i, vector, ext)
        product = values * ((screen / SHIFT - 1.0) * values - (1.0 / SHIFT) * lap)
        for b in range(8):
            accs[b % 2] = add_tile(accs[b % 2], product[8 * b : 8 * b + 8])
    hi, err = two_sum(accs[0][0], accs[1][0])
    inner[0:1, :], inner[1:2, :] = fold_rows((hi, accs[0][1] + accs[1][1] + err))


def couple(own, block, below, acc):
    half = own.shape[1] // 2
    for i in range(REACH):
        product = own[i, half:, :] * side_plane(i, block, True) if below else own[i, :half, :] * side_plane(i, block, False)
        for b in range(half // 8):
            acc = add_tile(acc, product[8 * b : 8 * b + 8])
    return acc


def couple_kernel(own, z_left, inner, kept, taken, row, part):
    zero = jnp.zeros((8, LANES), jnp.float32)
    faces = edge_faces(z_left[...], None)
    acc = (zero, zero)
    for i in range(REACH):
        product = own[i] * z_plane(i, faces)
        for b in range(8):
            acc = add_tile(acc, product[8 * b : 8 * b + 8])
    sides = df_scale(fold_rows(acc), -2.0 / SHIFT)
    part[0:1, :], part[1:2, :] = df_add(sides, (inner[0:1, :], inner[1:2, :]))
    lane = lane_ids((1, LANES))
    total, err = two_sum(kept[...], taken[...])
    low_lane = (lane >= MOM_LANE + 7) & (lane < MOM_LANE + 14) & is_odd("blk")
    row[...] = jnp.where(low_lane, total + pltpu.roll(err, 7, 1), total)


def send_kernel(own, far, near, part, row, out):
    zero = jnp.zeros((8, LANES), jnp.float32)

    def body(near_below, far_below):
        acc = couple(own, far, far_below, couple(own, near, near_below, (zero, zero)))
        hi, lo = fold_lanes(*df_add(df_scale(fold_rows(acc), -2.0 / SHIFT), (part[0:1, :], part[1:2, :])))
        lane = lane_ids((1, LANES))
        value = jnp.where(lane == HALF, hi, jnp.where(lane == HALF + 1, lo, row[...]))
        out[...] = jnp.broadcast_to(value, out.shape)

    with_sides(body)


def solve_krylov(moment):
    n00, n01, n11, n12, n22, n23, n33, n34 = moment
    nu = [n00, n01]
    nu.append(df_sub(df_scale(n11, 2.0), n00))
    nu.append(df_sub(df_scale(n12, 2.0), n01))
    nu.append(df_sub(df_scale(n22, 2.0), n00))
    nu.append(df_sub(df_scale(n23, 2.0), n01))
    nu.append(df_sub(df_scale(n33, 2.0), n00))

    def gram(i, j):
        if i == j == 0:
            return n00
        return df_scale(df_add(nu[i + j], nu[abs(i - j)]), 0.5)

    def moved(i, j):
        if i == 3 and j == 3:
            return n34
        if j == 0:
            return gram(i, 1)
        return df_scale(df_add(gram(i, j + 1), gram(i, j - 1)), 0.5)

    mat = {(i, j): df_add(moved(i, j), gram(i, j)) for i in range(4) for j in range(i + 1)}
    rhs = [df_scale(gram(i, 0), 1.0 / SHIFT) for i in range(4)]
    low, inverse = {}, []
    for k in range(4):
        inverse.append(1.0 / mat[k, k][0])
        for i in range(k + 1, 4):
            low[i, k] = df_over(mat[i, k], mat[k, k], inverse[k])
        for i in range(k + 1, 4):
            for j in range(k + 1, i + 1):
                mat[i, j] = df_sub(mat[i, j], df_mul(low[i, k], mat[j, k]))
            rhs[i] = df_sub(rhs[i], df_mul(low[i, k], rhs[k]))
    sol = [None] * 4
    for k in reversed(range(4)):
        value = df_over(rhs[k], mat[k, k], inverse[k])
        for i in range(k + 1, 4):
            value = df_sub(value, df_mul(low[i, k], sol[i]))
        sol[k] = value
    return [hi + lo for hi, lo in sol]


def final_kernel(received, both, grad, v0, v1, v2, v3, steps, changes, new_density, new_hartree, spread, density_here, hartree_here, sems):
    parts = [(received[8 * n : 8 * n + 8, :], jnp.zeros((8, LANES), jnp.float32)) for n in range(4)]
    for n in range(4, received.shape[0] // 8):
        parts[n % 4] = add_tile(parts[n % 4], received[8 * n : 8 * n + 8, :])
    while len(parts) > 1:
        half = len(parts) // 2
        merged = []
        for a, b in zip(parts[:half], parts[half:]):
            hi, err = two_sum(a[0], b[0])
            merged.append((hi, a[1] + b[1] + err))
        parts = merged
    hi, lo = fold(*parts[0], 0, (1, 2))
    lane = lane_ids((1, LANES))
    last, err = two_sum(hi[3:4], hi[7:8])
    err = err + (lo[3:4] + lo[7:8])
    first = hi[3:4]
    second = jnp.where(lane >= HALF, last, hi[7:8])
    low = jnp.where(lane >= HALF, err, lo[7:8])
    low = low + jnp.where(lane == HALF, pltpu.roll(second, LANES - 1, 1), pltpu.roll(second, LANES - 7, 1))
    for n, value in enumerate((first, second, low)):
        spread[LANES * n : LANES * n + LANES, :] = jnp.transpose(jnp.broadcast_to(value, (LANES, LANES)))

    def row(n):
        return spread[place(n) : place(n) + 1, :]

    def moment(n):
        at = LANES + (MOM_LANE + n if n < 7 else HALF)
        return quick_sum(spread[at : at + 1, :], spread[LANES + at : LANES + at + 1, :])

    mix = solve_krylov([moment(n) for n in range(8)])

    def s_s(i, j):
        return row(ROW_GRAM + PAIR_ROW[min(i, j), max(i, j)])

    def y_y(i, j):
        return row(ROW_GRAM + 36 + PAIR_ROW[min(i, j), max(i, j)])

    def s_y(i, j):
        return row(ROW_GRAM + 72 + 8 * i + j)

    pairs = range(HIST)
    theta, rest, inverse = [], [], []
    for i in pairs:
        curv, norm = s_y(i, i), s_s(i, i)
        kept = (1.0 - damp_floor) * norm
        damp = jnp.where(curv >= damp_floor * norm, 1.0, kept / jnp.maximum(norm - curv, kept))
        theta.append(damp)
        rest.append(1.0 - damp)
        inverse.append(1.0 / (damp * curv + (1.0 - damp) * norm))

    def s_bar(i, j):
        return theta[j] * s_y(i, j) + rest[j] * s_s(i, j)

    def bar_bar(i, j):
        return theta[i] * (theta[j] * y_y(i, j) + rest[j] * s_y(j, i)) + rest[i] * s_bar(i, j)

    last = HIST - 1
    scaling = s_bar(last, last) / bar_bar(last, last)

    def energy(n):
        value = row(ROW_BASE + 16 + n)
        for j in range(4):
            value = value + mix[j] * row(ROW_W + 17 * j + n)
        return value

    chem = energy(16) / row(ROW_BASE + 33)

    def gradient(n):
        return energy(n) - chem * row(ROW_BASE + n)

    s_grad = [gradient(i) for i in pairs]
    bar_grad = [theta[i] * gradient(HIST + i) + rest[i] * s_grad[i] for i in pairs]

    first = [None] * HIST
    pending = list(s_grad)
    for j in reversed(pairs):
        first[j] = inverse[j] * pending[j]
        for i in range(j):
            pending[i] = pending[i] - first[j] * s_bar(i, j)
    pending = list(bar_grad)
    for j in pairs:
        for i in pairs:
            pending[i] = pending[i] - first[j] * bar_bar(i, j)
    pending = [scaling * value for value in pending]
    step_mix, change_mix = [], []
    for j in pairs:
        net = first[j] - inverse[j] * pending[j]
        for i in range(j + 1, HIST):
            pending[i] = pending[i] + net * s_bar(j, i)
        change_mix.append((-step_length) * (-scaling * first[j] * theta[j]))
        step_mix.append((-step_length) * (net - scaling * first[j] * rest[j]))

    wide = lambda value: jnp.broadcast_to(value, (8, LANES))
    mix = [wide(value) for value in mix]
    chem, gain = wide(chem), wide((-step_length) * scaling)
    step_mix = [wide(value) for value in step_mix]
    change_mix = [wide(value) for value in change_mix]
    basis = (v0, v1, v2, v3)

    def leave(i):
        return [
            pltpu.make_async_copy(here.at[i], out.at[i], sems.at[n, i])
            for n, (here, out) in enumerate(((density_here, new_density), (hartree_here, new_hartree)))
        ]

    for i in range(REACH):
        for b in range(8):
            at = pl.ds(8 * b, 8)
            rho = both[REACH + i, at, :]
            lift = mix[0] * v0[i, at, :]
            for j in range(1, 4):
                lift = lift + mix[j] * basis[j][i, at, :]
            hartree_here[i, at, :] = both[i, at, :] + lift
            slope = grad[i, at, :] + 2.0 * rho * lift - chem * rho
            parts = [rho, gain * slope, step_mix[0] * steps[0, i, at, :], change_mix[0] * changes[0, i, at, :]]
            for f in range(1, HIST):
                parts[2] = parts[2] + step_mix[f] * steps[f, i, at, :]
                parts[3] = parts[3] + change_mix[f] * changes[f, i, at, :]
            density_here[i, at, :] = parts[0] + (parts[1] + (parts[2] + parts[3]))
        for copy in leave(i):
            copy.start()
    for i in range(REACH):
        for copy in leave(i):
            copy.wait()


def call(kernel, outs, args, scratch=(), flops=0, in_hbm=(), out_hbm=False):
    args = [pltpu.with_memory_space_constraint(x, pltpu.HBM) if n in in_hbm else x for n, x in enumerate(args)]
    shapes = [jax.ShapeDtypeStruct(shape, jnp.float32) for shape in outs]
    size = sum(4 * math.prod(a.shape) for a in (*args, *shapes))
    return pl.pallas_call(
        kernel,
        out_shape=shapes,
        in_specs=[pl.BlockSpec(memory_space=pltpu.HBM if n in in_hbm else pltpu.VMEM) for n in range(len(args))],
        out_specs=[pl.BlockSpec(memory_space=pltpu.HBM if out_hbm else pltpu.VMEM)] * len(outs),
        scratch_shapes=[pltpu.VMEM(s, jnp.float32) if isinstance(s, tuple) else s for s in scratch],
        cost_estimate=pl.CostEstimate(flops=flops, bytes_accessed=size, transcendentals=0),
        compiler_params=pltpu.CompilerParams(vmem_limit_bytes=VMEM_LIMIT),
    )(*args)


def ring(axis, step):
    size = lax.axis_size(axis)
    return [(i, (i + step) % size) for i in range(size)]


def swap(axis, odd_up):
    size = lax.axis_size(axis)
    return [(i, (i + (1 if i % 2 == odd_up else -1)) % size) for i in range(size)]


def after(values, *earlier):
    return lax.optimization_barrier((tuple(values), earlier))[0]


def x_halo(block):
    far = lax.ppermute(block, "blk", swap("blk", 1))
    return (lax.ppermute(block, "blk", swap("blk", 0)), far)


def z_halo(face_a, face_b):
    return (lax.ppermute(face_a, "gz", swap("gz", 0)), lax.ppermute(face_b, "gz", swap("gz", 1)))


def on_device(sqrt_density, ion_charge, ion_potential, hartree_prev, hist_steps, hist_changes):
    block = sqrt_density.shape
    ext = (block[0], block[1] + 16, block[2])
    face = (24, LANES)
    cells = math.prod(block)
    cells = math.prod(block)
    work = 300 * cells
    inputs = (hartree_prev, sqrt_density, ion_charge)
    halo = x_halo(hartree_prev)
    both, charge, *faces = call(
        launch_kernel,
        [(2 * REACH, *block[1:]), block, (48, LANES), (48, LANES)],
        inputs,
        [pltpu.SemaphoreType.DMA((3,))],
        in_hbm=(0, 1, 2),
    )
    ends = z_halo(*faces)
    density_ends = ends
    half = (REACH, block[1] // 2, LANES)

    def advance(gain, inner, halo, ends, last=False):
        (mid,) = call(functools.partial(z_kernel, gain), [block], [inner, *ends], flops=work)
        return call(
            functools.partial(last_x_kernel if last else x_kernel, gain),
            [block, half, half] if last else [block],
            [mid, *halo],
            flops=work,
        )

    def exchange(block_now):
        halo = x_halo(block_now)
        return halo, z_halo(*call(pack_kernel, [face, face], [block_now], flops=work))

    stored = hist_steps.shape
    inner, *history = call(
        side_one,
        [block, stored, stored],
        [both, charge, hist_steps, hist_changes],
        [ext, pltpu.SemaphoreType.DMA((2 * FETCHES,))],
        work,
        in_hbm=(2, 3),
    )
    (v0,) = advance(1.0, inner, halo, ends)
    halo, ends = exchange(v0)
    density_halo = x_halo(after((sqrt_density,), v0)[0])
    inner, r2, m2 = call(side_two, [block, (40, LANES), (8, LANES)], [v0, both, *history], [ext], work)
    (v1,) = advance(-1.0 / SHIFT, inner, halo, ends)
    halo, ends = exchange(v1)
    inner, grad, r3, m3 = call(
        side_three,
        [block, block, (56, LANES), (8, LANES)],
        [v0, v1, both, *density_halo, *density_ends, ion_potential, *history],
        [ext],
        work,
    )
    (v2,) = advance(-2.0 / SHIFT, inner, halo, ends)
    halo, ends = exchange(v2)
    inner, r4, m4 = call(
        side_four, [block, (112, LANES), (8, LANES)], [v1, v2, both, grad, *history], [ext], work
    )
    v3, to_near, to_far = advance(-2.0 / SHIFT, inner, halo, ends, last=True)
    far = lax.ppermute(to_far, "blk", swap("blk", 1))
    near = lax.ppermute(to_near, "blk", swap("blk", 0))
    (upper,) = call(pack_upper_kernel, [face], [v3], flops=work)
    z_left = lax.ppermute(upper, "gz", ring("gz", 1))
    kept, given, inner = call(
        side_five,
        [(1, LANES), (1, LANES), (8, LANES)],
        [v2, v3, both, *history, r2, r3, r4, m2, m3, m4],
        [(2 * LANES, LANES), (8, LANES), ext],
        work,
    )
    taken = lax.ppermute(given, "blk", swap("blk", 0))
    row, part = call(
        couple_kernel, [(1, LANES), (8, LANES)], [v3, z_left, inner, kept, taken], flops=work
    )
    devices = lax.axis_size("blk") * lax.axis_size("gz")
    (outgoing,) = call(send_kernel, [(devices, LANES)], [v3, far, near, part, row], flops=work)
    received = lax.all_to_all(outgoing.reshape(devices, 1, LANES), ("blk", "gz"), 0, 0, tiled=True)
    return tuple(
        call(
            final_kernel,
            [block, block],
            [received.reshape(devices, LANES), both, grad, v0, v1, v2, v3, *history],
            [(3 * LANES, LANES), block, block, pltpu.SemaphoreType.DMA((2, REACH))],
            work,
            out_hbm=True,
        )
    )


def solution(mesh):
    placed = (
        P("blk", None, "gz"),
        P("blk", None, "gz"),
        P("blk", None, "gz"),
        P("blk", None, "gz"),
        P(None, "blk", None, "gz"),
        P(None, "blk", None, "gz"),
    )
    return jax.shard_map(
        on_device,
        mesh=mesh,
        in_specs=placed,
        out_specs=(P("blk", None, "gz"), P("blk", None, "gz")),
        check_vma=False,
    )
```

```python
import functools
import math

import jax
import jax.numpy as jnp
from jax import lax
from jax.experimental import pallas as pl
from jax.experimental.pallas import tpu as pltpu
from jax.sharding import PartitionSpec as P

center = -5369.0 / 1800.0
coeffs = (12.0 / 7.0, -15.0 / 56.0, 10.0 / 189.0, -1.0 / 112.0, 2.0 / 825.0, -1.0 / 4752.0)
screen = 0.0025
spacing = 0.28
source_scale = 4.0 * math.pi * spacing * spacing
tf_scale = 5.0 / 3.0 * 2.871234
step_length = 0.01
damp_floor = 0.2

SHIFT = 2.0
HIST = 8
REACH = 6
LANES = 128
VMEM_LIMIT = 24 * 1024 * 1024

ROW_GRAM = 0
ROW_BASE = 136
ROW_W = 170
ROW_MOM = 238
HALF = 126


def place(n):
    return n if n < HALF else n + LANES - HALF


MOM_LANE = place(ROW_MOM) - LANES
PAIRS = tuple((i, j) for i in range(HIST) for j in range(i, HIST))
PAIR_ROW = {pair: row for row, pair in enumerate(PAIRS)}


def two_sum(a, b):
    s = a + b
    bb = s - a
    return s, (a - (s - bb)) + (b - bb)


def quick_sum(a, b):
    s = a + b
    return s, b - (s - a)


def split(a):
    t = 4097.0 * a
    hi = t - (t - a)
    return hi, a - hi


def two_prod(a, b):
    p = a * b
    ah, al = split(a)
    bh, bl = split(b)
    return p, ((ah * bh - p) + ah * bl + al * bh) + al * bl


def df_add(a, b):
    s, e = two_sum(a[0], b[0])
    return quick_sum(s, e + (a[1] + b[1]))


def df_neg(a):
    return (-a[0], -a[1])


def df_sub(a, b):
    return df_add(a, df_neg(b))


def df_scale(a, factor):
    return (a[0] * factor, a[1] * factor)


def df_mul(a, b):
    p, e = two_prod(a[0], b[0])
    return quick_sum(p, e + (a[0] * b[1] + a[1] * b[0]))


def df_over(a, b, inverse):
    q = a[0] * inverse
    p, e = two_prod(q, b[0])
    rest = ((a[0] - p) - e) + (a[1] - q * b[1])
    return quick_sum(q, rest * inverse)


def lane_ids(shape):
    return lax.broadcasted_iota(jnp.int32, shape, len(shape) - 1)


def inner_plane(i, own, ext):
    values = own[i]
    rows = values.shape[0]
    lane = lane_ids((rows, LANES))
    total = (3.0 * center) * values
    for k, weight in enumerate(coeffs, 1):
        pair = ext[i, 8 + k : 8 + k + rows, :] + ext[i, 8 - k : 8 - k + rows, :]
        if i + k < REACH:
            pair = pair + own[i + k]
        if i - k >= 0:
            pair = pair + own[i - k]
        up = pltpu.roll(jnp.where(lane < k, 0.0, values), LANES - k, 1)
        down = pltpu.roll(jnp.where(lane >= LANES - k, 0.0, values), k, 1)
        total = total + weight * (pair + (up + down))
    return total, values


def edge_faces(z_left, z_right):
    lane = lane_ids((24, LANES)) % 8
    lower = jnp.zeros((24, LANES), jnp.float32)
    upper = jnp.zeros((24, LANES), jnp.float32)
    for k, weight in enumerate(coeffs, 1):
        lower = lower + jnp.where(lane < k, weight * pltpu.roll(z_left, LANES - 8 + k, 1), 0.0)
        if z_right is not None:
            upper = upper + jnp.where(lane >= 8 - k, weight * pltpu.roll(z_right, 8 - k, 1), 0.0)
    return lower, upper


def side_plane(i, block, below, rows=slice(None)):
    total = None
    for k, weight in enumerate(coeffs, 1):
        layer = i - k + REACH if below else i + k - REACH
        if 0 <= layer < REACH:
            term = weight * block[layer, rows, :]
            total = term if total is None else total + term
    return total


def z_plane(i, faces, tiles=8):
    lane = lane_ids((8, LANES))
    lower, upper = (face[8 * (i // 2) : 8 * (i // 2) + 8] for face in faces)
    out = []
    for b in range(tiles):
        j = 8 * (i % 2) + b
        tile = jnp.where(lane < 8, pltpu.roll(lower, (LANES - 8 * j) % LANES, 1), 0.0)
        tile = jnp.where(lane >= LANES - 8, pltpu.roll(upper, (2 * LANES - 8 - 8 * j) % LANES, 1), tile)
        out.append(tile)
    return jnp.concatenate(out, axis=0)


def fill_ext(own, ext):
    rows = own.shape[1]
    ext[:, 8 : 8 + rows, :] = own[...]
    ext[:, 0:8, :] = own[:, rows - 8 : rows, :]
    ext[:, 8 + rows : 16 + rows, :] = own[:, 0:8, :]


def pack_faces(src, layers):
    lane = lane_ids((8, LANES))
    firsts, lasts = [], []
    for m in range(3):
        first = jnp.zeros((8, LANES), jnp.float32)
        last = jnp.zeros((8, LANES), jnp.float32)
        for j in range(16):
            n = 16 * m + j
            tile = src[layers + n // 8, 8 * (n % 8) : 8 * (n % 8) + 8, :]
            here = (lane >= 8 * j) & (lane < 8 * j + 8)
            first = jnp.where(here, pltpu.roll(tile, 8 * j, 1) if j else tile, first)
            last = jnp.where(here, pltpu.roll(tile, (8 * j + 8) % LANES, 1) if j < 15 else tile, last)
        firsts.append(first)
        lasts.append(last)
    return jnp.concatenate(firsts, axis=0), jnp.concatenate(lasts, axis=0)


def is_odd(axis):
    return lax.rem(lax.axis_index(axis), 2) == 1


def by_partner(lower, upper):
    odd = is_odd("gz")
    return jnp.where(odd, lower, upper), jnp.where(odd, upper, lower)


def by_side(first, second):
    odd = is_odd("gz")
    return jnp.where(odd, first, second), jnp.where(odd, second, first)


def with_sides(body):
    odd = is_odd("blk")

    @pl.when(odd)
    def _():
        body(True, False)

    @pl.when(jnp.logical_not(odd))
    def _():
        body(False, True)


def fold(hi, lo, axis, steps):
    for step in steps:
        hi, err = two_sum(hi, pltpu.roll(hi, step, axis))
        lo = lo + pltpu.roll(lo, step, axis) + err
    return hi, lo


def fold_rows(acc):
    hi, lo = fold(*acc, 0, (4, 2, 1))
    return hi[0:1], lo[0:1]


def fold_lanes(hi, lo):
    return quick_sum(*fold(hi, lo, 1, (64, 32, 16, 8, 4, 2, 1)))


def add_tile(acc, product):
    hi, err = two_sum(acc[0], product)
    return hi, acc[1] + err


def tile_of(ref, i, b):
    return ref[i, 8 * b : 8 * b + 8, :]


def store_moments(pairs, moments):
    zero = jnp.zeros((8, LANES), jnp.float32)

    def body(i, accs):
        for b in range(8):
            accs = tuple(
                add_tile(acc, tile_of(a, i, b) * tile_of(c, i, b)) for acc, (a, c) in zip(accs, pairs)
            )
        return accs

    accs = lax.fori_loop(0, REACH, body, tuple((zero, zero) for _ in pairs))
    for n, acc in enumerate(accs):
        moments[2 * n : 2 * n + 1, :], moments[2 * n + 1 : 2 * n + 2, :] = fold_rows(acc)


def collapse(acc):
    return jnp.sum(acc, axis=0, keepdims=True)


def launch_kernel(hartree, density, charge, both, charge_here, face_a, face_b, sems):
    places = (both.at[pl.ds(0, REACH)], both.at[pl.ds(REACH, REACH)], charge_here)
    copies = [
        pltpu.make_async_copy(src, dst, sems.at[n])
        for n, (src, dst) in enumerate(zip((hartree, density, charge), places))
    ]
    for copy in copies:
        copy.start()
    for n in range(2):
        copies[n].wait()
        rows = slice(24 * n, 24 * n + 24)
        face_a[rows, :], face_b[rows, :] = by_partner(*pack_faces(both, REACH * n))
    copies[2].wait()


def inner_residual(both, charge, out, ext):
    hartree = both.at[pl.ds(0, REACH)]
    fill_ext(hartree, ext)
    for i in range(REACH):
        lap, values = inner_plane(i, hartree, ext)
        rho = both[REACH + i]
        out[i] = source_scale * (rho * rho - charge[i]) - (screen * values - lap)


def inner_basis(own, prior, out, ext):
    fill_ext(own, ext)
    for i in range(REACH):
        lap, values = inner_plane(i, own, ext)
        moved = (screen / SHIFT - 1.0) * values - (1.0 / SHIFT) * lap
        out[i] = moved if prior is None else 2.0 * moved - prior[i]


def z_kernel(gain, inner, z_first, z_second, out):
    faces = edge_faces(*by_side(z_first[0:24, :], z_second[0:24, :]))
    for i in range(REACH):
        out[i] = inner[i] + gain * z_plane(i, faces)


def x_kernel(gain, inner, near, far, out):
    def body(near_below, far_below):
        for i in range(REACH):
            out[i] = inner[i] + gain * (side_plane(i, near, near_below) + side_plane(i, far, far_below))

    with_sides(body)


def last_x_kernel(gain, inner, near, far, out, to_near, to_far):
    half = out.shape[1] // 2

    def body(near_below, far_below):
        for i in range(REACH):
            plane = inner[i] + gain * (side_plane(i, near, near_below) + side_plane(i, far, far_below))
            out[i] = plane
            for ref, below in ((to_near, near_below), (to_far, far_below)):
                ref[i] = plane[:half] if below else plane[half:]

    with_sides(body)


def pack_kernel(block, face_a, face_b):
    face_a[...], face_b[...] = by_partner(*pack_faces(block, 0))


def pack_upper_kernel(block, face):
    face[...] = pack_faces(block, 0)[1]


def store(rows, base, values):
    for n, value in enumerate(values):
        rows[base + n : base + n + 1, :] = value


def gram_dots(left, right, pairs):
    zero = jnp.zeros((8, LANES), jnp.float32)

    def body(i, accs):
        for b in range(8):
            at = pl.ds(8 * b, 8)
            l_tiles = {p: left[p, i, at, :] for p in sorted({p for p, _ in pairs})}
            if left is right:
                r_tiles = l_tiles
            else:
                r_tiles = {q: right[q, i, at, :] for q in sorted({q for _, q in pairs})}
            accs = tuple(acc + l_tiles[p] * r_tiles[q] for acc, (p, q) in zip(accs, pairs))
        return accs

    accs = lax.fori_loop(0, REACH, body, tuple(zero for _ in pairs))
    return [collapse(acc) for acc in accs]


CROSS_PAIRS = tuple((i, j) for i in range(HIST) for j in range(HIST))


def field_dots(groups, others, plain=()):
    zero = jnp.zeros((8, LANES), jnp.float32)
    fields = [(group, f) for group in groups for f in range(HIST)]
    count = len(fields)

    def body(i, accs):
        accs = list(accs)
        for b in range(8):
            at = pl.ds(8 * b, 8)
            tiles = [other(i, b) for other in others]
            for f, (group, which) in enumerate(fields):
                field = group[which, i, at, :]
                for o, tile in enumerate(tiles):
                    accs[o * count + f] = accs[o * count + f] + field * tile
            for n, (one, two) in enumerate(plain, len(others) * count):
                accs[n] = accs[n] + one(i, b) * two(i, b)
        return tuple(accs)

    total = count * len(others) + len(plain)
    return [collapse(acc) for acc in lax.fori_loop(0, REACH, body, (zero,) * total)]


def base_gradient(both, near, far, z_first, z_second, potential, grad, ext):
    hartree = both.at[pl.ds(0, REACH)]
    density = both.at[pl.ds(REACH, REACH)]
    fill_ext(density, ext)
    faces = edge_faces(*by_side(z_first[24:48, :], z_second[24:48, :]))

    def body(near_below, far_below):
        for i in range(REACH):
            grad[i] = side_plane(i, near, near_below) + side_plane(i, far, far_below) + z_plane(i, faces)

    with_sides(body)
    for i in range(REACH):
        lap, rho = inner_plane(i, density, ext)
        power = jnp.exp(jnp.log(rho) * (4.0 / 3.0))
        grad[i] = 2.0 * rho * (hartree[i] + potential[i] + tf_scale * power) - (lap + grad[i]) * (
            1.0 / (spacing * spacing)
        )


def density_tile(both):
    return lambda i, b: tile_of(both, REACH + i, b)


def lifted_tile(both, vector):
    return lambda i, b: 2.0 * tile_of(both, REACH + i, b) * tile_of(vector, i, b)


FETCHES = 4


def side_one(both, charge, steps, changes, inner, steps_here, changes_here, rows, ext, sems):
    each = HIST // FETCHES
    copies = [
        pltpu.make_async_copy(src.at[pl.ds(each * n, each)], dst.at[pl.ds(each * n, each)], sems.at[FETCHES * m + n])
        for m, (src, dst) in enumerate(((steps, steps_here), (changes, changes_here)))
        for n in range(FETCHES)
    ]
    for copy in copies:
        copy.start()
    inner_residual(both, charge, inner, ext)
    for copy in copies[:FETCHES]:
        copy.wait()
    store(rows, 0, gram_dots(steps_here, steps_here, PAIRS))
    store(rows, 36, field_dots((steps_here,), [density_tile(both)]))
    for copy in copies[FETCHES:]:
        copy.wait()
    store(rows, 44, gram_dots(steps_here, changes_here, CROSS_PAIRS[:32]))


def side_two(vector, both, steps, changes, inner, rows, moments, ext):
    inner_basis(vector, None, inner, ext)
    lifted, rho = lifted_tile(both, vector), density_tile(both)
    by_step = field_dots((steps,), [lifted], [(rho, lifted)])
    by_change = field_dots((changes,), [lifted, rho])
    store(rows, 0, by_step[:8] + by_change[:8] + by_step[8:] + by_change[8:])
    store_moments([(vector, vector)], moments)


def side_three(prior, vector, both, near, far, z_first, z_second, potential, steps, changes, *outs):
    inner, grad, rows, moments, ext = outs
    inner_basis(vector, prior, inner, ext)
    lifted, rho = lifted_tile(both, vector), density_tile(both)
    store(rows, 0, field_dots((steps, changes), [lifted], [(rho, lifted)]))
    store_moments([(prior, vector), (vector, vector)], moments)
    base_gradient(both, near, far, z_first, z_second, potential, grad, ext)


def side_four(prior, vector, both, grad, steps, changes, inner, rows, moments, ext):
    inner_basis(vector, prior, inner, ext)
    lifted, rho = lifted_tile(both, vector), density_tile(both)
    slope = lambda i, b: tile_of(grad, i, b)
    values = field_dots((steps, changes), [lifted, slope], [(rho, lifted), (rho, slope), (rho, rho)])
    store(rows, 0, values[:16] + values[32:33] + values[16:32] + values[33:])
    store(rows, 35, gram_dots(changes, changes, PAIRS))
    store(rows, 71, gram_dots(steps, changes, CROSS_PAIRS[32:]))
    store_moments([(prior, vector), (vector, vector)], moments)


def side_five(prior, vector, both, steps, changes, r1, r2, r3, r4, m2, m3, m4, kept, given, table, m5):
    lifted, rho = lifted_tile(both, vector), density_tile(both)
    own = field_dots((steps, changes), [lifted], [(rho, lifted)])
    store_moments([(prior, vector), (vector, vector)], m5)
    table[...] = jnp.zeros_like(table)

    def put(base, ref, start, count):
        before = max(0, min(count, HALF - base))
        if before:
            table[base : base + before, :] = ref[start : start + before, :]
        if before < count:
            at = place(base + before)
            table[at : at + count - before, :] = ref[start + before : start + count, :]

    put(ROW_GRAM, r1, 0, 36)
    put(ROW_GRAM + 36, r4, 35, 36)
    put(ROW_GRAM + 72, r1, 44, 32)
    put(ROW_GRAM + 104, r4, 71, 32)
    put(ROW_BASE, r1, 36, 8)
    put(ROW_BASE + 8, r2, 17, 8)
    put(ROW_BASE + 16, r4, 17, 18)
    for n, rows in enumerate((r2, r3, r4)):
        put(ROW_W + 17 * n, rows, 0, 17)
    store(table, place(ROW_W + 51), own)

    order = [(m2, 0), (m3, 0), (m3, 1), (m4, 0), (m4, 1), (m5, 0), (m5, 1)]
    zero = jnp.zeros((1, LANES), jnp.float32)
    parts = [
        jnp.concatenate([ref[2 * which + low : 2 * which + low + 1, :] for ref, which in order] + [zero], axis=0)
        for low in range(2)
    ]
    hi, lo = fold_lanes(*parts)
    lane = lane_ids((1, LANES))
    first = jnp.sum(jnp.transpose(table[0:LANES, :]), axis=0, keepdims=True)
    second = jnp.sum(jnp.transpose(table[LANES : 2 * LANES, :]), axis=0, keepdims=True)
    for n in range(7):
        second = jnp.where(lane == MOM_LANE + n, hi[n : n + 1], second)
        second = jnp.where(lane == MOM_LANE + 7 + n, lo[n : n + 1], second)
    odd = is_odd("blk")
    kept[...] = jnp.where(odd, second, first)
    given[...] = jnp.where(odd, first, second)


def inner_moment_kernel(vector, inner, ext):
    fill_ext(vector, ext)
    zero = jnp.zeros((8, LANES), jnp.float32)
    accs = [(zero, zero) for _ in range(2)]
    for i in range(REACH):
        lap, values = inner_plane(i, vector, ext)
        product = values * ((screen / SHIFT - 1.0) * values - (1.0 / SHIFT) * lap)
        for b in range(8):
            accs[b % 2] = add_tile(accs[b % 2], product[8 * b : 8 * b + 8])
    hi, err = two_sum(accs[0][0], accs[1][0])
    inner[0:1, :], inner[1:2, :] = fold_rows((hi, accs[0][1] + accs[1][1] + err))


def couple(own, block, below, acc):
    half = own.shape[1] // 2
    for i in range(REACH):
        product = own[i, half:, :] * side_plane(i, block, True) if below else own[i, :half, :] * side_plane(i, block, False)
        for b in range(half // 8):
            acc = add_tile(acc, product[8 * b : 8 * b + 8])
    return acc


def couple_kernel(own, z_left, inner, kept, taken, row, part):
    zero = jnp.zeros((8, LANES), jnp.float32)
    faces = edge_faces(z_left[...], None)
    acc = (zero, zero)
    for i in range(REACH):
        product = own[i] * z_plane(i, faces)
        for b in range(8):
            acc = add_tile(acc, product[8 * b : 8 * b + 8])
    sides = df_scale(fold_rows(acc), -2.0 / SHIFT)
    part[0:1, :], part[1:2, :] = df_add(sides, (inner[0:1, :], inner[1:2, :]))
    lane = lane_ids((1, LANES))
    total, err = two_sum(kept[...], taken[...])
    low_lane = (lane >= MOM_LANE + 7) & (lane < MOM_LANE + 14) & is_odd("blk")
    row[...] = jnp.where(low_lane, total + pltpu.roll(err, 7, 1), total)


def send_kernel(own, far, near, part, row, out):
    zero = jnp.zeros((8, LANES), jnp.float32)

    def body(near_below, far_below):
        acc = couple(own, far, far_below, couple(own, near, near_below, (zero, zero)))
        hi, lo = fold_lanes(*df_add(df_scale(fold_rows(acc), -2.0 / SHIFT), (part[0:1, :], part[1:2, :])))
        lane = lane_ids((1, LANES))
        value = jnp.where(lane == HALF, hi, jnp.where(lane == HALF + 1, lo, row[...]))
        out[...] = jnp.broadcast_to(value, out.shape)

    with_sides(body)


def solve_krylov(moment):
    n00, n01, n11, n12, n22, n23, n33, n34 = moment
    nu = [n00, n01]
    nu.append(df_sub(df_scale(n11, 2.0), n00))
    nu.append(df_sub(df_scale(n12, 2.0), n01))
    nu.append(df_sub(df_scale(n22, 2.0), n00))
    nu.append(df_sub(df_scale(n23, 2.0), n01))
    nu.append(df_sub(df_scale(n33, 2.0), n00))

    def gram(i, j):
        if i == j == 0:
            return n00
        return df_scale(df_add(nu[i + j], nu[abs(i - j)]), 0.5)

    def moved(i, j):
        if i == 3 and j == 3:
            return n34
        if j == 0:
            return gram(i, 1)
        return df_scale(df_add(gram(i, j + 1), gram(i, j - 1)), 0.5)

    mat = {(i, j): df_add(moved(i, j), gram(i, j)) for i in range(4) for j in range(i + 1)}
    rhs = [df_scale(gram(i, 0), 1.0 / SHIFT) for i in range(4)]
    low, inverse = {}, []
    for k in range(4):
        inverse.append(1.0 / mat[k, k][0])
        for i in range(k + 1, 4):
            low[i, k] = df_over(mat[i, k], mat[k, k], inverse[k])
        for i in range(k + 1, 4):
            for j in range(k + 1, i + 1):
                mat[i, j] = df_sub(mat[i, j], df_mul(low[i, k], mat[j, k]))
            rhs[i] = df_sub(rhs[i], df_mul(low[i, k], rhs[k]))
    sol = [None] * 4
    for k in reversed(range(4)):
        value = df_over(rhs[k], mat[k, k], inverse[k])
        for i in range(k + 1, 4):
            value = df_sub(value, df_mul(low[i, k], sol[i]))
        sol[k] = value
    return [hi + lo for hi, lo in sol]


def final_kernel(received, both, grad, v0, v1, v2, v3, steps, changes, new_density, new_hartree, spread, density_here, hartree_here, sems):
    parts = [(received[8 * n : 8 * n + 8, :], jnp.zeros((8, LANES), jnp.float32)) for n in range(4)]
    for n in range(4, received.shape[0] // 8):
        parts[n % 4] = add_tile(parts[n % 4], received[8 * n : 8 * n + 8, :])
    while len(parts) > 1:
        half = len(parts) // 2
        merged = []
        for a, b in zip(parts[:half], parts[half:]):
            hi, err = two_sum(a[0], b[0])
            merged.append((hi, a[1] + b[1] + err))
        parts = merged
    hi, lo = fold(*parts[0], 0, (1, 2))
    lane = lane_ids((1, LANES))
    last, err = two_sum(hi[3:4], hi[7:8])
    err = err + (lo[3:4] + lo[7:8])
    first = hi[3:4]
    second = jnp.where(lane >= HALF, last, hi[7:8])
    low = jnp.where(lane >= HALF, err, lo[7:8])
    low = low + jnp.where(lane == HALF, pltpu.roll(second, LANES - 1, 1), pltpu.roll(second, LANES - 7, 1))
    for n, value in enumerate((first, second, low)):
        spread[LANES * n : LANES * n + LANES, :] = jnp.transpose(jnp.broadcast_to(value, (LANES, LANES)))

    def row(n):
        return spread[place(n) : place(n) + 1, :]

    def moment(n):
        at = LANES + (MOM_LANE + n if n < 7 else HALF)
        return quick_sum(spread[at : at + 1, :], spread[LANES + at : LANES + at + 1, :])

    mix = solve_krylov([moment(n) for n in range(8)])

    def s_s(i, j):
        return row(ROW_GRAM + PAIR_ROW[min(i, j), max(i, j)])

    def y_y(i, j):
        return row(ROW_GRAM + 36 + PAIR_ROW[min(i, j), max(i, j)])

    def s_y(i, j):
        return row(ROW_GRAM + 72 + 8 * i + j)

    pairs = range(HIST)
    theta, rest, inverse = [], [], []
    for i in pairs:
        curv, norm = s_y(i, i), s_s(i, i)
        kept = (1.0 - damp_floor) * norm
        damp = jnp.where(curv >= damp_floor * norm, 1.0, kept / jnp.maximum(norm - curv, kept))
        theta.append(damp)
        rest.append(1.0 - damp)
        inverse.append(1.0 / (damp * curv + (1.0 - damp) * norm))

    def s_bar(i, j):
        return theta[j] * s_y(i, j) + rest[j] * s_s(i, j)

    def bar_bar(i, j):
        return theta[i] * (theta[j] * y_y(i, j) + rest[j] * s_y(j, i)) + rest[i] * s_bar(i, j)

    last = HIST - 1
    scaling = s_bar(last, last) / bar_bar(last, last)

    def energy(n):
        value = row(ROW_BASE + 16 + n)
        for j in range(4):
            value = value + mix[j] * row(ROW_W + 17 * j + n)
        return value

    chem = energy(16) / row(ROW_BASE + 33)

    def gradient(n):
        return energy(n) - chem * row(ROW_BASE + n)

    s_grad = [gradient(i) for i in pairs]
    bar_grad = [theta[i] * gradient(HIST + i) + rest[i] * s_grad[i] for i in pairs]

    first = [None] * HIST
    pending = list(s_grad)
    for j in reversed(pairs):
        first[j] = inverse[j] * pending[j]
        for i in range(j):
            pending[i] = pending[i] - first[j] * s_bar(i, j)
    pending = list(bar_grad)
    for j in pairs:
        for i in pairs:
            pending[i] = pending[i] - first[j] * bar_bar(i, j)
    pending = [scaling * value for value in pending]
    step_mix, change_mix = [], []
    for j in pairs:
        net = first[j] - inverse[j] * pending[j]
        for i in range(j + 1, HIST):
            pending[i] = pending[i] + net * s_bar(j, i)
        change_mix.append((-step_length) * (-scaling * first[j] * theta[j]))
        step_mix.append((-step_length) * (net - scaling * first[j] * rest[j]))

    wide = lambda value: jnp.broadcast_to(value, (8, LANES))
    mix = [wide(value) for value in mix]
    chem, gain = wide(chem), wide((-step_length) * scaling)
    step_mix = [wide(value) for value in step_mix]
    change_mix = [wide(value) for value in change_mix]
    basis = (v0, v1, v2, v3)

    def leave(i):
        return [
            pltpu.make_async_copy(here.at[i], out.at[i], sems.at[n, i])
            for n, (here, out) in enumerate(((density_here, new_density), (hartree_here, new_hartree)))
        ]

    for i in range(REACH):
        for b in range(8):
            at = pl.ds(8 * b, 8)
            rho = both[REACH + i, at, :]
            lift = mix[0] * v0[i, at, :]
            for j in range(1, 4):
                lift = lift + mix[j] * basis[j][i, at, :]
            hartree_here[i, at, :] = both[i, at, :] + lift
            slope = grad[i, at, :] + 2.0 * rho * lift - chem * rho
            parts = [rho, gain * slope, step_mix[0] * steps[0, i, at, :], change_mix[0] * changes[0, i, at, :]]
            for f in range(1, HIST):
                parts[2] = parts[2] + step_mix[f] * steps[f, i, at, :]
                parts[3] = parts[3] + change_mix[f] * changes[f, i, at, :]
            density_here[i, at, :] = parts[0] + (parts[1] + (parts[2] + parts[3]))
        for copy in leave(i):
            copy.start()
    for i in range(REACH):
        for copy in leave(i):
            copy.wait()


def call(kernel, outs, args, scratch=(), flops=0, in_hbm=(), out_hbm=False):
    args = [pltpu.with_memory_space_constraint(x, pltpu.HBM) if n in in_hbm else x for n, x in enumerate(args)]
    shapes = [jax.ShapeDtypeStruct(shape, jnp.float32) for shape in outs]
    size = sum(4 * math.prod(a.shape) for a in (*args, *shapes))
    return pl.pallas_call(
        kernel,
        out_shape=shapes,
        in_specs=[pl.BlockSpec(memory_space=pltpu.HBM if n in in_hbm else pltpu.VMEM) for n in range(len(args))],
        out_specs=[pl.BlockSpec(memory_space=pltpu.HBM if out_hbm else pltpu.VMEM)] * len(outs),
        scratch_shapes=[pltpu.VMEM(s, jnp.float32) if isinstance(s, tuple) else s for s in scratch],
        cost_estimate=pl.CostEstimate(flops=flops, bytes_accessed=size, transcendentals=0),
        compiler_params=pltpu.CompilerParams(vmem_limit_bytes=VMEM_LIMIT),
    )(*args)


def ring(axis, step):
    size = lax.axis_size(axis)
    return [(i, (i + step) % size) for i in range(size)]


def swap(axis, odd_up):
    size = lax.axis_size(axis)
    return [(i, (i + (1 if i % 2 == odd_up else -1)) % size) for i in range(size)]


def after(values, *earlier):
    return lax.optimization_barrier((tuple(values), earlier))[0]


def x_halo(block):
    far = lax.ppermute(block, "blk", swap("blk", 1))
    return (lax.ppermute(block, "blk", swap("blk", 0)), far)


def z_halo(face_a, face_b):
    return (lax.ppermute(face_a, "gz", swap("gz", 0)), lax.ppermute(face_b, "gz", swap("gz", 1)))


def on_device(sqrt_density, ion_charge, ion_potential, hartree_prev, hist_steps, hist_changes):
    block = sqrt_density.shape
    ext = (block[0], block[1] + 16, block[2])
    face = (24, LANES)
    cells = math.prod(block)
    cells = math.prod(block)
    work = 300 * cells
    inputs = (hartree_prev, sqrt_density, ion_charge)
    halo = x_halo(hartree_prev)
    both, charge, *faces = call(
        launch_kernel,
        [(2 * REACH, *block[1:]), block, (48, LANES), (48, LANES)],
        inputs,
        [pltpu.SemaphoreType.DMA((3,))],
        in_hbm=(0, 1, 2),
    )
    ends = z_halo(*faces)
    density_ends = ends
    half = (REACH, block[1] // 2, LANES)

    def advance(gain, inner, halo, ends, last=False):
        (mid,) = call(functools.partial(z_kernel, gain), [block], [inner, *ends], flops=work)
        return call(
            functools.partial(last_x_kernel if last else x_kernel, gain),
            [block, half, half] if last else [block],
            [mid, *halo],
            flops=work,
        )

    def exchange(block_now):
        halo = x_halo(block_now)
        return halo, z_halo(*call(pack_kernel, [face, face], [block_now], flops=work))

    stored = hist_steps.shape
    inner, *history, r1 = call(
        side_one,
        [block, stored, stored, (80, LANES)],
        [both, charge, hist_steps, hist_changes],
        [ext, pltpu.SemaphoreType.DMA((2 * FETCHES,))],
        work,
        in_hbm=(2, 3),
    )
    (v0,) = advance(1.0, inner, halo, ends)
    halo, ends = exchange(v0)
    density_halo = x_halo(after((sqrt_density,), v0)[0])
    inner, r2, m2 = call(side_two, [block, (40, LANES), (8, LANES)], [v0, both, *history], [ext], work)
    (v1,) = advance(-1.0 / SHIFT, inner, halo, ends)
    halo, ends = exchange(v1)
    inner, grad, r3, m3 = call(
        side_three,
        [block, block, (24, LANES), (8, LANES)],
        [v0, v1, both, *density_halo, *density_ends, ion_potential, *history],
        [ext],
        work,
    )
    (v2,) = advance(-2.0 / SHIFT, inner, halo, ends)
    halo, ends = exchange(v2)
    inner, r4, m4 = call(
        side_four, [block, (112, LANES), (8, LANES)], [v1, v2, both, grad, *history], [ext], work
    )
    v3, to_near, to_far = advance(-2.0 / SHIFT, inner, halo, ends, last=True)
    far = lax.ppermute(to_far, "blk", swap("blk", 1))
    near = lax.ppermute(to_near, "blk", swap("blk", 0))
    (upper,) = call(pack_upper_kernel, [face], [v3], flops=work)
    z_left = lax.ppermute(upper, "gz", ring("gz", 1))
    kept, given = call(
        side_five,
        [(1, LANES), (1, LANES)],
        [v2, v3, both, *history, r1, r2, r3, r4, m2, m3, m4],
        [(2 * LANES, LANES), (8, LANES)],
        work,
    )
    taken = lax.ppermute(given, "blk", swap("blk", 0))
    (inner,) = call(inner_moment_kernel, [(8, LANES)], [after((v3,), given)[0]], [ext], work)
    row, part = call(couple_kernel, [(1, LANES), (8, LANES)], [v3, z_left, inner, kept, taken], flops=work)
    devices = lax.axis_size("blk") * lax.axis_size("gz")
    (outgoing,) = call(send_kernel, [(devices, LANES)], [v3, far, near, part, row], flops=work)
    received = lax.all_to_all(outgoing.reshape(devices, 1, LANES), ("blk", "gz"), 0, 0, tiled=True)
    return tuple(
        call(
            final_kernel,
            [block, block],
            [received.reshape(devices, LANES), both, grad, v0, v1, v2, v3, *history],
            [(3 * LANES, LANES), block, block, pltpu.SemaphoreType.DMA((2, REACH))],
            work,
            out_hbm=True,
        )
    )


def solution(mesh):
    placed = (
        P("blk", None, "gz"),
        P("blk", None, "gz"),
        P("blk", None, "gz"),
        P("blk", None, "gz"),
        P(None, "blk", None, "gz"),
        P(None, "blk", None, "gz"),
    )
    return jax.shard_map(
        on_device,
        mesh=mesh,
        in_specs=placed,
        out_specs=(P("blk", None, "gz"), P("blk", None, "gz")),
        check_vma=False,
    )
```

```python
import functools
import math

import jax
import jax.numpy as jnp
from jax import lax
from jax.experimental import pallas as pl
from jax.experimental.pallas import tpu as pltpu
from jax.sharding import PartitionSpec as P

center = -5369.0 / 1800.0
coeffs = (12.0 / 7.0, -15.0 / 56.0, 10.0 / 189.0, -1.0 / 112.0, 2.0 / 825.0, -1.0 / 4752.0)
screen = 0.0025
spacing = 0.28
source_scale = 4.0 * math.pi * spacing * spacing
tf_scale = 5.0 / 3.0 * 2.871234
step_length = 0.01
damp_floor = 0.2

SHIFT = 2.0
HIST = 8
REACH = 6
LANES = 128
VMEM_LIMIT = 24 * 1024 * 1024

ROW_GRAM = 0
ROW_BASE = 136
ROW_W = 170
ROW_MOM = 238
HALF = 126


def place(n):
    return n if n < HALF else n + LANES - HALF


MOM_LANE = place(ROW_MOM) - LANES
PAIRS = tuple((i, j) for i in range(HIST) for j in range(i, HIST))
PAIR_ROW = {pair: row for row, pair in enumerate(PAIRS)}


def two_sum(a, b):
    s = a + b
    bb = s - a
    return s, (a - (s - bb)) + (b - bb)


def quick_sum(a, b):
    s = a + b
    return s, b - (s - a)


def split(a):
    t = 4097.0 * a
    hi = t - (t - a)
    return hi, a - hi


def two_prod(a, b):
    p = a * b
    ah, al = split(a)
    bh, bl = split(b)
    return p, ((ah * bh - p) + ah * bl + al * bh) + al * bl


def df_add(a, b):
    s, e = two_sum(a[0], b[0])
    return quick_sum(s, e + (a[1] + b[1]))


def df_neg(a):
    return (-a[0], -a[1])


def df_sub(a, b):
    return df_add(a, df_neg(b))


def df_scale(a, factor):
    return (a[0] * factor, a[1] * factor)


def df_mul(a, b):
    p, e = two_prod(a[0], b[0])
    return quick_sum(p, e + (a[0] * b[1] + a[1] * b[0]))


def df_over(a, b, inverse):
    q = a[0] * inverse
    p, e = two_prod(q, b[0])
    rest = ((a[0] - p) - e) + (a[1] - q * b[1])
    return quick_sum(q, rest * inverse)


def lane_ids(shape):
    return lax.broadcasted_iota(jnp.int32, shape, len(shape) - 1)


def inner_plane(i, own, ext):
    values = own[i]
    rows = values.shape[0]
    lane = lane_ids((rows, LANES))
    total = (3.0 * center) * values
    for k, weight in enumerate(coeffs, 1):
        pair = ext[i, 8 + k : 8 + k + rows, :] + ext[i, 8 - k : 8 - k + rows, :]
        if i + k < REACH:
            pair = pair + own[i + k]
        if i - k >= 0:
            pair = pair + own[i - k]
        up = pltpu.roll(jnp.where(lane < k, 0.0, values), LANES - k, 1)
        down = pltpu.roll(jnp.where(lane >= LANES - k, 0.0, values), k, 1)
        total = total + weight * (pair + (up + down))
    return total, values


def edge_faces(z_left, z_right):
    lane = lane_ids((24, LANES)) % 8
    lower = jnp.zeros((24, LANES), jnp.float32)
    upper = jnp.zeros((24, LANES), jnp.float32)
    for k, weight in enumerate(coeffs, 1):
        lower = lower + jnp.where(lane < k, weight * pltpu.roll(z_left, LANES - 8 + k, 1), 0.0)
        if z_right is not None:
            upper = upper + jnp.where(lane >= 8 - k, weight * pltpu.roll(z_right, 8 - k, 1), 0.0)
    return lower, upper


def side_plane(i, block, below, rows=slice(None)):
    total = None
    for k, weight in enumerate(coeffs, 1):
        layer = i - k + REACH if below else i + k - REACH
        if 0 <= layer < REACH:
            term = weight * block[layer, rows, :]
            total = term if total is None else total + term
    return total


def z_plane(i, faces, tiles=8):
    lane = lane_ids((8, LANES))
    lower, upper = (face[8 * (i // 2) : 8 * (i // 2) + 8] for face in faces)
    out = []
    for b in range(tiles):
        j = 8 * (i % 2) + b
        tile = jnp.where(lane < 8, pltpu.roll(lower, (LANES - 8 * j) % LANES, 1), 0.0)
        tile = jnp.where(lane >= LANES - 8, pltpu.roll(upper, (2 * LANES - 8 - 8 * j) % LANES, 1), tile)
        out.append(tile)
    return jnp.concatenate(out, axis=0)


def fill_ext(own, ext):
    rows = own.shape[1]
    ext[:, 8 : 8 + rows, :] = own[...]
    ext[:, 0:8, :] = own[:, rows - 8 : rows, :]
    ext[:, 8 + rows : 16 + rows, :] = own[:, 0:8, :]


def pack_faces(src, layers):
    lane = lane_ids((8, LANES))
    firsts, lasts = [], []
    for m in range(3):
        first = jnp.zeros((8, LANES), jnp.float32)
        last = jnp.zeros((8, LANES), jnp.float32)
        for j in range(16):
            n = 16 * m + j
            tile = src[layers + n // 8, 8 * (n % 8) : 8 * (n % 8) + 8, :]
            here = (lane >= 8 * j) & (lane < 8 * j + 8)
            first = jnp.where(here, pltpu.roll(tile, 8 * j, 1) if j else tile, first)
            last = jnp.where(here, pltpu.roll(tile, (8 * j + 8) % LANES, 1) if j < 15 else tile, last)
        firsts.append(first)
        lasts.append(last)
    return jnp.concatenate(firsts, axis=0), jnp.concatenate(lasts, axis=0)


def is_odd(axis):
    return lax.rem(lax.axis_index(axis), 2) == 1


def by_partner(lower, upper):
    odd = is_odd("gz")
    return jnp.where(odd, lower, upper), jnp.where(odd, upper, lower)


def by_side(first, second):
    odd = is_odd("gz")
    return jnp.where(odd, first, second), jnp.where(odd, second, first)


def with_sides(body):
    odd = is_odd("blk")

    @pl.when(odd)
    def _():
        body(True, False)

    @pl.when(jnp.logical_not(odd))
    def _():
        body(False, True)


def fold(hi, lo, axis, steps):
    for step in steps:
        hi, err = two_sum(hi, pltpu.roll(hi, step, axis))
        lo = lo + pltpu.roll(lo, step, axis) + err
    return hi, lo


def fold_rows(acc):
    hi, lo = fold(*acc, 0, (4, 2, 1))
    return hi[0:1], lo[0:1]


def fold_lanes(hi, lo):
    return quick_sum(*fold(hi, lo, 1, (64, 32, 16, 8, 4, 2, 1)))


def add_tile(acc, product):
    hi, err = two_sum(acc[0], product)
    return hi, acc[1] + err


def tile_of(ref, i, b):
    return ref[i, 8 * b : 8 * b + 8, :]


def store_moments(pairs, moments):
    zero = jnp.zeros((8, LANES), jnp.float32)

    def body(i, accs):
        for b in range(8):
            accs = tuple(
                add_tile(acc, tile_of(a, i, b) * tile_of(c, i, b)) for acc, (a, c) in zip(accs, pairs)
            )
        return accs

    accs = lax.fori_loop(0, REACH, body, tuple((zero, zero) for _ in pairs))
    for n, acc in enumerate(accs):
        moments[2 * n : 2 * n + 1, :], moments[2 * n + 1 : 2 * n + 2, :] = fold_rows(acc)


def collapse(acc):
    return jnp.sum(acc, axis=0, keepdims=True)


def launch_kernel(hartree, density, charge, both, charge_here, face_a, face_b, sems):
    places = (both.at[pl.ds(0, REACH)], both.at[pl.ds(REACH, REACH)], charge_here)
    copies = [
        pltpu.make_async_copy(src, dst, sems.at[n])
        for n, (src, dst) in enumerate(zip((hartree, density, charge), places))
    ]
    for copy in copies:
        copy.start()
    for n in range(2):
        copies[n].wait()
        rows = slice(24 * n, 24 * n + 24)
        face_a[rows, :], face_b[rows, :] = by_partner(*pack_faces(both, REACH * n))
    copies[2].wait()


def inner_residual(both, charge, out, ext):
    hartree = both.at[pl.ds(0, REACH)]
    fill_ext(hartree, ext)
    for i in range(REACH):
        lap, values = inner_plane(i, hartree, ext)
        rho = both[REACH + i]
        out[i] = source_scale * (rho * rho - charge[i]) - (screen * values - lap)


def inner_basis(own, prior, out, ext):
    fill_ext(own, ext)
    for i in range(REACH):
        lap, values = inner_plane(i, own, ext)
        moved = (screen / SHIFT - 1.0) * values - (1.0 / SHIFT) * lap
        out[i] = moved if prior is None else 2.0 * moved - prior[i]


def z_kernel(gain, inner, z_first, z_second, out):
    faces = edge_faces(*by_side(z_first[0:24, :], z_second[0:24, :]))
    for i in range(REACH):
        out[i] = inner[i] + gain * z_plane(i, faces)


def x_kernel(gain, inner, near, far, out):
    def body(near_below, far_below):
        for i in range(REACH):
            out[i] = inner[i] + gain * (side_plane(i, near, near_below) + side_plane(i, far, far_below))

    with_sides(body)


def last_x_kernel(gain, inner, near, far, out, to_near, to_far):
    half = out.shape[1] // 2

    def body(near_below, far_below):
        for i in range(REACH):
            plane = inner[i] + gain * (side_plane(i, near, near_below) + side_plane(i, far, far_below))
            out[i] = plane
            for ref, below in ((to_near, near_below), (to_far, far_below)):
                ref[i] = plane[:half] if below else plane[half:]

    with_sides(body)


def pack_kernel(block, face_a, face_b):
    face_a[...], face_b[...] = by_partner(*pack_faces(block, 0))


def pack_upper_kernel(block, face):
    face[...] = pack_faces(block, 0)[1]


def store(rows, base, values):
    for n, value in enumerate(values):
        rows[base + n : base + n + 1, :] = value


def gram_dots(left, right, pairs):
    zero = jnp.zeros((8, LANES), jnp.float32)

    def body(i, accs):
        for b in range(8):
            at = pl.ds(8 * b, 8)
            l_tiles = {p: left[p, i, at, :] for p in sorted({p for p, _ in pairs})}
            if left is right:
                r_tiles = l_tiles
            else:
                r_tiles = {q: right[q, i, at, :] for q in sorted({q for _, q in pairs})}
            accs = tuple(acc + l_tiles[p] * r_tiles[q] for acc, (p, q) in zip(accs, pairs))
        return accs

    accs = lax.fori_loop(0, REACH, body, tuple(zero for _ in pairs))
    return [collapse(acc) for acc in accs]


CROSS_PAIRS = tuple((i, j) for i in range(HIST) for j in range(HIST))


def field_dots(groups, others, plain=()):
    zero = jnp.zeros((8, LANES), jnp.float32)
    fields = [(group, f) for group in groups for f in range(HIST)]
    count = len(fields)

    def body(i, accs):
        accs = list(accs)
        for b in range(8):
            at = pl.ds(8 * b, 8)
            tiles = [other(i, b) for other in others]
            for f, (group, which) in enumerate(fields):
                field = group[which, i, at, :]
                for o, tile in enumerate(tiles):
                    accs[o * count + f] = accs[o * count + f] + field * tile
            for n, (one, two) in enumerate(plain, len(others) * count):
                accs[n] = accs[n] + one(i, b) * two(i, b)
        return tuple(accs)

    total = count * len(others) + len(plain)
    return [collapse(acc) for acc in lax.fori_loop(0, REACH, body, (zero,) * total)]


def base_gradient(both, near, far, z_first, z_second, potential, grad, ext):
    hartree = both.at[pl.ds(0, REACH)]
    density = both.at[pl.ds(REACH, REACH)]
    fill_ext(density, ext)
    faces = edge_faces(*by_side(z_first[24:48, :], z_second[24:48, :]))

    def body(near_below, far_below):
        for i in range(REACH):
            grad[i] = side_plane(i, near, near_below) + side_plane(i, far, far_below) + z_plane(i, faces)

    with_sides(body)
    for i in range(REACH):
        lap, rho = inner_plane(i, density, ext)
        power = jnp.exp(jnp.log(rho) * (4.0 / 3.0))
        grad[i] = 2.0 * rho * (hartree[i] + potential[i] + tf_scale * power) - (lap + grad[i]) * (
            1.0 / (spacing * spacing)
        )


def density_tile(both):
    return lambda i, b: tile_of(both, REACH + i, b)


def lifted_tile(both, vector):
    return lambda i, b: 2.0 * tile_of(both, REACH + i, b) * tile_of(vector, i, b)


FETCHES = 4


def fetch(src, dst, sems):
    each = HIST // FETCHES
    return [
        pltpu.make_async_copy(src.at[pl.ds(each * n, each)], dst.at[pl.ds(each * n, each)], sems.at[n])
        for n in range(FETCHES)
    ]


def side_one(both, charge, steps, inner, steps_here, ext, sems):
    copies = fetch(steps, steps_here, sems)
    for copy in copies:
        copy.start()
    inner_residual(both, charge, inner, ext)
    for copy in copies:
        copy.wait()


def side_two(vector, both, near, far, z_first, z_second, potential, steps, changes, *outs):
    inner, grad, changes_here, rows, moments, ext, sems = outs
    copies = fetch(changes, changes_here, sems)
    for copy in copies:
        copy.start()
    inner_basis(vector, None, inner, ext)
    lifted, rho = lifted_tile(both, vector), density_tile(both)
    by_step = field_dots((steps,), [lifted, rho], [(rho, lifted)])
    store_moments([(vector, vector)], moments)
    base_gradient(both, near, far, z_first, z_second, potential, grad, ext)
    for copy in copies:
        copy.wait()
    by_change = field_dots((changes_here,), [lifted, rho])
    store(rows, 0, by_step[:8] + by_change[:8] + by_step[16:] + by_step[8:16] + by_change[8:])


def side_three(prior, vector, both, steps, changes, inner, rows, moments, ext):
    inner_basis(vector, prior, inner, ext)
    lifted, rho = lifted_tile(both, vector), density_tile(both)
    store(rows, 0, field_dots((steps, changes), [lifted], [(rho, lifted)]))
    store(rows, 17, gram_dots(steps, changes, CROSS_PAIRS[:32]))
    store(rows, 49, gram_dots(steps, steps, PAIRS))
    store_moments([(prior, vector), (vector, vector)], moments)


def side_four(prior, vector, both, grad, steps, changes, inner, rows, moments, ext):
    inner_basis(vector, prior, inner, ext)
    lifted, rho = lifted_tile(both, vector), density_tile(both)
    slope = lambda i, b: tile_of(grad, i, b)
    values = field_dots((steps, changes), [lifted, slope], [(rho, lifted), (rho, slope), (rho, rho)])
    store(rows, 0, values[:16] + values[32:33] + values[16:32] + values[33:])
    store(rows, 35, gram_dots(changes, changes, PAIRS))
    store(rows, 71, gram_dots(steps, changes, CROSS_PAIRS[32:]))
    store_moments([(prior, vector), (vector, vector)], moments)


def side_five(prior, vector, both, steps, changes, r2, r3, r4, m2, m3, m4, kept, given, table, m5):
    lifted, rho = lifted_tile(both, vector), density_tile(both)
    own = field_dots((steps, changes), [lifted], [(rho, lifted)])
    store_moments([(prior, vector), (vector, vector)], m5)
    table[...] = jnp.zeros_like(table)

    def put(base, ref, start, count):
        before = max(0, min(count, HALF - base))
        if before:
            table[base : base + before, :] = ref[start : start + before, :]
        if before < count:
            at = place(base + before)
            table[at : at + count - before, :] = ref[start + before : start + count, :]

    put(ROW_GRAM, r3, 49, 36)
    put(ROW_GRAM + 36, r4, 35, 36)
    put(ROW_GRAM + 72, r3, 17, 32)
    put(ROW_GRAM + 104, r4, 71, 32)
    put(ROW_BASE, r2, 17, 16)
    put(ROW_BASE + 16, r4, 17, 18)
    for n, rows in enumerate((r2, r3, r4)):
        put(ROW_W + 17 * n, rows, 0, 17)
    store(table, place(ROW_W + 51), own)

    order = [(m2, 0), (m3, 0), (m3, 1), (m4, 0), (m4, 1), (m5, 0), (m5, 1)]
    zero = jnp.zeros((1, LANES), jnp.float32)
    parts = [
        jnp.concatenate([ref[2 * which + low : 2 * which + low + 1, :] for ref, which in order] + [zero], axis=0)
        for low in range(2)
    ]
    hi, lo = fold_lanes(*parts)
    lane = lane_ids((1, LANES))
    first = jnp.sum(jnp.transpose(table[0:LANES, :]), axis=0, keepdims=True)
    second = jnp.sum(jnp.transpose(table[LANES : 2 * LANES, :]), axis=0, keepdims=True)
    for n in range(7):
        second = jnp.where(lane == MOM_LANE + n, hi[n : n + 1], second)
        second = jnp.where(lane == MOM_LANE + 7 + n, lo[n : n + 1], second)
    odd = is_odd("blk")
    kept[...] = jnp.where(odd, second, first)
    given[...] = jnp.where(odd, first, second)


def inner_moment_kernel(vector, inner, ext):
    fill_ext(vector, ext)
    zero = jnp.zeros((8, LANES), jnp.float32)
    accs = [(zero, zero) for _ in range(2)]
    for i in range(REACH):
        lap, values = inner_plane(i, vector, ext)
        product = values * ((screen / SHIFT - 1.0) * values - (1.0 / SHIFT) * lap)
        for b in range(8):
            accs[b % 2] = add_tile(accs[b % 2], product[8 * b : 8 * b + 8])
    hi, err = two_sum(accs[0][0], accs[1][0])
    inner[0:1, :], inner[1:2, :] = fold_rows((hi, accs[0][1] + accs[1][1] + err))


def couple(own, block, below, acc):
    half = own.shape[1] // 2
    for i in range(REACH):
        product = own[i, half:, :] * side_plane(i, block, True) if below else own[i, :half, :] * side_plane(i, block, False)
        for b in range(half // 8):
            acc = add_tile(acc, product[8 * b : 8 * b + 8])
    return acc


def couple_kernel(own, z_left, inner, kept, taken, row, part):
    zero = jnp.zeros((8, LANES), jnp.float32)
    faces = edge_faces(z_left[...], None)
    acc = (zero, zero)
    for i in range(REACH):
        product = own[i] * z_plane(i, faces)
        for b in range(8):
            acc = add_tile(acc, product[8 * b : 8 * b + 8])
    sides = df_scale(fold_rows(acc), -2.0 / SHIFT)
    part[0:1, :], part[1:2, :] = df_add(sides, (inner[0:1, :], inner[1:2, :]))
    lane = lane_ids((1, LANES))
    total, err = two_sum(kept[...], taken[...])
    low_lane = (lane >= MOM_LANE + 7) & (lane < MOM_LANE + 14) & is_odd("blk")
    row[...] = jnp.where(low_lane, total + pltpu.roll(err, 7, 1), total)


def send_kernel(own, far, near, part, row, out):
    zero = jnp.zeros((8, LANES), jnp.float32)

    def body(near_below, far_below):
        acc = couple(own, far, far_below, couple(own, near, near_below, (zero, zero)))
        hi, lo = fold_lanes(*df_add(df_scale(fold_rows(acc), -2.0 / SHIFT), (part[0:1, :], part[1:2, :])))
        lane = lane_ids((1, LANES))
        value = jnp.where(lane == HALF, hi, jnp.where(lane == HALF + 1, lo, row[...]))
        out[...] = jnp.broadcast_to(value, out.shape)

    with_sides(body)


def solve_krylov(moment):
    n00, n01, n11, n12, n22, n23, n33, n34 = moment
    nu = [n00, n01]
    nu.append(df_sub(df_scale(n11, 2.0), n00))
    nu.append(df_sub(df_scale(n12, 2.0), n01))
    nu.append(df_sub(df_scale(n22, 2.0), n00))
    nu.append(df_sub(df_scale(n23, 2.0), n01))
    nu.append(df_sub(df_scale(n33, 2.0), n00))

    def gram(i, j):
        if i == j == 0:
            return n00
        return df_scale(df_add(nu[i + j], nu[abs(i - j)]), 0.5)

    def moved(i, j):
        if i == 3 and j == 3:
            return n34
        if j == 0:
            return gram(i, 1)
        return df_scale(df_add(gram(i, j + 1), gram(i, j - 1)), 0.5)

    mat = {(i, j): df_add(moved(i, j), gram(i, j)) for i in range(4) for j in range(i + 1)}
    rhs = [df_scale(gram(i, 0), 1.0 / SHIFT) for i in range(4)]
    low, inverse = {}, []
    for k in range(4):
        inverse.append(1.0 / mat[k, k][0])
        for i in range(k + 1, 4):
            low[i, k] = df_over(mat[i, k], mat[k, k], inverse[k])
        for i in range(k + 1, 4):
            for j in range(k + 1, i + 1):
                mat[i, j] = df_sub(mat[i, j], df_mul(low[i, k], mat[j, k]))
            rhs[i] = df_sub(rhs[i], df_mul(low[i, k], rhs[k]))
    sol = [None] * 4
    for k in reversed(range(4)):
        value = df_over(rhs[k], mat[k, k], inverse[k])
        for i in range(k + 1, 4):
            value = df_sub(value, df_mul(low[i, k], sol[i]))
        sol[k] = value
    return [hi + lo for hi, lo in sol]


def final_kernel(received, both, grad, v0, v1, v2, v3, steps, changes, new_density, new_hartree, spread, density_here, hartree_here, sems):
    parts = [(received[8 * n : 8 * n + 8, :], jnp.zeros((8, LANES), jnp.float32)) for n in range(4)]
    for n in range(4, received.shape[0] // 8):
        parts[n % 4] = add_tile(parts[n % 4], received[8 * n : 8 * n + 8, :])
    while len(parts) > 1:
        half = len(parts) // 2
        merged = []
        for a, b in zip(parts[:half], parts[half:]):
            hi, err = two_sum(a[0], b[0])
            merged.append((hi, a[1] + b[1] + err))
        parts = merged
    hi, lo = fold(*parts[0], 0, (1, 2))
    lane = lane_ids((1, LANES))
    last, err = two_sum(hi[3:4], hi[7:8])
    err = err + (lo[3:4] + lo[7:8])
    first = hi[3:4]
    second = jnp.where(lane >= HALF, last, hi[7:8])
    low = jnp.where(lane >= HALF, err, lo[7:8])
    low = low + jnp.where(lane == HALF, pltpu.roll(second, LANES - 1, 1), pltpu.roll(second, LANES - 7, 1))
    for n, value in enumerate((first, second, low)):
        spread[LANES * n : LANES * n + LANES, :] = jnp.transpose(jnp.broadcast_to(value, (LANES, LANES)))

    def row(n):
        return spread[place(n) : place(n) + 1, :]

    def moment(n):
        at = LANES + (MOM_LANE + n if n < 7 else HALF)
        return quick_sum(spread[at : at + 1, :], spread[LANES + at : LANES + at + 1, :])

    mix = solve_krylov([moment(n) for n in range(8)])

    def s_s(i, j):
        return row(ROW_GRAM + PAIR_ROW[min(i, j), max(i, j)])

    def y_y(i, j):
        return row(ROW_GRAM + 36 + PAIR_ROW[min(i, j), max(i, j)])

    def s_y(i, j):
        return row(ROW_GRAM + 72 + 8 * i + j)

    pairs = range(HIST)
    theta, rest, inverse = [], [], []
    for i in pairs:
        curv, norm = s_y(i, i), s_s(i, i)
        kept = (1.0 - damp_floor) * norm
        damp = jnp.where(curv >= damp_floor * norm, 1.0, kept / jnp.maximum(norm - curv, kept))
        theta.append(damp)
        rest.append(1.0 - damp)
        inverse.append(1.0 / (damp * curv + (1.0 - damp) * norm))

    def s_bar(i, j):
        return theta[j] * s_y(i, j) + rest[j] * s_s(i, j)

    def bar_bar(i, j):
        return theta[i] * (theta[j] * y_y(i, j) + rest[j] * s_y(j, i)) + rest[i] * s_bar(i, j)

    last = HIST - 1
    scaling = s_bar(last, last) / bar_bar(last, last)

    def energy(n):
        value = row(ROW_BASE + 16 + n)
        for j in range(4):
            value = value + mix[j] * row(ROW_W + 17 * j + n)
        return value

    chem = energy(16) / row(ROW_BASE + 33)

    def gradient(n):
        return energy(n) - chem * row(ROW_BASE + n)

    s_grad = [gradient(i) for i in pairs]
    bar_grad = [theta[i] * gradient(HIST + i) + rest[i] * s_grad[i] for i in pairs]

    first = [None] * HIST
    pending = list(s_grad)
    for j in reversed(pairs):
        first[j] = inverse[j] * pending[j]
        for i in range(j):
            pending[i] = pending[i] - first[j] * s_bar(i, j)
    pending = list(bar_grad)
    for j in pairs:
        for i in pairs:
            pending[i] = pending[i] - first[j] * bar_bar(i, j)
    pending = [scaling * value for value in pending]
    step_mix, change_mix = [], []
    for j in pairs:
        net = first[j] - inverse[j] * pending[j]
        for i in range(j + 1, HIST):
            pending[i] = pending[i] + net * s_bar(j, i)
        change_mix.append((-step_length) * (-scaling * first[j] * theta[j]))
        step_mix.append((-step_length) * (net - scaling * first[j] * rest[j]))

    wide = lambda value: jnp.broadcast_to(value, (8, LANES))
    mix = [wide(value) for value in mix]
    chem, gain = wide(chem), wide((-step_length) * scaling)
    step_mix = [wide(value) for value in step_mix]
    change_mix = [wide(value) for value in change_mix]
    basis = (v0, v1, v2, v3)

    def leave(i):
        return [
            pltpu.make_async_copy(here.at[i], out.at[i], sems.at[n, i])
            for n, (here, out) in enumerate(((density_here, new_density), (hartree_here, new_hartree)))
        ]

    for i in range(REACH):
        for b in range(8):
            at = pl.ds(8 * b, 8)
            rho = both[REACH + i, at, :]
            lift = mix[0] * v0[i, at, :]
            for j in range(1, 4):
                lift = lift + mix[j] * basis[j][i, at, :]
            hartree_here[i, at, :] = both[i, at, :] + lift
            slope = grad[i, at, :] + 2.0 * rho * lift - chem * rho
            parts = [rho, gain * slope, step_mix[0] * steps[0, i, at, :], change_mix[0] * changes[0, i, at, :]]
            for f in range(1, HIST):
                parts[2] = parts[2] + step_mix[f] * steps[f, i, at, :]
                parts[3] = parts[3] + change_mix[f] * changes[f, i, at, :]
            density_here[i, at, :] = parts[0] + (parts[1] + (parts[2] + parts[3]))
        for copy in leave(i):
            copy.start()
    for i in range(REACH):
        for copy in leave(i):
            copy.wait()


def call(kernel, outs, args, scratch=(), flops=0, in_hbm=(), out_hbm=False):
    args = [pltpu.with_memory_space_constraint(x, pltpu.HBM) if n in in_hbm else x for n, x in enumerate(args)]
    shapes = [jax.ShapeDtypeStruct(shape, jnp.float32) for shape in outs]
    size = sum(4 * math.prod(a.shape) for a in (*args, *shapes))
    return pl.pallas_call(
        kernel,
        out_shape=shapes,
        in_specs=[pl.BlockSpec(memory_space=pltpu.HBM if n in in_hbm else pltpu.VMEM) for n in range(len(args))],
        out_specs=[pl.BlockSpec(memory_space=pltpu.HBM if out_hbm else pltpu.VMEM)] * len(outs),
        scratch_shapes=[pltpu.VMEM(s, jnp.float32) if isinstance(s, tuple) else s for s in scratch],
        cost_estimate=pl.CostEstimate(flops=flops, bytes_accessed=size, transcendentals=0),
        compiler_params=pltpu.CompilerParams(vmem_limit_bytes=VMEM_LIMIT),
    )(*args)


def ring(axis, step):
    size = lax.axis_size(axis)
    return [(i, (i + step) % size) for i in range(size)]


def swap(axis, odd_up):
    size = lax.axis_size(axis)
    return [(i, (i + (1 if i % 2 == odd_up else -1)) % size) for i in range(size)]


def after(values, *earlier):
    return lax.optimization_barrier((tuple(values), earlier))[0]


def x_halo(block):
    far = lax.ppermute(block, "blk", swap("blk", 1))
    return (lax.ppermute(block, "blk", swap("blk", 0)), far)


def z_halo(face_a, face_b):
    return (lax.ppermute(face_a, "gz", swap("gz", 0)), lax.ppermute(face_b, "gz", swap("gz", 1)))


def on_device(sqrt_density, ion_charge, ion_potential, hartree_prev, hist_steps, hist_changes):
    block = sqrt_density.shape
    ext = (block[0], block[1] + 16, block[2])
    face = (24, LANES)
    cells = math.prod(block)
    cells = math.prod(block)
    work = 300 * cells
    inputs = (hartree_prev, sqrt_density, ion_charge)
    halo = x_halo(hartree_prev)
    both, charge, *faces = call(
        launch_kernel,
        [(2 * REACH, *block[1:]), block, (48, LANES), (48, LANES)],
        inputs,
        [pltpu.SemaphoreType.DMA((3,))],
        in_hbm=(0, 1, 2),
    )
    ends = z_halo(*faces)
    density_ends = ends
    half = (REACH, block[1] // 2, LANES)

    def advance(gain, inner, halo, ends, last=False):
        (mid,) = call(functools.partial(z_kernel, gain), [block], [inner, *ends], flops=work)
        return call(
            functools.partial(last_x_kernel if last else x_kernel, gain),
            [block, half, half] if last else [block],
            [mid, *halo],
            flops=work,
        )

    def exchange(block_now):
        halo = x_halo(block_now)
        return halo, z_halo(*call(pack_kernel, [face, face], [block_now], flops=work))

    stored = hist_steps.shape
    inner, steps = call(
        side_one,
        [block, stored],
        [both, charge, hist_steps],
        [ext, pltpu.SemaphoreType.DMA((FETCHES,))],
        work,
        in_hbm=(2,),
    )
    density_far = lax.ppermute(after((sqrt_density,), *faces)[0], "blk", swap("blk", 1))
    (mid,) = call(functools.partial(z_kernel, 1.0), [block], [inner, *ends], flops=work)
    density_near = lax.ppermute(after((sqrt_density,), mid)[0], "blk", swap("blk", 0))
    (v0,) = call(functools.partial(x_kernel, 1.0), [block], [mid, *halo], flops=work)
    halo, ends = exchange(v0)
    inner, grad, changes, r2, m2 = call(
        side_two,
        [block, block, stored, (40, LANES), (8, LANES)],
        [v0, both, density_near, density_far, *density_ends, ion_potential, steps, hist_changes],
        [ext, pltpu.SemaphoreType.DMA((FETCHES,))],
        work,
        in_hbm=(8,),
    )
    history = (steps, changes)
    (v1,) = advance(-1.0 / SHIFT, inner, halo, ends)
    halo, ends = exchange(v1)
    inner, r3, m3 = call(
        side_three, [block, (88, LANES), (8, LANES)], [v0, v1, both, *history], [ext], work
    )
    (v2,) = advance(-2.0 / SHIFT, inner, halo, ends)
    halo, ends = exchange(v2)
    inner, r4, m4 = call(
        side_four, [block, (112, LANES), (8, LANES)], [v1, v2, both, grad, *history], [ext], work
    )
    v3, to_near, to_far = advance(-2.0 / SHIFT, inner, halo, ends, last=True)
    far = lax.ppermute(to_far, "blk", swap("blk", 1))
    near = lax.ppermute(to_near, "blk", swap("blk", 0))
    (upper,) = call(pack_upper_kernel, [face], [v3], flops=work)
    z_left = lax.ppermute(upper, "gz", ring("gz", 1))
    kept, given = call(
        side_five,
        [(1, LANES), (1, LANES)],
        [v2, v3, both, *history, r2, r3, r4, m2, m3, m4],
        [(2 * LANES, LANES), (8, LANES)],
        work,
    )
    taken = lax.ppermute(given, "blk", swap("blk", 0))
    (inner,) = call(inner_moment_kernel, [(8, LANES)], [after((v3,), given)[0]], [ext], work)
    row, part = call(couple_kernel, [(1, LANES), (8, LANES)], [v3, z_left, inner, kept, taken], flops=work)
    devices = lax.axis_size("blk") * lax.axis_size("gz")
    (outgoing,) = call(send_kernel, [(devices, LANES)], [v3, far, near, part, row], flops=work)
    received = lax.all_to_all(outgoing.reshape(devices, 1, LANES), ("blk", "gz"), 0, 0, tiled=True)
    return tuple(
        call(
            final_kernel,
            [block, block],
            [received.reshape(devices, LANES), both, grad, v0, v1, v2, v3, *history],
            [(3 * LANES, LANES), block, block, pltpu.SemaphoreType.DMA((2, REACH))],
            work,
            out_hbm=True,
        )
    )


def solution(mesh):
    placed = (
        P("blk", None, "gz"),
        P("blk", None, "gz"),
        P("blk", None, "gz"),
        P("blk", None, "gz"),
        P(None, "blk", None, "gz"),
        P(None, "blk", None, "gz"),
    )
    return jax.shard_map(
        on_device,
        mesh=mesh,
        in_specs=placed,
        out_specs=(P("blk", None, "gz"), P("blk", None, "gz")),
        check_vma=False,
    )
```

```python
import functools
import math

import jax
import jax.numpy as jnp
from jax import lax
from jax.experimental import pallas as pl
from jax.experimental.pallas import tpu as pltpu
from jax.sharding import PartitionSpec as P

center = -5369.0 / 1800.0
coeffs = (12.0 / 7.0, -15.0 / 56.0, 10.0 / 189.0, -1.0 / 112.0, 2.0 / 825.0, -1.0 / 4752.0)
screen = 0.0025
spacing = 0.28
source_scale = 4.0 * math.pi * spacing * spacing
tf_scale = 5.0 / 3.0 * 2.871234
step_length = 0.01
damp_floor = 0.2

SHIFT = 2.0
HIST = 8
REACH = 6
LANES = 128
VMEM_LIMIT = 24 * 1024 * 1024

ROW_GRAM = 0
ROW_BASE = 136
ROW_W = 170
ROW_MOM = 238
HALF = 126


def place(n):
    return n if n < HALF else n + LANES - HALF


MOM_LANE = place(ROW_MOM) - LANES
PAIRS = tuple((i, j) for i in range(HIST) for j in range(i, HIST))
PAIR_ROW = {pair: row for row, pair in enumerate(PAIRS)}


def two_sum(a, b):
    s = a + b
    bb = s - a
    return s, (a - (s - bb)) + (b - bb)


def quick_sum(a, b):
    s = a + b
    return s, b - (s - a)


def split(a):
    t = 4097.0 * a
    hi = t - (t - a)
    return hi, a - hi


def two_prod(a, b):
    p = a * b
    ah, al = split(a)
    bh, bl = split(b)
    return p, ((ah * bh - p) + ah * bl + al * bh) + al * bl


def df_add(a, b):
    s, e = two_sum(a[0], b[0])
    return quick_sum(s, e + (a[1] + b[1]))


def df_neg(a):
    return (-a[0], -a[1])


def df_sub(a, b):
    return df_add(a, df_neg(b))


def df_scale(a, factor):
    return (a[0] * factor, a[1] * factor)


def df_mul(a, b):
    p, e = two_prod(a[0], b[0])
    return quick_sum(p, e + (a[0] * b[1] + a[1] * b[0]))


def df_over(a, b, inverse):
    q = a[0] * inverse
    p, e = two_prod(q, b[0])
    rest = ((a[0] - p) - e) + (a[1] - q * b[1])
    return quick_sum(q, rest * inverse)


def lane_ids(shape):
    return lax.broadcasted_iota(jnp.int32, shape, len(shape) - 1)


def inner_plane(i, own, ext):
    values = own[i]
    rows = values.shape[0]
    lane = lane_ids((rows, LANES))
    total = (3.0 * center) * values
    for k, weight in enumerate(coeffs, 1):
        pair = ext[i, 8 + k : 8 + k + rows, :] + ext[i, 8 - k : 8 - k + rows, :]
        if i + k < REACH:
            pair = pair + own[i + k]
        if i - k >= 0:
            pair = pair + own[i - k]
        up = pltpu.roll(jnp.where(lane < k, 0.0, values), LANES - k, 1)
        down = pltpu.roll(jnp.where(lane >= LANES - k, 0.0, values), k, 1)
        total = total + weight * (pair + (up + down))
    return total, values


def edge_faces(z_left, z_right):
    lane = lane_ids((24, LANES)) % 8
    lower = jnp.zeros((24, LANES), jnp.float32)
    upper = jnp.zeros((24, LANES), jnp.float32)
    for k, weight in enumerate(coeffs, 1):
        lower = lower + jnp.where(lane < k, weight * pltpu.roll(z_left, LANES - 8 + k, 1), 0.0)
        if z_right is not None:
            upper = upper + jnp.where(lane >= 8 - k, weight * pltpu.roll(z_right, 8 - k, 1), 0.0)
    return lower, upper


def side_plane(i, block, below, rows=slice(None)):
    total = None
    for k, weight in enumerate(coeffs, 1):
        layer = i - k + REACH if below else i + k - REACH
        if 0 <= layer < REACH:
            term = weight * block[layer, rows, :]
            total = term if total is None else total + term
    return total


def z_plane(i, faces, tiles=8):
    lane = lane_ids((8, LANES))
    lower, upper = (face[8 * (i // 2) : 8 * (i // 2) + 8] for face in faces)
    out = []
    for b in range(tiles):
        j = 8 * (i % 2) + b
        tile = jnp.where(lane < 8, pltpu.roll(lower, (LANES - 8 * j) % LANES, 1), 0.0)
        tile = jnp.where(lane >= LANES - 8, pltpu.roll(upper, (2 * LANES - 8 - 8 * j) % LANES, 1), tile)
        out.append(tile)
    return jnp.concatenate(out, axis=0)


def fill_ext(own, ext):
    rows = own.shape[1]
    ext[:, 8 : 8 + rows, :] = own[...]
    ext[:, 0:8, :] = own[:, rows - 8 : rows, :]
    ext[:, 8 + rows : 16 + rows, :] = own[:, 0:8, :]


def pack_faces(src, layers):
    lane = lane_ids((8, LANES))
    firsts, lasts = [], []
    for m in range(3):
        first = jnp.zeros((8, LANES), jnp.float32)
        last = jnp.zeros((8, LANES), jnp.float32)
        for j in range(16):
            n = 16 * m + j
            tile = src[layers + n // 8, 8 * (n % 8) : 8 * (n % 8) + 8, :]
            here = (lane >= 8 * j) & (lane < 8 * j + 8)
            first = jnp.where(here, pltpu.roll(tile, 8 * j, 1) if j else tile, first)
            last = jnp.where(here, pltpu.roll(tile, (8 * j + 8) % LANES, 1) if j < 15 else tile, last)
        firsts.append(first)
        lasts.append(last)
    return jnp.concatenate(firsts, axis=0), jnp.concatenate(lasts, axis=0)


def is_odd(axis):
    return lax.rem(lax.axis_index(axis), 2) == 1


def by_partner(lower, upper):
    odd = is_odd("gz")
    return jnp.where(odd, lower, upper), jnp.where(odd, upper, lower)


def by_side(first, second):
    odd = is_odd("gz")
    return jnp.where(odd, first, second), jnp.where(odd, second, first)


def with_sides(body):
    odd = is_odd("blk")

    @pl.when(odd)
    def _():
        body(True, False)

    @pl.when(jnp.logical_not(odd))
    def _():
        body(False, True)


def fold(hi, lo, axis, steps):
    for step in steps:
        hi, err = two_sum(hi, pltpu.roll(hi, step, axis))
        lo = lo + pltpu.roll(lo, step, axis) + err
    return hi, lo


def fold_rows(acc):
    hi, lo = fold(*acc, 0, (4, 2, 1))
    return hi[0:1], lo[0:1]


def fold_lanes(hi, lo):
    return quick_sum(*fold(hi, lo, 1, (64, 32, 16, 8, 4, 2, 1)))


def add_tile(acc, product):
    hi, err = two_sum(acc[0], product)
    return hi, acc[1] + err


def tile_of(ref, i, b):
    return ref[i, 8 * b : 8 * b + 8, :]


def store_moments(pairs, moments):
    zero = jnp.zeros((8, LANES), jnp.float32)

    def body(i, accs):
        for b in range(8):
            accs = tuple(
                add_tile(acc, tile_of(a, i, b) * tile_of(c, i, b)) for acc, (a, c) in zip(accs, pairs)
            )
        return accs

    accs = lax.fori_loop(0, REACH, body, tuple((zero, zero) for _ in pairs))
    for n, acc in enumerate(accs):
        moments[2 * n : 2 * n + 1, :], moments[2 * n + 1 : 2 * n + 2, :] = fold_rows(acc)


def collapse(acc):
    return jnp.sum(acc, axis=0, keepdims=True)


def launch_kernel(hartree, density, charge, both, charge_here, face_a, face_b, sems):
    places = (both.at[pl.ds(0, REACH)], both.at[pl.ds(REACH, REACH)], charge_here)
    copies = [
        pltpu.make_async_copy(src, dst, sems.at[n])
        for n, (src, dst) in enumerate(zip((hartree, density, charge), places))
    ]
    for copy in copies:
        copy.start()
    for n in range(2):
        copies[n].wait()
        rows = slice(24 * n, 24 * n + 24)
        face_a[rows, :], face_b[rows, :] = by_partner(*pack_faces(both, REACH * n))
    copies[2].wait()


def inner_residual(both, charge, out, ext):
    hartree = both.at[pl.ds(0, REACH)]
    fill_ext(hartree, ext)
    for i in range(REACH):
        lap, values = inner_plane(i, hartree, ext)
        rho = both[REACH + i]
        out[i] = source_scale * (rho * rho - charge[i]) - (screen * values - lap)


def inner_basis(own, prior, out, ext):
    fill_ext(own, ext)
    for i in range(REACH):
        lap, values = inner_plane(i, own, ext)
        moved = (screen / SHIFT - 1.0) * values - (1.0 / SHIFT) * lap
        out[i] = moved if prior is None else 2.0 * moved - prior[i]


def z_kernel(gain, inner, z_first, z_second, out):
    faces = edge_faces(*by_side(z_first[0:24, :], z_second[0:24, :]))
    for i in range(REACH):
        out[i] = inner[i] + gain * z_plane(i, faces)


def x_kernel(gain, inner, near, far, out):
    def body(near_below, far_below):
        for i in range(REACH):
            out[i] = inner[i] + gain * (side_plane(i, near, near_below) + side_plane(i, far, far_below))

    with_sides(body)


def last_x_kernel(gain, inner, near, far, out, to_near, to_far):
    half = out.shape[1] // 2

    def body(near_below, far_below):
        for i in range(REACH):
            plane = inner[i] + gain * (side_plane(i, near, near_below) + side_plane(i, far, far_below))
            out[i] = plane
            for ref, below in ((to_near, near_below), (to_far, far_below)):
                ref[i] = plane[:half] if below else plane[half:]

    with_sides(body)


def pack_kernel(block, face_a, face_b):
    face_a[...], face_b[...] = by_partner(*pack_faces(block, 0))


def pack_upper_kernel(block, face):
    face[...] = pack_faces(block, 0)[1]


def store(rows, base, values):
    for n, value in enumerate(values):
        rows[base + n : base + n + 1, :] = value


def gram_dots(left, right, pairs):
    zero = jnp.zeros((8, LANES), jnp.float32)

    def body(i, accs):
        for b in range(8):
            at = pl.ds(8 * b, 8)
            l_tiles = {p: left[p, i, at, :] for p in sorted({p for p, _ in pairs})}
            if left is right:
                r_tiles = l_tiles
            else:
                r_tiles = {q: right[q, i, at, :] for q in sorted({q for _, q in pairs})}
            accs = tuple(acc + l_tiles[p] * r_tiles[q] for acc, (p, q) in zip(accs, pairs))
        return accs

    accs = lax.fori_loop(0, REACH, body, tuple(zero for _ in pairs))
    return [collapse(acc) for acc in accs]


CROSS_PAIRS = tuple((i, j) for i in range(HIST) for j in range(HIST))


def field_dots(groups, others, plain=()):
    zero = jnp.zeros((8, LANES), jnp.float32)
    fields = [(group, f) for group in groups for f in range(HIST)]
    count = len(fields)

    def body(i, accs):
        accs = list(accs)
        for b in range(8):
            at = pl.ds(8 * b, 8)
            tiles = [other(i, b) for other in others]
            for f, (group, which) in enumerate(fields):
                field = group[which, i, at, :]
                for o, tile in enumerate(tiles):
                    accs[o * count + f] = accs[o * count + f] + field * tile
            for n, (one, two) in enumerate(plain, len(others) * count):
                accs[n] = accs[n] + one(i, b) * two(i, b)
        return tuple(accs)

    total = count * len(others) + len(plain)
    return [collapse(acc) for acc in lax.fori_loop(0, REACH, body, (zero,) * total)]


def base_gradient(both, near, far, z_first, z_second, potential, grad, ext):
    hartree = both.at[pl.ds(0, REACH)]
    density = both.at[pl.ds(REACH, REACH)]
    fill_ext(density, ext)
    faces = edge_faces(*by_side(z_first[24:48, :], z_second[24:48, :]))

    def body(near_below, far_below):
        for i in range(REACH):
            grad[i] = side_plane(i, near, near_below) + side_plane(i, far, far_below) + z_plane(i, faces)

    with_sides(body)
    for i in range(REACH):
        lap, rho = inner_plane(i, density, ext)
        power = jnp.exp(jnp.log(rho) * (4.0 / 3.0))
        grad[i] = 2.0 * rho * (hartree[i] + potential[i] + tf_scale * power) - (lap + grad[i]) * (
            1.0 / (spacing * spacing)
        )


def density_tile(both):
    return lambda i, b: tile_of(both, REACH + i, b)


def lifted_tile(both, vector):
    return lambda i, b: 2.0 * tile_of(both, REACH + i, b) * tile_of(vector, i, b)


def side_one(both, charge, inner, ext):
    inner_residual(both, charge, inner, ext)


def side_two(vector, both, near, far, z_first, z_second, potential, steps, *outs):
    inner, grad, rows, moments, ext = outs
    inner_basis(vector, None, inner, ext)
    lifted, rho = lifted_tile(both, vector), density_tile(both)
    store(rows, 0, field_dots((steps,), [lifted, rho], [(rho, lifted)]))
    store_moments([(vector, vector)], moments)
    base_gradient(both, near, far, z_first, z_second, potential, grad, ext)


def side_three(prior, vector, both, steps, changes, inner, rows, moments, ext):
    inner_basis(vector, prior, inner, ext)
    before, lifted, rho = lifted_tile(both, prior), lifted_tile(both, vector), density_tile(both)
    by_step = field_dots((steps,), [lifted], [(rho, lifted)])
    by_change = field_dots((changes,), [before, rho, lifted])
    store(rows, 0, by_step[:8] + by_change[16:] + by_step[8:] + by_change[:16])
    store(rows, 33, gram_dots(steps, changes, CROSS_PAIRS[:32]))
    store(rows, 65, gram_dots(steps, steps, PAIRS))
    store_moments([(prior, vector), (vector, vector)], moments)


def side_four(prior, vector, both, grad, steps, changes, inner, rows, moments, ext):
    inner_basis(vector, prior, inner, ext)
    lifted, rho = lifted_tile(both, vector), density_tile(both)
    slope = lambda i, b: tile_of(grad, i, b)
    values = field_dots((steps, changes), [lifted, slope], [(rho, lifted), (rho, slope), (rho, rho)])
    store(rows, 0, values[:16] + values[32:33] + values[16:32] + values[33:])
    store(rows, 35, gram_dots(changes, changes, PAIRS))
    store(rows, 71, gram_dots(steps, changes, CROSS_PAIRS[32:]))
    store_moments([(prior, vector), (vector, vector)], moments)


def side_five(prior, vector, both, steps, changes, r2, r3, r4, m2, m3, m4, kept, given, table, m5):
    lifted, rho = lifted_tile(both, vector), density_tile(both)
    own = field_dots((steps, changes), [lifted], [(rho, lifted)])
    store_moments([(prior, vector), (vector, vector)], m5)
    table[...] = jnp.zeros_like(table)

    def put(base, ref, start, count):
        before = max(0, min(count, HALF - base))
        if before:
            table[base : base + before, :] = ref[start : start + before, :]
        if before < count:
            at = place(base + before)
            table[at : at + count - before, :] = ref[start + before : start + count, :]

    put(ROW_GRAM, r3, 65, 36)
    put(ROW_GRAM + 36, r4, 35, 36)
    put(ROW_GRAM + 72, r3, 33, 32)
    put(ROW_GRAM + 104, r4, 71, 32)
    put(ROW_BASE, r2, 8, 8)
    put(ROW_BASE + 8, r3, 25, 8)
    put(ROW_BASE + 16, r4, 17, 18)
    put(ROW_W, r2, 0, 8)
    put(ROW_W + 8, r3, 17, 8)
    put(ROW_W + 16, r2, 16, 1)
    put(ROW_W + 17, r3, 0, 17)
    put(ROW_W + 34, r4, 0, 17)
    store(table, place(ROW_W + 51), own)

    order = [(m2, 0), (m3, 0), (m3, 1), (m4, 0), (m4, 1), (m5, 0), (m5, 1)]
    zero = jnp.zeros((1, LANES), jnp.float32)
    parts = [
        jnp.concatenate([ref[2 * which + low : 2 * which + low + 1, :] for ref, which in order] + [zero], axis=0)
        for low in range(2)
    ]
    hi, lo = fold_lanes(*parts)
    lane = lane_ids((1, LANES))
    first = jnp.sum(jnp.transpose(table[0:LANES, :]), axis=0, keepdims=True)
    second = jnp.sum(jnp.transpose(table[LANES : 2 * LANES, :]), axis=0, keepdims=True)
    for n in range(7):
        second = jnp.where(lane == MOM_LANE + n, hi[n : n + 1], second)
        second = jnp.where(lane == MOM_LANE + 7 + n, lo[n : n + 1], second)
    odd = is_odd("blk")
    kept[...] = jnp.where(odd, second, first)
    given[...] = jnp.where(odd, first, second)


def inner_moment_kernel(vector, inner, ext):
    fill_ext(vector, ext)
    zero = jnp.zeros((8, LANES), jnp.float32)
    accs = [(zero, zero) for _ in range(2)]
    for i in range(REACH):
        lap, values = inner_plane(i, vector, ext)
        product = values * ((screen / SHIFT - 1.0) * values - (1.0 / SHIFT) * lap)
        for b in range(8):
            accs[b % 2] = add_tile(accs[b % 2], product[8 * b : 8 * b + 8])
    hi, err = two_sum(accs[0][0], accs[1][0])
    inner[0:1, :], inner[1:2, :] = fold_rows((hi, accs[0][1] + accs[1][1] + err))


def couple(own, block, below, acc):
    half = own.shape[1] // 2
    for i in range(REACH):
        product = own[i, half:, :] * side_plane(i, block, True) if below else own[i, :half, :] * side_plane(i, block, False)
        for b in range(half // 8):
            acc = add_tile(acc, product[8 * b : 8 * b + 8])
    return acc


def couple_kernel(own, z_left, inner, kept, taken, row, part):
    zero = jnp.zeros((8, LANES), jnp.float32)
    faces = edge_faces(z_left[...], None)
    acc = (zero, zero)
    for i in range(REACH):
        product = own[i] * z_plane(i, faces)
        for b in range(8):
            acc = add_tile(acc, product[8 * b : 8 * b + 8])
    sides = df_scale(fold_rows(acc), -2.0 / SHIFT)
    part[0:1, :], part[1:2, :] = df_add(sides, (inner[0:1, :], inner[1:2, :]))
    lane = lane_ids((1, LANES))
    total, err = two_sum(kept[...], taken[...])
    low_lane = (lane >= MOM_LANE + 7) & (lane < MOM_LANE + 14) & is_odd("blk")
    row[...] = jnp.where(low_lane, total + pltpu.roll(err, 7, 1), total)


def send_kernel(own, far, near, part, row, out):
    zero = jnp.zeros((8, LANES), jnp.float32)

    def body(near_below, far_below):
        acc = couple(own, far, far_below, couple(own, near, near_below, (zero, zero)))
        hi, lo = fold_lanes(*df_add(df_scale(fold_rows(acc), -2.0 / SHIFT), (part[0:1, :], part[1:2, :])))
        lane = lane_ids((1, LANES))
        value = jnp.where(lane == HALF, hi, jnp.where(lane == HALF + 1, lo, row[...]))
        out[...] = jnp.broadcast_to(value, out.shape)

    with_sides(body)


def solve_krylov(moment):
    n00, n01, n11, n12, n22, n23, n33, n34 = moment
    nu = [n00, n01]
    nu.append(df_sub(df_scale(n11, 2.0), n00))
    nu.append(df_sub(df_scale(n12, 2.0), n01))
    nu.append(df_sub(df_scale(n22, 2.0), n00))
    nu.append(df_sub(df_scale(n23, 2.0), n01))
    nu.append(df_sub(df_scale(n33, 2.0), n00))

    def gram(i, j):
        if i == j == 0:
            return n00
        return df_scale(df_add(nu[i + j], nu[abs(i - j)]), 0.5)

    def moved(i, j):
        if i == 3 and j == 3:
            return n34
        if j == 0:
            return gram(i, 1)
        return df_scale(df_add(gram(i, j + 1), gram(i, j - 1)), 0.5)

    mat = {(i, j): df_add(moved(i, j), gram(i, j)) for i in range(4) for j in range(i + 1)}
    rhs = [df_scale(gram(i, 0), 1.0 / SHIFT) for i in range(4)]
    low, inverse = {}, []
    for k in range(4):
        inverse.append(1.0 / mat[k, k][0])
        for i in range(k + 1, 4):
            low[i, k] = df_over(mat[i, k], mat[k, k], inverse[k])
        for i in range(k + 1, 4):
            for j in range(k + 1, i + 1):
                mat[i, j] = df_sub(mat[i, j], df_mul(low[i, k], mat[j, k]))
            rhs[i] = df_sub(rhs[i], df_mul(low[i, k], rhs[k]))
    sol = [None] * 4
    for k in reversed(range(4)):
        value = df_over(rhs[k], mat[k, k], inverse[k])
        for i in range(k + 1, 4):
            value = df_sub(value, df_mul(low[i, k], sol[i]))
        sol[k] = value
    return [hi + lo for hi, lo in sol]


def final_kernel(received, both, grad, v0, v1, v2, v3, steps, changes, new_density, new_hartree, spread, density_here, hartree_here, sems):
    parts = [(received[8 * n : 8 * n + 8, :], jnp.zeros((8, LANES), jnp.float32)) for n in range(4)]
    for n in range(4, received.shape[0] // 8):
        parts[n % 4] = add_tile(parts[n % 4], received[8 * n : 8 * n + 8, :])
    while len(parts) > 1:
        half = len(parts) // 2
        merged = []
        for a, b in zip(parts[:half], parts[half:]):
            hi, err = two_sum(a[0], b[0])
            merged.append((hi, a[1] + b[1] + err))
        parts = merged
    hi, lo = fold(*parts[0], 0, (1, 2))
    lane = lane_ids((1, LANES))
    last, err = two_sum(hi[3:4], hi[7:8])
    err = err + (lo[3:4] + lo[7:8])
    first = hi[3:4]
    second = jnp.where(lane >= HALF, last, hi[7:8])
    low = jnp.where(lane >= HALF, err, lo[7:8])
    low = low + jnp.where(lane == HALF, pltpu.roll(second, LANES - 1, 1), pltpu.roll(second, LANES - 7, 1))
    for n, value in enumerate((first, second, low)):
        spread[LANES * n : LANES * n + LANES, :] = jnp.transpose(jnp.broadcast_to(value, (LANES, LANES)))

    def row(n):
        return spread[place(n) : place(n) + 1, :]

    def moment(n):
        at = LANES + (MOM_LANE + n if n < 7 else HALF)
        return quick_sum(spread[at : at + 1, :], spread[LANES + at : LANES + at + 1, :])

    mix = solve_krylov([moment(n) for n in range(8)])

    def s_s(i, j):
        return row(ROW_GRAM + PAIR_ROW[min(i, j), max(i, j)])

    def y_y(i, j):
        return row(ROW_GRAM + 36 + PAIR_ROW[min(i, j), max(i, j)])

    def s_y(i, j):
        return row(ROW_GRAM + 72 + 8 * i + j)

    pairs = range(HIST)
    theta, rest, inverse = [], [], []
    for i in pairs:
        curv, norm = s_y(i, i), s_s(i, i)
        kept = (1.0 - damp_floor) * norm
        damp = jnp.where(curv >= damp_floor * norm, 1.0, kept / jnp.maximum(norm - curv, kept))
        theta.append(damp)
        rest.append(1.0 - damp)
        inverse.append(1.0 / (damp * curv + (1.0 - damp) * norm))

    def s_bar(i, j):
        return theta[j] * s_y(i, j) + rest[j] * s_s(i, j)

    def bar_bar(i, j):
        return theta[i] * (theta[j] * y_y(i, j) + rest[j] * s_y(j, i)) + rest[i] * s_bar(i, j)

    last = HIST - 1
    scaling = s_bar(last, last) / bar_bar(last, last)

    def energy(n):
        value = row(ROW_BASE + 16 + n)
        for j in range(4):
            value = value + mix[j] * row(ROW_W + 17 * j + n)
        return value

    chem = energy(16) / row(ROW_BASE + 33)

    def gradient(n):
        return energy(n) - chem * row(ROW_BASE + n)

    s_grad = [gradient(i) for i in pairs]
    bar_grad = [theta[i] * gradient(HIST + i) + rest[i] * s_grad[i] for i in pairs]

    first = [None] * HIST
    pending = list(s_grad)
    for j in reversed(pairs):
        first[j] = inverse[j] * pending[j]
        for i in range(j):
            pending[i] = pending[i] - first[j] * s_bar(i, j)
    pending = list(bar_grad)
    for j in pairs:
        for i in pairs:
            pending[i] = pending[i] - first[j] * bar_bar(i, j)
    pending = [scaling * value for value in pending]
    step_mix, change_mix = [], []
    for j in pairs:
        net = first[j] - inverse[j] * pending[j]
        for i in range(j + 1, HIST):
            pending[i] = pending[i] + net * s_bar(j, i)
        change_mix.append((-step_length) * (-scaling * first[j] * theta[j]))
        step_mix.append((-step_length) * (net - scaling * first[j] * rest[j]))

    wide = lambda value: jnp.broadcast_to(value, (8, LANES))
    mix = [wide(value) for value in mix]
    chem, gain = wide(chem), wide((-step_length) * scaling)
    step_mix = [wide(value) for value in step_mix]
    change_mix = [wide(value) for value in change_mix]
    basis = (v0, v1, v2, v3)

    def leave(i):
        return [
            pltpu.make_async_copy(here.at[i], out.at[i], sems.at[n, i])
            for n, (here, out) in enumerate(((density_here, new_density), (hartree_here, new_hartree)))
        ]

    for i in range(REACH):
        for b in range(8):
            at = pl.ds(8 * b, 8)
            rho = both[REACH + i, at, :]
            lift = mix[0] * v0[i, at, :]
            for j in range(1, 4):
                lift = lift + mix[j] * basis[j][i, at, :]
            hartree_here[i, at, :] = both[i, at, :] + lift
            slope = grad[i, at, :] + 2.0 * rho * lift - chem * rho
            parts = [rho, gain * slope, step_mix[0] * steps[0, i, at, :], change_mix[0] * changes[0, i, at, :]]
            for f in range(1, HIST):
                parts[2] = parts[2] + step_mix[f] * steps[f, i, at, :]
                parts[3] = parts[3] + change_mix[f] * changes[f, i, at, :]
            density_here[i, at, :] = parts[0] + (parts[1] + (parts[2] + parts[3]))
        for copy in leave(i):
            copy.start()
    for i in range(REACH):
        for copy in leave(i):
            copy.wait()


def call(kernel, outs, args, scratch=(), flops=0, in_hbm=(), out_hbm=False):
    args = [pltpu.with_memory_space_constraint(x, pltpu.HBM) if n in in_hbm else x for n, x in enumerate(args)]
    shapes = [jax.ShapeDtypeStruct(shape, jnp.float32) for shape in outs]
    size = sum(4 * math.prod(a.shape) for a in (*args, *shapes))
    return pl.pallas_call(
        kernel,
        out_shape=shapes,
        in_specs=[pl.BlockSpec(memory_space=pltpu.HBM if n in in_hbm else pltpu.VMEM) for n in range(len(args))],
        out_specs=[pl.BlockSpec(memory_space=pltpu.HBM if out_hbm else pltpu.VMEM)] * len(outs),
        scratch_shapes=[pltpu.VMEM(s, jnp.float32) if isinstance(s, tuple) else s for s in scratch],
        cost_estimate=pl.CostEstimate(flops=flops, bytes_accessed=size, transcendentals=0),
        compiler_params=pltpu.CompilerParams(vmem_limit_bytes=VMEM_LIMIT),
    )(*args)


def ring(axis, step):
    size = lax.axis_size(axis)
    return [(i, (i + step) % size) for i in range(size)]


def swap(axis, odd_up):
    size = lax.axis_size(axis)
    return [(i, (i + (1 if i % 2 == odd_up else -1)) % size) for i in range(size)]


def after(values, *earlier):
    return lax.optimization_barrier((tuple(values), earlier))[0]


def x_halo(block):
    far = lax.ppermute(block, "blk", swap("blk", 1))
    return (lax.ppermute(block, "blk", swap("blk", 0)), far)


def z_halo(face_a, face_b):
    return (lax.ppermute(face_a, "gz", swap("gz", 0)), lax.ppermute(face_b, "gz", swap("gz", 1)))


def on_device(sqrt_density, ion_charge, ion_potential, hartree_prev, hist_steps, hist_changes):
    block = sqrt_density.shape
    ext = (block[0], block[1] + 16, block[2])
    face = (24, LANES)
    cells = math.prod(block)
    history = (hist_steps, hist_changes)
    cells = math.prod(block)
    history = (hist_steps, hist_changes)
    work = 300 * cells
    inputs = (hartree_prev, sqrt_density, ion_charge)
    halo = x_halo(hartree_prev)
    both, charge, *faces = call(
        launch_kernel,
        [(2 * REACH, *block[1:]), block, (48, LANES), (48, LANES)],
        inputs,
        [pltpu.SemaphoreType.DMA((3,))],
        in_hbm=(0, 1, 2),
    )
    ends = z_halo(*faces)
    density_ends = ends
    half = (REACH, block[1] // 2, LANES)

    def advance(gain, inner, halo, ends, last=False):
        (mid,) = call(functools.partial(z_kernel, gain), [block], [inner, *ends], flops=work)
        return call(
            functools.partial(last_x_kernel if last else x_kernel, gain),
            [block, half, half] if last else [block],
            [mid, *halo],
            flops=work,
        )

    def exchange(block_now):
        halo = x_halo(block_now)
        return halo, z_halo(*call(pack_kernel, [face, face], [block_now], flops=work))

    (inner,) = call(side_one, [block], [both, charge], [ext], work)
    density_far = lax.ppermute(after((sqrt_density,), *faces)[0], "blk", swap("blk", 1))
    (mid,) = call(functools.partial(z_kernel, 1.0), [block], [inner, *ends], flops=work)
    density_near = lax.ppermute(after((sqrt_density,), mid)[0], "blk", swap("blk", 0))
    (v0,) = call(functools.partial(x_kernel, 1.0), [block], [mid, *halo], flops=work)
    halo, ends = exchange(v0)
    inner, grad, r2, m2 = call(
        side_two,
        [block, block, (24, LANES), (8, LANES)],
        [v0, both, density_near, density_far, *density_ends, ion_potential, hist_steps],
        [ext],
        work,
    )
    (v1,) = advance(-1.0 / SHIFT, inner, halo, ends)
    halo, ends = exchange(v1)
    inner, r3, m3 = call(
        side_three, [block, (104, LANES), (8, LANES)], [v0, v1, both, *history], [ext], work
    )
    (v2,) = advance(-2.0 / SHIFT, inner, halo, ends)
    halo, ends = exchange(v2)
    inner, r4, m4 = call(
        side_four, [block, (112, LANES), (8, LANES)], [v1, v2, both, grad, *history], [ext], work
    )
    v3, to_near, to_far = advance(-2.0 / SHIFT, inner, halo, ends, last=True)
    far = lax.ppermute(to_far, "blk", swap("blk", 1))
    near = lax.ppermute(to_near, "blk", swap("blk", 0))
    (upper,) = call(pack_upper_kernel, [face], [v3], flops=work)
    z_left = lax.ppermute(upper, "gz", ring("gz", 1))
    kept, given = call(
        side_five,
        [(1, LANES), (1, LANES)],
        [v2, v3, both, *history, r2, r3, r4, m2, m3, m4],
        [(2 * LANES, LANES), (8, LANES)],
        work,
    )
    taken = lax.ppermute(given, "blk", swap("blk", 0))
    (inner,) = call(inner_moment_kernel, [(8, LANES)], [after((v3,), given)[0]], [ext], work)
    row, part = call(couple_kernel, [(1, LANES), (8, LANES)], [v3, z_left, inner, kept, taken], flops=work)
    devices = lax.axis_size("blk") * lax.axis_size("gz")
    (outgoing,) = call(send_kernel, [(devices, LANES)], [v3, far, near, part, row], flops=work)
    received = lax.all_to_all(outgoing.reshape(devices, 1, LANES), ("blk", "gz"), 0, 0, tiled=True)
    return tuple(
        call(
            final_kernel,
            [block, block],
            [received.reshape(devices, LANES), both, grad, v0, v1, v2, v3, *history],
            [(3 * LANES, LANES), block, block, pltpu.SemaphoreType.DMA((2, REACH))],
            work,
            out_hbm=True,
        )
    )


def solution(mesh):
    placed = (
        P("blk", None, "gz"),
        P("blk", None, "gz"),
        P("blk", None, "gz"),
        P("blk", None, "gz"),
        P(None, "blk", None, "gz"),
        P(None, "blk", None, "gz"),
    )
    return jax.shard_map(
        on_device,
        mesh=mesh,
        in_specs=placed,
        out_specs=(P("blk", None, "gz"), P("blk", None, "gz")),
        check_vma=False,
    )
```

```python
import functools
import math

import jax
import jax.numpy as jnp
from jax import lax
from jax.experimental import pallas as pl
from jax.experimental.pallas import tpu as pltpu
from jax.sharding import PartitionSpec as P

center = -5369.0 / 1800.0
coeffs = (12.0 / 7.0, -15.0 / 56.0, 10.0 / 189.0, -1.0 / 112.0, 2.0 / 825.0, -1.0 / 4752.0)
screen = 0.0025
spacing = 0.28
source_scale = 4.0 * math.pi * spacing * spacing
tf_scale = 5.0 / 3.0 * 2.871234
step_length = 0.01
damp_floor = 0.2

SHIFT = 2.0
HIST = 8
REACH = 6
LANES = 128
VMEM_LIMIT = 24 * 1024 * 1024

ROW_GRAM = 0
ROW_BASE = 136
ROW_W = 170
ROW_MOM = 238
HALF = 126


def place(n):
    return n if n < HALF else n + LANES - HALF


MOM_LANE = place(ROW_MOM) - LANES
PAIRS = tuple((i, j) for i in range(HIST) for j in range(i, HIST))
PAIR_ROW = {pair: row for row, pair in enumerate(PAIRS)}


def two_sum(a, b):
    s = a + b
    bb = s - a
    return s, (a - (s - bb)) + (b - bb)


def quick_sum(a, b):
    s = a + b
    return s, b - (s - a)


def split(a):
    t = 4097.0 * a
    hi = t - (t - a)
    return hi, a - hi


def two_prod(a, b):
    p = a * b
    ah, al = split(a)
    bh, bl = split(b)
    return p, ((ah * bh - p) + ah * bl + al * bh) + al * bl


def df_add(a, b):
    s, e = two_sum(a[0], b[0])
    return quick_sum(s, e + (a[1] + b[1]))


def df_neg(a):
    return (-a[0], -a[1])


def df_sub(a, b):
    return df_add(a, df_neg(b))


def df_scale(a, factor):
    return (a[0] * factor, a[1] * factor)


def df_mul(a, b):
    p, e = two_prod(a[0], b[0])
    return quick_sum(p, e + (a[0] * b[1] + a[1] * b[0]))


def df_over(a, b, inverse):
    q = a[0] * inverse
    p, e = two_prod(q, b[0])
    rest = ((a[0] - p) - e) + (a[1] - q * b[1])
    return quick_sum(q, rest * inverse)


def lane_ids(shape):
    return lax.broadcasted_iota(jnp.int32, shape, len(shape) - 1)


def inner_plane(i, own, ext):
    values = own[i]
    rows = values.shape[0]
    lane = lane_ids((rows, LANES))
    total = (3.0 * center) * values
    for k, weight in enumerate(coeffs, 1):
        pair = ext[i, 8 + k : 8 + k + rows, :] + ext[i, 8 - k : 8 - k + rows, :]
        if i + k < REACH:
            pair = pair + own[i + k]
        if i - k >= 0:
            pair = pair + own[i - k]
        up = pltpu.roll(jnp.where(lane < k, 0.0, values), LANES - k, 1)
        down = pltpu.roll(jnp.where(lane >= LANES - k, 0.0, values), k, 1)
        total = total + weight * (pair + (up + down))
    return total, values


def edge_faces(z_left, z_right):
    lane = lane_ids((24, LANES)) % 8
    lower = jnp.zeros((24, LANES), jnp.float32)
    upper = jnp.zeros((24, LANES), jnp.float32)
    for k, weight in enumerate(coeffs, 1):
        lower = lower + jnp.where(lane < k, weight * pltpu.roll(z_left, LANES - 8 + k, 1), 0.0)
        if z_right is not None:
            upper = upper + jnp.where(lane >= 8 - k, weight * pltpu.roll(z_right, 8 - k, 1), 0.0)
    return lower, upper


def side_plane(i, block, below, rows=slice(None)):
    total = None
    for k, weight in enumerate(coeffs, 1):
        layer = i - k + REACH if below else i + k - REACH
        if 0 <= layer < REACH:
            term = weight * block[layer, rows, :]
            total = term if total is None else total + term
    return total


def z_plane(i, faces, tiles=8):
    lane = lane_ids((8, LANES))
    lower, upper = (face[8 * (i // 2) : 8 * (i // 2) + 8] for face in faces)
    out = []
    for b in range(tiles):
        j = 8 * (i % 2) + b
        tile = jnp.where(lane < 8, pltpu.roll(lower, (LANES - 8 * j) % LANES, 1), 0.0)
        tile = jnp.where(lane >= LANES - 8, pltpu.roll(upper, (2 * LANES - 8 - 8 * j) % LANES, 1), tile)
        out.append(tile)
    return jnp.concatenate(out, axis=0)


def fill_ext(own, ext):
    rows = own.shape[1]
    ext[:, 8 : 8 + rows, :] = own[...]
    ext[:, 0:8, :] = own[:, rows - 8 : rows, :]
    ext[:, 8 + rows : 16 + rows, :] = own[:, 0:8, :]


def pack_faces(src, layers):
    lane = lane_ids((8, LANES))
    firsts, lasts = [], []
    for m in range(3):
        first = jnp.zeros((8, LANES), jnp.float32)
        last = jnp.zeros((8, LANES), jnp.float32)
        for j in range(16):
            n = 16 * m + j
            tile = src[layers + n // 8, 8 * (n % 8) : 8 * (n % 8) + 8, :]
            here = (lane >= 8 * j) & (lane < 8 * j + 8)
            first = jnp.where(here, pltpu.roll(tile, 8 * j, 1) if j else tile, first)
            last = jnp.where(here, pltpu.roll(tile, (8 * j + 8) % LANES, 1) if j < 15 else tile, last)
        firsts.append(first)
        lasts.append(last)
    return jnp.concatenate(firsts, axis=0), jnp.concatenate(lasts, axis=0)


def is_odd(axis):
    return lax.rem(lax.axis_index(axis), 2) == 1


def by_partner(lower, upper):
    odd = is_odd("gz")
    return jnp.where(odd, lower, upper), jnp.where(odd, upper, lower)


def by_side(first, second):
    odd = is_odd("gz")
    return jnp.where(odd, first, second), jnp.where(odd, second, first)


def with_sides(body):
    odd = is_odd("blk")

    @pl.when(odd)
    def _():
        body(True, False)

    @pl.when(jnp.logical_not(odd))
    def _():
        body(False, True)


def fold(hi, lo, axis, steps):
    for step in steps:
        hi, err = two_sum(hi, pltpu.roll(hi, step, axis))
        lo = lo + pltpu.roll(lo, step, axis) + err
    return hi, lo


def fold_rows(acc):
    hi, lo = fold(*acc, 0, (4, 2, 1))
    return hi[0:1], lo[0:1]


def fold_lanes(hi, lo):
    return quick_sum(*fold(hi, lo, 1, (64, 32, 16, 8, 4, 2, 1)))


def add_tile(acc, product):
    hi, err = two_sum(acc[0], product)
    return hi, acc[1] + err


def tile_of(ref, i, b):
    return ref[i, 8 * b : 8 * b + 8, :]


def store_moments(pairs, moments):
    zero = jnp.zeros((8, LANES), jnp.float32)

    def body(i, accs):
        for b in range(8):
            accs = tuple(
                add_tile(acc, tile_of(a, i, b) * tile_of(c, i, b)) for acc, (a, c) in zip(accs, pairs)
            )
        return accs

    accs = lax.fori_loop(0, REACH, body, tuple((zero, zero) for _ in pairs))
    for n, acc in enumerate(accs):
        moments[2 * n : 2 * n + 1, :], moments[2 * n + 1 : 2 * n + 2, :] = fold_rows(acc)


def collapse(acc):
    return jnp.sum(acc, axis=0, keepdims=True)


def launch_kernel(hartree, density, charge, both, charge_here, face_a, face_b, sems):
    places = (both.at[pl.ds(0, REACH)], both.at[pl.ds(REACH, REACH)], charge_here)
    copies = [
        pltpu.make_async_copy(src, dst, sems.at[n])
        for n, (src, dst) in enumerate(zip((hartree, density, charge), places))
    ]
    for copy in copies:
        copy.start()
    for n in range(2):
        copies[n].wait()
        rows = slice(24 * n, 24 * n + 24)
        face_a[rows, :], face_b[rows, :] = by_partner(*pack_faces(both, REACH * n))
    copies[2].wait()


def inner_residual(both, charge, out, ext):
    hartree = both.at[pl.ds(0, REACH)]
    fill_ext(hartree, ext)
    for i in range(REACH):
        lap, values = inner_plane(i, hartree, ext)
        rho = both[REACH + i]
        out[i] = source_scale * (rho * rho - charge[i]) - (screen * values - lap)


def inner_basis(own, prior, out, ext):
    fill_ext(own, ext)
    for i in range(REACH):
        lap, values = inner_plane(i, own, ext)
        moved = (screen / SHIFT - 1.0) * values - (1.0 / SHIFT) * lap
        out[i] = moved if prior is None else 2.0 * moved - prior[i]


def z_kernel(gain, inner, z_first, z_second, out):
    faces = edge_faces(*by_side(z_first[0:24, :], z_second[0:24, :]))
    for i in range(REACH):
        out[i] = inner[i] + gain * z_plane(i, faces)


def x_kernel(gain, inner, near, far, out):
    def body(near_below, far_below):
        for i in range(REACH):
            out[i] = inner[i] + gain * (side_plane(i, near, near_below) + side_plane(i, far, far_below))

    with_sides(body)


def last_x_kernel(gain, inner, near, far, out, to_near, to_far):
    half = out.shape[1] // 2

    def body(near_below, far_below):
        for i in range(REACH):
            plane = inner[i] + gain * (side_plane(i, near, near_below) + side_plane(i, far, far_below))
            out[i] = plane
            for ref, below in ((to_near, near_below), (to_far, far_below)):
                ref[i] = plane[:half] if below else plane[half:]

    with_sides(body)


def pack_kernel(block, face_a, face_b):
    face_a[...], face_b[...] = by_partner(*pack_faces(block, 0))


def pack_upper_kernel(block, face):
    face[...] = pack_faces(block, 0)[1]


def store(rows, base, values):
    for n, value in enumerate(values):
        rows[base + n : base + n + 1, :] = value


def gram_dots(left, right, pairs):
    zero = jnp.zeros((8, LANES), jnp.float32)

    def body(i, accs):
        for b in range(8):
            at = pl.ds(8 * b, 8)
            l_tiles = {p: left[p, i, at, :] for p in sorted({p for p, _ in pairs})}
            if left is right:
                r_tiles = l_tiles
            else:
                r_tiles = {q: right[q, i, at, :] for q in sorted({q for _, q in pairs})}
            accs = tuple(acc + l_tiles[p] * r_tiles[q] for acc, (p, q) in zip(accs, pairs))
        return accs

    accs = lax.fori_loop(0, REACH, body, tuple(zero for _ in pairs))
    return [collapse(acc) for acc in accs]


CROSS_PAIRS = tuple((i, j) for i in range(HIST) for j in range(HIST))


def field_dots(groups, others, plain=()):
    zero = jnp.zeros((8, LANES), jnp.float32)
    fields = [(group, f) for group in groups for f in range(HIST)]
    count = len(fields)

    def body(i, accs):
        accs = list(accs)
        for b in range(8):
            at = pl.ds(8 * b, 8)
            tiles = [other(i, b) for other in others]
            for f, (group, which) in enumerate(fields):
                field = group[which, i, at, :]
                for o, tile in enumerate(tiles):
                    accs[o * count + f] = accs[o * count + f] + field * tile
            for n, (one, two) in enumerate(plain, len(others) * count):
                accs[n] = accs[n] + one(i, b) * two(i, b)
        return tuple(accs)

    total = count * len(others) + len(plain)
    return [collapse(acc) for acc in lax.fori_loop(0, REACH, body, (zero,) * total)]


def base_gradient(both, near, far, z_first, z_second, potential, grad, ext):
    hartree = both.at[pl.ds(0, REACH)]
    density = both.at[pl.ds(REACH, REACH)]
    fill_ext(density, ext)
    faces = edge_faces(*by_side(z_first[24:48, :], z_second[24:48, :]))

    def body(near_below, far_below):
        for i in range(REACH):
            grad[i] = side_plane(i, near, near_below) + side_plane(i, far, far_below) + z_plane(i, faces)

    with_sides(body)
    for i in range(REACH):
        lap, rho = inner_plane(i, density, ext)
        power = jnp.exp(jnp.log(rho) * (4.0 / 3.0))
        grad[i] = 2.0 * rho * (hartree[i] + potential[i] + tf_scale * power) - (lap + grad[i]) * (
            1.0 / (spacing * spacing)
        )


def density_tile(both):
    return lambda i, b: tile_of(both, REACH + i, b)


def lifted_tile(both, vector):
    return lambda i, b: 2.0 * tile_of(both, REACH + i, b) * tile_of(vector, i, b)


FETCHES = 4


def side_one(both, charge, steps, changes, inner, steps_here, changes_here, rows, ext, sems):
    each = HIST // FETCHES
    copies = [
        pltpu.make_async_copy(src.at[pl.ds(each * n, each)], dst.at[pl.ds(each * n, each)], sems.at[FETCHES * m + n])
        for m, (src, dst) in enumerate(((steps, steps_here), (changes, changes_here)))
        for n in range(FETCHES)
    ]
    for copy in copies:
        copy.start()
    inner_residual(both, charge, inner, ext)
    for copy in copies[:FETCHES]:
        copy.wait()
    store(rows, 0, gram_dots(steps_here, steps_here, PAIRS))
    store(rows, 36, field_dots((steps_here,), [density_tile(both)]))
    for copy in copies[FETCHES:]:
        copy.wait()


def side_two(vector, inner, ext):
    inner_basis(vector, None, inner, ext)


def side_three(prior, vector, both, near, far, z_first, z_second, potential, steps, changes, *outs):
    inner, grad, rows, moments, ext = outs
    inner_basis(vector, prior, inner, ext)
    before, lifted, rho = lifted_tile(both, prior), lifted_tile(both, vector), density_tile(both)
    values = field_dots((steps, changes), [before, lifted], [(rho, before), (rho, lifted)])
    store(rows, 0, values[:16] + values[32:33] + values[16:32] + values[33:])
    store(rows, 34, gram_dots(steps, changes, CROSS_PAIRS[:32]))
    store_moments([(prior, prior), (prior, vector), (vector, vector)], moments)
    base_gradient(both, near, far, z_first, z_second, potential, grad, ext)


def side_four(prior, vector, both, grad, steps, changes, inner, rows, moments, ext):
    inner_basis(vector, prior, inner, ext)
    lifted, rho = lifted_tile(both, vector), density_tile(both)
    slope = lambda i, b: tile_of(grad, i, b)
    by_step = field_dots((steps,), [lifted, slope], [(rho, lifted), (rho, slope), (rho, rho)])
    by_change = field_dots((changes,), [lifted, slope, rho])
    values = by_step[:8] + by_change[:8] + by_step[16:17] + by_step[8:16] + by_change[8:16] + by_step[17:]
    store(rows, 0, values + by_change[16:])
    store(rows, 43, gram_dots(changes, changes, PAIRS))
    store(rows, 79, gram_dots(steps, changes, CROSS_PAIRS[32:]))
    store_moments([(prior, vector), (vector, vector)], moments)


def side_five(prior, vector, both, steps, changes, r1, r3, r4, m3, m4, kept, given, table, m5):
    lifted, rho = lifted_tile(both, vector), density_tile(both)
    own = field_dots((steps, changes), [lifted], [(rho, lifted)])
    store_moments([(prior, vector), (vector, vector)], m5)
    table[...] = jnp.zeros_like(table)

    def put(base, ref, start, count):
        before = max(0, min(count, HALF - base))
        if before:
            table[base : base + before, :] = ref[start : start + before, :]
        if before < count:
            at = place(base + before)
            table[at : at + count - before, :] = ref[start + before : start + count, :]

    put(ROW_GRAM, r1, 0, 36)
    put(ROW_GRAM + 36, r4, 43, 36)
    put(ROW_GRAM + 72, r3, 34, 32)
    put(ROW_GRAM + 104, r4, 79, 32)
    put(ROW_BASE, r1, 36, 8)
    put(ROW_BASE + 8, r4, 35, 8)
    put(ROW_BASE + 16, r4, 17, 18)
    put(ROW_W, r3, 0, 34)
    put(ROW_W + 34, r4, 0, 17)
    store(table, place(ROW_W + 51), own)

    order = [(m3, 0), (m3, 1), (m3, 2), (m4, 0), (m4, 1), (m5, 0), (m5, 1)]
    zero = jnp.zeros((1, LANES), jnp.float32)
    parts = [
        jnp.concatenate([ref[2 * which + low : 2 * which + low + 1, :] for ref, which in order] + [zero], axis=0)
        for low in range(2)
    ]
    hi, lo = fold_lanes(*parts)
    lane = lane_ids((1, LANES))
    first = jnp.sum(jnp.transpose(table[0:LANES, :]), axis=0, keepdims=True)
    second = jnp.sum(jnp.transpose(table[LANES : 2 * LANES, :]), axis=0, keepdims=True)
    for n in range(7):
        second = jnp.where(lane == MOM_LANE + n, hi[n : n + 1], second)
        second = jnp.where(lane == MOM_LANE + 7 + n, lo[n : n + 1], second)
    odd = is_odd("blk")
    kept[...] = jnp.where(odd, second, first)
    given[...] = jnp.where(odd, first, second)


def inner_moment_kernel(vector, inner, ext):
    fill_ext(vector, ext)
    zero = jnp.zeros((8, LANES), jnp.float32)
    accs = [(zero, zero) for _ in range(2)]
    for i in range(REACH):
        lap, values = inner_plane(i, vector, ext)
        product = values * ((screen / SHIFT - 1.0) * values - (1.0 / SHIFT) * lap)
        for b in range(8):
            accs[b % 2] = add_tile(accs[b % 2], product[8 * b : 8 * b + 8])
    hi, err = two_sum(accs[0][0], accs[1][0])
    inner[0:1, :], inner[1:2, :] = fold_rows((hi, accs[0][1] + accs[1][1] + err))


def couple(own, block, below, acc):
    half = own.shape[1] // 2
    for i in range(REACH):
        product = own[i, half:, :] * side_plane(i, block, True) if below else own[i, :half, :] * side_plane(i, block, False)
        for b in range(half // 8):
            acc = add_tile(acc, product[8 * b : 8 * b + 8])
    return acc


def couple_kernel(own, z_left, inner, kept, taken, row, part):
    zero = jnp.zeros((8, LANES), jnp.float32)
    faces = edge_faces(z_left[...], None)
    acc = (zero, zero)
    for i in range(REACH):
        product = own[i] * z_plane(i, faces)
        for b in range(8):
            acc = add_tile(acc, product[8 * b : 8 * b + 8])
    sides = df_scale(fold_rows(acc), -2.0 / SHIFT)
    part[0:1, :], part[1:2, :] = df_add(sides, (inner[0:1, :], inner[1:2, :]))
    lane = lane_ids((1, LANES))
    total, err = two_sum(kept[...], taken[...])
    low_lane = (lane >= MOM_LANE + 7) & (lane < MOM_LANE + 14) & is_odd("blk")
    row[...] = jnp.where(low_lane, total + pltpu.roll(err, 7, 1), total)


def send_kernel(own, far, near, part, row, out):
    zero = jnp.zeros((8, LANES), jnp.float32)

    def body(near_below, far_below):
        acc = couple(own, far, far_below, couple(own, near, near_below, (zero, zero)))
        hi, lo = fold_lanes(*df_add(df_scale(fold_rows(acc), -2.0 / SHIFT), (part[0:1, :], part[1:2, :])))
        lane = lane_ids((1, LANES))
        value = jnp.where(lane == HALF, hi, jnp.where(lane == HALF + 1, lo, row[...]))
        out[...] = jnp.broadcast_to(value, out.shape)

    with_sides(body)


def solve_krylov(moment):
    n00, n01, n11, n12, n22, n23, n33, n34 = moment
    nu = [n00, n01]
    nu.append(df_sub(df_scale(n11, 2.0), n00))
    nu.append(df_sub(df_scale(n12, 2.0), n01))
    nu.append(df_sub(df_scale(n22, 2.0), n00))
    nu.append(df_sub(df_scale(n23, 2.0), n01))
    nu.append(df_sub(df_scale(n33, 2.0), n00))

    def gram(i, j):
        if i == j == 0:
            return n00
        return df_scale(df_add(nu[i + j], nu[abs(i - j)]), 0.5)

    def moved(i, j):
        if i == 3 and j == 3:
            return n34
        if j == 0:
            return gram(i, 1)
        return df_scale(df_add(gram(i, j + 1), gram(i, j - 1)), 0.5)

    mat = {(i, j): df_add(moved(i, j), gram(i, j)) for i in range(4) for j in range(i + 1)}
    rhs = [df_scale(gram(i, 0), 1.0 / SHIFT) for i in range(4)]
    low, inverse = {}, []
    for k in range(4):
        inverse.append(1.0 / mat[k, k][0])
        for i in range(k + 1, 4):
            low[i, k] = df_over(mat[i, k], mat[k, k], inverse[k])
        for i in range(k + 1, 4):
            for j in range(k + 1, i + 1):
                mat[i, j] = df_sub(mat[i, j], df_mul(low[i, k], mat[j, k]))
            rhs[i] = df_sub(rhs[i], df_mul(low[i, k], rhs[k]))
    sol = [None] * 4
    for k in reversed(range(4)):
        value = df_over(rhs[k], mat[k, k], inverse[k])
        for i in range(k + 1, 4):
            value = df_sub(value, df_mul(low[i, k], sol[i]))
        sol[k] = value
    return [hi + lo for hi, lo in sol]


def final_kernel(received, both, grad, v0, v1, v2, v3, steps, changes, new_density, new_hartree, spread, density_here, hartree_here, sems):
    parts = [(received[8 * n : 8 * n + 8, :], jnp.zeros((8, LANES), jnp.float32)) for n in range(4)]
    for n in range(4, received.shape[0] // 8):
        parts[n % 4] = add_tile(parts[n % 4], received[8 * n : 8 * n + 8, :])
    while len(parts) > 1:
        half = len(parts) // 2
        merged = []
        for a, b in zip(parts[:half], parts[half:]):
            hi, err = two_sum(a[0], b[0])
            merged.append((hi, a[1] + b[1] + err))
        parts = merged
    hi, lo = fold(*parts[0], 0, (1, 2))
    lane = lane_ids((1, LANES))
    last, err = two_sum(hi[3:4], hi[7:8])
    err = err + (lo[3:4] + lo[7:8])
    first = hi[3:4]
    second = jnp.where(lane >= HALF, last, hi[7:8])
    low = jnp.where(lane >= HALF, err, lo[7:8])
    low = low + jnp.where(lane == HALF, pltpu.roll(second, LANES - 1, 1), pltpu.roll(second, LANES - 7, 1))
    for n, value in enumerate((first, second, low)):
        spread[LANES * n : LANES * n + LANES, :] = jnp.transpose(jnp.broadcast_to(value, (LANES, LANES)))

    def row(n):
        return spread[place(n) : place(n) + 1, :]

    def moment(n):
        at = LANES + (MOM_LANE + n if n < 7 else HALF)
        return quick_sum(spread[at : at + 1, :], spread[LANES + at : LANES + at + 1, :])

    mix = solve_krylov([moment(n) for n in range(8)])

    def s_s(i, j):
        return row(ROW_GRAM + PAIR_ROW[min(i, j), max(i, j)])

    def y_y(i, j):
        return row(ROW_GRAM + 36 + PAIR_ROW[min(i, j), max(i, j)])

    def s_y(i, j):
        return row(ROW_GRAM + 72 + 8 * i + j)

    pairs = range(HIST)
    theta, rest, inverse = [], [], []
    for i in pairs:
        curv, norm = s_y(i, i), s_s(i, i)
        kept = (1.0 - damp_floor) * norm
        damp = jnp.where(curv >= damp_floor * norm, 1.0, kept / jnp.maximum(norm - curv, kept))
        theta.append(damp)
        rest.append(1.0 - damp)
        inverse.append(1.0 / (damp * curv + (1.0 - damp) * norm))

    def s_bar(i, j):
        return theta[j] * s_y(i, j) + rest[j] * s_s(i, j)

    def bar_bar(i, j):
        return theta[i] * (theta[j] * y_y(i, j) + rest[j] * s_y(j, i)) + rest[i] * s_bar(i, j)

    last = HIST - 1
    scaling = s_bar(last, last) / bar_bar(last, last)

    def energy(n):
        value = row(ROW_BASE + 16 + n)
        for j in range(4):
            value = value + mix[j] * row(ROW_W + 17 * j + n)
        return value

    chem = energy(16) / row(ROW_BASE + 33)

    def gradient(n):
        return energy(n) - chem * row(ROW_BASE + n)

    s_grad = [gradient(i) for i in pairs]
    bar_grad = [theta[i] * gradient(HIST + i) + rest[i] * s_grad[i] for i in pairs]

    first = [None] * HIST
    pending = list(s_grad)
    for j in reversed(pairs):
        first[j] = inverse[j] * pending[j]
        for i in range(j):
            pending[i] = pending[i] - first[j] * s_bar(i, j)
    pending = list(bar_grad)
    for j in pairs:
        for i in pairs:
            pending[i] = pending[i] - first[j] * bar_bar(i, j)
    pending = [scaling * value for value in pending]
    step_mix, change_mix = [], []
    for j in pairs:
        net = first[j] - inverse[j] * pending[j]
        for i in range(j + 1, HIST):
            pending[i] = pending[i] + net * s_bar(j, i)
        change_mix.append((-step_length) * (-scaling * first[j] * theta[j]))
        step_mix.append((-step_length) * (net - scaling * first[j] * rest[j]))

    wide = lambda value: jnp.broadcast_to(value, (8, LANES))
    mix = [wide(value) for value in mix]
    chem, gain = wide(chem), wide((-step_length) * scaling)
    step_mix = [wide(value) for value in step_mix]
    change_mix = [wide(value) for value in change_mix]
    basis = (v0, v1, v2, v3)

    def leave(i):
        return [
            pltpu.make_async_copy(here.at[i], out.at[i], sems.at[n, i])
            for n, (here, out) in enumerate(((density_here, new_density), (hartree_here, new_hartree)))
        ]

    for i in range(REACH):
        for b in range(8):
            at = pl.ds(8 * b, 8)
            rho = both[REACH + i, at, :]
            lift = mix[0] * v0[i, at, :]
            for j in range(1, 4):
                lift = lift + mix[j] * basis[j][i, at, :]
            hartree_here[i, at, :] = both[i, at, :] + lift
            slope = grad[i, at, :] + 2.0 * rho * lift - chem * rho
            parts = [rho, gain * slope, step_mix[0] * steps[0, i, at, :], change_mix[0] * changes[0, i, at, :]]
            for f in range(1, HIST):
                parts[2] = parts[2] + step_mix[f] * steps[f, i, at, :]
                parts[3] = parts[3] + change_mix[f] * changes[f, i, at, :]
            density_here[i, at, :] = parts[0] + (parts[1] + (parts[2] + parts[3]))
        for copy in leave(i):
            copy.start()
    for i in range(REACH):
        for copy in leave(i):
            copy.wait()


def call(kernel, outs, args, scratch=(), flops=0, in_hbm=(), out_hbm=False):
    args = [pltpu.with_memory_space_constraint(x, pltpu.HBM) if n in in_hbm else x for n, x in enumerate(args)]
    shapes = [jax.ShapeDtypeStruct(shape, jnp.float32) for shape in outs]
    size = sum(4 * math.prod(a.shape) for a in (*args, *shapes))
    return pl.pallas_call(
        kernel,
        out_shape=shapes,
        in_specs=[pl.BlockSpec(memory_space=pltpu.HBM if n in in_hbm else pltpu.VMEM) for n in range(len(args))],
        out_specs=[pl.BlockSpec(memory_space=pltpu.HBM if out_hbm else pltpu.VMEM)] * len(outs),
        scratch_shapes=[pltpu.VMEM(s, jnp.float32) if isinstance(s, tuple) else s for s in scratch],
        cost_estimate=pl.CostEstimate(flops=flops, bytes_accessed=size, transcendentals=0),
        compiler_params=pltpu.CompilerParams(vmem_limit_bytes=VMEM_LIMIT),
    )(*args)


def ring(axis, step):
    size = lax.axis_size(axis)
    return [(i, (i + step) % size) for i in range(size)]


def swap(axis, odd_up):
    size = lax.axis_size(axis)
    return [(i, (i + (1 if i % 2 == odd_up else -1)) % size) for i in range(size)]


def after(values, *earlier):
    return lax.optimization_barrier((tuple(values), earlier))[0]


def x_halo(block):
    far = lax.ppermute(block, "blk", swap("blk", 1))
    return (lax.ppermute(block, "blk", swap("blk", 0)), far)


def z_halo(face_a, face_b):
    return (lax.ppermute(face_a, "gz", swap("gz", 0)), lax.ppermute(face_b, "gz", swap("gz", 1)))


def on_device(sqrt_density, ion_charge, ion_potential, hartree_prev, hist_steps, hist_changes):
    block = sqrt_density.shape
    ext = (block[0], block[1] + 16, block[2])
    face = (24, LANES)
    cells = math.prod(block)
    cells = math.prod(block)
    work = 300 * cells
    inputs = (hartree_prev, sqrt_density, ion_charge)
    halo = x_halo(hartree_prev)
    both, charge, *faces = call(
        launch_kernel,
        [(2 * REACH, *block[1:]), block, (48, LANES), (48, LANES)],
        inputs,
        [pltpu.SemaphoreType.DMA((3,))],
        in_hbm=(0, 1, 2),
    )
    ends = z_halo(*faces)
    density_ends = ends
    half = (REACH, block[1] // 2, LANES)

    def advance(gain, inner, halo, ends, last=False):
        (mid,) = call(functools.partial(z_kernel, gain), [block], [inner, *ends], flops=work)
        return call(
            functools.partial(last_x_kernel if last else x_kernel, gain),
            [block, half, half] if last else [block],
            [mid, *halo],
            flops=work,
        )

    def exchange(block_now):
        halo = x_halo(block_now)
        return halo, z_halo(*call(pack_kernel, [face, face], [block_now], flops=work))

    stored = hist_steps.shape
    inner, *history, r1 = call(
        side_one,
        [block, stored, stored, (48, LANES)],
        [both, charge, hist_steps, hist_changes],
        [ext, pltpu.SemaphoreType.DMA((2 * FETCHES,))],
        work,
        in_hbm=(2, 3),
    )
    (v0,) = advance(1.0, inner, halo, ends)
    halo, ends = exchange(v0)
    density_halo = x_halo(after((sqrt_density,), v0)[0])
    (inner,) = call(side_two, [block], [v0], [ext], work)
    (v1,) = advance(-1.0 / SHIFT, inner, halo, ends)
    halo, ends = exchange(v1)
    inner, grad, r3, m3 = call(
        side_three,
        [block, block, (72, LANES), (8, LANES)],
        [v0, v1, both, *density_halo, *density_ends, ion_potential, *history],
        [ext],
        work,
    )
    (v2,) = advance(-2.0 / SHIFT, inner, halo, ends)
    halo, ends = exchange(v2)
    inner, r4, m4 = call(
        side_four, [block, (112, LANES), (8, LANES)], [v1, v2, both, grad, *history], [ext], work
    )
    v3, to_near, to_far = advance(-2.0 / SHIFT, inner, halo, ends, last=True)
    far = lax.ppermute(to_far, "blk", swap("blk", 1))
    near = lax.ppermute(to_near, "blk", swap("blk", 0))
    (upper,) = call(pack_upper_kernel, [face], [v3], flops=work)
    z_left = lax.ppermute(upper, "gz", ring("gz", 1))
    kept, given = call(
        side_five,
        [(1, LANES), (1, LANES)],
        [v2, v3, both, *history, r1, r3, r4, m3, m4],
        [(2 * LANES, LANES), (8, LANES)],
        work,
    )
    taken = lax.ppermute(given, "blk", swap("blk", 0))
    (inner,) = call(inner_moment_kernel, [(8, LANES)], [after((v3,), given)[0]], [ext], work)
    row, part = call(couple_kernel, [(1, LANES), (8, LANES)], [v3, z_left, inner, kept, taken], flops=work)
    devices = lax.axis_size("blk") * lax.axis_size("gz")
    (outgoing,) = call(send_kernel, [(devices, LANES)], [v3, far, near, part, row], flops=work)
    received = lax.all_to_all(outgoing.reshape(devices, 1, LANES), ("blk", "gz"), 0, 0, tiled=True)
    return tuple(
        call(
            final_kernel,
            [block, block],
            [received.reshape(devices, LANES), both, grad, v0, v1, v2, v3, *history],
            [(3 * LANES, LANES), block, block, pltpu.SemaphoreType.DMA((2, REACH))],
            work,
            out_hbm=True,
        )
    )


def solution(mesh):
    placed = (
        P("blk", None, "gz"),
        P("blk", None, "gz"),
        P("blk", None, "gz"),
        P("blk", None, "gz"),
        P(None, "blk", None, "gz"),
        P(None, "blk", None, "gz"),
    )
    return jax.shard_map(
        on_device,
        mesh=mesh,
        in_specs=placed,
        out_specs=(P("blk", None, "gz"), P("blk", None, "gz")),
        check_vma=False,
    )
```

```python
import functools
import math

import jax
import jax.numpy as jnp
from jax import lax
from jax.experimental import pallas as pl
from jax.experimental.pallas import tpu as pltpu
from jax.sharding import PartitionSpec as P

center = -5369.0 / 1800.0
coeffs = (12.0 / 7.0, -15.0 / 56.0, 10.0 / 189.0, -1.0 / 112.0, 2.0 / 825.0, -1.0 / 4752.0)
screen = 0.0025
spacing = 0.28
source_scale = 4.0 * math.pi * spacing * spacing
tf_scale = 5.0 / 3.0 * 2.871234
step_length = 0.01
damp_floor = 0.2

SHIFT = 2.0
HIST = 8
REACH = 6
LANES = 128
VMEM_LIMIT = 24 * 1024 * 1024

ROW_GRAM = 0
ROW_BASE = 136
ROW_W = 170
ROW_MOM = 238
HALF = 126


def place(n):
    return n if n < HALF else n + LANES - HALF


MOM_LANE = place(ROW_MOM) - LANES
PAIRS = tuple((i, j) for i in range(HIST) for j in range(i, HIST))
PAIR_ROW = {pair: row for row, pair in enumerate(PAIRS)}


def two_sum(a, b):
    s = a + b
    bb = s - a
    return s, (a - (s - bb)) + (b - bb)


def quick_sum(a, b):
    s = a + b
    return s, b - (s - a)


def split(a):
    t = 4097.0 * a
    hi = t - (t - a)
    return hi, a - hi


def two_prod(a, b):
    p = a * b
    ah, al = split(a)
    bh, bl = split(b)
    return p, ((ah * bh - p) + ah * bl + al * bh) + al * bl


def df_add(a, b):
    s, e = two_sum(a[0], b[0])
    return quick_sum(s, e + (a[1] + b[1]))


def df_neg(a):
    return (-a[0], -a[1])


def df_sub(a, b):
    return df_add(a, df_neg(b))


def df_scale(a, factor):
    return (a[0] * factor, a[1] * factor)


def df_mul(a, b):
    p, e = two_prod(a[0], b[0])
    return quick_sum(p, e + (a[0] * b[1] + a[1] * b[0]))


def df_over(a, b, inverse):
    q = a[0] * inverse
    p, e = two_prod(q, b[0])
    rest = ((a[0] - p) - e) + (a[1] - q * b[1])
    return quick_sum(q, rest * inverse)


def lane_ids(shape):
    return lax.broadcasted_iota(jnp.int32, shape, len(shape) - 1)


def z_matrix():
    shape = (LANES, LANES)
    apart = jnp.abs(lax.broadcasted_iota(jnp.int32, shape, 0) - lax.broadcasted_iota(jnp.int32, shape, 1))
    matrix = jnp.where(apart == 0, 3.0 * center, 0.0)
    for k, weight in enumerate(coeffs, 1):
        matrix = jnp.where(apart == k, weight, matrix)
    return matrix


def inner_planes(own, ext):
    fill_ext(own, ext)
    layers, rows, lanes = own.shape
    along_z = lax.dot_general(
        own[...].reshape(layers * rows, lanes),
        z_matrix(),
        (((1,), (0,)), ((), ())),
        precision=lax.Precision.HIGHEST,
        preferred_element_type=jnp.float32,
    )
    for i in range(layers):
        total = along_z[rows * i : rows * i + rows]
        for k, weight in enumerate(coeffs, 1):
            pair = ext[i, 8 + k : 8 + k + rows, :] + ext[i, 8 - k : 8 - k + rows, :]
            if i + k < layers:
                pair = pair + own[i + k]
            if i - k >= 0:
                pair = pair + own[i - k]
            total = total + weight * pair
        yield i, total, own[i]


def edge_faces(z_left, z_right):
    lane = lane_ids((24, LANES)) % 8
    lower = jnp.zeros((24, LANES), jnp.float32)
    upper = jnp.zeros((24, LANES), jnp.float32)
    for k, weight in enumerate(coeffs, 1):
        lower = lower + jnp.where(lane < k, weight * pltpu.roll(z_left, LANES - 8 + k, 1), 0.0)
        if z_right is not None:
            upper = upper + jnp.where(lane >= 8 - k, weight * pltpu.roll(z_right, 8 - k, 1), 0.0)
    return lower, upper


def side_plane(i, block, below, rows=slice(None)):
    total = None
    for k, weight in enumerate(coeffs, 1):
        layer = i - k + REACH if below else i + k - REACH
        if 0 <= layer < REACH:
            term = weight * block[layer, rows, :]
            total = term if total is None else total + term
    return total


def z_plane(i, faces, tiles=8):
    lane = lane_ids((8, LANES))
    lower, upper = (face[8 * (i // 2) : 8 * (i // 2) + 8] for face in faces)
    out = []
    for b in range(tiles):
        j = 8 * (i % 2) + b
        tile = jnp.where(lane < 8, pltpu.roll(lower, (LANES - 8 * j) % LANES, 1), 0.0)
        tile = jnp.where(lane >= LANES - 8, pltpu.roll(upper, (2 * LANES - 8 - 8 * j) % LANES, 1), tile)
        out.append(tile)
    return jnp.concatenate(out, axis=0)


def fill_ext(own, ext):
    rows = own.shape[1]
    ext[:, 8 : 8 + rows, :] = own[...]
    ext[:, 0:8, :] = own[:, rows - 8 : rows, :]
    ext[:, 8 + rows : 16 + rows, :] = own[:, 0:8, :]


def pack_faces(src, layers):
    lane = lane_ids((8, LANES))
    firsts, lasts = [], []
    for m in range(3):
        first = jnp.zeros((8, LANES), jnp.float32)
        last = jnp.zeros((8, LANES), jnp.float32)
        for j in range(16):
            n = 16 * m + j
            tile = src[layers + n // 8, 8 * (n % 8) : 8 * (n % 8) + 8, :]
            here = (lane >= 8 * j) & (lane < 8 * j + 8)
            first = jnp.where(here, pltpu.roll(tile, 8 * j, 1) if j else tile, first)
            last = jnp.where(here, pltpu.roll(tile, (8 * j + 8) % LANES, 1) if j < 15 else tile, last)
        firsts.append(first)
        lasts.append(last)
    return jnp.concatenate(firsts, axis=0), jnp.concatenate(lasts, axis=0)


def is_odd(axis):
    return lax.rem(lax.axis_index(axis), 2) == 1


def by_partner(lower, upper):
    odd = is_odd("gz")
    return jnp.where(odd, lower, upper), jnp.where(odd, upper, lower)


def by_side(first, second):
    odd = is_odd("gz")
    return jnp.where(odd, first, second), jnp.where(odd, second, first)


def with_sides(body):
    odd = is_odd("blk")

    @pl.when(odd)
    def _():
        body(True, False)

    @pl.when(jnp.logical_not(odd))
    def _():
        body(False, True)


def fold(hi, lo, axis, steps):
    for step in steps:
        hi, err = two_sum(hi, pltpu.roll(hi, step, axis))
        lo = lo + pltpu.roll(lo, step, axis) + err
    return hi, lo


def fold_rows(acc):
    hi, lo = fold(*acc, 0, (4, 2, 1))
    return hi[0:1], lo[0:1]


def fold_lanes(hi, lo):
    return quick_sum(*fold(hi, lo, 1, (64, 32, 16, 8, 4, 2, 1)))


def add_tile(acc, product):
    hi, err = two_sum(acc[0], product)
    return hi, acc[1] + err


def tile_of(ref, i, b):
    return ref[i, 8 * b : 8 * b + 8, :]


def store_moments(pairs, moments):
    zero = jnp.zeros((8, LANES), jnp.float32)

    def body(i, accs):
        for b in range(8):
            accs = tuple(
                add_tile(acc, tile_of(a, i, b) * tile_of(c, i, b)) for acc, (a, c) in zip(accs, pairs)
            )
        return accs

    accs = lax.fori_loop(0, REACH, body, tuple((zero, zero) for _ in pairs))
    for n, acc in enumerate(accs):
        moments[2 * n : 2 * n + 1, :], moments[2 * n + 1 : 2 * n + 2, :] = fold_rows(acc)


def collapse(acc):
    return jnp.sum(acc, axis=0, keepdims=True)


def launch_kernel(hartree, density, charge, both, charge_here, face_a, face_b, sems):
    places = (both.at[pl.ds(0, REACH)], both.at[pl.ds(REACH, REACH)], charge_here)
    copies = [
        pltpu.make_async_copy(src, dst, sems.at[n])
        for n, (src, dst) in enumerate(zip((hartree, density, charge), places))
    ]
    for copy in copies:
        copy.start()
    for n in range(2):
        copies[n].wait()
        rows = slice(24 * n, 24 * n + 24)
        face_a[rows, :], face_b[rows, :] = by_partner(*pack_faces(both, REACH * n))
    copies[2].wait()


def inner_residual(both, charge, out, ext):
    hartree = both.at[pl.ds(0, REACH)]
    for i, lap, values in inner_planes(hartree, ext):
        rho = both[REACH + i]
        out[i] = source_scale * (rho * rho - charge[i]) - (screen * values - lap)


def inner_basis(own, prior, out, ext):
    for i, lap, values in inner_planes(own, ext):
        moved = (screen / SHIFT - 1.0) * values - (1.0 / SHIFT) * lap
        out[i] = moved if prior is None else 2.0 * moved - prior[i]


def z_kernel(gain, inner, z_first, z_second, out):
    faces = edge_faces(*by_side(z_first[0:24, :], z_second[0:24, :]))
    for i in range(REACH):
        out[i] = inner[i] + gain * z_plane(i, faces)


def x_kernel(gain, inner, near, far, out):
    def body(near_below, far_below):
        for i in range(REACH):
            out[i] = inner[i] + gain * (side_plane(i, near, near_below) + side_plane(i, far, far_below))

    with_sides(body)


def last_x_kernel(gain, inner, near, far, out, to_near, to_far):
    half = out.shape[1] // 2

    def body(near_below, far_below):
        for i in range(REACH):
            plane = inner[i] + gain * (side_plane(i, near, near_below) + side_plane(i, far, far_below))
            out[i] = plane
            for ref, below in ((to_near, near_below), (to_far, far_below)):
                ref[i] = plane[:half] if below else plane[half:]

    with_sides(body)


def pack_kernel(block, face_a, face_b):
    face_a[...], face_b[...] = by_partner(*pack_faces(block, 0))


def pack_upper_kernel(block, face):
    face[...] = pack_faces(block, 0)[1]


def store(rows, base, values):
    for n, value in enumerate(values):
        rows[base + n : base + n + 1, :] = value


def gram_dots(left, right, pairs):
    zero = jnp.zeros((8, LANES), jnp.float32)

    def body(i, accs):
        for b in range(8):
            at = pl.ds(8 * b, 8)
            l_tiles = {p: left[p, i, at, :] for p in sorted({p for p, _ in pairs})}
            if left is right:
                r_tiles = l_tiles
            else:
                r_tiles = {q: right[q, i, at, :] for q in sorted({q for _, q in pairs})}
            accs = tuple(acc + l_tiles[p] * r_tiles[q] for acc, (p, q) in zip(accs, pairs))
        return accs

    accs = lax.fori_loop(0, REACH, body, tuple(zero for _ in pairs))
    return [collapse(acc) for acc in accs]


CROSS_PAIRS = tuple((i, j) for i in range(HIST) for j in range(HIST))


def field_dots(groups, others, plain=()):
    zero = jnp.zeros((8, LANES), jnp.float32)
    fields = [(group, f) for group in groups for f in range(HIST)]
    count = len(fields)

    def body(i, accs):
        accs = list(accs)
        for b in range(8):
            at = pl.ds(8 * b, 8)
            tiles = [other(i, b) for other in others]
            for f, (group, which) in enumerate(fields):
                field = group[which, i, at, :]
                for o, tile in enumerate(tiles):
                    accs[o * count + f] = accs[o * count + f] + field * tile
            for n, (one, two) in enumerate(plain, len(others) * count):
                accs[n] = accs[n] + one(i, b) * two(i, b)
        return tuple(accs)

    total = count * len(others) + len(plain)
    return [collapse(acc) for acc in lax.fori_loop(0, REACH, body, (zero,) * total)]


def base_gradient(both, near, far, z_first, z_second, potential, grad, ext):
    hartree = both.at[pl.ds(0, REACH)]
    density = both.at[pl.ds(REACH, REACH)]
    faces = edge_faces(*by_side(z_first[24:48, :], z_second[24:48, :]))

    def body(near_below, far_below):
        for i in range(REACH):
            grad[i] = side_plane(i, near, near_below) + side_plane(i, far, far_below) + z_plane(i, faces)

    with_sides(body)
    for i, lap, rho in inner_planes(density, ext):
        power = jnp.exp(jnp.log(rho) * (4.0 / 3.0))
        grad[i] = 2.0 * rho * (hartree[i] + potential[i] + tf_scale * power) - (lap + grad[i]) * (
            1.0 / (spacing * spacing)
        )


def density_tile(both):
    return lambda i, b: tile_of(both, REACH + i, b)


def lifted_tile(both, vector):
    return lambda i, b: 2.0 * tile_of(both, REACH + i, b) * tile_of(vector, i, b)


FETCHES = 4


def side_one(both, charge, steps, changes, inner, steps_here, changes_here, rows, ext, sems):
    each = HIST // FETCHES
    copies = [
        pltpu.make_async_copy(src.at[pl.ds(each * n, each)], dst.at[pl.ds(each * n, each)], sems.at[FETCHES * m + n])
        for m, (src, dst) in enumerate(((steps, steps_here), (changes, changes_here)))
        for n in range(FETCHES)
    ]
    for copy in copies:
        copy.start()
    inner_residual(both, charge, inner, ext)
    for copy in copies[:FETCHES]:
        copy.wait()
    store(rows, 0, gram_dots(steps_here, steps_here, PAIRS))
    store(rows, 36, field_dots((steps_here,), [density_tile(both)]))
    for copy in copies[FETCHES:]:
        copy.wait()


def side_two(vector, inner, ext):
    inner_basis(vector, None, inner, ext)


def side_three(prior, vector, both, near, far, z_first, z_second, potential, steps, changes, *outs):
    inner, grad, rows, moments, ext = outs
    inner_basis(vector, prior, inner, ext)
    before, lifted, rho = lifted_tile(both, prior), lifted_tile(both, vector), density_tile(both)
    values = field_dots((steps, changes), [before, lifted], [(rho, before), (rho, lifted)])
    store(rows, 0, values[:16] + values[32:33] + values[16:32] + values[33:])
    store(rows, 34, gram_dots(steps, changes, CROSS_PAIRS[:32]))
    store_moments([(prior, prior), (prior, vector), (vector, vector)], moments)
    base_gradient(both, near, far, z_first, z_second, potential, grad, ext)


def side_four(prior, vector, both, grad, steps, changes, inner, rows, moments, ext):
    inner_basis(vector, prior, inner, ext)
    lifted, rho = lifted_tile(both, vector), density_tile(both)
    slope = lambda i, b: tile_of(grad, i, b)
    by_step = field_dots((steps,), [lifted, slope], [(rho, lifted), (rho, slope), (rho, rho)])
    by_change = field_dots((changes,), [lifted, slope, rho])
    values = by_step[:8] + by_change[:8] + by_step[16:17] + by_step[8:16] + by_change[8:16] + by_step[17:]
    store(rows, 0, values + by_change[16:])
    store(rows, 43, gram_dots(changes, changes, PAIRS))
    store(rows, 79, gram_dots(steps, changes, CROSS_PAIRS[32:]))
    store_moments([(prior, vector), (vector, vector)], moments)


def side_five(prior, vector, both, steps, changes, r1, r3, r4, m3, m4, kept, given, table, m5):
    lifted, rho = lifted_tile(both, vector), density_tile(both)
    own = field_dots((steps, changes), [lifted], [(rho, lifted)])
    store_moments([(prior, vector), (vector, vector)], m5)
    table[...] = jnp.zeros_like(table)

    def put(base, ref, start, count):
        before = max(0, min(count, HALF - base))
        if before:
            table[base : base + before, :] = ref[start : start + before, :]
        if before < count:
            at = place(base + before)
            table[at : at + count - before, :] = ref[start + before : start + count, :]

    put(ROW_GRAM, r1, 0, 36)
    put(ROW_GRAM + 36, r4, 43, 36)
    put(ROW_GRAM + 72, r3, 34, 32)
    put(ROW_GRAM + 104, r4, 79, 32)
    put(ROW_BASE, r1, 36, 8)
    put(ROW_BASE + 8, r4, 35, 8)
    put(ROW_BASE + 16, r4, 17, 18)
    put(ROW_W, r3, 0, 34)
    put(ROW_W + 34, r4, 0, 17)
    store(table, place(ROW_W + 51), own)

    order = [(m3, 0), (m3, 1), (m3, 2), (m4, 0), (m4, 1), (m5, 0), (m5, 1)]
    zero = jnp.zeros((1, LANES), jnp.float32)
    parts = [
        jnp.concatenate([ref[2 * which + low : 2 * which + low + 1, :] for ref, which in order] + [zero], axis=0)
        for low in range(2)
    ]
    hi, lo = fold_lanes(*parts)
    lane = lane_ids((1, LANES))
    first = jnp.sum(jnp.transpose(table[0:LANES, :]), axis=0, keepdims=True)
    second = jnp.sum(jnp.transpose(table[LANES : 2 * LANES, :]), axis=0, keepdims=True)
    for n in range(7):
        second = jnp.where(lane == MOM_LANE + n, hi[n : n + 1], second)
        second = jnp.where(lane == MOM_LANE + 7 + n, lo[n : n + 1], second)
    odd = is_odd("blk")
    kept[...] = jnp.where(odd, second, first)
    given[...] = jnp.where(odd, first, second)


def inner_moment_kernel(vector, inner, ext):
    zero = jnp.zeros((8, LANES), jnp.float32)
    accs = [(zero, zero) for _ in range(2)]
    for i, lap, values in inner_planes(vector, ext):
        product = values * ((screen / SHIFT - 1.0) * values - (1.0 / SHIFT) * lap)
        for b in range(8):
            accs[b % 2] = add_tile(accs[b % 2], product[8 * b : 8 * b + 8])
    hi, err = two_sum(accs[0][0], accs[1][0])
    inner[0:1, :], inner[1:2, :] = fold_rows((hi, accs[0][1] + accs[1][1] + err))


def couple(own, block, below, acc):
    half = own.shape[1] // 2
    for i in range(REACH):
        product = own[i, half:, :] * side_plane(i, block, True) if below else own[i, :half, :] * side_plane(i, block, False)
        for b in range(half // 8):
            acc = add_tile(acc, product[8 * b : 8 * b + 8])
    return acc


def couple_kernel(own, z_left, inner, kept, taken, row, part):
    zero = jnp.zeros((8, LANES), jnp.float32)
    faces = edge_faces(z_left[...], None)
    acc = (zero, zero)
    for i in range(REACH):
        product = own[i] * z_plane(i, faces)
        for b in range(8):
            acc = add_tile(acc, product[8 * b : 8 * b + 8])
    sides = df_scale(fold_rows(acc), -2.0 / SHIFT)
    part[0:1, :], part[1:2, :] = df_add(sides, (inner[0:1, :], inner[1:2, :]))
    lane = lane_ids((1, LANES))
    total, err = two_sum(kept[...], taken[...])
    low_lane = (lane >= MOM_LANE + 7) & (lane < MOM_LANE + 14) & is_odd("blk")
    row[...] = jnp.where(low_lane, total + pltpu.roll(err, 7, 1), total)


def send_kernel(own, far, near, part, row, out):
    zero = jnp.zeros((8, LANES), jnp.float32)

    def body(near_below, far_below):
        acc = couple(own, far, far_below, couple(own, near, near_below, (zero, zero)))
        hi, lo = fold_lanes(*df_add(df_scale(fold_rows(acc), -2.0 / SHIFT), (part[0:1, :], part[1:2, :])))
        lane = lane_ids((1, LANES))
        value = jnp.where(lane == HALF, hi, jnp.where(lane == HALF + 1, lo, row[...]))
        out[...] = jnp.broadcast_to(value, out.shape)

    with_sides(body)


def solve_krylov(moment):
    n00, n01, n11, n12, n22, n23, n33, n34 = moment
    nu = [n00, n01]
    nu.append(df_sub(df_scale(n11, 2.0), n00))
    nu.append(df_sub(df_scale(n12, 2.0), n01))
    nu.append(df_sub(df_scale(n22, 2.0), n00))
    nu.append(df_sub(df_scale(n23, 2.0), n01))
    nu.append(df_sub(df_scale(n33, 2.0), n00))

    def gram(i, j):
        if i == j == 0:
            return n00
        return df_scale(df_add(nu[i + j], nu[abs(i - j)]), 0.5)

    def moved(i, j):
        if i == 3 and j == 3:
            return n34
        if j == 0:
            return gram(i, 1)
        return df_scale(df_add(gram(i, j + 1), gram(i, j - 1)), 0.5)

    mat = {(i, j): df_add(moved(i, j), gram(i, j)) for i in range(4) for j in range(i + 1)}
    rhs = [df_scale(gram(i, 0), 1.0 / SHIFT) for i in range(4)]
    low, inverse = {}, []
    for k in range(4):
        inverse.append(1.0 / mat[k, k][0])
        for i in range(k + 1, 4):
            low[i, k] = df_over(mat[i, k], mat[k, k], inverse[k])
        for i in range(k + 1, 4):
            for j in range(k + 1, i + 1):
                mat[i, j] = df_sub(mat[i, j], df_mul(low[i, k], mat[j, k]))
            rhs[i] = df_sub(rhs[i], df_mul(low[i, k], rhs[k]))
    sol = [None] * 4
    for k in reversed(range(4)):
        value = df_over(rhs[k], mat[k, k], inverse[k])
        for i in range(k + 1, 4):
            value = df_sub(value, df_mul(low[i, k], sol[i]))
        sol[k] = value
    return [hi + lo for hi, lo in sol]


def final_kernel(received, both, grad, v0, v1, v2, v3, steps, changes, new_density, new_hartree, spread, density_here, hartree_here, sems):
    parts = [(received[8 * n : 8 * n + 8, :], jnp.zeros((8, LANES), jnp.float32)) for n in range(4)]
    for n in range(4, received.shape[0] // 8):
        parts[n % 4] = add_tile(parts[n % 4], received[8 * n : 8 * n + 8, :])
    while len(parts) > 1:
        half = len(parts) // 2
        merged = []
        for a, b in zip(parts[:half], parts[half:]):
            hi, err = two_sum(a[0], b[0])
            merged.append((hi, a[1] + b[1] + err))
        parts = merged
    hi, lo = fold(*parts[0], 0, (1, 2))
    lane = lane_ids((1, LANES))
    last, err = two_sum(hi[3:4], hi[7:8])
    err = err + (lo[3:4] + lo[7:8])
    first = hi[3:4]
    second = jnp.where(lane >= HALF, last, hi[7:8])
    low = jnp.where(lane >= HALF, err, lo[7:8])
    low = low + jnp.where(lane == HALF, pltpu.roll(second, LANES - 1, 1), pltpu.roll(second, LANES - 7, 1))
    for n, value in enumerate((first, second, low)):
        spread[LANES * n : LANES * n + LANES, :] = jnp.transpose(jnp.broadcast_to(value, (LANES, LANES)))

    def row(n):
        return spread[place(n) : place(n) + 1, :]

    def moment(n):
        at = LANES + (MOM_LANE + n if n < 7 else HALF)
        return quick_sum(spread[at : at + 1, :], spread[LANES + at : LANES + at + 1, :])

    mix = solve_krylov([moment(n) for n in range(8)])

    def s_s(i, j):
        return row(ROW_GRAM + PAIR_ROW[min(i, j), max(i, j)])

    def y_y(i, j):
        return row(ROW_GRAM + 36 + PAIR_ROW[min(i, j), max(i, j)])

    def s_y(i, j):
        return row(ROW_GRAM + 72 + 8 * i + j)

    pairs = range(HIST)
    theta, rest, inverse = [], [], []
    for i in pairs:
        curv, norm = s_y(i, i), s_s(i, i)
        kept = (1.0 - damp_floor) * norm
        damp = jnp.where(curv >= damp_floor * norm, 1.0, kept / jnp.maximum(norm - curv, kept))
        theta.append(damp)
        rest.append(1.0 - damp)
        inverse.append(1.0 / (damp * curv + (1.0 - damp) * norm))

    def s_bar(i, j):
        return theta[j] * s_y(i, j) + rest[j] * s_s(i, j)

    def bar_bar(i, j):
        return theta[i] * (theta[j] * y_y(i, j) + rest[j] * s_y(j, i)) + rest[i] * s_bar(i, j)

    last = HIST - 1
    scaling = s_bar(last, last) / bar_bar(last, last)

    def energy(n):
        value = row(ROW_BASE + 16 + n)
        for j in range(4):
            value = value + mix[j] * row(ROW_W + 17 * j + n)
        return value

    chem = energy(16) / row(ROW_BASE + 33)

    def gradient(n):
        return energy(n) - chem * row(ROW_BASE + n)

    s_grad = [gradient(i) for i in pairs]
    bar_grad = [theta[i] * gradient(HIST + i) + rest[i] * s_grad[i] for i in pairs]

    first = [None] * HIST
    pending = list(s_grad)
    for j in reversed(pairs):
        first[j] = inverse[j] * pending[j]
        for i in range(j):
            pending[i] = pending[i] - first[j] * s_bar(i, j)
    pending = list(bar_grad)
    for j in pairs:
        for i in pairs:
            pending[i] = pending[i] - first[j] * bar_bar(i, j)
    pending = [scaling * value for value in pending]
    step_mix, change_mix = [], []
    for j in pairs:
        net = first[j] - inverse[j] * pending[j]
        for i in range(j + 1, HIST):
            pending[i] = pending[i] + net * s_bar(j, i)
        change_mix.append((-step_length) * (-scaling * first[j] * theta[j]))
        step_mix.append((-step_length) * (net - scaling * first[j] * rest[j]))

    wide = lambda value: jnp.broadcast_to(value, (8, LANES))
    mix = [wide(value) for value in mix]
    chem, gain = wide(chem), wide((-step_length) * scaling)
    step_mix = [wide(value) for value in step_mix]
    change_mix = [wide(value) for value in change_mix]
    basis = (v0, v1, v2, v3)

    def leave(i):
        return [
            pltpu.make_async_copy(here.at[i], out.at[i], sems.at[n, i])
            for n, (here, out) in enumerate(((density_here, new_density), (hartree_here, new_hartree)))
        ]

    for i in range(REACH):
        for b in range(8):
            at = pl.ds(8 * b, 8)
            rho = both[REACH + i, at, :]
            lift = mix[0] * v0[i, at, :]
            for j in range(1, 4):
                lift = lift + mix[j] * basis[j][i, at, :]
            hartree_here[i, at, :] = both[i, at, :] + lift
            slope = grad[i, at, :] + 2.0 * rho * lift - chem * rho
            parts = [rho, gain * slope, step_mix[0] * steps[0, i, at, :], change_mix[0] * changes[0, i, at, :]]
            for f in range(1, HIST):
                parts[2] = parts[2] + step_mix[f] * steps[f, i, at, :]
                parts[3] = parts[3] + change_mix[f] * changes[f, i, at, :]
            density_here[i, at, :] = parts[0] + (parts[1] + (parts[2] + parts[3]))
        for copy in leave(i):
            copy.start()
    for i in range(REACH):
        for copy in leave(i):
            copy.wait()


def call(kernel, outs, args, scratch=(), flops=0, in_hbm=(), out_hbm=False):
    args = [pltpu.with_memory_space_constraint(x, pltpu.HBM) if n in in_hbm else x for n, x in enumerate(args)]
    shapes = [jax.ShapeDtypeStruct(shape, jnp.float32) for shape in outs]
    size = sum(4 * math.prod(a.shape) for a in (*args, *shapes))
    return pl.pallas_call(
        kernel,
        out_shape=shapes,
        in_specs=[pl.BlockSpec(memory_space=pltpu.HBM if n in in_hbm else pltpu.VMEM) for n in range(len(args))],
        out_specs=[pl.BlockSpec(memory_space=pltpu.HBM if out_hbm else pltpu.VMEM)] * len(outs),
        scratch_shapes=[pltpu.VMEM(s, jnp.float32) if isinstance(s, tuple) else s for s in scratch],
        cost_estimate=pl.CostEstimate(flops=flops, bytes_accessed=size, transcendentals=0),
        compiler_params=pltpu.CompilerParams(vmem_limit_bytes=VMEM_LIMIT),
    )(*args)


def ring(axis, step):
    size = lax.axis_size(axis)
    return [(i, (i + step) % size) for i in range(size)]


def swap(axis, odd_up):
    size = lax.axis_size(axis)
    return [(i, (i + (1 if i % 2 == odd_up else -1)) % size) for i in range(size)]


def after(values, *earlier):
    return lax.optimization_barrier((tuple(values), earlier))[0]


def x_halo(block):
    far = lax.ppermute(block, "blk", swap("blk", 1))
    return (lax.ppermute(block, "blk", swap("blk", 0)), far)


def z_halo(face_a, face_b):
    return (lax.ppermute(face_a, "gz", swap("gz", 0)), lax.ppermute(face_b, "gz", swap("gz", 1)))


def on_device(sqrt_density, ion_charge, ion_potential, hartree_prev, hist_steps, hist_changes):
    block = sqrt_density.shape
    ext = (block[0], block[1] + 16, block[2])
    face = (24, LANES)
    cells = math.prod(block)
    cells = math.prod(block)
    work = 300 * cells
    inputs = (hartree_prev, sqrt_density, ion_charge)
    halo = x_halo(hartree_prev)
    both, charge, *faces = call(
        launch_kernel,
        [(2 * REACH, *block[1:]), block, (48, LANES), (48, LANES)],
        inputs,
        [pltpu.SemaphoreType.DMA((3,))],
        in_hbm=(0, 1, 2),
    )
    ends = z_halo(*faces)
    density_ends = ends
    half = (REACH, block[1] // 2, LANES)

    def advance(gain, inner, halo, ends, last=False):
        (mid,) = call(functools.partial(z_kernel, gain), [block], [inner, *ends], flops=work)
        return call(
            functools.partial(last_x_kernel if last else x_kernel, gain),
            [block, half, half] if last else [block],
            [mid, *halo],
            flops=work,
        )

    def exchange(block_now):
        halo = x_halo(block_now)
        return halo, z_halo(*call(pack_kernel, [face, face], [block_now], flops=work))

    stored = hist_steps.shape
    inner, *history, r1 = call(
        side_one,
        [block, stored, stored, (48, LANES)],
        [both, charge, hist_steps, hist_changes],
        [ext, pltpu.SemaphoreType.DMA((2 * FETCHES,))],
        work,
        in_hbm=(2, 3),
    )
    (v0,) = advance(1.0, inner, halo, ends)
    halo, ends = exchange(v0)
    density_halo = x_halo(after((sqrt_density,), v0)[0])
    (inner,) = call(side_two, [block], [v0], [ext], work)
    (v1,) = advance(-1.0 / SHIFT, inner, halo, ends)
    halo, ends = exchange(v1)
    inner, grad, r3, m3 = call(
        side_three,
        [block, block, (72, LANES), (8, LANES)],
        [v0, v1, both, *density_halo, *density_ends, ion_potential, *history],
        [ext],
        work,
    )
    (v2,) = advance(-2.0 / SHIFT, inner, halo, ends)
    halo, ends = exchange(v2)
    inner, r4, m4 = call(
        side_four, [block, (112, LANES), (8, LANES)], [v1, v2, both, grad, *history], [ext], work
    )
    v3, to_near, to_far = advance(-2.0 / SHIFT, inner, halo, ends, last=True)
    far = lax.ppermute(to_far, "blk", swap("blk", 1))
    near = lax.ppermute(to_near, "blk", swap("blk", 0))
    (upper,) = call(pack_upper_kernel, [face], [v3], flops=work)
    z_left = lax.ppermute(upper, "gz", ring("gz", 1))
    kept, given = call(
        side_five,
        [(1, LANES), (1, LANES)],
        [v2, v3, both, *history, r1, r3, r4, m3, m4],
        [(2 * LANES, LANES), (8, LANES)],
        work,
    )
    taken = lax.ppermute(given, "blk", swap("blk", 0))
    (inner,) = call(inner_moment_kernel, [(8, LANES)], [after((v3,), given)[0]], [ext], work)
    row, part = call(couple_kernel, [(1, LANES), (8, LANES)], [v3, z_left, inner, kept, taken], flops=work)
    devices = lax.axis_size("blk") * lax.axis_size("gz")
    (outgoing,) = call(send_kernel, [(devices, LANES)], [v3, far, near, part, row], flops=work)
    received = lax.all_to_all(outgoing.reshape(devices, 1, LANES), ("blk", "gz"), 0, 0, tiled=True)
    return tuple(
        call(
            final_kernel,
            [block, block],
            [received.reshape(devices, LANES), both, grad, v0, v1, v2, v3, *history],
            [(3 * LANES, LANES), block, block, pltpu.SemaphoreType.DMA((2, REACH))],
            work,
            out_hbm=True,
        )
    )


def solution(mesh):
    placed = (
        P("blk", None, "gz"),
        P("blk", None, "gz"),
        P("blk", None, "gz"),
        P("blk", None, "gz"),
        P(None, "blk", None, "gz"),
        P(None, "blk", None, "gz"),
    )
    return jax.shard_map(
        on_device,
        mesh=mesh,
        in_specs=placed,
        out_specs=(P("blk", None, "gz"), P("blk", None, "gz")),
        check_vma=False,
    )
```

```python
import functools
import math

import jax
import jax.numpy as jnp
from jax import lax
from jax.experimental import pallas as pl
from jax.experimental.pallas import tpu as pltpu
from jax.sharding import PartitionSpec as P

center = -5369.0 / 1800.0
coeffs = (12.0 / 7.0, -15.0 / 56.0, 10.0 / 189.0, -1.0 / 112.0, 2.0 / 825.0, -1.0 / 4752.0)
screen = 0.0025
spacing = 0.28
source_scale = 4.0 * math.pi * spacing * spacing
tf_scale = 5.0 / 3.0 * 2.871234
step_length = 0.01
damp_floor = 0.2

SHIFT = 2.0
HIST = 8
REACH = 6
LANES = 128
VMEM_LIMIT = 24 * 1024 * 1024

ROW_GRAM = 0
ROW_BASE = 136
ROW_W = 170
ROW_MOM = 238
HALF = 126


def place(n):
    return n if n < HALF else n + LANES - HALF


MOM_LANE = place(ROW_MOM) - LANES
PAIRS = tuple((i, j) for i in range(HIST) for j in range(i, HIST))
PAIR_ROW = {pair: row for row, pair in enumerate(PAIRS)}


def two_sum(a, b):
    s = a + b
    bb = s - a
    return s, (a - (s - bb)) + (b - bb)


def quick_sum(a, b):
    s = a + b
    return s, b - (s - a)


def split(a):
    t = 4097.0 * a
    hi = t - (t - a)
    return hi, a - hi


def two_prod(a, b):
    p = a * b
    ah, al = split(a)
    bh, bl = split(b)
    return p, ((ah * bh - p) + ah * bl + al * bh) + al * bl


def df_add(a, b):
    s, e = two_sum(a[0], b[0])
    return quick_sum(s, e + (a[1] + b[1]))


def df_neg(a):
    return (-a[0], -a[1])


def df_sub(a, b):
    return df_add(a, df_neg(b))


def df_scale(a, factor):
    return (a[0] * factor, a[1] * factor)


def df_mul(a, b):
    p, e = two_prod(a[0], b[0])
    return quick_sum(p, e + (a[0] * b[1] + a[1] * b[0]))


def df_over(a, b, inverse):
    q = a[0] * inverse
    p, e = two_prod(q, b[0])
    rest = ((a[0] - p) - e) + (a[1] - q * b[1])
    return quick_sum(q, rest * inverse)


def lane_ids(shape):
    return lax.broadcasted_iota(jnp.int32, shape, len(shape) - 1)


def z_matrix():
    shape = (LANES, LANES)
    apart = jnp.abs(lax.broadcasted_iota(jnp.int32, shape, 0) - lax.broadcasted_iota(jnp.int32, shape, 1))
    matrix = jnp.where(apart == 0, 3.0 * center, 0.0)
    for k, weight in enumerate(coeffs, 1):
        matrix = jnp.where(apart == k, weight, matrix)
    return matrix


def inner_planes(own, ext):
    fill_ext(own, ext)
    layers, rows, lanes = own.shape
    along_z = lax.dot_general(
        own[...].reshape(layers * rows, lanes),
        z_matrix(),
        (((1,), (0,)), ((), ())),
        precision=lax.Precision.HIGHEST,
        preferred_element_type=jnp.float32,
    )
    for i in range(layers):
        total = along_z[rows * i : rows * i + rows]
        for k, weight in enumerate(coeffs, 1):
            pair = ext[i, 8 + k : 8 + k + rows, :] + ext[i, 8 - k : 8 - k + rows, :]
            if i + k < layers:
                pair = pair + own[i + k]
            if i - k >= 0:
                pair = pair + own[i - k]
            total = total + weight * pair
        yield i, total, own[i]


def edge_faces(z_left, z_right):
    lane = lane_ids((24, LANES)) % 8
    lower = jnp.zeros((24, LANES), jnp.float32)
    upper = jnp.zeros((24, LANES), jnp.float32)
    for k, weight in enumerate(coeffs, 1):
        lower = lower + jnp.where(lane < k, weight * pltpu.roll(z_left, LANES - 8 + k, 1), 0.0)
        if z_right is not None:
            upper = upper + jnp.where(lane >= 8 - k, weight * pltpu.roll(z_right, 8 - k, 1), 0.0)
    return lower, upper


def side_plane(i, block, below, rows=slice(None)):
    total = None
    for k, weight in enumerate(coeffs, 1):
        layer = i - k + REACH if below else i + k - REACH
        if 0 <= layer < REACH:
            term = weight * block[layer, rows, :]
            total = term if total is None else total + term
    return total


def z_plane(i, faces, tiles=8):
    lane = lane_ids((8, LANES))
    lower, upper = (face[8 * (i // 2) : 8 * (i // 2) + 8] for face in faces)
    out = []
    for b in range(tiles):
        j = 8 * (i % 2) + b
        tile = jnp.where(lane < 8, pltpu.roll(lower, (LANES - 8 * j) % LANES, 1), 0.0)
        tile = jnp.where(lane >= LANES - 8, pltpu.roll(upper, (2 * LANES - 8 - 8 * j) % LANES, 1), tile)
        out.append(tile)
    return jnp.concatenate(out, axis=0)


def fill_ext(own, ext):
    rows = own.shape[1]
    ext[:, 8 : 8 + rows, :] = own[...]
    ext[:, 0:8, :] = own[:, rows - 8 : rows, :]
    ext[:, 8 + rows : 16 + rows, :] = own[:, 0:8, :]


def pack_faces(src, layers):
    lane = lane_ids((8, LANES))
    firsts, lasts = [], []
    for m in range(3):
        first = jnp.zeros((8, LANES), jnp.float32)
        last = jnp.zeros((8, LANES), jnp.float32)
        for j in range(16):
            n = 16 * m + j
            tile = src[layers + n // 8, 8 * (n % 8) : 8 * (n % 8) + 8, :]
            here = (lane >= 8 * j) & (lane < 8 * j + 8)
            first = jnp.where(here, pltpu.roll(tile, 8 * j, 1) if j else tile, first)
            last = jnp.where(here, pltpu.roll(tile, (8 * j + 8) % LANES, 1) if j < 15 else tile, last)
        firsts.append(first)
        lasts.append(last)
    return jnp.concatenate(firsts, axis=0), jnp.concatenate(lasts, axis=0)


def is_odd(axis):
    return lax.rem(lax.axis_index(axis), 2) == 1


def by_partner(lower, upper):
    odd = is_odd("gz")
    return jnp.where(odd, lower, upper), jnp.where(odd, upper, lower)


def by_side(first, second):
    odd = is_odd("gz")
    return jnp.where(odd, first, second), jnp.where(odd, second, first)


def with_sides(body):
    odd = is_odd("blk")

    @pl.when(odd)
    def _():
        body(True, False)

    @pl.when(jnp.logical_not(odd))
    def _():
        body(False, True)


def fold(hi, lo, axis, steps):
    for step in steps:
        hi, err = two_sum(hi, pltpu.roll(hi, step, axis))
        lo = lo + pltpu.roll(lo, step, axis) + err
    return hi, lo


def fold_rows(acc):
    hi, lo = fold(*acc, 0, (4, 2, 1))
    return hi[0:1], lo[0:1]


def fold_lanes(hi, lo):
    return quick_sum(*fold(hi, lo, 1, (64, 32, 16, 8, 4, 2, 1)))


def add_tile(acc, product):
    hi, err = two_sum(acc[0], product)
    return hi, acc[1] + err


def tile_of(ref, i, b):
    return ref[i, 8 * b : 8 * b + 8, :]


def store_moments(pairs, moments):
    zero = jnp.zeros((8, LANES), jnp.float32)

    def body(i, accs):
        for b in range(8):
            accs = tuple(
                add_tile(acc, tile_of(a, i, b) * tile_of(c, i, b)) for acc, (a, c) in zip(accs, pairs)
            )
        return accs

    accs = lax.fori_loop(0, REACH, body, tuple((zero, zero) for _ in pairs))
    for n, acc in enumerate(accs):
        moments[2 * n : 2 * n + 1, :], moments[2 * n + 1 : 2 * n + 2, :] = fold_rows(acc)


def collapse(acc):
    return jnp.sum(acc, axis=0, keepdims=True)


def launch_kernel(hartree, density, charge, both, charge_here, face_a, face_b, sems):
    places = (both.at[pl.ds(0, REACH)], both.at[pl.ds(REACH, REACH)], charge_here)
    copies = [
        pltpu.make_async_copy(src, dst, sems.at[n])
        for n, (src, dst) in enumerate(zip((hartree, density, charge), places))
    ]
    for copy in copies:
        copy.start()
    for n in range(2):
        copies[n].wait()
        rows = slice(24 * n, 24 * n + 24)
        face_a[rows, :], face_b[rows, :] = by_partner(*pack_faces(both, REACH * n))
    copies[2].wait()


def inner_residual(both, charge, out, ext):
    hartree = both.at[pl.ds(0, REACH)]
    for i, lap, values in inner_planes(hartree, ext):
        rho = both[REACH + i]
        out[i] = source_scale * (rho * rho - charge[i]) - (screen * values - lap)


def inner_basis(own, prior, out, ext):
    for i, lap, values in inner_planes(own, ext):
        moved = (screen / SHIFT - 1.0) * values - (1.0 / SHIFT) * lap
        out[i] = moved if prior is None else 2.0 * moved - prior[i]


def z_kernel(gain, inner, z_first, z_second, out):
    faces = edge_faces(*by_side(z_first[0:24, :], z_second[0:24, :]))
    for i in range(REACH):
        out[i] = inner[i] + gain * z_plane(i, faces)


def x_kernel(gain, inner, near, far, out):
    def body(near_below, far_below):
        for i in range(REACH):
            out[i] = inner[i] + gain * (side_plane(i, near, near_below) + side_plane(i, far, far_below))

    with_sides(body)


def last_x_kernel(gain, inner, near, far, out, to_near, to_far):
    half = out.shape[1] // 2

    def body(near_below, far_below):
        for i in range(REACH):
            plane = inner[i] + gain * (side_plane(i, near, near_below) + side_plane(i, far, far_below))
            out[i] = plane
            for ref, below in ((to_near, near_below), (to_far, far_below)):
                ref[i] = plane[:half] if below else plane[half:]

    with_sides(body)


def pack_kernel(block, face_a, face_b):
    face_a[...], face_b[...] = by_partner(*pack_faces(block, 0))


def pack_upper_kernel(block, face):
    face[...] = pack_faces(block, 0)[1]


def store(rows, base, values):
    for n, value in enumerate(values):
        rows[base + n : base + n + 1, :] = value


def gram_dots(left, right, pairs):
    zero = jnp.zeros((8, LANES), jnp.float32)

    def body(i, accs):
        for b in range(8):
            at = pl.ds(8 * b, 8)
            l_tiles = {p: left[p, i, at, :] for p in sorted({p for p, _ in pairs})}
            if left is right:
                r_tiles = l_tiles
            else:
                r_tiles = {q: right[q, i, at, :] for q in sorted({q for _, q in pairs})}
            accs = tuple(acc + l_tiles[p] * r_tiles[q] for acc, (p, q) in zip(accs, pairs))
        return accs

    accs = lax.fori_loop(0, REACH, body, tuple(zero for _ in pairs))
    return [collapse(acc) for acc in accs]


CROSS_PAIRS = tuple((i, j) for i in range(HIST) for j in range(HIST))


def field_dots(groups, others, plain=()):
    zero = jnp.zeros((8, LANES), jnp.float32)
    fields = [(group, f) for group in groups for f in range(HIST)]
    count = len(fields)

    def body(i, accs):
        accs = list(accs)
        for b in range(8):
            at = pl.ds(8 * b, 8)
            tiles = [other(i, b) for other in others]
            for f, (group, which) in enumerate(fields):
                field = group[which, i, at, :]
                for o, tile in enumerate(tiles):
                    accs[o * count + f] = accs[o * count + f] + field * tile
            for n, (one, two) in enumerate(plain, len(others) * count):
                accs[n] = accs[n] + one(i, b) * two(i, b)
        return tuple(accs)

    total = count * len(others) + len(plain)
    return [collapse(acc) for acc in lax.fori_loop(0, REACH, body, (zero,) * total)]


def base_gradient(both, near, far, z_first, z_second, potential, grad, ext):
    hartree = both.at[pl.ds(0, REACH)]
    density = both.at[pl.ds(REACH, REACH)]
    faces = edge_faces(*by_side(z_first[24:48, :], z_second[24:48, :]))

    def body(near_below, far_below):
        for i in range(REACH):
            grad[i] = side_plane(i, near, near_below) + side_plane(i, far, far_below) + z_plane(i, faces)

    with_sides(body)
    for i, lap, rho in inner_planes(density, ext):
        power = jnp.exp(jnp.log(rho) * (4.0 / 3.0))
        grad[i] = 2.0 * rho * (hartree[i] + potential[i] + tf_scale * power) - (lap + grad[i]) * (
            1.0 / (spacing * spacing)
        )


def density_tile(both):
    return lambda i, b: tile_of(both, REACH + i, b)


def lifted_tile(both, vector):
    return lambda i, b: 2.0 * tile_of(both, REACH + i, b) * tile_of(vector, i, b)


FETCHES = 4


def side_one(both, charge, steps, changes, inner, steps_here, changes_here, rows, ext, sems):
    each = HIST // FETCHES
    copies = [
        pltpu.make_async_copy(src.at[pl.ds(each * n, each)], dst.at[pl.ds(each * n, each)], sems.at[FETCHES * m + n])
        for m, (src, dst) in enumerate(((steps, steps_here), (changes, changes_here)))
        for n in range(FETCHES)
    ]
    for copy in copies:
        copy.start()
    inner_residual(both, charge, inner, ext)
    for copy in copies[:FETCHES]:
        copy.wait()
    store(rows, 0, gram_dots(steps_here, steps_here, PAIRS))
    store(rows, 36, field_dots((steps_here,), [density_tile(both)]))
    for copy in copies[FETCHES:]:
        copy.wait()
    store(rows, 44, gram_dots(changes_here, changes_here, PAIRS))
    store(rows, 80, gram_dots(steps_here, changes_here, CROSS_PAIRS[:32]))


def side_two(vector, inner, ext):
    inner_basis(vector, None, inner, ext)


def side_three(prior, vector, both, near, far, z_first, z_second, potential, steps, changes, *outs):
    inner, grad, rows, moments, ext = outs
    inner_basis(vector, prior, inner, ext)
    before, lifted, rho = lifted_tile(both, prior), lifted_tile(both, vector), density_tile(both)
    values = field_dots((steps, changes), [before, lifted], [(rho, before), (rho, lifted)])
    store(rows, 0, values[:16] + values[32:33] + values[16:32] + values[33:])
    store_moments([(prior, prior), (prior, vector), (vector, vector)], moments)
    base_gradient(both, near, far, z_first, z_second, potential, grad, ext)


def side_four(prior, vector, both, grad, steps, changes, inner, rows, moments, ext):
    inner_basis(vector, prior, inner, ext)
    lifted, rho = lifted_tile(both, vector), density_tile(both)
    slope = lambda i, b: tile_of(grad, i, b)
    by_step = field_dots((steps,), [lifted, slope], [(rho, lifted), (rho, slope), (rho, rho)])
    by_change = field_dots((changes,), [lifted, slope, rho])
    values = by_step[:8] + by_change[:8] + by_step[16:17] + by_step[8:16] + by_change[8:16] + by_step[17:]
    store(rows, 0, values + by_change[16:])
    store(rows, 43, gram_dots(steps, changes, CROSS_PAIRS[32:]))
    store_moments([(prior, vector), (vector, vector)], moments)


def side_five(prior, vector, both, steps, changes, r1, r3, r4, m3, m4, kept, given, table, m5):
    lifted, rho = lifted_tile(both, vector), density_tile(both)
    own = field_dots((steps, changes), [lifted], [(rho, lifted)])
    store_moments([(prior, vector), (vector, vector)], m5)
    table[...] = jnp.zeros_like(table)

    def put(base, ref, start, count):
        before = max(0, min(count, HALF - base))
        if before:
            table[base : base + before, :] = ref[start : start + before, :]
        if before < count:
            at = place(base + before)
            table[at : at + count - before, :] = ref[start + before : start + count, :]

    put(ROW_GRAM, r1, 0, 36)
    put(ROW_GRAM + 36, r1, 44, 36)
    put(ROW_GRAM + 72, r1, 80, 32)
    put(ROW_GRAM + 104, r4, 43, 32)
    put(ROW_BASE, r1, 36, 8)
    put(ROW_BASE + 8, r4, 35, 8)
    put(ROW_BASE + 16, r4, 17, 18)
    put(ROW_W, r3, 0, 34)
    put(ROW_W + 34, r4, 0, 17)
    store(table, place(ROW_W + 51), own)

    order = [(m3, 0), (m3, 1), (m3, 2), (m4, 0), (m4, 1), (m5, 0), (m5, 1)]
    zero = jnp.zeros((1, LANES), jnp.float32)
    parts = [
        jnp.concatenate([ref[2 * which + low : 2 * which + low + 1, :] for ref, which in order] + [zero], axis=0)
        for low in range(2)
    ]
    hi, lo = fold_lanes(*parts)
    lane = lane_ids((1, LANES))
    first = jnp.sum(jnp.transpose(table[0:LANES, :]), axis=0, keepdims=True)
    second = jnp.sum(jnp.transpose(table[LANES : 2 * LANES, :]), axis=0, keepdims=True)
    for n in range(7):
        second = jnp.where(lane == MOM_LANE + n, hi[n : n + 1], second)
        second = jnp.where(lane == MOM_LANE + 7 + n, lo[n : n + 1], second)
    odd = is_odd("blk")
    kept[...] = jnp.where(odd, second, first)
    given[...] = jnp.where(odd, first, second)


def inner_moment_kernel(vector, inner, ext):
    zero = jnp.zeros((8, LANES), jnp.float32)
    accs = [(zero, zero) for _ in range(2)]
    for i, lap, values in inner_planes(vector, ext):
        product = values * ((screen / SHIFT - 1.0) * values - (1.0 / SHIFT) * lap)
        for b in range(8):
            accs[b % 2] = add_tile(accs[b % 2], product[8 * b : 8 * b + 8])
    hi, err = two_sum(accs[0][0], accs[1][0])
    inner[0:1, :], inner[1:2, :] = fold_rows((hi, accs[0][1] + accs[1][1] + err))


def couple(own, block, below, acc):
    half = own.shape[1] // 2
    for i in range(REACH):
        product = own[i, half:, :] * side_plane(i, block, True) if below else own[i, :half, :] * side_plane(i, block, False)
        for b in range(half // 8):
            acc = add_tile(acc, product[8 * b : 8 * b + 8])
    return acc


def couple_kernel(own, z_left, inner, kept, taken, row, part):
    zero = jnp.zeros((8, LANES), jnp.float32)
    faces = edge_faces(z_left[...], None)
    acc = (zero, zero)
    for i in range(REACH):
        product = own[i] * z_plane(i, faces)
        for b in range(8):
            acc = add_tile(acc, product[8 * b : 8 * b + 8])
    sides = df_scale(fold_rows(acc), -2.0 / SHIFT)
    part[0:1, :], part[1:2, :] = df_add(sides, (inner[0:1, :], inner[1:2, :]))
    lane = lane_ids((1, LANES))
    total, err = two_sum(kept[...], taken[...])
    low_lane = (lane >= MOM_LANE + 7) & (lane < MOM_LANE + 14) & is_odd("blk")
    row[...] = jnp.where(low_lane, total + pltpu.roll(err, 7, 1), total)


def send_kernel(own, far, near, part, row, out):
    zero = jnp.zeros((8, LANES), jnp.float32)

    def body(near_below, far_below):
        acc = couple(own, far, far_below, couple(own, near, near_below, (zero, zero)))
        hi, lo = fold_lanes(*df_add(df_scale(fold_rows(acc), -2.0 / SHIFT), (part[0:1, :], part[1:2, :])))
        lane = lane_ids((1, LANES))
        value = jnp.where(lane == HALF, hi, jnp.where(lane == HALF + 1, lo, row[...]))
        out[...] = jnp.broadcast_to(value, out.shape)

    with_sides(body)


def solve_krylov(moment):
    n00, n01, n11, n12, n22, n23, n33, n34 = moment
    nu = [n00, n01]
    nu.append(df_sub(df_scale(n11, 2.0), n00))
    nu.append(df_sub(df_scale(n12, 2.0), n01))
    nu.append(df_sub(df_scale(n22, 2.0), n00))
    nu.append(df_sub(df_scale(n23, 2.0), n01))
    nu.append(df_sub(df_scale(n33, 2.0), n00))

    def gram(i, j):
        if i == j == 0:
            return n00
        return df_scale(df_add(nu[i + j], nu[abs(i - j)]), 0.5)

    def moved(i, j):
        if i == 3 and j == 3:
            return n34
        if j == 0:
            return gram(i, 1)
        return df_scale(df_add(gram(i, j + 1), gram(i, j - 1)), 0.5)

    mat = {(i, j): df_add(moved(i, j), gram(i, j)) for i in range(4) for j in range(i + 1)}
    rhs = [df_scale(gram(i, 0), 1.0 / SHIFT) for i in range(4)]
    low, inverse = {}, []
    for k in range(4):
        inverse.append(1.0 / mat[k, k][0])
        for i in range(k + 1, 4):
            low[i, k] = df_over(mat[i, k], mat[k, k], inverse[k])
        for i in range(k + 1, 4):
            for j in range(k + 1, i + 1):
                mat[i, j] = df_sub(mat[i, j], df_mul(low[i, k], mat[j, k]))
            rhs[i] = df_sub(rhs[i], df_mul(low[i, k], rhs[k]))
    sol = [None] * 4
    for k in reversed(range(4)):
        value = df_over(rhs[k], mat[k, k], inverse[k])
        for i in range(k + 1, 4):
            value = df_sub(value, df_mul(low[i, k], sol[i]))
        sol[k] = value
    return [hi + lo for hi, lo in sol]


def final_kernel(received, both, grad, v0, v1, v2, v3, steps, changes, new_density, new_hartree, spread, density_here, hartree_here, sems):
    parts = [(received[8 * n : 8 * n + 8, :], jnp.zeros((8, LANES), jnp.float32)) for n in range(4)]
    for n in range(4, received.shape[0] // 8):
        parts[n % 4] = add_tile(parts[n % 4], received[8 * n : 8 * n + 8, :])
    while len(parts) > 1:
        half = len(parts) // 2
        merged = []
        for a, b in zip(parts[:half], parts[half:]):
            hi, err = two_sum(a[0], b[0])
            merged.append((hi, a[1] + b[1] + err))
        parts = merged
    hi, lo = fold(*parts[0], 0, (1, 2))
    lane = lane_ids((1, LANES))
    last, err = two_sum(hi[3:4], hi[7:8])
    err = err + (lo[3:4] + lo[7:8])
    first = hi[3:4]
    second = jnp.where(lane >= HALF, last, hi[7:8])
    low = jnp.where(lane >= HALF, err, lo[7:8])
    low = low + jnp.where(lane == HALF, pltpu.roll(second, LANES - 1, 1), pltpu.roll(second, LANES - 7, 1))
    for n, value in enumerate((first, second, low)):
        spread[LANES * n : LANES * n + LANES, :] = jnp.transpose(jnp.broadcast_to(value, (LANES, LANES)))

    def row(n):
        return spread[place(n) : place(n) + 1, :]

    def moment(n):
        at = LANES + (MOM_LANE + n if n < 7 else HALF)
        return quick_sum(spread[at : at + 1, :], spread[LANES + at : LANES + at + 1, :])

    mix = solve_krylov([moment(n) for n in range(8)])

    def s_s(i, j):
        return row(ROW_GRAM + PAIR_ROW[min(i, j), max(i, j)])

    def y_y(i, j):
        return row(ROW_GRAM + 36 + PAIR_ROW[min(i, j), max(i, j)])

    def s_y(i, j):
        return row(ROW_GRAM + 72 + 8 * i + j)

    pairs = range(HIST)
    theta, rest, inverse = [], [], []
    for i in pairs:
        curv, norm = s_y(i, i), s_s(i, i)
        kept = (1.0 - damp_floor) * norm
        damp = jnp.where(curv >= damp_floor * norm, 1.0, kept / jnp.maximum(norm - curv, kept))
        theta.append(damp)
        rest.append(1.0 - damp)
        inverse.append(1.0 / (damp * curv + (1.0 - damp) * norm))

    def s_bar(i, j):
        return theta[j] * s_y(i, j) + rest[j] * s_s(i, j)

    def bar_bar(i, j):
        return theta[i] * (theta[j] * y_y(i, j) + rest[j] * s_y(j, i)) + rest[i] * s_bar(i, j)

    last = HIST - 1
    scaling = s_bar(last, last) / bar_bar(last, last)

    def energy(n):
        value = row(ROW_BASE + 16 + n)
        for j in range(4):
            value = value + mix[j] * row(ROW_W + 17 * j + n)
        return value

    chem = energy(16) / row(ROW_BASE + 33)

    def gradient(n):
        return energy(n) - chem * row(ROW_BASE + n)

    s_grad = [gradient(i) for i in pairs]
    bar_grad = [theta[i] * gradient(HIST + i) + rest[i] * s_grad[i] for i in pairs]

    first = [None] * HIST
    pending = list(s_grad)
    for j in reversed(pairs):
        first[j] = inverse[j] * pending[j]
        for i in range(j):
            pending[i] = pending[i] - first[j] * s_bar(i, j)
    pending = list(bar_grad)
    for j in pairs:
        for i in pairs:
            pending[i] = pending[i] - first[j] * bar_bar(i, j)
    pending = [scaling * value for value in pending]
    step_mix, change_mix = [], []
    for j in pairs:
        net = first[j] - inverse[j] * pending[j]
        for i in range(j + 1, HIST):
            pending[i] = pending[i] + net * s_bar(j, i)
        change_mix.append((-step_length) * (-scaling * first[j] * theta[j]))
        step_mix.append((-step_length) * (net - scaling * first[j] * rest[j]))

    wide = lambda value: jnp.broadcast_to(value, (8, LANES))
    mix = [wide(value) for value in mix]
    chem, gain = wide(chem), wide((-step_length) * scaling)
    step_mix = [wide(value) for value in step_mix]
    change_mix = [wide(value) for value in change_mix]
    basis = (v0, v1, v2, v3)

    def leave(i):
        return [
            pltpu.make_async_copy(here.at[i], out.at[i], sems.at[n, i])
            for n, (here, out) in enumerate(((density_here, new_density), (hartree_here, new_hartree)))
        ]

    for i in range(REACH):
        for b in range(8):
            at = pl.ds(8 * b, 8)
            rho = both[REACH + i, at, :]
            lift = mix[0] * v0[i, at, :]
            for j in range(1, 4):
                lift = lift + mix[j] * basis[j][i, at, :]
            hartree_here[i, at, :] = both[i, at, :] + lift
            slope = grad[i, at, :] + 2.0 * rho * lift - chem * rho
            parts = [rho, gain * slope, step_mix[0] * steps[0, i, at, :], change_mix[0] * changes[0, i, at, :]]
            for f in range(1, HIST):
                parts[2] = parts[2] + step_mix[f] * steps[f, i, at, :]
                parts[3] = parts[3] + change_mix[f] * changes[f, i, at, :]
            density_here[i, at, :] = parts[0] + (parts[1] + (parts[2] + parts[3]))
        for copy in leave(i):
            copy.start()
    for i in range(REACH):
        for copy in leave(i):
            copy.wait()


def call(kernel, outs, args, scratch=(), flops=0, in_hbm=(), out_hbm=False):
    args = [pltpu.with_memory_space_constraint(x, pltpu.HBM) if n in in_hbm else x for n, x in enumerate(args)]
    shapes = [jax.ShapeDtypeStruct(shape, jnp.float32) for shape in outs]
    size = sum(4 * math.prod(a.shape) for a in (*args, *shapes))
    return pl.pallas_call(
        kernel,
        out_shape=shapes,
        in_specs=[pl.BlockSpec(memory_space=pltpu.HBM if n in in_hbm else pltpu.VMEM) for n in range(len(args))],
        out_specs=[pl.BlockSpec(memory_space=pltpu.HBM if out_hbm else pltpu.VMEM)] * len(outs),
        scratch_shapes=[pltpu.VMEM(s, jnp.float32) if isinstance(s, tuple) else s for s in scratch],
        cost_estimate=pl.CostEstimate(flops=flops, bytes_accessed=size, transcendentals=0),
        compiler_params=pltpu.CompilerParams(vmem_limit_bytes=VMEM_LIMIT),
    )(*args)


def ring(axis, step):
    size = lax.axis_size(axis)
    return [(i, (i + step) % size) for i in range(size)]


def swap(axis, odd_up):
    size = lax.axis_size(axis)
    return [(i, (i + (1 if i % 2 == odd_up else -1)) % size) for i in range(size)]


def after(values, *earlier):
    return lax.optimization_barrier((tuple(values), earlier))[0]


def x_halo(block):
    far = lax.ppermute(block, "blk", swap("blk", 1))
    return (lax.ppermute(block, "blk", swap("blk", 0)), far)


def z_halo(face_a, face_b):
    return (lax.ppermute(face_a, "gz", swap("gz", 0)), lax.ppermute(face_b, "gz", swap("gz", 1)))


def on_device(sqrt_density, ion_charge, ion_potential, hartree_prev, hist_steps, hist_changes):
    block = sqrt_density.shape
    ext = (block[0], block[1] + 16, block[2])
    face = (24, LANES)
    cells = math.prod(block)
    cells = math.prod(block)
    work = 300 * cells
    inputs = (hartree_prev, sqrt_density, ion_charge)
    halo = x_halo(hartree_prev)
    both, charge, *faces = call(
        launch_kernel,
        [(2 * REACH, *block[1:]), block, (48, LANES), (48, LANES)],
        inputs,
        [pltpu.SemaphoreType.DMA((3,))],
        in_hbm=(0, 1, 2),
    )
    ends = z_halo(*faces)
    density_ends = ends
    half = (REACH, block[1] // 2, LANES)

    def advance(gain, inner, halo, ends, last=False):
        (mid,) = call(functools.partial(z_kernel, gain), [block], [inner, *ends], flops=work)
        return call(
            functools.partial(last_x_kernel if last else x_kernel, gain),
            [block, half, half] if last else [block],
            [mid, *halo],
            flops=work,
        )

    def exchange(block_now):
        halo = x_halo(block_now)
        return halo, z_halo(*call(pack_kernel, [face, face], [block_now], flops=work))

    stored = hist_steps.shape
    inner, *history, r1 = call(
        side_one,
        [block, stored, stored, (112, LANES)],
        [both, charge, hist_steps, hist_changes],
        [ext, pltpu.SemaphoreType.DMA((2 * FETCHES,))],
        work,
        in_hbm=(2, 3),
    )
    (v0,) = advance(1.0, inner, halo, ends)
    halo, ends = exchange(v0)
    density_halo = x_halo(after((sqrt_density,), v0)[0])
    (inner,) = call(side_two, [block], [v0], [ext], work)
    (v1,) = advance(-1.0 / SHIFT, inner, halo, ends)
    halo, ends = exchange(v1)
    inner, grad, r3, m3 = call(
        side_three,
        [block, block, (40, LANES), (8, LANES)],
        [v0, v1, both, *density_halo, *density_ends, ion_potential, *history],
        [ext],
        work,
    )
    (v2,) = advance(-2.0 / SHIFT, inner, halo, ends)
    halo, ends = exchange(v2)
    inner, r4, m4 = call(
        side_four, [block, (80, LANES), (8, LANES)], [v1, v2, both, grad, *history], [ext], work
    )
    v3, to_near, to_far = advance(-2.0 / SHIFT, inner, halo, ends, last=True)
    far = lax.ppermute(to_far, "blk", swap("blk", 1))
    near = lax.ppermute(to_near, "blk", swap("blk", 0))
    (upper,) = call(pack_upper_kernel, [face], [v3], flops=work)
    z_left = lax.ppermute(upper, "gz", ring("gz", 1))
    kept, given = call(
        side_five,
        [(1, LANES), (1, LANES)],
        [v2, v3, both, *history, r1, r3, r4, m3, m4],
        [(2 * LANES, LANES), (8, LANES)],
        work,
    )
    taken = lax.ppermute(given, "blk", swap("blk", 0))
    (inner,) = call(inner_moment_kernel, [(8, LANES)], [after((v3,), given)[0]], [ext], work)
    row, part = call(couple_kernel, [(1, LANES), (8, LANES)], [v3, z_left, inner, kept, taken], flops=work)
    devices = lax.axis_size("blk") * lax.axis_size("gz")
    (outgoing,) = call(send_kernel, [(devices, LANES)], [v3, far, near, part, row], flops=work)
    received = lax.all_to_all(outgoing.reshape(devices, 1, LANES), ("blk", "gz"), 0, 0, tiled=True)
    return tuple(
        call(
            final_kernel,
            [block, block],
            [received.reshape(devices, LANES), both, grad, v0, v1, v2, v3, *history],
            [(3 * LANES, LANES), block, block, pltpu.SemaphoreType.DMA((2, REACH))],
            work,
            out_hbm=True,
        )
    )


def solution(mesh):
    placed = (
        P("blk", None, "gz"),
        P("blk", None, "gz"),
        P("blk", None, "gz"),
        P("blk", None, "gz"),
        P(None, "blk", None, "gz"),
        P(None, "blk", None, "gz"),
    )
    return jax.shard_map(
        on_device,
        mesh=mesh,
        in_specs=placed,
        out_specs=(P("blk", None, "gz"), P("blk", None, "gz")),
        check_vma=False,
    )
```

```python
import functools
import math

import jax
import jax.numpy as jnp
from jax import lax
from jax.experimental import pallas as pl
from jax.experimental.pallas import tpu as pltpu
from jax.sharding import PartitionSpec as P

center = -5369.0 / 1800.0
coeffs = (12.0 / 7.0, -15.0 / 56.0, 10.0 / 189.0, -1.0 / 112.0, 2.0 / 825.0, -1.0 / 4752.0)
screen = 0.0025
spacing = 0.28
source_scale = 4.0 * math.pi * spacing * spacing
tf_scale = 5.0 / 3.0 * 2.871234
step_length = 0.01
damp_floor = 0.2

SHIFT = 2.0
HIST = 8
REACH = 6
LANES = 128
VMEM_LIMIT = 24 * 1024 * 1024

ROW_GRAM = 0
ROW_BASE = 136
ROW_W = 170
ROW_MOM = 238
HALF = 126


def place(n):
    return n if n < HALF else n + LANES - HALF


MOM_LANE = place(ROW_MOM) - LANES
PAIRS = tuple((i, j) for i in range(HIST) for j in range(i, HIST))
PAIR_ROW = {pair: row for row, pair in enumerate(PAIRS)}


def two_sum(a, b):
    s = a + b
    bb = s - a
    return s, (a - (s - bb)) + (b - bb)


def quick_sum(a, b):
    s = a + b
    return s, b - (s - a)


def split(a):
    t = 4097.0 * a
    hi = t - (t - a)
    return hi, a - hi


def two_prod(a, b):
    p = a * b
    ah, al = split(a)
    bh, bl = split(b)
    return p, ((ah * bh - p) + ah * bl + al * bh) + al * bl


def df_add(a, b):
    s, e = two_sum(a[0], b[0])
    return quick_sum(s, e + (a[1] + b[1]))


def df_neg(a):
    return (-a[0], -a[1])


def df_sub(a, b):
    return df_add(a, df_neg(b))


def df_scale(a, factor):
    return (a[0] * factor, a[1] * factor)


def df_mul(a, b):
    p, e = two_prod(a[0], b[0])
    return quick_sum(p, e + (a[0] * b[1] + a[1] * b[0]))


def df_over(a, b, inverse):
    q = a[0] * inverse
    p, e = two_prod(q, b[0])
    rest = ((a[0] - p) - e) + (a[1] - q * b[1])
    return quick_sum(q, rest * inverse)


def lane_ids(shape):
    return lax.broadcasted_iota(jnp.int32, shape, len(shape) - 1)


def z_matrix():
    shape = (LANES, LANES)
    apart = jnp.abs(lax.broadcasted_iota(jnp.int32, shape, 0) - lax.broadcasted_iota(jnp.int32, shape, 1))
    matrix = jnp.where(apart == 0, 3.0 * center, 0.0)
    for k, weight in enumerate(coeffs, 1):
        matrix = jnp.where(apart == k, weight, matrix)
    return matrix


def inner_planes(own, ext):
    fill_ext(own, ext)
    layers, rows, lanes = own.shape
    along_z = lax.dot_general(
        own[...].reshape(layers * rows, lanes),
        z_matrix(),
        (((1,), (0,)), ((), ())),
        precision=lax.Precision.HIGHEST,
        preferred_element_type=jnp.float32,
    )
    for i in range(layers):
        total = along_z[rows * i : rows * i + rows]
        for k, weight in enumerate(coeffs, 1):
            pair = ext[i, 8 + k : 8 + k + rows, :] + ext[i, 8 - k : 8 - k + rows, :]
            if i + k < layers:
                pair = pair + own[i + k]
            if i - k >= 0:
                pair = pair + own[i - k]
            total = total + weight * pair
        yield i, total, own[i]


def edge_faces(z_left, z_right):
    lane = lane_ids((24, LANES)) % 8
    lower = jnp.zeros((24, LANES), jnp.float32)
    upper = jnp.zeros((24, LANES), jnp.float32)
    for k, weight in enumerate(coeffs, 1):
        lower = lower + jnp.where(lane < k, weight * pltpu.roll(z_left, LANES - 8 + k, 1), 0.0)
        if z_right is not None:
            upper = upper + jnp.where(lane >= 8 - k, weight * pltpu.roll(z_right, 8 - k, 1), 0.0)
    return lower, upper


def side_plane(i, block, below, rows=slice(None)):
    total = None
    for k, weight in enumerate(coeffs, 1):
        layer = i - k + REACH if below else i + k - REACH
        if 0 <= layer < REACH:
            term = weight * block[layer, rows, :]
            total = term if total is None else total + term
    return total


def z_plane(i, faces, tiles=8):
    lane = lane_ids((8, LANES))
    lower, upper = (face[8 * (i // 2) : 8 * (i // 2) + 8] for face in faces)
    out = []
    for b in range(tiles):
        j = 8 * (i % 2) + b
        tile = jnp.where(lane < 8, pltpu.roll(lower, (LANES - 8 * j) % LANES, 1), 0.0)
        tile = jnp.where(lane >= LANES - 8, pltpu.roll(upper, (2 * LANES - 8 - 8 * j) % LANES, 1), tile)
        out.append(tile)
    return jnp.concatenate(out, axis=0)


def fill_ext(own, ext):
    rows = own.shape[1]
    ext[:, 8 : 8 + rows, :] = own[...]
    ext[:, 0:8, :] = own[:, rows - 8 : rows, :]
    ext[:, 8 + rows : 16 + rows, :] = own[:, 0:8, :]


def pack_faces(src, layers):
    lane = lane_ids((8, LANES))
    firsts, lasts = [], []
    for m in range(3):
        first = jnp.zeros((8, LANES), jnp.float32)
        last = jnp.zeros((8, LANES), jnp.float32)
        for j in range(16):
            n = 16 * m + j
            tile = src[layers + n // 8, 8 * (n % 8) : 8 * (n % 8) + 8, :]
            here = (lane >= 8 * j) & (lane < 8 * j + 8)
            first = jnp.where(here, pltpu.roll(tile, 8 * j, 1) if j else tile, first)
            last = jnp.where(here, pltpu.roll(tile, (8 * j + 8) % LANES, 1) if j < 15 else tile, last)
        firsts.append(first)
        lasts.append(last)
    return jnp.concatenate(firsts, axis=0), jnp.concatenate(lasts, axis=0)


def is_odd(axis):
    return lax.rem(lax.axis_index(axis), 2) == 1


def by_partner(lower, upper):
    odd = is_odd("gz")
    return jnp.where(odd, lower, upper), jnp.where(odd, upper, lower)


def by_side(first, second):
    odd = is_odd("gz")
    return jnp.where(odd, first, second), jnp.where(odd, second, first)


def with_sides(body):
    odd = is_odd("blk")

    @pl.when(odd)
    def _():
        body(True, False)

    @pl.when(jnp.logical_not(odd))
    def _():
        body(False, True)


def fold(hi, lo, axis, steps):
    for step in steps:
        hi, err = two_sum(hi, pltpu.roll(hi, step, axis))
        lo = lo + pltpu.roll(lo, step, axis) + err
    return hi, lo


def fold_rows(acc):
    hi, lo = fold(*acc, 0, (4, 2, 1))
    return hi[0:1], lo[0:1]


def fold_lanes(hi, lo):
    return quick_sum(*fold(hi, lo, 1, (64, 32, 16, 8, 4, 2, 1)))


def add_tile(acc, product):
    hi, err = two_sum(acc[0], product)
    return hi, acc[1] + err


def tile_of(ref, i, b):
    return ref[i, 8 * b : 8 * b + 8, :]


def store_moments(pairs, moments):
    zero = jnp.zeros((8, LANES), jnp.float32)

    def body(i, accs):
        for b in range(8):
            accs = tuple(
                add_tile(acc, tile_of(a, i, b) * tile_of(c, i, b)) for acc, (a, c) in zip(accs, pairs)
            )
        return accs

    accs = lax.fori_loop(0, REACH, body, tuple((zero, zero) for _ in pairs))
    for n, acc in enumerate(accs):
        moments[2 * n : 2 * n + 1, :], moments[2 * n + 1 : 2 * n + 2, :] = fold_rows(acc)


def collapse(acc):
    return jnp.sum(acc, axis=0, keepdims=True)


def launch_kernel(hartree, density, charge, both, charge_here, face_a, face_b, sems):
    places = (both.at[pl.ds(0, REACH)], both.at[pl.ds(REACH, REACH)], charge_here)
    copies = [
        pltpu.make_async_copy(src, dst, sems.at[n])
        for n, (src, dst) in enumerate(zip((hartree, density, charge), places))
    ]
    for copy in copies:
        copy.start()
    for n in range(2):
        copies[n].wait()
        rows = slice(24 * n, 24 * n + 24)
        face_a[rows, :], face_b[rows, :] = by_partner(*pack_faces(both, REACH * n))
    copies[2].wait()


def inner_residual(both, charge, out, ext):
    hartree = both.at[pl.ds(0, REACH)]
    for i, lap, values in inner_planes(hartree, ext):
        rho = both[REACH + i]
        out[i] = source_scale * (rho * rho - charge[i]) - (screen * values - lap)


def inner_basis(own, prior, out, ext):
    for i, lap, values in inner_planes(own, ext):
        moved = (screen / SHIFT - 1.0) * values - (1.0 / SHIFT) * lap
        out[i] = moved if prior is None else 2.0 * moved - prior[i]


def z_kernel(gain, inner, z_first, z_second, out):
    faces = edge_faces(*by_side(z_first[0:24, :], z_second[0:24, :]))
    for i in range(REACH):
        out[i] = inner[i] + gain * z_plane(i, faces)


def x_kernel(gain, inner, near, far, out):
    def body(near_below, far_below):
        for i in range(REACH):
            out[i] = inner[i] + gain * (side_plane(i, near, near_below) + side_plane(i, far, far_below))

    with_sides(body)


def last_x_kernel(gain, inner, near, far, out, to_near, to_far):
    half = out.shape[1] // 2

    def body(near_below, far_below):
        for i in range(REACH):
            plane = inner[i] + gain * (side_plane(i, near, near_below) + side_plane(i, far, far_below))
            out[i] = plane
            for ref, below in ((to_near, near_below), (to_far, far_below)):
                ref[i] = plane[:half] if below else plane[half:]

    with_sides(body)


def pack_kernel(block, face_a, face_b):
    face_a[...], face_b[...] = by_partner(*pack_faces(block, 0))


def pack_upper_kernel(block, face):
    face[...] = pack_faces(block, 0)[1]


def store(rows, base, values):
    for n, value in enumerate(values):
        rows[base + n : base + n + 1, :] = value


def gram_dots(left, right, pairs):
    zero = jnp.zeros((8, LANES), jnp.float32)

    def body(i, accs):
        for b in range(8):
            at = pl.ds(8 * b, 8)
            l_tiles = {p: left[p, i, at, :] for p in sorted({p for p, _ in pairs})}
            if left is right:
                r_tiles = l_tiles
            else:
                r_tiles = {q: right[q, i, at, :] for q in sorted({q for _, q in pairs})}
            accs = tuple(acc + l_tiles[p] * r_tiles[q] for acc, (p, q) in zip(accs, pairs))
        return accs

    accs = lax.fori_loop(0, REACH, body, tuple(zero for _ in pairs))
    return [collapse(acc) for acc in accs]


CROSS_PAIRS = tuple((i, j) for i in range(HIST) for j in range(HIST))


def field_dots(groups, others, plain=()):
    zero = jnp.zeros((8, LANES), jnp.float32)
    fields = [(group, f) for group in groups for f in range(HIST)]
    count = len(fields)

    def body(i, accs):
        accs = list(accs)
        for b in range(8):
            at = pl.ds(8 * b, 8)
            tiles = [other(i, b) for other in others]
            for f, (group, which) in enumerate(fields):
                field = group[which, i, at, :]
                for o, tile in enumerate(tiles):
                    accs[o * count + f] = accs[o * count + f] + field * tile
            for n, (one, two) in enumerate(plain, len(others) * count):
                accs[n] = accs[n] + one(i, b) * two(i, b)
        return tuple(accs)

    total = count * len(others) + len(plain)
    return [collapse(acc) for acc in lax.fori_loop(0, REACH, body, (zero,) * total)]


def base_gradient(both, near, far, z_first, z_second, potential, grad, ext):
    hartree = both.at[pl.ds(0, REACH)]
    density = both.at[pl.ds(REACH, REACH)]
    faces = edge_faces(*by_side(z_first[24:48, :], z_second[24:48, :]))

    def body(near_below, far_below):
        for i in range(REACH):
            grad[i] = side_plane(i, near, near_below) + side_plane(i, far, far_below) + z_plane(i, faces)

    with_sides(body)
    for i, lap, rho in inner_planes(density, ext):
        power = jnp.exp(jnp.log(rho) * (4.0 / 3.0))
        grad[i] = 2.0 * rho * (hartree[i] + potential[i] + tf_scale * power) - (lap + grad[i]) * (
            1.0 / (spacing * spacing)
        )


def density_tile(both):
    return lambda i, b: tile_of(both, REACH + i, b)


def lifted_tile(both, vector):
    return lambda i, b: 2.0 * tile_of(both, REACH + i, b) * tile_of(vector, i, b)


FETCHES = 4


def side_one(both, charge, steps, changes, inner, steps_here, changes_here, rows, ext, sems):
    each = HIST // FETCHES
    copies = [
        pltpu.make_async_copy(src.at[pl.ds(each * n, each)], dst.at[pl.ds(each * n, each)], sems.at[FETCHES * m + n])
        for m, (src, dst) in enumerate(((steps, steps_here), (changes, changes_here)))
        for n in range(FETCHES)
    ]
    for copy in copies:
        copy.start()
    inner_residual(both, charge, inner, ext)
    for copy in copies[:FETCHES]:
        copy.wait()
    store(rows, 0, gram_dots(steps_here, steps_here, PAIRS))
    store(rows, 36, field_dots((steps_here,), [density_tile(both)]))
    for copy in copies[FETCHES:]:
        copy.wait()


def side_two(vector, inner, ext):
    inner_basis(vector, None, inner, ext)


def side_three(prior, vector, both, near, far, z_first, z_second, potential, steps, changes, *outs):
    inner, grad, rows, moments, ext = outs
    inner_basis(vector, prior, inner, ext)
    before, lifted, rho = lifted_tile(both, prior), lifted_tile(both, vector), density_tile(both)
    values = field_dots((steps, changes), [before, lifted], [(rho, before), (rho, lifted)])
    store(rows, 0, values[:16] + values[32:33] + values[16:32] + values[33:])
    store(rows, 34, gram_dots(steps, changes, CROSS_PAIRS[:32]))
    store_moments([(prior, prior), (prior, vector), (vector, vector)], moments)
    base_gradient(both, near, far, z_first, z_second, potential, grad, ext)


def side_four(prior, vector, both, grad, steps, changes, r1, r3, m3, inner, sums, rows, moments, table, ext):
    inner_basis(vector, prior, inner, ext)
    lifted, rho = lifted_tile(both, vector), density_tile(both)
    slope = lambda i, b: tile_of(grad, i, b)
    by_step = field_dots((steps,), [lifted, slope], [(rho, lifted), (rho, slope), (rho, rho)])
    by_change = field_dots((changes,), [lifted, slope, rho])
    values = by_step[:8] + by_change[:8] + by_step[16:17] + by_step[8:16] + by_change[8:16] + by_step[17:]
    store(rows, 0, values + by_change[16:])
    store(rows, 43, gram_dots(changes, changes, PAIRS))
    store(rows, 79, gram_dots(steps, changes, CROSS_PAIRS[32:]))
    store_moments([(prior, vector), (vector, vector)], moments)

    table[...] = jnp.zeros_like(table)

    def put(base, ref, start, count):
        before = max(0, min(count, HALF - base))
        if before:
            table[base : base + before, :] = ref[start : start + before, :]
        if before < count:
            at = place(base + before)
            table[at : at + count - before, :] = ref[start + before : start + count, :]

    put(ROW_GRAM, r1, 0, 36)
    put(ROW_GRAM + 36, rows, 43, 36)
    put(ROW_GRAM + 72, r3, 34, 32)
    put(ROW_GRAM + 104, rows, 79, 32)
    put(ROW_BASE, r1, 36, 8)
    put(ROW_BASE + 8, rows, 35, 8)
    put(ROW_BASE + 16, rows, 17, 18)
    put(ROW_W, r3, 0, 34)
    put(ROW_W + 34, rows, 0, 17)
    second = jnp.sum(jnp.transpose(table[LANES : 2 * LANES, :]), axis=0, keepdims=True)
    sums[0:1, :] = jnp.sum(jnp.transpose(table[0:LANES, :]), axis=0, keepdims=True)
    sums[1:2, :] = put_moments(second, [(m3, 0), (m3, 1), (m3, 2), (moments, 0), (moments, 1)], 0)


def put_moments(row, order, start):
    zero = jnp.zeros((8 - len(order), LANES), jnp.float32)
    parts = [
        jnp.concatenate([ref[2 * which + low : 2 * which + low + 1, :] for ref, which in order] + [zero], axis=0)
        for low in range(2)
    ]
    hi, lo = fold_lanes(*parts)
    lane = lane_ids((1, LANES))
    for n in range(len(order)):
        row = jnp.where(lane == MOM_LANE + start + n, hi[n : n + 1], row)
        row = jnp.where(lane == MOM_LANE + 7 + start + n, lo[n : n + 1], row)
    return row


def side_five(prior, vector, both, steps, changes, sums, kept, given, table, m5):
    lifted, rho = lifted_tile(both, vector), density_tile(both)
    table[...] = jnp.zeros_like(table)
    store(table, place(ROW_W + 51) - LANES, field_dots((steps, changes), [lifted], [(rho, lifted)]))
    store_moments([(prior, vector), (vector, vector)], m5)
    second = sums[1:2, :] + jnp.sum(jnp.transpose(table[...]), axis=0, keepdims=True)
    first, second = sums[0:1, :], put_moments(second, [(m5, 0), (m5, 1)], 5)
    odd = is_odd("blk")
    kept[...] = jnp.where(odd, second, first)
    given[...] = jnp.where(odd, first, second)


def inner_moment_kernel(vector, inner, ext):
    zero = jnp.zeros((8, LANES), jnp.float32)
    accs = [(zero, zero) for _ in range(2)]
    for i, lap, values in inner_planes(vector, ext):
        product = values * ((screen / SHIFT - 1.0) * values - (1.0 / SHIFT) * lap)
        for b in range(8):
            accs[b % 2] = add_tile(accs[b % 2], product[8 * b : 8 * b + 8])
    hi, err = two_sum(accs[0][0], accs[1][0])
    inner[0:1, :], inner[1:2, :] = fold_rows((hi, accs[0][1] + accs[1][1] + err))


def couple(own, block, below, acc):
    half = own.shape[1] // 2
    for i in range(REACH):
        product = own[i, half:, :] * side_plane(i, block, True) if below else own[i, :half, :] * side_plane(i, block, False)
        for b in range(half // 8):
            acc = add_tile(acc, product[8 * b : 8 * b + 8])
    return acc


def send_kernel(own, far, near, z_left, inner, kept, taken, out):
    faces = edge_faces(z_left[...], None)

    def body(near_below, far_below):
        zero = jnp.zeros((8, LANES), jnp.float32)
        accs = [(zero, zero) for _ in range(2)]
        for i in range(REACH):
            product = own[i] * z_plane(i, faces)
            for b in range(8):
                accs[b % 2] = add_tile(accs[b % 2], product[8 * b : 8 * b + 8])
        accs = [couple(own, far, far_below, accs[0]), couple(own, near, near_below, accs[1])]
        hi, err = two_sum(accs[0][0], accs[1][0])
        sides = fold_rows((hi, accs[0][1] + accs[1][1] + err))
        hi, lo = fold_lanes(*df_add(df_scale(sides, -2.0 / SHIFT), (inner[0:1, :], inner[1:2, :])))
        lane = lane_ids((1, LANES))
        row, err = two_sum(kept[...], taken[...])
        low_lane = (lane >= MOM_LANE + 7) & (lane < MOM_LANE + 14) & is_odd("blk")
        row = jnp.where(low_lane, row + pltpu.roll(err, 7, 1), row)
        row = jnp.where(lane == HALF, hi, jnp.where(lane == HALF + 1, lo, row))
        out[...] = jnp.broadcast_to(row, out.shape)

    with_sides(body)


def solve_krylov(moment):
    n00, n01, n11, n12, n22, n23, n33, n34 = moment
    nu = [n00, n01]
    nu.append(df_sub(df_scale(n11, 2.0), n00))
    nu.append(df_sub(df_scale(n12, 2.0), n01))
    nu.append(df_sub(df_scale(n22, 2.0), n00))
    nu.append(df_sub(df_scale(n23, 2.0), n01))
    nu.append(df_sub(df_scale(n33, 2.0), n00))

    def gram(i, j):
        if i == j == 0:
            return n00
        return df_scale(df_add(nu[i + j], nu[abs(i - j)]), 0.5)

    def moved(i, j):
        if i == 3 and j == 3:
            return n34
        if j == 0:
            return gram(i, 1)
        return df_scale(df_add(gram(i, j + 1), gram(i, j - 1)), 0.5)

    mat = {(i, j): df_add(moved(i, j), gram(i, j)) for i in range(4) for j in range(i + 1)}
    rhs = [df_scale(gram(i, 0), 1.0 / SHIFT) for i in range(4)]
    low, inverse = {}, []
    for k in range(4):
        inverse.append(1.0 / mat[k, k][0])
        for i in range(k + 1, 4):
            low[i, k] = df_over(mat[i, k], mat[k, k], inverse[k])
        for i in range(k + 1, 4):
            for j in range(k + 1, i + 1):
                mat[i, j] = df_sub(mat[i, j], df_mul(low[i, k], mat[j, k]))
            rhs[i] = df_sub(rhs[i], df_mul(low[i, k], rhs[k]))
    sol = [None] * 4
    for k in reversed(range(4)):
        value = df_over(rhs[k], mat[k, k], inverse[k])
        for i in range(k + 1, 4):
            value = df_sub(value, df_mul(low[i, k], sol[i]))
        sol[k] = value
    return [hi + lo for hi, lo in sol]


def final_kernel(received, both, grad, v0, v1, v2, v3, steps, changes, new_density, new_hartree, spread, density_here, hartree_here, sems):
    parts = [(received[8 * n : 8 * n + 8, :], jnp.zeros((8, LANES), jnp.float32)) for n in range(4)]
    for n in range(4, received.shape[0] // 8):
        parts[n % 4] = add_tile(parts[n % 4], received[8 * n : 8 * n + 8, :])
    while len(parts) > 1:
        half = len(parts) // 2
        merged = []
        for a, b in zip(parts[:half], parts[half:]):
            hi, err = two_sum(a[0], b[0])
            merged.append((hi, a[1] + b[1] + err))
        parts = merged
    hi, lo = fold(*parts[0], 0, (1, 2))
    lane = lane_ids((1, LANES))
    last, err = two_sum(hi[3:4], hi[7:8])
    err = err + (lo[3:4] + lo[7:8])
    first = hi[3:4]
    second = jnp.where(lane >= HALF, last, hi[7:8])
    low = jnp.where(lane >= HALF, err, lo[7:8])
    low = low + jnp.where(lane == HALF, pltpu.roll(second, LANES - 1, 1), pltpu.roll(second, LANES - 7, 1))
    for n, value in enumerate((first, second, low)):
        spread[LANES * n : LANES * n + LANES, :] = jnp.transpose(jnp.broadcast_to(value, (LANES, LANES)))

    def row(n):
        return spread[place(n) : place(n) + 1, :]

    def moment(n):
        at = LANES + (MOM_LANE + n if n < 7 else HALF)
        return quick_sum(spread[at : at + 1, :], spread[LANES + at : LANES + at + 1, :])

    mix = solve_krylov([moment(n) for n in range(8)])

    def s_s(i, j):
        return row(ROW_GRAM + PAIR_ROW[min(i, j), max(i, j)])

    def y_y(i, j):
        return row(ROW_GRAM + 36 + PAIR_ROW[min(i, j), max(i, j)])

    def s_y(i, j):
        return row(ROW_GRAM + 72 + 8 * i + j)

    pairs = range(HIST)
    theta, rest, inverse = [], [], []
    for i in pairs:
        curv, norm = s_y(i, i), s_s(i, i)
        kept = (1.0 - damp_floor) * norm
        damp = jnp.where(curv >= damp_floor * norm, 1.0, kept / jnp.maximum(norm - curv, kept))
        theta.append(damp)
        rest.append(1.0 - damp)
        inverse.append(1.0 / (damp * curv + (1.0 - damp) * norm))

    def s_bar(i, j):
        return theta[j] * s_y(i, j) + rest[j] * s_s(i, j)

    def bar_bar(i, j):
        return theta[i] * (theta[j] * y_y(i, j) + rest[j] * s_y(j, i)) + rest[i] * s_bar(i, j)

    last = HIST - 1
    scaling = s_bar(last, last) / bar_bar(last, last)

    def energy(n):
        value = row(ROW_BASE + 16 + n)
        for j in range(4):
            value = value + mix[j] * row(ROW_W + 17 * j + n)
        return value

    chem = energy(16) / row(ROW_BASE + 33)

    def gradient(n):
        return energy(n) - chem * row(ROW_BASE + n)

    s_grad = [gradient(i) for i in pairs]
    bar_grad = [theta[i] * gradient(HIST + i) + rest[i] * s_grad[i] for i in pairs]

    first = [None] * HIST
    pending = list(s_grad)
    for j in reversed(pairs):
        first[j] = inverse[j] * pending[j]
        for i in range(j):
            pending[i] = pending[i] - first[j] * s_bar(i, j)
    pending = list(bar_grad)
    for j in pairs:
        for i in pairs:
            pending[i] = pending[i] - first[j] * bar_bar(i, j)
    pending = [scaling * value for value in pending]
    step_mix, change_mix = [], []
    for j in pairs:
        net = first[j] - inverse[j] * pending[j]
        for i in range(j + 1, HIST):
            pending[i] = pending[i] + net * s_bar(j, i)
        change_mix.append((-step_length) * (-scaling * first[j] * theta[j]))
        step_mix.append((-step_length) * (net - scaling * first[j] * rest[j]))

    wide = lambda value: jnp.broadcast_to(value, (8, LANES))
    mix = [wide(value) for value in mix]
    chem, gain = wide(chem), wide((-step_length) * scaling)
    step_mix = [wide(value) for value in step_mix]
    change_mix = [wide(value) for value in change_mix]
    basis = (v0, v1, v2, v3)

    def leave(i):
        return [
            pltpu.make_async_copy(here.at[i], out.at[i], sems.at[n, i])
            for n, (here, out) in enumerate(((density_here, new_density), (hartree_here, new_hartree)))
        ]

    for i in range(REACH):
        for b in range(8):
            at = pl.ds(8 * b, 8)
            rho = both[REACH + i, at, :]
            lift = mix[0] * v0[i, at, :]
            for j in range(1, 4):
                lift = lift + mix[j] * basis[j][i, at, :]
            hartree_here[i, at, :] = both[i, at, :] + lift
            slope = grad[i, at, :] + 2.0 * rho * lift - chem * rho
            parts = [rho, gain * slope, step_mix[0] * steps[0, i, at, :], change_mix[0] * changes[0, i, at, :]]
            for f in range(1, HIST):
                parts[2] = parts[2] + step_mix[f] * steps[f, i, at, :]
                parts[3] = parts[3] + change_mix[f] * changes[f, i, at, :]
            density_here[i, at, :] = parts[0] + (parts[1] + (parts[2] + parts[3]))
        for copy in leave(i):
            copy.start()
    for i in range(REACH):
        for copy in leave(i):
            copy.wait()


def call(kernel, outs, args, scratch=(), flops=0, in_hbm=(), out_hbm=False):
    args = [pltpu.with_memory_space_constraint(x, pltpu.HBM) if n in in_hbm else x for n, x in enumerate(args)]
    shapes = [jax.ShapeDtypeStruct(shape, jnp.float32) for shape in outs]
    size = sum(4 * math.prod(a.shape) for a in (*args, *shapes))
    return pl.pallas_call(
        kernel,
        out_shape=shapes,
        in_specs=[pl.BlockSpec(memory_space=pltpu.HBM if n in in_hbm else pltpu.VMEM) for n in range(len(args))],
        out_specs=[pl.BlockSpec(memory_space=pltpu.HBM if out_hbm else pltpu.VMEM)] * len(outs),
        scratch_shapes=[pltpu.VMEM(s, jnp.float32) if isinstance(s, tuple) else s for s in scratch],
        cost_estimate=pl.CostEstimate(flops=flops, bytes_accessed=size, transcendentals=0),
        compiler_params=pltpu.CompilerParams(vmem_limit_bytes=VMEM_LIMIT),
    )(*args)


def ring(axis, step):
    size = lax.axis_size(axis)
    return [(i, (i + step) % size) for i in range(size)]


def swap(axis, odd_up):
    size = lax.axis_size(axis)
    return [(i, (i + (1 if i % 2 == odd_up else -1)) % size) for i in range(size)]


def after(values, *earlier):
    return lax.optimization_barrier((tuple(values), earlier))[0]


def x_halo(block):
    far = lax.ppermute(block, "blk", swap("blk", 1))
    return (lax.ppermute(block, "blk", swap("blk", 0)), far)


def z_halo(face_a, face_b):
    return (lax.ppermute(face_a, "gz", swap("gz", 0)), lax.ppermute(face_b, "gz", swap("gz", 1)))


def on_device(sqrt_density, ion_charge, ion_potential, hartree_prev, hist_steps, hist_changes):
    block = sqrt_density.shape
    ext = (block[0], block[1] + 16, block[2])
    face = (24, LANES)
    cells = math.prod(block)
    cells = math.prod(block)
    work = 300 * cells
    inputs = (hartree_prev, sqrt_density, ion_charge)
    halo = x_halo(hartree_prev)
    both, charge, *faces = call(
        launch_kernel,
        [(2 * REACH, *block[1:]), block, (48, LANES), (48, LANES)],
        inputs,
        [pltpu.SemaphoreType.DMA((3,))],
        in_hbm=(0, 1, 2),
    )
    ends = z_halo(*faces)
    density_ends = ends
    half = (REACH, block[1] // 2, LANES)

    def advance(gain, inner, halo, ends, last=False):
        (mid,) = call(functools.partial(z_kernel, gain), [block], [inner, *ends], flops=work)
        return call(
            functools.partial(last_x_kernel if last else x_kernel, gain),
            [block, half, half] if last else [block],
            [mid, *halo],
            flops=work,
        )

    def exchange(block_now):
        halo = x_halo(block_now)
        return halo, z_halo(*call(pack_kernel, [face, face], [block_now], flops=work))

    stored = hist_steps.shape
    inner, *history, r1 = call(
        side_one,
        [block, stored, stored, (48, LANES)],
        [both, charge, hist_steps, hist_changes],
        [ext, pltpu.SemaphoreType.DMA((2 * FETCHES,))],
        work,
        in_hbm=(2, 3),
    )
    (v0,) = advance(1.0, inner, halo, ends)
    halo, ends = exchange(v0)
    density_halo = x_halo(after((sqrt_density,), v0)[0])
    (inner,) = call(side_two, [block], [v0], [ext], work)
    (v1,) = advance(-1.0 / SHIFT, inner, halo, ends)
    halo, ends = exchange(v1)
    inner, grad, r3, m3 = call(
        side_three,
        [block, block, (72, LANES), (8, LANES)],
        [v0, v1, both, *density_halo, *density_ends, ion_potential, *history],
        [ext],
        work,
    )
    (v2,) = advance(-2.0 / SHIFT, inner, halo, ends)
    halo, ends = exchange(v2)
    inner, sums = call(
        side_four,
        [block, (2, LANES)],
        [v1, v2, both, grad, *history, r1, r3, m3],
        [(112, LANES), (8, LANES), (2 * LANES, LANES), ext],
        work,
    )
    v3, to_near, to_far = advance(-2.0 / SHIFT, inner, halo, ends, last=True)
    far = lax.ppermute(to_far, "blk", swap("blk", 1))
    near = lax.ppermute(to_near, "blk", swap("blk", 0))
    (upper,) = call(pack_upper_kernel, [face], [v3], flops=work)
    z_left = lax.ppermute(upper, "gz", ring("gz", 1))
    kept, given = call(
        side_five,
        [(1, LANES), (1, LANES)],
        [v2, v3, both, *history, sums],
        [(LANES, LANES), (8, LANES)],
        work,
    )
    taken = lax.ppermute(given, "blk", swap("blk", 0))
    (inner,) = call(inner_moment_kernel, [(8, LANES)], [after((v3,), given)[0]], [ext], work)
    devices = lax.axis_size("blk") * lax.axis_size("gz")
    (outgoing,) = call(send_kernel, [(devices, LANES)], [v3, far, near, z_left, inner, kept, taken], flops=work)
    received = lax.all_to_all(outgoing.reshape(devices, 1, LANES), ("blk", "gz"), 0, 0, tiled=True)
    return tuple(
        call(
            final_kernel,
            [block, block],
            [received.reshape(devices, LANES), both, grad, v0, v1, v2, v3, *history],
            [(3 * LANES, LANES), block, block, pltpu.SemaphoreType.DMA((2, REACH))],
            work,
            out_hbm=True,
        )
    )


def solution(mesh):
    placed = (
        P("blk", None, "gz"),
        P("blk", None, "gz"),
        P("blk", None, "gz"),
        P("blk", None, "gz"),
        P(None, "blk", None, "gz"),
        P(None, "blk", None, "gz"),
    )
    return jax.shard_map(
        on_device,
        mesh=mesh,
        in_specs=placed,
        out_specs=(P("blk", None, "gz"), P("blk", None, "gz")),
        check_vma=False,
    )
```

```python
import functools
import math

import jax
import jax.numpy as jnp
from jax import lax
from jax.experimental import pallas as pl
from jax.experimental.pallas import tpu as pltpu
from jax.sharding import PartitionSpec as P

center = -5369.0 / 1800.0
coeffs = (12.0 / 7.0, -15.0 / 56.0, 10.0 / 189.0, -1.0 / 112.0, 2.0 / 825.0, -1.0 / 4752.0)
screen = 0.0025
spacing = 0.28
source_scale = 4.0 * math.pi * spacing * spacing
tf_scale = 5.0 / 3.0 * 2.871234
step_length = 0.01
damp_floor = 0.2

SHIFT = 2.0
HIST = 8
REACH = 6
LANES = 128
VMEM_LIMIT = 24 * 1024 * 1024

ROW_GRAM = 0
ROW_BASE = 136
ROW_W = 170
ROW_MOM = 238
HALF = 126


def place(n):
    return n if n < HALF else n + LANES - HALF


MOM_LANE = place(ROW_MOM) - LANES
PAIRS = tuple((i, j) for i in range(HIST) for j in range(i, HIST))
PAIR_ROW = {pair: row for row, pair in enumerate(PAIRS)}


def two_sum(a, b):
    s = a + b
    bb = s - a
    return s, (a - (s - bb)) + (b - bb)


def quick_sum(a, b):
    s = a + b
    return s, b - (s - a)


def split(a):
    t = 4097.0 * a
    hi = t - (t - a)
    return hi, a - hi


def two_prod(a, b):
    p = a * b
    ah, al = split(a)
    bh, bl = split(b)
    return p, ((ah * bh - p) + ah * bl + al * bh) + al * bl


def df_add(a, b):
    s, e = two_sum(a[0], b[0])
    return quick_sum(s, e + (a[1] + b[1]))


def df_neg(a):
    return (-a[0], -a[1])


def df_sub(a, b):
    return df_add(a, df_neg(b))


def df_scale(a, factor):
    return (a[0] * factor, a[1] * factor)


def df_mul(a, b):
    p, e = two_prod(a[0], b[0])
    return quick_sum(p, e + (a[0] * b[1] + a[1] * b[0]))


def df_over(a, b, inverse):
    q = a[0] * inverse
    p, e = two_prod(q, b[0])
    rest = ((a[0] - p) - e) + (a[1] - q * b[1])
    return quick_sum(q, rest * inverse)


def lane_ids(shape):
    return lax.broadcasted_iota(jnp.int32, shape, len(shape) - 1)


def z_matrix():
    shape = (LANES, LANES)
    apart = jnp.abs(lax.broadcasted_iota(jnp.int32, shape, 0) - lax.broadcasted_iota(jnp.int32, shape, 1))
    matrix = jnp.where(apart == 0, 3.0 * center, 0.0)
    for k, weight in enumerate(coeffs, 1):
        matrix = jnp.where(apart == k, weight, matrix)
    return matrix


def inner_planes(own, ext):
    fill_ext(own, ext)
    layers, rows, lanes = own.shape
    along_z = lax.dot_general(
        own[...].reshape(layers * rows, lanes),
        z_matrix(),
        (((1,), (0,)), ((), ())),
        precision=lax.Precision.HIGHEST,
        preferred_element_type=jnp.float32,
    )
    for i in range(layers):
        total = along_z[rows * i : rows * i + rows]
        for k, weight in enumerate(coeffs, 1):
            pair = ext[i, 8 + k : 8 + k + rows, :] + ext[i, 8 - k : 8 - k + rows, :]
            if i + k < layers:
                pair = pair + own[i + k]
            if i - k >= 0:
                pair = pair + own[i - k]
            total = total + weight * pair
        yield i, total, own[i]


def edge_faces(z_left, z_right):
    lane = lane_ids((24, LANES)) % 8
    lower = jnp.zeros((24, LANES), jnp.float32)
    upper = jnp.zeros((24, LANES), jnp.float32)
    for k, weight in enumerate(coeffs, 1):
        lower = lower + jnp.where(lane < k, weight * pltpu.roll(z_left, LANES - 8 + k, 1), 0.0)
        if z_right is not None:
            upper = upper + jnp.where(lane >= 8 - k, weight * pltpu.roll(z_right, 8 - k, 1), 0.0)
    return lower, upper


def side_plane(i, block, below, rows=slice(None)):
    total = None
    for k, weight in enumerate(coeffs, 1):
        layer = i - k + REACH if below else i + k - REACH
        if 0 <= layer < REACH:
            term = weight * block[layer, rows, :]
            total = term if total is None else total + term
    return total


def z_plane(i, faces, tiles=8):
    lane = lane_ids((8, LANES))
    lower, upper = (face[8 * (i // 2) : 8 * (i // 2) + 8] for face in faces)
    out = []
    for b in range(tiles):
        j = 8 * (i % 2) + b
        tile = jnp.where(lane < 8, pltpu.roll(lower, (LANES - 8 * j) % LANES, 1), 0.0)
        tile = jnp.where(lane >= LANES - 8, pltpu.roll(upper, (2 * LANES - 8 - 8 * j) % LANES, 1), tile)
        out.append(tile)
    return jnp.concatenate(out, axis=0)


def fill_ext(own, ext):
    rows = own.shape[1]
    ext[:, 8 : 8 + rows, :] = own[...]
    ext[:, 0:8, :] = own[:, rows - 8 : rows, :]
    ext[:, 8 + rows : 16 + rows, :] = own[:, 0:8, :]


def pack_faces(src, layers):
    lane = lane_ids((8, LANES))
    firsts, lasts = [], []
    for m in range(3):
        first = jnp.zeros((8, LANES), jnp.float32)
        last = jnp.zeros((8, LANES), jnp.float32)
        for j in range(16):
            n = 16 * m + j
            tile = src[layers + n // 8, 8 * (n % 8) : 8 * (n % 8) + 8, :]
            here = (lane >= 8 * j) & (lane < 8 * j + 8)
            first = jnp.where(here, pltpu.roll(tile, 8 * j, 1) if j else tile, first)
            last = jnp.where(here, pltpu.roll(tile, (8 * j + 8) % LANES, 1) if j < 15 else tile, last)
        firsts.append(first)
        lasts.append(last)
    return jnp.concatenate(firsts, axis=0), jnp.concatenate(lasts, axis=0)


def is_odd(axis):
    return lax.rem(lax.axis_index(axis), 2) == 1


def by_partner(lower, upper):
    odd = is_odd("gz")
    return jnp.where(odd, lower, upper), jnp.where(odd, upper, lower)


def by_side(first, second):
    odd = is_odd("gz")
    return jnp.where(odd, first, second), jnp.where(odd, second, first)


def with_sides(body):
    odd = is_odd("blk")

    @pl.when(odd)
    def _():
        body(True, False)

    @pl.when(jnp.logical_not(odd))
    def _():
        body(False, True)


def fold(hi, lo, axis, steps):
    for step in steps:
        hi, err = two_sum(hi, pltpu.roll(hi, step, axis))
        lo = lo + pltpu.roll(lo, step, axis) + err
    return hi, lo


def fold_rows(acc):
    hi, lo = fold(*acc, 0, (4, 2, 1))
    return hi[0:1], lo[0:1]


def fold_lanes(hi, lo):
    return quick_sum(*fold(hi, lo, 1, (64, 32, 16, 8, 4, 2, 1)))


def add_tile(acc, product):
    hi, err = two_sum(acc[0], product)
    return hi, acc[1] + err


def tile_of(ref, i, b):
    return ref[i, 8 * b : 8 * b + 8, :]


def store_moments(pairs, moments):
    zero = jnp.zeros((8, LANES), jnp.float32)

    def body(i, accs):
        for b in range(8):
            accs = tuple(
                add_tile(acc, tile_of(a, i, b) * tile_of(c, i, b)) for acc, (a, c) in zip(accs, pairs)
            )
        return accs

    accs = lax.fori_loop(0, REACH, body, tuple((zero, zero) for _ in pairs))
    for n, acc in enumerate(accs):
        moments[2 * n : 2 * n + 1, :], moments[2 * n + 1 : 2 * n + 2, :] = fold_rows(acc)


def collapse(acc):
    return jnp.sum(acc, axis=0, keepdims=True)


def launch_kernel(hartree, density, charge, both, charge_here, face_a, face_b, sems):
    places = (both.at[pl.ds(0, REACH)], both.at[pl.ds(REACH, REACH)], charge_here)
    copies = [
        pltpu.make_async_copy(src, dst, sems.at[n])
        for n, (src, dst) in enumerate(zip((hartree, density, charge), places))
    ]
    for copy in copies:
        copy.start()
    for n in range(2):
        copies[n].wait()
        rows = slice(24 * n, 24 * n + 24)
        face_a[rows, :], face_b[rows, :] = by_partner(*pack_faces(both, REACH * n))
    copies[2].wait()


def inner_residual(both, charge, out, ext):
    hartree = both.at[pl.ds(0, REACH)]
    for i, lap, values in inner_planes(hartree, ext):
        rho = both[REACH + i]
        out[i] = source_scale * (rho * rho - charge[i]) - (screen * values - lap)


def inner_basis(own, prior, out, ext):
    for i, lap, values in inner_planes(own, ext):
        moved = (screen / SHIFT - 1.0) * values - (1.0 / SHIFT) * lap
        out[i] = moved if prior is None else 2.0 * moved - prior[i]


def z_kernel(gain, inner, z_first, z_second, out):
    faces = edge_faces(*by_side(z_first[0:24, :], z_second[0:24, :]))
    for i in range(REACH):
        out[i] = inner[i] + gain * z_plane(i, faces)


def x_kernel(gain, inner, near, far, out):
    def body(near_below, far_below):
        for i in range(REACH):
            out[i] = inner[i] + gain * (side_plane(i, near, near_below) + side_plane(i, far, far_below))

    with_sides(body)


def last_x_kernel(gain, inner, near, far, out, to_near, to_far):
    half = out.shape[1] // 2

    def body(near_below, far_below):
        for i in range(REACH):
            plane = inner[i] + gain * (side_plane(i, near, near_below) + side_plane(i, far, far_below))
            out[i] = plane
            for ref, below in ((to_near, near_below), (to_far, far_below)):
                ref[i] = plane[:half] if below else plane[half:]

    with_sides(body)


def pack_kernel(block, face_a, face_b):
    face_a[...], face_b[...] = by_partner(*pack_faces(block, 0))


def pack_upper_kernel(block, face):
    face[...] = pack_faces(block, 0)[1]


def store(rows, base, values):
    for n, value in enumerate(values):
        rows[base + n : base + n + 1, :] = value


def gram_dots(left, right, pairs):
    zero = jnp.zeros((8, LANES), jnp.float32)

    def body(i, accs):
        for b in range(8):
            at = pl.ds(8 * b, 8)
            l_tiles = {p: left[p, i, at, :] for p in sorted({p for p, _ in pairs})}
            if left is right:
                r_tiles = l_tiles
            else:
                r_tiles = {q: right[q, i, at, :] for q in sorted({q for _, q in pairs})}
            accs = tuple(acc + l_tiles[p] * r_tiles[q] for acc, (p, q) in zip(accs, pairs))
        return accs

    accs = lax.fori_loop(0, REACH, body, tuple(zero for _ in pairs))
    return [collapse(acc) for acc in accs]


CROSS_PAIRS = tuple((i, j) for i in range(HIST) for j in range(HIST))


def field_dots(groups, others, plain=()):
    zero = jnp.zeros((8, LANES), jnp.float32)
    fields = [(group, f) for group in groups for f in range(HIST)]
    count = len(fields)

    def body(i, accs):
        accs = list(accs)
        for b in range(8):
            at = pl.ds(8 * b, 8)
            tiles = [other(i, b) for other in others]
            for f, (group, which) in enumerate(fields):
                field = group[which, i, at, :]
                for o, tile in enumerate(tiles):
                    accs[o * count + f] = accs[o * count + f] + field * tile
            for n, (one, two) in enumerate(plain, len(others) * count):
                accs[n] = accs[n] + one(i, b) * two(i, b)
        return tuple(accs)

    total = count * len(others) + len(plain)
    return [collapse(acc) for acc in lax.fori_loop(0, REACH, body, (zero,) * total)]


def base_gradient(both, near, far, z_first, z_second, potential, grad, ext):
    hartree = both.at[pl.ds(0, REACH)]
    density = both.at[pl.ds(REACH, REACH)]
    faces = edge_faces(*by_side(z_first[24:48, :], z_second[24:48, :]))

    def body(near_below, far_below):
        for i in range(REACH):
            grad[i] = side_plane(i, near, near_below) + side_plane(i, far, far_below) + z_plane(i, faces)

    with_sides(body)
    for i, lap, rho in inner_planes(density, ext):
        power = jnp.exp(jnp.log(rho) * (4.0 / 3.0))
        grad[i] = 2.0 * rho * (hartree[i] + potential[i] + tf_scale * power) - (lap + grad[i]) * (
            1.0 / (spacing * spacing)
        )


def density_tile(both):
    return lambda i, b: tile_of(both, REACH + i, b)


def lifted_tile(both, vector):
    return lambda i, b: 2.0 * tile_of(both, REACH + i, b) * tile_of(vector, i, b)


FETCHES = 4


def side_one(both, charge, steps, changes, inner, steps_here, changes_here, rows, ext, sems):
    each = HIST // FETCHES
    copies = [
        pltpu.make_async_copy(src.at[pl.ds(each * n, each)], dst.at[pl.ds(each * n, each)], sems.at[FETCHES * m + n])
        for m, (src, dst) in enumerate(((steps, steps_here), (changes, changes_here)))
        for n in range(FETCHES)
    ]
    for copy in copies:
        copy.start()
    inner_residual(both, charge, inner, ext)
    for copy in copies[:FETCHES]:
        copy.wait()
    store(rows, 0, gram_dots(steps_here, steps_here, PAIRS))
    store(rows, 36, field_dots((steps_here,), [density_tile(both)]))
    for copy in copies[FETCHES:]:
        copy.wait()
    store(rows, 44, gram_dots(changes_here, changes_here, PAIRS))


def side_two(vector, inner, ext):
    inner_basis(vector, None, inner, ext)


def side_three(prior, vector, both, near, far, z_first, z_second, potential, steps, changes, *outs):
    inner, grad, rows, moments, ext = outs
    inner_basis(vector, prior, inner, ext)
    before, lifted, rho = lifted_tile(both, prior), lifted_tile(both, vector), density_tile(both)
    values = field_dots((steps, changes), [before, lifted], [(rho, before), (rho, lifted)])
    store(rows, 0, values[:16] + values[32:33] + values[16:32] + values[33:])
    store(rows, 34, gram_dots(steps, changes, CROSS_PAIRS[:32]))
    store_moments([(prior, prior), (prior, vector), (vector, vector)], moments)
    base_gradient(both, near, far, z_first, z_second, potential, grad, ext)


def side_four(prior, vector, both, grad, steps, changes, r1, r3, m3, inner, sums, rows, moments, table, ext):
    inner_basis(vector, prior, inner, ext)
    lifted, rho = lifted_tile(both, vector), density_tile(both)
    slope = lambda i, b: tile_of(grad, i, b)
    by_step = field_dots((steps,), [lifted, slope], [(rho, lifted), (rho, slope), (rho, rho)])
    by_change = field_dots((changes,), [lifted, slope, rho])
    values = by_step[:8] + by_change[:8] + by_step[16:17] + by_step[8:16] + by_change[8:16] + by_step[17:]
    store(rows, 0, values + by_change[16:])
    store(rows, 43, gram_dots(steps, changes, CROSS_PAIRS[32:]))
    store_moments([(prior, vector), (vector, vector)], moments)

    table[...] = jnp.zeros_like(table)

    def put(base, ref, start, count):
        before = max(0, min(count, HALF - base))
        if before:
            table[base : base + before, :] = ref[start : start + before, :]
        if before < count:
            at = place(base + before)
            table[at : at + count - before, :] = ref[start + before : start + count, :]

    put(ROW_GRAM, r1, 0, 36)
    put(ROW_GRAM + 36, r1, 44, 36)
    put(ROW_GRAM + 72, r3, 34, 32)
    put(ROW_GRAM + 104, rows, 43, 32)
    put(ROW_BASE, r1, 36, 8)
    put(ROW_BASE + 8, rows, 35, 8)
    put(ROW_BASE + 16, rows, 17, 18)
    put(ROW_W, r3, 0, 34)
    put(ROW_W + 34, rows, 0, 17)
    second = jnp.sum(jnp.transpose(table[LANES : 2 * LANES, :]), axis=0, keepdims=True)
    sums[0:1, :] = jnp.sum(jnp.transpose(table[0:LANES, :]), axis=0, keepdims=True)
    sums[1:2, :] = put_moments(second, [(m3, 0), (m3, 1), (m3, 2), (moments, 0), (moments, 1)], 0)


def put_moments(row, order, start):
    zero = jnp.zeros((8 - len(order), LANES), jnp.float32)
    parts = [
        jnp.concatenate([ref[2 * which + low : 2 * which + low + 1, :] for ref, which in order] + [zero], axis=0)
        for low in range(2)
    ]
    hi, lo = fold_lanes(*parts)
    lane = lane_ids((1, LANES))
    for n in range(len(order)):
        row = jnp.where(lane == MOM_LANE + start + n, hi[n : n + 1], row)
        row = jnp.where(lane == MOM_LANE + 7 + start + n, lo[n : n + 1], row)
    return row


def side_five(prior, vector, both, steps, changes, sums, kept, given, table, m5):
    lifted, rho = lifted_tile(both, vector), density_tile(both)
    table[...] = jnp.zeros_like(table)
    store(table, place(ROW_W + 51) - LANES, field_dots((steps, changes), [lifted], [(rho, lifted)]))
    store_moments([(prior, vector), (vector, vector)], m5)
    second = sums[1:2, :] + jnp.sum(jnp.transpose(table[...]), axis=0, keepdims=True)
    first, second = sums[0:1, :], put_moments(second, [(m5, 0), (m5, 1)], 5)
    odd = is_odd("blk")
    kept[...] = jnp.where(odd, second, first)
    given[...] = jnp.where(odd, first, second)


def inner_moment_kernel(vector, inner, ext):
    zero = jnp.zeros((8, LANES), jnp.float32)
    accs = [(zero, zero) for _ in range(2)]
    for i, lap, values in inner_planes(vector, ext):
        product = values * ((screen / SHIFT - 1.0) * values - (1.0 / SHIFT) * lap)
        for b in range(8):
            accs[b % 2] = add_tile(accs[b % 2], product[8 * b : 8 * b + 8])
    hi, err = two_sum(accs[0][0], accs[1][0])
    inner[0:1, :], inner[1:2, :] = fold_rows((hi, accs[0][1] + accs[1][1] + err))


def couple(own, block, below, acc):
    half = own.shape[1] // 2
    for i in range(REACH):
        product = own[i, half:, :] * side_plane(i, block, True) if below else own[i, :half, :] * side_plane(i, block, False)
        for b in range(half // 8):
            acc = add_tile(acc, product[8 * b : 8 * b + 8])
    return acc


def send_kernel(own, far, near, z_left, inner, kept, taken, out):
    faces = edge_faces(z_left[...], None)

    def body(near_below, far_below):
        zero = jnp.zeros((8, LANES), jnp.float32)
        accs = [(zero, zero) for _ in range(2)]
        for i in range(REACH):
            product = own[i] * z_plane(i, faces)
            for b in range(8):
                accs[b % 2] = add_tile(accs[b % 2], product[8 * b : 8 * b + 8])
        accs = [couple(own, far, far_below, accs[0]), couple(own, near, near_below, accs[1])]
        hi, err = two_sum(accs[0][0], accs[1][0])
        sides = fold_rows((hi, accs[0][1] + accs[1][1] + err))
        hi, lo = fold_lanes(*df_add(df_scale(sides, -2.0 / SHIFT), (inner[0:1, :], inner[1:2, :])))
        lane = lane_ids((1, LANES))
        row, err = two_sum(kept[...], taken[...])
        low_lane = (lane >= MOM_LANE + 7) & (lane < MOM_LANE + 14) & is_odd("blk")
        row = jnp.where(low_lane, row + pltpu.roll(err, 7, 1), row)
        row = jnp.where(lane == HALF, hi, jnp.where(lane == HALF + 1, lo, row))
        out[...] = jnp.broadcast_to(row, out.shape)

    with_sides(body)


def solve_krylov(moment):
    n00, n01, n11, n12, n22, n23, n33, n34 = moment
    nu = [n00, n01]
    nu.append(df_sub(df_scale(n11, 2.0), n00))
    nu.append(df_sub(df_scale(n12, 2.0), n01))
    nu.append(df_sub(df_scale(n22, 2.0), n00))
    nu.append(df_sub(df_scale(n23, 2.0), n01))
    nu.append(df_sub(df_scale(n33, 2.0), n00))

    def gram(i, j):
        if i == j == 0:
            return n00
        return df_scale(df_add(nu[i + j], nu[abs(i - j)]), 0.5)

    def moved(i, j):
        if i == 3 and j == 3:
            return n34
        if j == 0:
            return gram(i, 1)
        return df_scale(df_add(gram(i, j + 1), gram(i, j - 1)), 0.5)

    mat = {(i, j): df_add(moved(i, j), gram(i, j)) for i in range(4) for j in range(i + 1)}
    rhs = [df_scale(gram(i, 0), 1.0 / SHIFT) for i in range(4)]
    low, inverse = {}, []
    for k in range(4):
        inverse.append(1.0 / mat[k, k][0])
        for i in range(k + 1, 4):
            low[i, k] = df_over(mat[i, k], mat[k, k], inverse[k])
        for i in range(k + 1, 4):
            for j in range(k + 1, i + 1):
                mat[i, j] = df_sub(mat[i, j], df_mul(low[i, k], mat[j, k]))
            rhs[i] = df_sub(rhs[i], df_mul(low[i, k], rhs[k]))
    sol = [None] * 4
    for k in reversed(range(4)):
        value = df_over(rhs[k], mat[k, k], inverse[k])
        for i in range(k + 1, 4):
            value = df_sub(value, df_mul(low[i, k], sol[i]))
        sol[k] = value
    return [hi + lo for hi, lo in sol]


def final_kernel(received, both, grad, v0, v1, v2, v3, steps, changes, new_density, new_hartree, spread, density_here, hartree_here, sems):
    parts = [(received[8 * n : 8 * n + 8, :], jnp.zeros((8, LANES), jnp.float32)) for n in range(4)]
    for n in range(4, received.shape[0] // 8):
        parts[n % 4] = add_tile(parts[n % 4], received[8 * n : 8 * n + 8, :])
    while len(parts) > 1:
        half = len(parts) // 2
        merged = []
        for a, b in zip(parts[:half], parts[half:]):
            hi, err = two_sum(a[0], b[0])
            merged.append((hi, a[1] + b[1] + err))
        parts = merged
    hi, lo = fold(*parts[0], 0, (1, 2))
    lane = lane_ids((1, LANES))
    last, err = two_sum(hi[3:4], hi[7:8])
    err = err + (lo[3:4] + lo[7:8])
    first = hi[3:4]
    second = jnp.where(lane >= HALF, last, hi[7:8])
    low = jnp.where(lane >= HALF, err, lo[7:8])
    low = low + jnp.where(lane == HALF, pltpu.roll(second, LANES - 1, 1), pltpu.roll(second, LANES - 7, 1))
    for n, value in enumerate((first, second, low)):
        spread[LANES * n : LANES * n + LANES, :] = jnp.transpose(jnp.broadcast_to(value, (LANES, LANES)))

    def row(n):
        return spread[place(n) : place(n) + 1, :]

    def moment(n):
        at = LANES + (MOM_LANE + n if n < 7 else HALF)
        return quick_sum(spread[at : at + 1, :], spread[LANES + at : LANES + at + 1, :])

    mix = solve_krylov([moment(n) for n in range(8)])

    def s_s(i, j):
        return row(ROW_GRAM + PAIR_ROW[min(i, j), max(i, j)])

    def y_y(i, j):
        return row(ROW_GRAM + 36 + PAIR_ROW[min(i, j), max(i, j)])

    def s_y(i, j):
        return row(ROW_GRAM + 72 + 8 * i + j)

    pairs = range(HIST)
    theta, rest, inverse = [], [], []
    for i in pairs:
        curv, norm = s_y(i, i), s_s(i, i)
        kept = (1.0 - damp_floor) * norm
        damp = jnp.where(curv >= damp_floor * norm, 1.0, kept / jnp.maximum(norm - curv, kept))
        theta.append(damp)
        rest.append(1.0 - damp)
        inverse.append(1.0 / (damp * curv + (1.0 - damp) * norm))

    def s_bar(i, j):
        return theta[j] * s_y(i, j) + rest[j] * s_s(i, j)

    def bar_bar(i, j):
        return theta[i] * (theta[j] * y_y(i, j) + rest[j] * s_y(j, i)) + rest[i] * s_bar(i, j)

    last = HIST - 1
    scaling = s_bar(last, last) / bar_bar(last, last)

    def energy(n):
        value = row(ROW_BASE + 16 + n)
        for j in range(4):
            value = value + mix[j] * row(ROW_W + 17 * j + n)
        return value

    chem = energy(16) / row(ROW_BASE + 33)

    def gradient(n):
        return energy(n) - chem * row(ROW_BASE + n)

    s_grad = [gradient(i) for i in pairs]
    bar_grad = [theta[i] * gradient(HIST + i) + rest[i] * s_grad[i] for i in pairs]

    first = [None] * HIST
    pending = list(s_grad)
    for j in reversed(pairs):
        first[j] = inverse[j] * pending[j]
        for i in range(j):
            pending[i] = pending[i] - first[j] * s_bar(i, j)
    pending = list(bar_grad)
    for j in pairs:
        for i in pairs:
            pending[i] = pending[i] - first[j] * bar_bar(i, j)
    pending = [scaling * value for value in pending]
    step_mix, change_mix = [], []
    for j in pairs:
        net = first[j] - inverse[j] * pending[j]
        for i in range(j + 1, HIST):
            pending[i] = pending[i] + net * s_bar(j, i)
        change_mix.append((-step_length) * (-scaling * first[j] * theta[j]))
        step_mix.append((-step_length) * (net - scaling * first[j] * rest[j]))

    wide = lambda value: jnp.broadcast_to(value, (8, LANES))
    mix = [wide(value) for value in mix]
    chem, gain = wide(chem), wide((-step_length) * scaling)
    step_mix = [wide(value) for value in step_mix]
    change_mix = [wide(value) for value in change_mix]
    basis = (v0, v1, v2, v3)

    def leave(i):
        return [
            pltpu.make_async_copy(here.at[i], out.at[i], sems.at[n, i])
            for n, (here, out) in enumerate(((density_here, new_density), (hartree_here, new_hartree)))
        ]

    for i in range(REACH):
        for b in range(8):
            at = pl.ds(8 * b, 8)
            rho = both[REACH + i, at, :]
            lift = mix[0] * v0[i, at, :]
            for j in range(1, 4):
                lift = lift + mix[j] * basis[j][i, at, :]
            hartree_here[i, at, :] = both[i, at, :] + lift
            slope = grad[i, at, :] + 2.0 * rho * lift - chem * rho
            parts = [rho, gain * slope, step_mix[0] * steps[0, i, at, :], change_mix[0] * changes[0, i, at, :]]
            for f in range(1, HIST):
                parts[2] = parts[2] + step_mix[f] * steps[f, i, at, :]
                parts[3] = parts[3] + change_mix[f] * changes[f, i, at, :]
            density_here[i, at, :] = parts[0] + (parts[1] + (parts[2] + parts[3]))
        for copy in leave(i):
            copy.start()
    for i in range(REACH):
        for copy in leave(i):
            copy.wait()


def call(kernel, outs, args, scratch=(), flops=0, in_hbm=(), out_hbm=False):
    args = [pltpu.with_memory_space_constraint(x, pltpu.HBM) if n in in_hbm else x for n, x in enumerate(args)]
    shapes = [jax.ShapeDtypeStruct(shape, jnp.float32) for shape in outs]
    size = sum(4 * math.prod(a.shape) for a in (*args, *shapes))
    return pl.pallas_call(
        kernel,
        out_shape=shapes,
        in_specs=[pl.BlockSpec(memory_space=pltpu.HBM if n in in_hbm else pltpu.VMEM) for n in range(len(args))],
        out_specs=[pl.BlockSpec(memory_space=pltpu.HBM if out_hbm else pltpu.VMEM)] * len(outs),
        scratch_shapes=[pltpu.VMEM(s, jnp.float32) if isinstance(s, tuple) else s for s in scratch],
        cost_estimate=pl.CostEstimate(flops=flops, bytes_accessed=size, transcendentals=0),
        compiler_params=pltpu.CompilerParams(vmem_limit_bytes=VMEM_LIMIT),
    )(*args)


def ring(axis, step):
    size = lax.axis_size(axis)
    return [(i, (i + step) % size) for i in range(size)]


def swap(axis, odd_up):
    size = lax.axis_size(axis)
    return [(i, (i + (1 if i % 2 == odd_up else -1)) % size) for i in range(size)]


def after(values, *earlier):
    return lax.optimization_barrier((tuple(values), earlier))[0]


def x_halo(block):
    far = lax.ppermute(block, "blk", swap("blk", 1))
    return (lax.ppermute(block, "blk", swap("blk", 0)), far)


def z_halo(face_a, face_b):
    return (lax.ppermute(face_a, "gz", swap("gz", 0)), lax.ppermute(face_b, "gz", swap("gz", 1)))


def on_device(sqrt_density, ion_charge, ion_potential, hartree_prev, hist_steps, hist_changes):
    block = sqrt_density.shape
    ext = (block[0], block[1] + 16, block[2])
    face = (24, LANES)
    cells = math.prod(block)
    cells = math.prod(block)
    work = 300 * cells
    inputs = (hartree_prev, sqrt_density, ion_charge)
    halo = x_halo(hartree_prev)
    both, charge, *faces = call(
        launch_kernel,
        [(2 * REACH, *block[1:]), block, (48, LANES), (48, LANES)],
        inputs,
        [pltpu.SemaphoreType.DMA((3,))],
        in_hbm=(0, 1, 2),
    )
    ends = z_halo(*faces)
    density_ends = ends
    half = (REACH, block[1] // 2, LANES)

    def advance(gain, inner, halo, ends, last=False):
        (mid,) = call(functools.partial(z_kernel, gain), [block], [inner, *ends], flops=work)
        return call(
            functools.partial(last_x_kernel if last else x_kernel, gain),
            [block, half, half] if last else [block],
            [mid, *halo],
            flops=work,
        )

    def exchange(block_now):
        halo = x_halo(block_now)
        return halo, z_halo(*call(pack_kernel, [face, face], [block_now], flops=work))

    stored = hist_steps.shape
    inner, *history, r1 = call(
        side_one,
        [block, stored, stored, (80, LANES)],
        [both, charge, hist_steps, hist_changes],
        [ext, pltpu.SemaphoreType.DMA((2 * FETCHES,))],
        work,
        in_hbm=(2, 3),
    )
    (v0,) = advance(1.0, inner, halo, ends)
    halo, ends = exchange(v0)
    density_halo = x_halo(after((sqrt_density,), v0)[0])
    (inner,) = call(side_two, [block], [v0], [ext], work)
    (v1,) = advance(-1.0 / SHIFT, inner, halo, ends)
    halo, ends = exchange(v1)
    inner, grad, r3, m3 = call(
        side_three,
        [block, block, (72, LANES), (8, LANES)],
        [v0, v1, both, *density_halo, *density_ends, ion_potential, *history],
        [ext],
        work,
    )
    (v2,) = advance(-2.0 / SHIFT, inner, halo, ends)
    halo, ends = exchange(v2)
    inner, sums = call(
        side_four,
        [block, (2, LANES)],
        [v1, v2, both, grad, *history, r1, r3, m3],
        [(80, LANES), (8, LANES), (2 * LANES, LANES), ext],
        work,
    )
    v3, to_near, to_far = advance(-2.0 / SHIFT, inner, halo, ends, last=True)
    far = lax.ppermute(to_far, "blk", swap("blk", 1))
    near = lax.ppermute(to_near, "blk", swap("blk", 0))
    (upper,) = call(pack_upper_kernel, [face], [v3], flops=work)
    z_left = lax.ppermute(upper, "gz", ring("gz", 1))
    kept, given = call(
        side_five,
        [(1, LANES), (1, LANES)],
        [v2, v3, both, *history, sums],
        [(LANES, LANES), (8, LANES)],
        work,
    )
    taken = lax.ppermute(given, "blk", swap("blk", 0))
    (inner,) = call(inner_moment_kernel, [(8, LANES)], [after((v3,), given)[0]], [ext], work)
    devices = lax.axis_size("blk") * lax.axis_size("gz")
    (outgoing,) = call(send_kernel, [(devices, LANES)], [v3, far, near, z_left, inner, kept, taken], flops=work)
    received = lax.all_to_all(outgoing.reshape(devices, 1, LANES), ("blk", "gz"), 0, 0, tiled=True)
    return tuple(
        call(
            final_kernel,
            [block, block],
            [received.reshape(devices, LANES), both, grad, v0, v1, v2, v3, *history],
            [(3 * LANES, LANES), block, block, pltpu.SemaphoreType.DMA((2, REACH))],
            work,
            out_hbm=True,
        )
    )


def solution(mesh):
    placed = (
        P("blk", None, "gz"),
        P("blk", None, "gz"),
        P("blk", None, "gz"),
        P("blk", None, "gz"),
        P(None, "blk", None, "gz"),
        P(None, "blk", None, "gz"),
    )
    return jax.shard_map(
        on_device,
        mesh=mesh,
        in_specs=placed,
        out_specs=(P("blk", None, "gz"), P("blk", None, "gz")),
        check_vma=False,
    )
```

```python
import functools
import math

import jax
import jax.numpy as jnp
from jax import lax
from jax.experimental import pallas as pl
from jax.experimental.pallas import tpu as pltpu
from jax.sharding import PartitionSpec as P

center = -5369.0 / 1800.0
coeffs = (12.0 / 7.0, -15.0 / 56.0, 10.0 / 189.0, -1.0 / 112.0, 2.0 / 825.0, -1.0 / 4752.0)
screen = 0.0025
spacing = 0.28
source_scale = 4.0 * math.pi * spacing * spacing
tf_scale = 5.0 / 3.0 * 2.871234
step_length = 0.01
damp_floor = 0.2

SHIFT = 2.0
HIST = 8
REACH = 6
LANES = 128
VMEM_LIMIT = 24 * 1024 * 1024

ROW_GRAM = 0
ROW_BASE = 136
ROW_W = 170
ROW_MOM = 238
HALF = 126


def place(n):
    return n if n < HALF else n + LANES - HALF


MOM_LANE = place(ROW_MOM) - LANES
PAIRS = tuple((i, j) for i in range(HIST) for j in range(i, HIST))
PAIR_ROW = {pair: row for row, pair in enumerate(PAIRS)}


def two_sum(a, b):
    s = a + b
    bb = s - a
    return s, (a - (s - bb)) + (b - bb)


def quick_sum(a, b):
    s = a + b
    return s, b - (s - a)


def split(a):
    t = 4097.0 * a
    hi = t - (t - a)
    return hi, a - hi


def two_prod(a, b):
    p = a * b
    ah, al = split(a)
    bh, bl = split(b)
    return p, ((ah * bh - p) + ah * bl + al * bh) + al * bl


def df_add(a, b):
    s, e = two_sum(a[0], b[0])
    return quick_sum(s, e + (a[1] + b[1]))


def df_neg(a):
    return (-a[0], -a[1])


def df_sub(a, b):
    return df_add(a, df_neg(b))


def df_scale(a, factor):
    return (a[0] * factor, a[1] * factor)


def df_mul(a, b):
    p, e = two_prod(a[0], b[0])
    return quick_sum(p, e + (a[0] * b[1] + a[1] * b[0]))


def df_over(a, b, inverse):
    q = a[0] * inverse
    p, e = two_prod(q, b[0])
    rest = ((a[0] - p) - e) + (a[1] - q * b[1])
    return quick_sum(q, rest * inverse)


def lane_ids(shape):
    return lax.broadcasted_iota(jnp.int32, shape, len(shape) - 1)


def z_matrix():
    shape = (LANES, LANES)
    apart = jnp.abs(lax.broadcasted_iota(jnp.int32, shape, 0) - lax.broadcasted_iota(jnp.int32, shape, 1))
    matrix = jnp.where(apart == 0, 3.0 * center, 0.0)
    for k, weight in enumerate(coeffs, 1):
        matrix = jnp.where(apart == k, weight, matrix)
    return matrix


def inner_planes(own, ext):
    fill_ext(own, ext)
    layers, rows, lanes = own.shape
    along_z = lax.dot_general(
        own[...].reshape(layers * rows, lanes),
        z_matrix(),
        (((1,), (0,)), ((), ())),
        precision=lax.Precision.HIGHEST,
        preferred_element_type=jnp.float32,
    )
    for i in range(layers):
        total = along_z[rows * i : rows * i + rows]
        for k, weight in enumerate(coeffs, 1):
            pair = ext[i, 8 + k : 8 + k + rows, :] + ext[i, 8 - k : 8 - k + rows, :]
            if i + k < layers:
                pair = pair + own[i + k]
            if i - k >= 0:
                pair = pair + own[i - k]
            total = total + weight * pair
        yield i, total, own[i]


def edge_faces(z_left, z_right):
    lane = lane_ids((24, LANES)) % 8
    lower = jnp.zeros((24, LANES), jnp.float32)
    upper = jnp.zeros((24, LANES), jnp.float32)
    for k, weight in enumerate(coeffs, 1):
        lower = lower + jnp.where(lane < k, weight * pltpu.roll(z_left, LANES - 8 + k, 1), 0.0)
        if z_right is not None:
            upper = upper + jnp.where(lane >= 8 - k, weight * pltpu.roll(z_right, 8 - k, 1), 0.0)
    return lower, upper


def side_plane(i, block, below, rows=slice(None)):
    total = None
    for k, weight in enumerate(coeffs, 1):
        layer = i - k + REACH if below else i + k - REACH
        if 0 <= layer < REACH:
            term = weight * block[layer, rows, :]
            total = term if total is None else total + term
    return total


def z_plane(i, faces, tiles=8):
    lane = lane_ids((8, LANES))
    lower, upper = (face[8 * (i // 2) : 8 * (i // 2) + 8] for face in faces)
    out = []
    for b in range(tiles):
        j = 8 * (i % 2) + b
        tile = jnp.where(lane < 8, pltpu.roll(lower, (LANES - 8 * j) % LANES, 1), 0.0)
        tile = jnp.where(lane >= LANES - 8, pltpu.roll(upper, (2 * LANES - 8 - 8 * j) % LANES, 1), tile)
        out.append(tile)
    return jnp.concatenate(out, axis=0)


def fill_ext(own, ext):
    rows = own.shape[1]
    ext[:, 8 : 8 + rows, :] = own[...]
    ext[:, 0:8, :] = own[:, rows - 8 : rows, :]
    ext[:, 8 + rows : 16 + rows, :] = own[:, 0:8, :]


def pack_faces(src, layers):
    lane = lane_ids((8, LANES))
    firsts, lasts = [], []
    for m in range(3):
        first = jnp.zeros((8, LANES), jnp.float32)
        last = jnp.zeros((8, LANES), jnp.float32)
        for j in range(16):
            n = 16 * m + j
            tile = src[layers + n // 8, 8 * (n % 8) : 8 * (n % 8) + 8, :]
            here = (lane >= 8 * j) & (lane < 8 * j + 8)
            first = jnp.where(here, pltpu.roll(tile, 8 * j, 1) if j else tile, first)
            last = jnp.where(here, pltpu.roll(tile, (8 * j + 8) % LANES, 1) if j < 15 else tile, last)
        firsts.append(first)
        lasts.append(last)
    return jnp.concatenate(firsts, axis=0), jnp.concatenate(lasts, axis=0)


def is_odd(axis):
    return lax.rem(lax.axis_index(axis), 2) == 1


def by_partner(lower, upper):
    odd = is_odd("gz")
    return jnp.where(odd, lower, upper), jnp.where(odd, upper, lower)


def by_side(first, second):
    odd = is_odd("gz")
    return jnp.where(odd, first, second), jnp.where(odd, second, first)


def with_sides(body):
    odd = is_odd("blk")

    @pl.when(odd)
    def _():
        body(True, False)

    @pl.when(jnp.logical_not(odd))
    def _():
        body(False, True)


def fold(hi, lo, axis, steps):
    for step in steps:
        hi, err = two_sum(hi, pltpu.roll(hi, step, axis))
        lo = lo + pltpu.roll(lo, step, axis) + err
    return hi, lo


def fold_rows(acc):
    hi, lo = fold(*acc, 0, (4, 2, 1))
    return hi[0:1], lo[0:1]


def fold_lanes(hi, lo):
    return quick_sum(*fold(hi, lo, 1, (64, 32, 16, 8, 4, 2, 1)))


def add_tile(acc, product):
    hi, err = two_sum(acc[0], product)
    return hi, acc[1] + err


def tile_of(ref, i, b):
    return ref[i, 8 * b : 8 * b + 8, :]


def store_moments(pairs, moments):
    zero = jnp.zeros((8, LANES), jnp.float32)

    def body(i, accs):
        for b in range(8):
            accs = tuple(
                add_tile(acc, tile_of(a, i, b) * tile_of(c, i, b)) for acc, (a, c) in zip(accs, pairs)
            )
        return accs

    accs = lax.fori_loop(0, REACH, body, tuple((zero, zero) for _ in pairs))
    for n, acc in enumerate(accs):
        moments[2 * n : 2 * n + 1, :], moments[2 * n + 1 : 2 * n + 2, :] = fold_rows(acc)


def collapse(acc):
    return jnp.sum(acc, axis=0, keepdims=True)


def launch_kernel(hartree, density, charge, both, charge_here, face_a, face_b, sems):
    places = (both.at[pl.ds(0, REACH)], both.at[pl.ds(REACH, REACH)], charge_here)
    copies = [
        pltpu.make_async_copy(src, dst, sems.at[n])
        for n, (src, dst) in enumerate(zip((hartree, density, charge), places))
    ]
    for copy in copies:
        copy.start()
    for n in range(2):
        copies[n].wait()
        rows = slice(24 * n, 24 * n + 24)
        face_a[rows, :], face_b[rows, :] = by_partner(*pack_faces(both, REACH * n))
    copies[2].wait()


def inner_residual(both, charge, out, ext):
    hartree = both.at[pl.ds(0, REACH)]
    for i, lap, values in inner_planes(hartree, ext):
        rho = both[REACH + i]
        out[i] = source_scale * (rho * rho - charge[i]) - (screen * values - lap)


def inner_basis(own, prior, out, ext):
    for i, lap, values in inner_planes(own, ext):
        moved = (screen / SHIFT - 1.0) * values - (1.0 / SHIFT) * lap
        out[i] = moved if prior is None else 2.0 * moved - prior[i]


def z_kernel(gain, inner, z_first, z_second, out):
    faces = edge_faces(*by_side(z_first[0:24, :], z_second[0:24, :]))
    for i in range(REACH):
        out[i] = inner[i] + gain * z_plane(i, faces)


def x_kernel(gain, inner, near, far, out):
    def body(near_below, far_below):
        for i in range(REACH):
            out[i] = inner[i] + gain * (side_plane(i, near, near_below) + side_plane(i, far, far_below))

    with_sides(body)


def last_x_kernel(gain, inner, near, far, out, to_near, to_far):
    half = out.shape[1] // 2

    def body(near_below, far_below):
        for i in range(REACH):
            plane = inner[i] + gain * (side_plane(i, near, near_below) + side_plane(i, far, far_below))
            out[i] = plane
            for ref, below in ((to_near, near_below), (to_far, far_below)):
                ref[i] = plane[:half] if below else plane[half:]

    with_sides(body)


def pack_kernel(block, face_a, face_b):
    face_a[...], face_b[...] = by_partner(*pack_faces(block, 0))


def pack_upper_kernel(block, face):
    face[...] = pack_faces(block, 0)[1]


def store(rows, base, values):
    for n, value in enumerate(values):
        rows[base + n : base + n + 1, :] = value


def gram_dots(left, right, pairs):
    zero = jnp.zeros((8, LANES), jnp.float32)

    def body(i, accs):
        for b in range(8):
            at = pl.ds(8 * b, 8)
            l_tiles = {p: left[p, i, at, :] for p in sorted({p for p, _ in pairs})}
            if left is right:
                r_tiles = l_tiles
            else:
                r_tiles = {q: right[q, i, at, :] for q in sorted({q for _, q in pairs})}
            accs = tuple(acc + l_tiles[p] * r_tiles[q] for acc, (p, q) in zip(accs, pairs))
        return accs

    accs = lax.fori_loop(0, REACH, body, tuple(zero for _ in pairs))
    return [collapse(acc) for acc in accs]


CROSS_PAIRS = tuple((i, j) for i in range(HIST) for j in range(HIST))


def field_dots(groups, others, plain=()):
    zero = jnp.zeros((8, LANES), jnp.float32)
    fields = [(group, f) for group in groups for f in range(HIST)]
    count = len(fields)

    def body(i, accs):
        accs = list(accs)
        for b in range(8):
            at = pl.ds(8 * b, 8)
            tiles = [other(i, b) for other in others]
            for f, (group, which) in enumerate(fields):
                field = group[which, i, at, :]
                for o, tile in enumerate(tiles):
                    accs[o * count + f] = accs[o * count + f] + field * tile
            for n, (one, two) in enumerate(plain, len(others) * count):
                accs[n] = accs[n] + one(i, b) * two(i, b)
        return tuple(accs)

    total = count * len(others) + len(plain)
    return [collapse(acc) for acc in lax.fori_loop(0, REACH, body, (zero,) * total)]


def base_gradient(both, near, far, z_first, z_second, potential, grad, ext):
    hartree = both.at[pl.ds(0, REACH)]
    density = both.at[pl.ds(REACH, REACH)]
    faces = edge_faces(*by_side(z_first[24:48, :], z_second[24:48, :]))

    def body(near_below, far_below):
        for i in range(REACH):
            grad[i] = side_plane(i, near, near_below) + side_plane(i, far, far_below) + z_plane(i, faces)

    with_sides(body)
    for i, lap, rho in inner_planes(density, ext):
        power = jnp.exp(jnp.log(rho) * (4.0 / 3.0))
        grad[i] = 2.0 * rho * (hartree[i] + potential[i] + tf_scale * power) - (lap + grad[i]) * (
            1.0 / (spacing * spacing)
        )


def density_tile(both):
    return lambda i, b: tile_of(both, REACH + i, b)


def lifted_tile(both, vector):
    return lambda i, b: 2.0 * tile_of(both, REACH + i, b) * tile_of(vector, i, b)


FETCHES = 4


def side_one(both, charge, steps, changes, inner, steps_here, changes_here, rows, ext, sems):
    each = HIST // FETCHES
    copies = [
        pltpu.make_async_copy(src.at[pl.ds(each * n, each)], dst.at[pl.ds(each * n, each)], sems.at[FETCHES * m + n])
        for m, (src, dst) in enumerate(((steps, steps_here), (changes, changes_here)))
        for n in range(FETCHES)
    ]
    for copy in copies:
        copy.start()
    inner_residual(both, charge, inner, ext)
    for copy in copies[:FETCHES]:
        copy.wait()
    store(rows, 0, gram_dots(steps_here, steps_here, PAIRS))
    store(rows, 36, field_dots((steps_here,), [density_tile(both)]))
    for copy in copies[FETCHES:]:
        copy.wait()
    store(rows, 44, gram_dots(steps_here, changes_here, CROSS_PAIRS[32:]))


def side_two(vector, inner, ext):
    inner_basis(vector, None, inner, ext)


def side_three(prior, vector, both, near, far, z_first, z_second, potential, steps, changes, *outs):
    inner, grad, rows, moments, ext = outs
    inner_basis(vector, prior, inner, ext)
    before, lifted, rho = lifted_tile(both, prior), lifted_tile(both, vector), density_tile(both)
    values = field_dots((steps, changes), [before, lifted], [(rho, before), (rho, lifted)])
    store(rows, 0, values[:16] + values[32:33] + values[16:32] + values[33:])
    store(rows, 34, gram_dots(steps, changes, CROSS_PAIRS[:32]))
    store_moments([(prior, prior), (prior, vector), (vector, vector)], moments)
    base_gradient(both, near, far, z_first, z_second, potential, grad, ext)


def side_four(prior, vector, both, grad, steps, changes, r1, r3, m3, inner, sums, rows, moments, table, ext):
    inner_basis(vector, prior, inner, ext)
    lifted, rho = lifted_tile(both, vector), density_tile(both)
    slope = lambda i, b: tile_of(grad, i, b)
    by_step = field_dots((steps,), [lifted, slope], [(rho, lifted), (rho, slope), (rho, rho)])
    by_change = field_dots((changes,), [lifted, slope, rho])
    values = by_step[:8] + by_change[:8] + by_step[16:17] + by_step[8:16] + by_change[8:16] + by_step[17:]
    store(rows, 0, values + by_change[16:])
    store(rows, 43, gram_dots(changes, changes, PAIRS))
    store_moments([(prior, vector), (vector, vector)], moments)

    table[...] = jnp.zeros_like(table)

    def put(base, ref, start, count):
        before = max(0, min(count, HALF - base))
        if before:
            table[base : base + before, :] = ref[start : start + before, :]
        if before < count:
            at = place(base + before)
            table[at : at + count - before, :] = ref[start + before : start + count, :]

    put(ROW_GRAM, r1, 0, 36)
    put(ROW_GRAM + 36, rows, 43, 36)
    put(ROW_GRAM + 72, r3, 34, 32)
    put(ROW_GRAM + 104, r1, 44, 32)
    put(ROW_BASE, r1, 36, 8)
    put(ROW_BASE + 8, rows, 35, 8)
    put(ROW_BASE + 16, rows, 17, 18)
    put(ROW_W, r3, 0, 34)
    put(ROW_W + 34, rows, 0, 17)
    second = jnp.sum(jnp.transpose(table[LANES : 2 * LANES, :]), axis=0, keepdims=True)
    sums[0:1, :] = jnp.sum(jnp.transpose(table[0:LANES, :]), axis=0, keepdims=True)
    sums[1:2, :] = put_moments(second, [(m3, 0), (m3, 1), (m3, 2), (moments, 0), (moments, 1)], 0)


def put_moments(row, order, start):
    zero = jnp.zeros((8 - len(order), LANES), jnp.float32)
    parts = [
        jnp.concatenate([ref[2 * which + low : 2 * which + low + 1, :] for ref, which in order] + [zero], axis=0)
        for low in range(2)
    ]
    hi, lo = fold_lanes(*parts)
    lane = lane_ids((1, LANES))
    for n in range(len(order)):
        row = jnp.where(lane == MOM_LANE + start + n, hi[n : n + 1], row)
        row = jnp.where(lane == MOM_LANE + 7 + start + n, lo[n : n + 1], row)
    return row


def side_five(prior, vector, both, steps, changes, sums, kept, given, table, m5):
    lifted, rho = lifted_tile(both, vector), density_tile(both)
    table[...] = jnp.zeros_like(table)
    store(table, place(ROW_W + 51) - LANES, field_dots((steps, changes), [lifted], [(rho, lifted)]))
    store_moments([(prior, vector), (vector, vector)], m5)
    second = sums[1:2, :] + jnp.sum(jnp.transpose(table[...]), axis=0, keepdims=True)
    first, second = sums[0:1, :], put_moments(second, [(m5, 0), (m5, 1)], 5)
    odd = is_odd("blk")
    kept[...] = jnp.where(odd, second, first)
    given[...] = jnp.where(odd, first, second)


def inner_moment_kernel(vector, inner, ext):
    zero = jnp.zeros((8, LANES), jnp.float32)
    accs = [(zero, zero) for _ in range(2)]
    for i, lap, values in inner_planes(vector, ext):
        product = values * ((screen / SHIFT - 1.0) * values - (1.0 / SHIFT) * lap)
        for b in range(8):
            accs[b % 2] = add_tile(accs[b % 2], product[8 * b : 8 * b + 8])
    hi, err = two_sum(accs[0][0], accs[1][0])
    inner[0:1, :], inner[1:2, :] = fold_rows((hi, accs[0][1] + accs[1][1] + err))


def couple(own, block, below, acc):
    half = own.shape[1] // 2
    for i in range(REACH):
        product = own[i, half:, :] * side_plane(i, block, True) if below else own[i, :half, :] * side_plane(i, block, False)
        for b in range(half // 8):
            acc = add_tile(acc, product[8 * b : 8 * b + 8])
    return acc


def send_kernel(own, far, near, z_left, inner, kept, taken, out):
    faces = edge_faces(z_left[...], None)

    def body(near_below, far_below):
        zero = jnp.zeros((8, LANES), jnp.float32)
        accs = [(zero, zero) for _ in range(2)]
        for i in range(REACH):
            product = own[i] * z_plane(i, faces)
            for b in range(8):
                accs[b % 2] = add_tile(accs[b % 2], product[8 * b : 8 * b + 8])
        accs = [couple(own, far, far_below, accs[0]), couple(own, near, near_below, accs[1])]
        hi, err = two_sum(accs[0][0], accs[1][0])
        sides = fold_rows((hi, accs[0][1] + accs[1][1] + err))
        hi, lo = fold_lanes(*df_add(df_scale(sides, -2.0 / SHIFT), (inner[0:1, :], inner[1:2, :])))
        lane = lane_ids((1, LANES))
        row, err = two_sum(kept[...], taken[...])
        low_lane = (lane >= MOM_LANE + 7) & (lane < MOM_LANE + 14) & is_odd("blk")
        row = jnp.where(low_lane, row + pltpu.roll(err, 7, 1), row)
        row = jnp.where(lane == HALF, hi, jnp.where(lane == HALF + 1, lo, row))
        out[...] = jnp.broadcast_to(row, out.shape)

    with_sides(body)


def solve_krylov(moment):
    n00, n01, n11, n12, n22, n23, n33, n34 = moment
    nu = [n00, n01]
    nu.append(df_sub(df_scale(n11, 2.0), n00))
    nu.append(df_sub(df_scale(n12, 2.0), n01))
    nu.append(df_sub(df_scale(n22, 2.0), n00))
    nu.append(df_sub(df_scale(n23, 2.0), n01))
    nu.append(df_sub(df_scale(n33, 2.0), n00))

    def gram(i, j):
        if i == j == 0:
            return n00
        return df_scale(df_add(nu[i + j], nu[abs(i - j)]), 0.5)

    def moved(i, j):
        if i == 3 and j == 3:
            return n34
        if j == 0:
            return gram(i, 1)
        return df_scale(df_add(gram(i, j + 1), gram(i, j - 1)), 0.5)

    mat = {(i, j): df_add(moved(i, j), gram(i, j)) for i in range(4) for j in range(i + 1)}
    rhs = [df_scale(gram(i, 0), 1.0 / SHIFT) for i in range(4)]
    low, inverse = {}, []
    for k in range(4):
        inverse.append(1.0 / mat[k, k][0])
        for i in range(k + 1, 4):
            low[i, k] = df_over(mat[i, k], mat[k, k], inverse[k])
        for i in range(k + 1, 4):
            for j in range(k + 1, i + 1):
                mat[i, j] = df_sub(mat[i, j], df_mul(low[i, k], mat[j, k]))
            rhs[i] = df_sub(rhs[i], df_mul(low[i, k], rhs[k]))
    sol = [None] * 4
    for k in reversed(range(4)):
        value = df_over(rhs[k], mat[k, k], inverse[k])
        for i in range(k + 1, 4):
            value = df_sub(value, df_mul(low[i, k], sol[i]))
        sol[k] = value
    return [hi + lo for hi, lo in sol]


def final_kernel(received, both, grad, v0, v1, v2, v3, steps, changes, new_density, new_hartree, spread, density_here, hartree_here, sems):
    parts = [(received[8 * n : 8 * n + 8, :], jnp.zeros((8, LANES), jnp.float32)) for n in range(4)]
    for n in range(4, received.shape[0] // 8):
        parts[n % 4] = add_tile(parts[n % 4], received[8 * n : 8 * n + 8, :])
    while len(parts) > 1:
        half = len(parts) // 2
        merged = []
        for a, b in zip(parts[:half], parts[half:]):
            hi, err = two_sum(a[0], b[0])
            merged.append((hi, a[1] + b[1] + err))
        parts = merged
    hi, lo = fold(*parts[0], 0, (1, 2))
    lane = lane_ids((1, LANES))
    last, err = two_sum(hi[3:4], hi[7:8])
    err = err + (lo[3:4] + lo[7:8])
    first = hi[3:4]
    second = jnp.where(lane >= HALF, last, hi[7:8])
    low = jnp.where(lane >= HALF, err, lo[7:8])
    low = low + jnp.where(lane == HALF, pltpu.roll(second, LANES - 1, 1), pltpu.roll(second, LANES - 7, 1))
    for n, value in enumerate((first, second, low)):
        spread[LANES * n : LANES * n + LANES, :] = jnp.transpose(jnp.broadcast_to(value, (LANES, LANES)))

    def row(n):
        return spread[place(n) : place(n) + 1, :]

    def moment(n):
        at = LANES + (MOM_LANE + n if n < 7 else HALF)
        return quick_sum(spread[at : at + 1, :], spread[LANES + at : LANES + at + 1, :])

    mix = solve_krylov([moment(n) for n in range(8)])

    def s_s(i, j):
        return row(ROW_GRAM + PAIR_ROW[min(i, j), max(i, j)])

    def y_y(i, j):
        return row(ROW_GRAM + 36 + PAIR_ROW[min(i, j), max(i, j)])

    def s_y(i, j):
        return row(ROW_GRAM + 72 + 8 * i + j)

    pairs = range(HIST)
    theta, rest, inverse = [], [], []
    for i in pairs:
        curv, norm = s_y(i, i), s_s(i, i)
        kept = (1.0 - damp_floor) * norm
        damp = jnp.where(curv >= damp_floor * norm, 1.0, kept / jnp.maximum(norm - curv, kept))
        theta.append(damp)
        rest.append(1.0 - damp)
        inverse.append(1.0 / (damp * curv + (1.0 - damp) * norm))

    def s_bar(i, j):
        return theta[j] * s_y(i, j) + rest[j] * s_s(i, j)

    def bar_bar(i, j):
        return theta[i] * (theta[j] * y_y(i, j) + rest[j] * s_y(j, i)) + rest[i] * s_bar(i, j)

    last = HIST - 1
    scaling = s_bar(last, last) / bar_bar(last, last)

    def energy(n):
        value = row(ROW_BASE + 16 + n)
        for j in range(4):
            value = value + mix[j] * row(ROW_W + 17 * j + n)
        return value

    chem = energy(16) / row(ROW_BASE + 33)

    def gradient(n):
        return energy(n) - chem * row(ROW_BASE + n)

    s_grad = [gradient(i) for i in pairs]
    bar_grad = [theta[i] * gradient(HIST + i) + rest[i] * s_grad[i] for i in pairs]

    first = [None] * HIST
    pending = list(s_grad)
    for j in reversed(pairs):
        first[j] = inverse[j] * pending[j]
        for i in range(j):
            pending[i] = pending[i] - first[j] * s_bar(i, j)
    pending = list(bar_grad)
    for j in pairs:
        for i in pairs:
            pending[i] = pending[i] - first[j] * bar_bar(i, j)
    pending = [scaling * value for value in pending]
    step_mix, change_mix = [], []
    for j in pairs:
        net = first[j] - inverse[j] * pending[j]
        for i in range(j + 1, HIST):
            pending[i] = pending[i] + net * s_bar(j, i)
        change_mix.append((-step_length) * (-scaling * first[j] * theta[j]))
        step_mix.append((-step_length) * (net - scaling * first[j] * rest[j]))

    wide = lambda value: jnp.broadcast_to(value, (8, LANES))
    mix = [wide(value) for value in mix]
    chem, gain = wide(chem), wide((-step_length) * scaling)
    step_mix = [wide(value) for value in step_mix]
    change_mix = [wide(value) for value in change_mix]
    basis = (v0, v1, v2, v3)

    def leave(i):
        return [
            pltpu.make_async_copy(here.at[i], out.at[i], sems.at[n, i])
            for n, (here, out) in enumerate(((density_here, new_density), (hartree_here, new_hartree)))
        ]

    for i in range(REACH):
        for b in range(8):
            at = pl.ds(8 * b, 8)
            rho = both[REACH + i, at, :]
            lift = mix[0] * v0[i, at, :]
            for j in range(1, 4):
                lift = lift + mix[j] * basis[j][i, at, :]
            hartree_here[i, at, :] = both[i, at, :] + lift
            slope = grad[i, at, :] + 2.0 * rho * lift - chem * rho
            parts = [rho, gain * slope, step_mix[0] * steps[0, i, at, :], change_mix[0] * changes[0, i, at, :]]
            for f in range(1, HIST):
                parts[2] = parts[2] + step_mix[f] * steps[f, i, at, :]
                parts[3] = parts[3] + change_mix[f] * changes[f, i, at, :]
            density_here[i, at, :] = parts[0] + (parts[1] + (parts[2] + parts[3]))
        for copy in leave(i):
            copy.start()
    for i in range(REACH):
        for copy in leave(i):
            copy.wait()


def call(kernel, outs, args, scratch=(), flops=0, in_hbm=(), out_hbm=False):
    args = [pltpu.with_memory_space_constraint(x, pltpu.HBM) if n in in_hbm else x for n, x in enumerate(args)]
    shapes = [jax.ShapeDtypeStruct(shape, jnp.float32) for shape in outs]
    size = sum(4 * math.prod(a.shape) for a in (*args, *shapes))
    return pl.pallas_call(
        kernel,
        out_shape=shapes,
        in_specs=[pl.BlockSpec(memory_space=pltpu.HBM if n in in_hbm else pltpu.VMEM) for n in range(len(args))],
        out_specs=[pl.BlockSpec(memory_space=pltpu.HBM if out_hbm else pltpu.VMEM)] * len(outs),
        scratch_shapes=[pltpu.VMEM(s, jnp.float32) if isinstance(s, tuple) else s for s in scratch],
        cost_estimate=pl.CostEstimate(flops=flops, bytes_accessed=size, transcendentals=0),
        compiler_params=pltpu.CompilerParams(vmem_limit_bytes=VMEM_LIMIT),
    )(*args)


def ring(axis, step):
    size = lax.axis_size(axis)
    return [(i, (i + step) % size) for i in range(size)]


def swap(axis, odd_up):
    size = lax.axis_size(axis)
    return [(i, (i + (1 if i % 2 == odd_up else -1)) % size) for i in range(size)]


def after(values, *earlier):
    return lax.optimization_barrier((tuple(values), earlier))[0]


def x_halo(block):
    far = lax.ppermute(block, "blk", swap("blk", 1))
    return (lax.ppermute(block, "blk", swap("blk", 0)), far)


def z_halo(face_a, face_b):
    return (lax.ppermute(face_a, "gz", swap("gz", 0)), lax.ppermute(face_b, "gz", swap("gz", 1)))


def on_device(sqrt_density, ion_charge, ion_potential, hartree_prev, hist_steps, hist_changes):
    block = sqrt_density.shape
    ext = (block[0], block[1] + 16, block[2])
    face = (24, LANES)
    cells = math.prod(block)
    cells = math.prod(block)
    work = 300 * cells
    inputs = (hartree_prev, sqrt_density, ion_charge)
    halo = x_halo(hartree_prev)
    both, charge, *faces = call(
        launch_kernel,
        [(2 * REACH, *block[1:]), block, (48, LANES), (48, LANES)],
        inputs,
        [pltpu.SemaphoreType.DMA((3,))],
        in_hbm=(0, 1, 2),
    )
    ends = z_halo(*faces)
    density_ends = ends
    half = (REACH, block[1] // 2, LANES)

    def advance(gain, inner, halo, ends, last=False):
        (mid,) = call(functools.partial(z_kernel, gain), [block], [inner, *ends], flops=work)
        return call(
            functools.partial(last_x_kernel if last else x_kernel, gain),
            [block, half, half] if last else [block],
            [mid, *halo],
            flops=work,
        )

    def exchange(block_now):
        halo = x_halo(block_now)
        return halo, z_halo(*call(pack_kernel, [face, face], [block_now], flops=work))

    stored = hist_steps.shape
    inner, *history, r1 = call(
        side_one,
        [block, stored, stored, (80, LANES)],
        [both, charge, hist_steps, hist_changes],
        [ext, pltpu.SemaphoreType.DMA((2 * FETCHES,))],
        work,
        in_hbm=(2, 3),
    )
    (v0,) = advance(1.0, inner, halo, ends)
    halo, ends = exchange(v0)
    density_halo = x_halo(after((sqrt_density,), v0)[0])
    (inner,) = call(side_two, [block], [v0], [ext], work)
    (v1,) = advance(-1.0 / SHIFT, inner, halo, ends)
    halo, ends = exchange(v1)
    inner, grad, r3, m3 = call(
        side_three,
        [block, block, (72, LANES), (8, LANES)],
        [v0, v1, both, *density_halo, *density_ends, ion_potential, *history],
        [ext],
        work,
    )
    (v2,) = advance(-2.0 / SHIFT, inner, halo, ends)
    halo, ends = exchange(v2)
    inner, sums = call(
        side_four,
        [block, (2, LANES)],
        [v1, v2, both, grad, *history, r1, r3, m3],
        [(80, LANES), (8, LANES), (2 * LANES, LANES), ext],
        work,
    )
    v3, to_near, to_far = advance(-2.0 / SHIFT, inner, halo, ends, last=True)
    far = lax.ppermute(to_far, "blk", swap("blk", 1))
    near = lax.ppermute(to_near, "blk", swap("blk", 0))
    (upper,) = call(pack_upper_kernel, [face], [v3], flops=work)
    z_left = lax.ppermute(upper, "gz", ring("gz", 1))
    kept, given = call(
        side_five,
        [(1, LANES), (1, LANES)],
        [v2, v3, both, *history, sums],
        [(LANES, LANES), (8, LANES)],
        work,
    )
    taken = lax.ppermute(given, "blk", swap("blk", 0))
    (inner,) = call(inner_moment_kernel, [(8, LANES)], [after((v3,), given)[0]], [ext], work)
    devices = lax.axis_size("blk") * lax.axis_size("gz")
    (outgoing,) = call(send_kernel, [(devices, LANES)], [v3, far, near, z_left, inner, kept, taken], flops=work)
    received = lax.all_to_all(outgoing.reshape(devices, 1, LANES), ("blk", "gz"), 0, 0, tiled=True)
    return tuple(
        call(
            final_kernel,
            [block, block],
            [received.reshape(devices, LANES), both, grad, v0, v1, v2, v3, *history],
            [(3 * LANES, LANES), block, block, pltpu.SemaphoreType.DMA((2, REACH))],
            work,
            out_hbm=True,
        )
    )


def solution(mesh):
    placed = (
        P("blk", None, "gz"),
        P("blk", None, "gz"),
        P("blk", None, "gz"),
        P("blk", None, "gz"),
        P(None, "blk", None, "gz"),
        P(None, "blk", None, "gz"),
    )
    return jax.shard_map(
        on_device,
        mesh=mesh,
        in_specs=placed,
        out_specs=(P("blk", None, "gz"), P("blk", None, "gz")),
        check_vma=False,
    )
```
